32 devices in a mesh: band: 4 (over y, x), stream: 8 (over z, core).
Axes of the slice: x: 2, y: 2, z: 4, core: 2. Of those that a mesh axis runs over, the one named last changes fastest.
Arguments:
- spectrum: float32 [512, 2, 1025], P('stream'), may hold values from -6 to 6
- segments: int32 [8, 64], P('stream'), may hold values from 0 to 2, never falling along the last dimension, each value on 1 to 32 neighbouring positions
- widths: int32 [41], replicated, may hold values from 1 to 128, 1025 in all
- groups: int32 [41], replicated, may hold values from 0 to 3, as said below
- cotangent: float32 [512, 48, 2, 128], P('stream', 'band'), may hold values from -6 to 6
- splitter: float32 [48, 256, 128], P('band', 'stream'), may hold values from -0.375 to 0.375
- widener: float32 [48, 128, 512], P('band', None, 'stream'), may hold values from -0.5 to 0.5
- masker: float32 [48, 512, 512], P('band', 'stream'), may hold values from -0.25 to 0.25
- banding: float32 [48, 1920], P('band', 'stream'), may hold values from -1.5 to 1.5
- intake: float32 [2, 2, 128, 1024], P(None, None, None, 'stream'), may hold values from -0.5 to 0.5
- recurrence: float32 [2, 2, 256, 1024], P(None, None, None, 'stream'), may hold values from -0.375 to 0.375
- outtake: float32 [2, 512, 128], P(None, 'stream'), may hold values from -0.25 to 0.25
- scalers: float32 [2, 2432], P(None, 'stream'), may hold values from -1.5 to 1.5
- splitter_first_moment: float32 [48, 256, 128], P('band', 'stream'), may hold values from -0.001953125 to 0.001953125
- widener_first_moment: float32 [48, 128, 512], P('band', None, 'stream'), may hold values from -0.001953125 to 0.001953125
- masker_first_moment: float32 [48, 512, 512], P('band', 'stream'), may hold values from -0.001953125 to 0.001953125
- banding_first_moment: float32 [48, 1920], P('band', 'stream'), may hold values from -0.0068359375 to 0.0068359375
- intake_mean: float32 [2, 2, 128, 1024], P(None, None, None, 'stream'), may hold values from -0.001953125 to 0.001953125
- recurrence_mean: float32 [2, 2, 256, 1024], P(None, None, None, 'stream'), may hold values from -0.001953125 to 0.001953125
- outtake_mean: float32 [2, 512, 128], P(None, 'stream'), may hold values from -0.001953125 to 0.001953125
- scalers_mean: float32 [2, 2432], P(None, 'stream'), may hold values from -0.0068359375 to 0.0068359375
- splitter_second_moment: float32 [48, 256, 128], P('band', 'stream'), may hold values from 6.5436584e-10 to 1.0469853e-08
- widener_second_moment: float32 [48, 128, 512], P('band', None, 'stream'), may hold values from 6.5436584e-10 to 1.0469853e-08
- masker_second_moment: float32 [48, 512, 512], P('band', 'stream'), may hold values from 6.5436584e-10 to 1.0469853e-08
- banding_second_moment: float32 [48, 1920], P('band', 'stream'), may hold values from 2.0939707e-08 to 3.1409562e-07
- intake_power: float32 [2, 2, 128, 1024], P(None, None, None, 'stream'), may hold values from 6.5436584e-10 to 1.0469853e-08
- recurrence_power: float32 [2, 2, 256, 1024], P(None, None, None, 'stream'), may hold values from 6.5436584e-10 to 1.0469853e-08
- outtake_power: float32 [2, 512, 128], P(None, 'stream'), may hold values from 6.5436584e-10 to 1.0469853e-08
- scalers_power: float32 [2, 2432], P(None, 'stream'), may hold values from 2.0939707e-08 to 3.1409562e-07
Outputs:
- masks: float32 [512, 48, 2, 128], P('stream', 'band')
- spectrum_grad: float32 [512, 2, 1025], P('stream')
- grad_norm: float32 [], replicated
- fresh_splitter: float32 [48, 256, 128], P('band', 'stream')
- fresh_widener: float32 [48, 128, 512], P('band', None, 'stream')
- fresh_masker: float32 [48, 512, 512], P('band', 'stream')
- fresh_banding: float32 [48, 1920], P('band', 'stream')
- fresh_intake: float32 [2, 2, 128, 1024], P(None, None, None, 'stream')
- fresh_recurrence: float32 [2, 2, 256, 1024], P(None, None, None, 'stream')
- fresh_outtake: float32 [2, 512, 128], P(None, 'stream')
- fresh_scalers: float32 [2, 2432], P(None, 'stream')
- mean_splitter: float32 [48, 256, 128], P('band', 'stream')
- mean_widener: float32 [48, 128, 512], P('band', None, 'stream')
- mean_masker: float32 [48, 512, 512], P('band', 'stream')
- mean_banding: float32 [48, 1920], P('band', 'stream')
- mean_intake: float32 [2, 2, 128, 1024], P(None, None, None, 'stream')
- mean_recurrence: float32 [2, 2, 256, 1024], P(None, None, None, 'stream')
- mean_outtake: float32 [2, 512, 128], P(None, 'stream')
- mean_scalers: float32 [2, 2432], P(None, 'stream')
- power_splitter: float32 [48, 256, 128], P('band', 'stream')
- power_widener: float32 [48, 128, 512], P('band', None, 'stream')
- power_masker: float32 [48, 512, 512], P('band', 'stream')
- power_banding: float32 [48, 1920], P('band', 'stream')
- power_intake: float32 [2, 2, 128, 1024], P(None, None, None, 'stream')
- power_recurrence: float32 [2, 2, 256, 1024], P(None, None, None, 'stream')
- power_outtake: float32 [2, 512, 128], P(None, 'stream')
- power_scalers: float32 [2, 2432], P(None, 'stream')
The draws below stay inside these ranges and needn't reach their ends.
Inputs may be any that keep to these rules, and one draw needn't show every extreme that they name: Each of the 4 groups holds 1 to 12 bands, and one group holds exactly 12. `segments`: in each stream the clip number never falls; each clip has 1 to 32 frames. The widths sum to 1025; the widest band has exactly 128 bins.
All inputs are finite; a program needn't handle non-finite values.
Results may differ from the reference program's by a relative error of at most 0.0003.
Values sent between devices are 32-bit elements; how exact they have to be, the bound alone decides.
A program may use at most 256 MiB of HBM per device.

```python
import math
import jax
import jax.numpy as jnp
import numpy as np
from jax import lax

EMBED_FEATURES = 128
H = 256
MASK_HIDDEN = 512
NB = 41
F = 1025
WIDEST_BINS = 128
SLOTS = 12
SEGS = 3
STEP = 10
STREAM_FRAMES = 64
SEG_MOST = 32
STREAMS = 8
ALL_FRAMES = 512
SLOT_TOTAL = 48
BAND_VECTOR = 1920
RVEC = 2432
PARAM_TOTAL = 19102464
N_BAND = 4
N_STREAM = 8


def draw_groups(key, part):
    ordering = jax.random.permutation(jax.random.fold_in(key, 11), NB)
    busiest = jax.random.randint(jax.random.fold_in(key, 12), (), 0, N_BAND)
    rotation = jax.random.randint(jax.random.fold_in(key, 13), (), 0, N_BAND - 1)
    position = jnp.arange(NB, dtype=jnp.int32)
    others = (position - SLOTS + rotation) % (N_BAND - 1)
    target = jnp.where(position < SLOTS, busiest, (busiest + 1 + others) % N_BAND).astype(jnp.int32)
    return jnp.zeros((NB,), jnp.int32).at[ordering].set(target)


def block_levels(stream_key, shape, shards, low, top_value):
    def one(dim, blocks):
        steps = jax.random.uniform(jax.random.fold_in(jax.random.fold_in(stream_key, 6), dim), (blocks,), jnp.float32, low / len(shards), top_value / len(shards))
        return jnp.repeat(jnp.exp(steps), shape[dim] // blocks).reshape((-1,) + (1,) * (len(shape) - dim - 1))

    level = one(*shards[0])
    for cut in shards[1:]:
        level = level * one(*cut)
    return level


def split_up(count, total, reach, lean):
    loads = [(1 << 20) // math.isqrt(rank ** lean) + 1 for rank in range(2, count + 1)]
    surplus, counts = total - reach - (count - 1), [1] * (count - 1)
    while surplus > 0:
        movable = [i for i in range(count - 1) if counts[i] < reach]
        whole, remaining = sum([loads[i] for i in movable]), surplus
        for i in movable:
            more = min(reach - counts[i], max(1, remaining * loads[i] // whole), surplus)
            counts[i] = counts[i] + more
            surplus = surplus - more
    return np.array([reach] + counts)


def uneven(own_key, count, total, limit, skew):
    if count == 2:
        one = jax.random.randint(own_key, (), max(1, total - limit), min(limit, total - 1) + 1)
        return jnp.stack([one, total - one])
    lengths = jnp.asarray(split_up(count, total, limit, skew), jnp.int32)
    twos = (count - 1) // 2
    source_of, receiver = lengths[1:1 + 2 * twos:2], lengths[2:2 + 2 * twos:2]
    slack = jnp.minimum(source_of - 1, limit - receiver)
    passed = jax.random.randint(jax.random.fold_in(own_key, 1), (twos,), 0, 1 << 20) % (slack + 1)
    lengths = lengths.at[1:1 + 2 * twos:2].set(source_of - passed).at[2:2 + 2 * twos:2].set(receiver + passed)
    return lengths[jax.random.permutation(jax.random.fold_in(own_key, 2), count)]


def normal_values(stream_key, extent, scale, limit, split=(), held_as=jnp.bfloat16):
    level = block_levels(stream_key, extent, split, -0.22, 0.18) if split else 1.0
    drawn = jax.random.normal(stream_key, extent, jnp.float32) * scale * level
    return jnp.minimum(jnp.maximum(drawn, -limit), limit).astype(held_as)


def setup_inputs(seed: int = 0) -> dict:
    key_list = jax.random.split(jax.random.key(seed), 30)
    return {
        "spectrum": normal_values(key_list[0], (ALL_FRAMES, 2, F), 1.0, 6.0, ((0, 8),), jnp.float32),
        "segments": jax.vmap(lambda own: jnp.searchsorted(jnp.cumsum(uneven(own, SEGS, STREAM_FRAMES, SEG_MOST, 0)), jnp.arange(STREAM_FRAMES), side="right"))(jax.random.split(key_list[1], STREAMS)).reshape((STREAMS, STREAM_FRAMES)).astype(jnp.int32),
        "widths": uneven(key_list[2], NB, F, WIDEST_BINS, 2).astype(jnp.int32),
        "groups": draw_groups(jax.random.fold_in(key_list[29], 71), 0),
        "cotangent": normal_values(key_list[4], (ALL_FRAMES, SLOT_TOTAL, 2, WIDEST_BINS), 1.0, 6.0, ((0, 8), (1, 4)), jnp.float32),
        "splitter": normal_values(key_list[5], (SLOT_TOTAL, 2 * WIDEST_BINS, EMBED_FEATURES), (2 * WIDEST_BINS) ** -0.5, 0.375, ((0, 4), (1, 8)), jnp.float32),
        "widener": normal_values(key_list[6], (SLOT_TOTAL, EMBED_FEATURES, MASK_HIDDEN), EMBED_FEATURES ** -0.5, 0.5, ((0, 4), (2, 8)), jnp.float32),
        "masker": normal_values(key_list[7], (SLOT_TOTAL, MASK_HIDDEN, 4 * WIDEST_BINS), MASK_HIDDEN ** -0.5, 0.25, ((0, 4), (1, 8)), jnp.float32),
        "banding": normal_values(key_list[8], (SLOT_TOTAL, BAND_VECTOR), 0.3, 1.5, ((0, 4), (1, 8)), jnp.float32),
        "intake": normal_values(key_list[9], (2, 2, EMBED_FEATURES, 4 * H), EMBED_FEATURES ** -0.5, 0.5, ((3, 8),), jnp.float32),
        "recurrence": normal_values(key_list[10], (2, 2, H, 4 * H), H ** -0.5, 0.375, ((3, 8),), jnp.float32),
        "outtake": normal_values(key_list[11], (2, 2 * H, EMBED_FEATURES), (2 * H) ** -0.5, 0.25, ((1, 8),), jnp.float32),
        "scalers": normal_values(key_list[12], (2, RVEC), 0.3, 1.5, ((1, 8),), jnp.float32),
        "splitter_first_moment": normal_values(key_list[13], (SLOT_TOTAL, 2 * WIDEST_BINS, EMBED_FEATURES), (0.55 / PARAM_TOTAL ** 0.5), 0.001953125, ((0, 4), (1, 8)), jnp.float32),
        "widener_first_moment": normal_values(key_list[14], (SLOT_TOTAL, EMBED_FEATURES, MASK_HIDDEN), (0.55 / PARAM_TOTAL ** 0.5), 0.001953125, ((0, 4), (2, 8)), jnp.float32),
        "masker_first_moment": normal_values(key_list[15], (SLOT_TOTAL, MASK_HIDDEN, 4 * WIDEST_BINS), (0.55 / PARAM_TOTAL ** 0.5), 0.001953125, ((0, 4), (1, 8)), jnp.float32),
        "banding_first_moment": normal_values(key_list[16], (SLOT_TOTAL, BAND_VECTOR), (2.0 / PARAM_TOTAL ** 0.5), 0.0068359375, ((0, 4), (1, 8)), jnp.float32),
        "intake_mean": normal_values(key_list[17], (2, 2, EMBED_FEATURES, 4 * H), (0.55 / PARAM_TOTAL ** 0.5), 0.001953125, ((3, 8),), jnp.float32),
        "recurrence_mean": normal_values(key_list[18], (2, 2, H, 4 * H), (0.55 / PARAM_TOTAL ** 0.5), 0.001953125, ((3, 8),), jnp.float32),
        "outtake_mean": normal_values(key_list[19], (2, 2 * H, EMBED_FEATURES), (0.55 / PARAM_TOTAL ** 0.5), 0.001953125, ((1, 8),), jnp.float32),
        "scalers_mean": normal_values(key_list[20], (2, RVEC), (2.0 / PARAM_TOTAL ** 0.5), 0.0068359375, ((1, 8),), jnp.float32),
        "splitter_second_moment": jnp.clip(jnp.exp(math.log(1.0469853428674014e-08) - 2.7725887 * jax.random.uniform(key_list[21], (SLOT_TOTAL, 2 * WIDEST_BINS, EMBED_FEATURES), jnp.float32) ** block_levels(key_list[21], (SLOT_TOTAL, 2 * WIDEST_BINS, EMBED_FEATURES), ((0, 4), (1, 8)), -0.2, 0.2)), 6.543658392921259e-10, 1.0469853428674014e-08),
        "widener_second_moment": jnp.clip(jnp.exp(math.log(1.0469853428674014e-08) - 2.7725887 * jax.random.uniform(key_list[22], (SLOT_TOTAL, EMBED_FEATURES, MASK_HIDDEN), jnp.float32) ** block_levels(key_list[22], (SLOT_TOTAL, EMBED_FEATURES, MASK_HIDDEN), ((0, 4), (2, 8)), -0.2, 0.2)), 6.543658392921259e-10, 1.0469853428674014e-08),
        "masker_second_moment": jnp.clip(jnp.exp(math.log(1.0469853428674014e-08) - 2.7725887 * jax.random.uniform(key_list[23], (SLOT_TOTAL, MASK_HIDDEN, 4 * WIDEST_BINS), jnp.float32) ** block_levels(key_list[23], (SLOT_TOTAL, MASK_HIDDEN, 4 * WIDEST_BINS), ((0, 4), (1, 8)), -0.2, 0.2)), 6.543658392921259e-10, 1.0469853428674014e-08),
        "banding_second_moment": jnp.clip(jnp.exp(math.log(3.140956152947183e-07) - 2.7080502 * jax.random.uniform(key_list[24], (SLOT_TOTAL, BAND_VECTOR), jnp.float32) ** block_levels(key_list[24], (SLOT_TOTAL, BAND_VECTOR), ((0, 4), (1, 8)), -0.2, 0.2)), 2.0939706857348028e-08, 3.140956152947183e-07),
        "intake_power": jnp.clip(jnp.exp(math.log(1.0469853428674014e-08) - 2.7725887 * jax.random.uniform(key_list[25], (2, 2, EMBED_FEATURES, 4 * H), jnp.float32) ** block_levels(key_list[25], (2, 2, EMBED_FEATURES, 4 * H), ((3, 8),), -0.2, 0.2)), 6.543658392921259e-10, 1.0469853428674014e-08),
        "recurrence_power": jnp.clip(jnp.exp(math.log(1.0469853428674014e-08) - 2.7725887 * jax.random.uniform(key_list[26], (2, 2, H, 4 * H), jnp.float32) ** block_levels(key_list[26], (2, 2, H, 4 * H), ((3, 8),), -0.2, 0.2)), 6.543658392921259e-10, 1.0469853428674014e-08),
        "outtake_power": jnp.clip(jnp.exp(math.log(1.0469853428674014e-08) - 2.7725887 * jax.random.uniform(key_list[27], (2, 2 * H, EMBED_FEATURES), jnp.float32) ** block_levels(key_list[27], (2, 2 * H, EMBED_FEATURES), ((1, 8),), -0.2, 0.2)), 6.543658392921259e-10, 1.0469853428674014e-08),
        "scalers_power": jnp.clip(jnp.exp(math.log(3.140956152947183e-07) - 2.7080502 * jax.random.uniform(key_list[28], (2, RVEC), jnp.float32) ** block_levels(key_list[28], (2, RVEC), ((1, 8),), -0.2, 0.2)), 2.0939706857348028e-08, 3.140956152947183e-07),
    }


CLIP_NORM = 5.0
LEARN_RATE = 0.5
BETA_ONE = 0.9
BETA_TWO = 0.999
ADAM_EPS = 1e-06
DECAY_RATE = 0.01
NORM_EPS = 1e-05
VAR_FLOOR = 0.25
MATMUL_PRECISION = lax.Precision.HIGHEST

def group_norm(values, gain_raw, shift):
    center = values - lax.optimization_barrier(jnp.mean(values, axis=-1, keepdims=True))
    spread = lax.optimization_barrier(jnp.mean(center * center, axis=-1, keepdims=True))
    return center * lax.rsqrt(spread + NORM_EPS) * (1.0 + gain_raw) + shift

def band_valid(band_widths, wmax):
    offsets = jnp.arange(wmax, dtype=jnp.int32)
    inside = (offsets[None, :] < band_widths[:, None]).astype(jnp.float32)
    return jnp.concatenate([inside, inside], axis=1)

def split_forward(spectrum, weight_matrix, vectors, edges, band_widths, wmax, dmodel):
    frames = spectrum.shape[0]
    counted = edges.shape[0]
    offsets = jnp.arange(wmax, dtype=jnp.int32)
    index = jnp.minimum(edges[:, None] + offsets[None, :], spectrum.shape[2] - 1).astype(jnp.int32)
    taken = jnp.take(spectrum, index.reshape(-1), axis=2)
    taken = taken.reshape(frames, 2, counted, wmax).transpose(0, 2, 1, 3).reshape(frames, counted, 2 * wmax)
    valid = band_valid(band_widths, wmax)
    entries = jnp.maximum(2 * band_widths, 1).astype(jnp.float32)
    center_mean = lax.optimization_barrier(jnp.sum(taken * valid, axis=-1)) / entries
    center = (taken - center_mean[..., None]) * valid
    spread = lax.optimization_barrier(jnp.sum(center * center, axis=-1)) / entries
    width_two = 2 * wmax
    scaled = center * lax.rsqrt(jnp.maximum(spread, VAR_FLOOR))[..., None]
    normalized_rows = (scaled * (1.0 + vectors[:, :width_two]) + vectors[:, width_two:2 * width_two]) * valid
    projected_rows = jnp.einsum('vwc,wco->vwo', normalized_rows, weight_matrix, precision=MATMUL_PRECISION)
    return projected_rows + vectors[:, 2 * width_two:2 * width_two + dmodel]

def module_gates(values, vector, w_in, dmodel, hidden):
    normalized_rows = group_norm(values, vector[:dmodel], vector[dmodel:2 * dmodel])
    gates = jnp.einsum('lbd,edk->lebk', normalized_rows, w_in, precision=MATMUL_PRECISION)
    gates = gates + vector[2 * dmodel:2 * dmodel + 8 * hidden].reshape(2, 1, 4 * hidden)
    return jnp.stack([gates[:, 0], jnp.flip(gates[:, 1], 0)], axis=1)

def module_output(values, states, w_out, vector, dmodel, hidden):
    joined = jnp.concatenate([states[:, 0], jnp.flip(states[:, 1], 0)], axis=-1)
    mixed_in = jnp.einsum('lbj,jd->lbd', joined, w_out, precision=MATMUL_PRECISION)
    return values + mixed_in + vector[2 * dmodel + 8 * hidden:]

def recur_states(gates, w_rec, keep):
    hidden = w_rec.shape[1]
    start = jnp.zeros((2, gates.shape[2], hidden), jnp.float32)

    def advance(carry, inputs):
        states, memory = carry
        drive, kept = inputs
        prior = states * kept[:, None, None]
        total = drive + jnp.einsum('ebh,ehk->ebk', prior, w_rec, precision=MATMUL_PRECISION)
        ingate = jax.nn.sigmoid(total[..., :hidden])
        forget = jax.nn.sigmoid(total[..., hidden:2 * hidden])
        candidate = jnp.tanh(total[..., 2 * hidden:3 * hidden])
        outgate = jax.nn.sigmoid(total[..., 3 * hidden:])
        memory_new = forget * memory * kept[:, None, None] + ingate * candidate
        states_new = outgate * jnp.tanh(memory_new)
        return ((states_new, memory_new), states_new)
    unused, states_all = lax.scan(advance, (start, start), (gates, keep))
    return states_all

def module_forward(values, vector, w_in, w_rec, w_out, keep, dmodel, hidden):
    gates = module_gates(values, vector, w_in, dmodel, hidden)
    states = recur_states(gates, w_rec, keep)
    return module_output(values, states, w_out, vector, dmodel, hidden)

def mask_forward(values, vectors, w_wide, w_mask, valid, wmax, dmodel, mlp):
    width_two = 2 * wmax
    base = 2 * width_two + dmodel
    normalized_rows = group_norm(values, vectors[:, base:base + dmodel], vectors[:, base + dmodel:base + 2 * dmodel])
    widened = jnp.einsum('tsd,sdm->tsm', normalized_rows, w_wide, precision=MATMUL_PRECISION)
    widened = jnp.tanh(widened + vectors[:, base + 2 * dmodel:base + 2 * dmodel + mlp])
    raw_out = jnp.einsum('tsm,smk->tsk', widened, w_mask, precision=MATMUL_PRECISION)
    raw_out = raw_out + vectors[:, base + 2 * dmodel + mlp:]
    result = raw_out[..., :width_two] * jax.nn.sigmoid(raw_out[..., width_two:]) * valid
    return result.reshape(values.shape[0], values.shape[1], 2, wmax)

def keep_flags(segment_row):
    same = (segment_row[1:] == segment_row[:-1]).astype(jnp.float32)
    leading = jnp.zeros((1,), jnp.float32)
    return jnp.stack([jnp.concatenate([leading, same]), jnp.concatenate([leading, jnp.flip(same, 0)])], axis=1)

def lamb_moments(gradient, mean_old, power_old, factor):
    clipped = gradient * factor
    mean_new = BETA_ONE * mean_old + (1.0 - BETA_ONE) * clipped
    power_new = BETA_TWO * power_old + (1.0 - BETA_TWO) * clipped * clipped
    return (mean_new, power_new)

def lamb_direction(weight_matrix, mean_new, power_new, decay):
    corrected = mean_new / (1.0 - BETA_ONE ** STEP)
    scale_root = jnp.sqrt(power_new / (1.0 - BETA_TWO ** STEP)) + ADAM_EPS
    return corrected / scale_root + decay * weight_matrix

def reference(spectrum, segments, widths, groups, cotangent, splitter, widener, masker, banding, intake, recurrence, outtake, scalers, splitter_first_moment, widener_first_moment, masker_first_moment, banding_first_moment, intake_mean, recurrence_mean, outtake_mean, scalers_mean, splitter_second_moment, widener_second_moment, masker_second_moment, banding_second_moment, intake_power, recurrence_power, outtake_power, scalers_power):
    members = (groups[:, None] == jnp.arange(N_BAND, dtype=jnp.int32)[None, :]).astype(jnp.int32)
    ranking = lax.optimization_barrier(jnp.sum(jnp.cumsum(members, axis=0) * members, axis=1)) - 1
    band_slot_index = (groups * SLOTS + ranking).astype(jnp.int32)
    edges = (jnp.cumsum(widths) - widths).astype(jnp.int32)
    valid = band_valid(widths, WIDEST_BINS)
    band_keep = jnp.ones((NB, 2), jnp.float32)

    def forward(params, spectrum_row, time_keep):
        w_split, w_wide, w_mask, v_band, w_in, w_rec, w_out, v_rnn = params
        embedded = split_forward(spectrum_row, w_split[band_slot_index], v_band[band_slot_index], edges, widths, WIDEST_BINS, EMBED_FEATURES)
        time_out = module_forward(embedded, v_rnn[0], w_in[0], w_rec[0], w_out[0], time_keep, EMBED_FEATURES, H)
        band_out = module_forward(jnp.transpose(time_out, (1, 0, 2)), v_rnn[1], w_in[1], w_rec[1], w_out[1], band_keep, EMBED_FEATURES, H)
        mixed = jnp.transpose(band_out, (1, 0, 2))
        per_band_masks = mask_forward(mixed, v_band[band_slot_index], w_wide[band_slot_index], w_mask[band_slot_index], valid, WIDEST_BINS, EMBED_FEATURES, MASK_HIDDEN)
        return jnp.zeros((spectrum_row.shape[0], SLOT_TOTAL, 2, WIDEST_BINS), jnp.float32).at[:, band_slot_index].set(per_band_masks)
    params = (splitter, widener, masker, banding, intake, recurrence, outtake, scalers)
    spec_rows = spectrum.reshape(N_STREAM, STREAM_FRAMES, 2, F)
    cotangent_rows = cotangent.reshape(N_STREAM, STREAM_FRAMES, SLOT_TOTAL, 2, WIDEST_BINS)

    def one_stream(totals, inputs):
        spectrum_row, segment_row, cot_row = inputs
        time_keep = keep_flags(segment_row)
        outputs, pullback = jax.vjp(lambda weights_in, spec_in: forward(weights_in, spec_in, time_keep), params, spectrum_row)
        grad_params, grad_spec = pullback(cot_row)
        totals = jax.tree.map(jnp.add, totals, grad_params)
        return (totals, (outputs, grad_spec))
    start = jax.tree.map(jnp.zeros_like, params)
    grads, (mask_row_values, grad_rows) = lax.scan(one_stream, start, (spec_rows, segments, cotangent_rows))
    masks = mask_row_values.reshape(ALL_FRAMES, SLOT_TOTAL, 2, WIDEST_BINS)
    spectrum_grad = grad_rows.reshape(ALL_FRAMES, 2, F)
    squares = jnp.float32(0.0)
    for gradient in grads:
        squares = squares + jnp.sum(gradient * gradient)
    grad_norm = jnp.sqrt(squares)
    factor = jnp.minimum(1.0, CLIP_NORM / grad_norm)
    means_old = (splitter_first_moment, widener_first_moment, masker_first_moment, banding_first_moment, intake_mean, recurrence_mean, outtake_mean, scalers_mean)
    powers_old = (splitter_second_moment, widener_second_moment, masker_second_moment, banding_second_moment, intake_power, recurrence_power, outtake_power, scalers_power)
    decays = (DECAY_RATE, DECAY_RATE, DECAY_RATE, 0.0, DECAY_RATE, DECAY_RATE, DECAY_RATE, 0.0)
    fresh_list = []
    mean_list = []
    power_list = []
    for position in range(8):
        mean_new, power_new = lamb_moments(grads[position], means_old[position], powers_old[position], factor)
        direction = lamb_direction(params[position], mean_new, power_new, decays[position])
        weight_norm = jnp.sqrt(jnp.sum(params[position] * params[position]))
        ratio = weight_norm / jnp.sqrt(jnp.sum(direction * direction) + 1e-12)
        fresh_list.append(params[position] - LEARN_RATE * ratio * direction)
        mean_list.append(mean_new)
        power_list.append(power_new)
    return (masks, spectrum_grad, grad_norm, fresh_list[0], fresh_list[1], fresh_list[2], fresh_list[3], fresh_list[4], fresh_list[5], fresh_list[6], fresh_list[7], mean_list[0], mean_list[1], mean_list[2], mean_list[3], mean_list[4], mean_list[5], mean_list[6], mean_list[7], power_list[0], power_list[1], power_list[2], power_list[3], power_list[4], power_list[5], power_list[6], power_list[7])
```

```python
from functools import partial
import math

import jax
import jax.numpy as jnp
from jax import lax
from jax.experimental import pallas as pl
from jax.experimental.pallas import tpu as pltpu
from jax.sharding import PartitionSpec as P

STEP = 10
CLIP_NORM = 5.0
LEARN_RATE = 0.5
BETA_ONE = 0.9
BETA_TWO = 0.999
ADAM_EPS = 1e-06
DECAY_RATE = 0.01
NORM_EPS = 1e-05
VAR_FLOOR = 0.25
CLIPS = 3
CLIP_MOST = 32
LANES = 128
VMEM_BYTES = 60 * 1024 * 1024

AB = (((1,), (0,)), ((), ()))
ABT = (((1,), (1,)), ((), ()))
ATB = (((0,), (0,)), ((), ()))


def split(x):
    hi = x.astype(jnp.bfloat16)
    lo = (x - hi.astype(jnp.float32)).astype(jnp.bfloat16)
    return hi, lo


def dot1(a, b, dims):
    return lax.dot_general(a, b, dims, preferred_element_type=jnp.float32)


def dot_parts(a, b, dims):
    return dot1(a[0], b[0], dims) + (dot1(a[1], b[0], dims) + dot1(a[0], b[1], dims))


def dot3(a, b, dims):
    return dot_parts(split(a), split(b), dims)


def sigmoid(x):
    return 0.5 * jnp.tanh(0.5 * x) + 0.5


def norm_stats(x):
    center = x - jnp.mean(x, axis=-1, keepdims=True)
    spread = jnp.mean(center * center, axis=-1, keepdims=True)
    scale = lax.rsqrt(spread + NORM_EPS)
    return center * scale, scale


def norm_back(grad_unit, unit, scale):
    first = jnp.mean(grad_unit, axis=-1, keepdims=True)
    second = jnp.mean(grad_unit * unit, axis=-1, keepdims=True)
    return scale * (grad_unit - first - unit * second)


def column_sum(x):
    return jnp.sum(x, axis=0, keepdims=True)


def gates_forward(x_flat, act, w_in, vec, rows, block):
    hidden4 = w_in.shape[2]
    dmodel = w_in.shape[1]
    parts = [split(w_in[e]) for e in range(2)]

    def one(r, carry):
        start = pl.multiple_of(r * block, block)
        unit, unused = norm_stats(x_flat(start, block))
        n = split(unit * (1.0 + vec[0:1, :dmodel]) + vec[0:1, dmodel : 2 * dmodel])
        for e in range(2):
            bias = vec[0:1, 2 * dmodel + hidden4 * e : 2 * dmodel + hidden4 * (e + 1)]
            z = dot_parts(n, parts[e], AB) + bias
            act[e][pl.ds(r * (block // 16), block // 16)] = z.reshape(block // 16, 16, hidden4)
        return carry

    lax.fori_loop(0, rows // block, one, 0)


def run_forward(steps, places, act, tc, cp, hp, h, w_rec, hi_ref, lo_ref, state, memory):
    hidden = w_rec.shape[1]
    for e in range(2):
        hi_ref[e], lo_ref[e] = split(w_rec[e])
        state[e][...] = jnp.zeros_like(state[e])
        memory[e][...] = jnp.zeros_like(memory[e])

    def step(j, carry):
        work = []
        for e in range(2):
            at = places(e, j)
            prior = state[e][...]
            hi, lo = split(prior)
            rows = prior.shape[0]
            first = dot1(jnp.concatenate([hi, lo], axis=0), hi_ref[e], AB)
            drive = [act[e][p] for p in at]
            drive = drive[0] if len(drive) == 1 else jnp.concatenate(drive, axis=0)
            z = first[:rows] + first[rows:] + dot1(hi, lo_ref[e], AB) + drive
            work.append((at, prior, z))
        for e in range(2):
            at, prior, z = work[e]
            ingate = sigmoid(z[:, :hidden])
            forget = sigmoid(z[:, hidden : 2 * hidden])
            candidate = jnp.tanh(z[:, 2 * hidden : 3 * hidden])
            outgate = sigmoid(z[:, 3 * hidden :])
            before = memory[e][...]
            now = forget * before + ingate * candidate
            squashed = jnp.tanh(now)
            out = outgate * squashed
            memory[e][...] = now
            state[e][...] = out
            for k, p in enumerate(at):
                part = slice(16 * k, 16 * (k + 1))
                act[e][p, :, :hidden] = ingate[part]
                act[e][p, :, hidden : 2 * hidden] = forget[part]
                act[e][p, :, 2 * hidden : 3 * hidden] = candidate[part]
                act[e][p, :, 3 * hidden :] = outgate[part]
                tc[e][p] = squashed[part]
                cp[e][p] = before[part]
                hp[e][p] = prior[part]
                h[e][p] = out[part]
        return carry

    lax.fori_loop(0, steps, step, 0)


def output_forward(count, h, w_out, vec):
    hidden = h[0].shape[2]
    dmodel = w_out.shape[1]
    total = vec[0:1, vec.shape[1] - dmodel :]
    for e in range(2):
        states = h[e][:count].reshape(count * 16, hidden)
        total = total + dot3(states, w_out[hidden * e : hidden * (e + 1)], AB)
    return total


def run_backward(steps, places, act, dz_ref, tc, cp, dh, w_rec, hi_ref, lo_ref, grad_h, grad_c):
    hidden = w_rec.shape[1]
    for e in range(2):
        hi_ref[e], lo_ref[e] = split(w_rec[e])
        grad_h[e][...] = jnp.zeros_like(grad_h[e])
        grad_c[e][...] = jnp.zeros_like(grad_c[e])

    def load(ref, at):
        got = [ref[p] for p in at]
        return got[0] if len(got) == 1 else jnp.concatenate(got, axis=0)

    def step(back, carry):
        j = steps - 1 - back
        work = []
        for e in range(2):
            at = places(e, j)
            gates = load(act[e], at)
            ingate = gates[:, :hidden]
            forget = gates[:, hidden : 2 * hidden]
            candidate = gates[:, 2 * hidden : 3 * hidden]
            outgate = gates[:, 3 * hidden :]
            squashed = load(tc[e], at)
            before = load(cp[e], at)
            total_h = load(dh[e], at) + grad_h[e][...]
            total_c = grad_c[e][...] + total_h * outgate * (1.0 - squashed * squashed)
            dz = jnp.concatenate(
                [
                    total_c * candidate * ingate * (1.0 - ingate),
                    total_c * before * forget * (1.0 - forget),
                    total_c * ingate * (1.0 - candidate * candidate),
                    total_h * squashed * outgate * (1.0 - outgate),
                ],
                axis=1,
            )
            grad_c[e][...] = total_c * forget
            for k, p in enumerate(at):
                dz_ref[e][p] = dz[16 * k : 16 * (k + 1)]
            work.append(dz)
        for e in range(2):
            hi, lo = split(work[e])
            rows = hi.shape[0]
            first = dot1(jnp.concatenate([hi, lo], axis=0), hi_ref[e], ABT)
            grad_h[e][...] = first[:rows] + first[rows:] + dot1(hi, lo_ref[e], ABT)
        return carry

    lax.fori_loop(0, steps, step, 0)


def states_backward(count, dy_flat, dh, h, w_out, g_out):
    hidden = h[0].shape[2]
    dy = split(dy_flat)
    for e in range(2):
        part = slice(hidden * e, hidden * (e + 1))
        dh[e][:count] = dot_parts(dy, split(w_out[part]), ABT).reshape(count, 16, hidden)
        g_out[part] = dot3_parts_first(h[e][:count].reshape(count * 16, hidden), dy)


def dot3_parts_first(a, b_parts):
    return dot_parts(split(a), b_parts, ATB)


def gates_backward(count, x_flat, dy_flat, dz_ref, hp, w_in, vec, g_in, g_rec, g_vec):
    dmodel = w_in.shape[1]
    hidden = hp[0].shape[2]
    hidden4 = 4 * hidden
    rows = count * 16
    unit, scale = norm_stats(x_flat)
    gain = 1.0 + vec[0:1, :dmodel]
    n = split(unit * gain + vec[0:1, dmodel : 2 * dmodel])
    dn = jnp.zeros((rows, dmodel), jnp.float32)
    for e in range(2):
        before = split(hp[e][:count].reshape(rows, hidden))
        for q in range(4):
            part = slice(hidden * q, hidden * (q + 1))
            dz_q = dz_ref[e][:count, :, part].reshape(rows, hidden)
            dz = split(dz_q)
            g_rec[e, :, part] = dot_parts(before, dz, ATB)
            g_in[e, :, part] = dot_parts(n, dz, ATB)
            dn = dn + dot_parts(dz, split(w_in[e, :, part]), ABT)
            base = 2 * dmodel + hidden4 * e + hidden * q
            g_vec[0:1, base : base + hidden] = column_sum(dz_q)
    g_vec[0:1, :dmodel] = column_sum(dn * unit)
    g_vec[0:1, dmodel : 2 * dmodel] = column_sum(dn)
    g_vec[0:1, vec.shape[1] - dmodel :] = column_sum(dy_flat)
    return dy_flat + norm_back(dn * gain, unit, scale)


def clip_places(clips, spare):
    def places(e, j):
        found = []
        for c in range(CLIPS):
            start, length = clips[0, c], clips[1, c]
            frame = start + j if e == 0 else start + length - 1 - j
            found.append(jnp.where(j < length, frame, spare))
        return found

    return places


def window_of(edge):
    base = pl.multiple_of((edge // LANES) * LANES, LANES)
    return base, lax.rem(edge, LANES)


def split_rows(spec, edge, width, frames):
    wmax = LANES
    base, shift = window_of(edge)
    window = spec[:, pl.ds(base, 2 * LANES)]
    taken = pltpu.roll(window, lax.rem(2 * LANES - shift, 2 * LANES), 1)[:, :wmax]
    taken = jnp.concatenate([taken[:frames], taken[frames:]], axis=1)
    lane = lax.broadcasted_iota(jnp.int32, (frames, wmax), 1)
    inside = (lane < width).astype(jnp.float32)
    valid = jnp.concatenate([inside, inside], axis=1)
    entries = jnp.maximum(2 * width, 1).astype(jnp.float32)
    mean = jnp.sum(taken * valid, axis=-1, keepdims=True) / entries
    center = (taken - mean) * valid
    spread = jnp.sum(center * center, axis=-1, keepdims=True) / entries
    scale = lax.rsqrt(jnp.maximum(spread, VAR_FLOOR))
    moving = jnp.where(spread > VAR_FLOOR, 1.0, jnp.where(spread == VAR_FLOOR, 0.5, 0.0))
    return center * scale, scale, valid, moving, entries


def time_forward_kernel(
    places_s, clips, spec, w_split, v_band, w_in, w_rec, w_out, vec,
    out, x, act0, act1, tc0, tc1, cp0, cp1, hp0, hp1, h0, h1,
    hi_ref, lo_ref, s0, s1, m0, m1, y, mixed,
):
    slots = w_split.shape[0]
    frames = x.shape[0]
    dmodel = w_split.shape[2]
    wide = w_split.shape[1]
    x[...] = jnp.zeros_like(x)
    for a in (act0, act1):
        a[frames] = jnp.zeros_like(a[frames])

    def one_slot(s, carry):
        unit, unused, valid, moving, entries = split_rows(spec, places_s[0, s], places_s[1, s], frames)
        row = v_band[s]
        z = (unit * (1.0 + row[:, :wide]) + row[:, wide : 2 * wide]) * valid
        y[s] = dot3(z, w_split[s], AB) + row[:, 2 * wide : 2 * wide + dmodel]
        return carry

    lax.fori_loop(0, slots, one_slot, 0)
    for s in range(slots):
        x[:, s, :] = y[s]
    act = (act0, act1)
    block = 256

    def x_flat(start, size):
        return x[pl.ds(start // 16, size // 16)].reshape(size, dmodel)

    gates_forward(x_flat, act, w_in, vec, frames * 16, block)
    run_forward(
        CLIP_MOST, clip_places(clips, frames), act, (tc0, tc1), (cp0, cp1), (hp0, hp1), (h0, h1),
        w_rec, hi_ref, lo_ref, (s0, s1), (m0, m1),
    )
    total = output_forward(frames, (h0, h1), w_out, vec)
    x_all = x[...].reshape(frames * 16, dmodel)
    mixed[...] = (x_all + total).reshape(frames, 16, dmodel)
    parts, unused_slots, quarter, unused = out.shape
    for s in range(slots):
        for q in range(parts):
            out[q, s] = mixed[q * quarter : (q + 1) * quarter, s, :]


def f32(shape):
    return jax.ShapeDtypeStruct(shape, jnp.float32)


def saved_shapes(count, hidden):
    wide = [f32((count, 16, 4 * hidden))] * 2
    thin = [f32((count, 16, hidden))] * 8
    return wide + thin


def rec_scratch(rows, hidden):
    return [
        pltpu.VMEM((2, hidden, 4 * hidden), jnp.bfloat16),
        pltpu.VMEM((2, hidden, 4 * hidden), jnp.bfloat16),
    ] + [pltpu.VMEM((rows, hidden), jnp.float32)] * 4


SMEM = pl.BlockSpec(memory_space=pltpu.SMEM)
VMEM = pl.BlockSpec(memory_space=pltpu.VMEM)
PARAMS = pltpu.CompilerParams(vmem_limit_bytes=VMEM_BYTES)


def time_forward(slot_places, clips, spec, w_split, v_band, w_in, w_rec, w_out, vec, parts):
    slots, wide, dmodel = w_split.shape
    hidden = w_rec.shape[1]
    frames = spec.shape[0] // 2
    return pl.pallas_call(
        time_forward_kernel,
        out_shape=[f32((parts, slots, frames // parts, dmodel)), f32((frames, 16, dmodel))]
        + saved_shapes(frames + 1, hidden),
        in_specs=[SMEM, SMEM] + [VMEM] * 7,
        out_specs=[VMEM] * 12,
        scratch_shapes=rec_scratch(16 * CLIPS, hidden)
        + [pltpu.VMEM((slots, frames, dmodel), jnp.float32)]
        + [pltpu.VMEM((frames, 16, dmodel), jnp.float32)],
        compiler_params=PARAMS,
        name="time_forward",
    )(slot_places, clips, spec, w_split, v_band, w_in, w_rec, w_out, vec)


def time_backward_kernel(
    places_s, clips, dy_in, spec, x, act0, act1, tc0, tc1, cp0, cp1, hp0, hp1, h0, h1,
    w_split, v_band, w_in, w_rec, w_out, vec,
    d_spec, g_split, g_band, g_in, g_rec, g_out, g_vec,
    hi_ref, lo_ref, s0, s1, m0, m1, dy, dh0, dh1, dz0, dz1,
):
    slots, wide, dmodel = w_split.shape
    frames = x.shape[0]
    parts, unused_slots, quarter, unused = dy_in.shape
    dy[...] = jnp.zeros_like(dy)
    for s in range(slots):
        for q in range(parts):
            dy[q * quarter : (q + 1) * quarter, s, :] = dy_in[q, s]
    dy_flat = dy[...].reshape(frames * 16, dmodel)
    states_backward(frames, dy_flat, (dh0, dh1), (h0, h1), w_out, g_out)
    for d in (dh0, dh1):
        d[frames] = jnp.zeros_like(d[frames])
    run_backward(
        CLIP_MOST, clip_places(clips, frames), (act0, act1), (dz0, dz1), (tc0, tc1), (cp0, cp1), (dh0, dh1),
        w_rec, hi_ref, lo_ref, (s0, s1), (m0, m1),
    )
    x_flat = x[...].reshape(frames * 16, dmodel)
    dx = gates_backward(frames, x_flat, dy[...].reshape(frames * 16, dmodel), (dz0, dz1), (hp0, hp1), w_in, vec, g_in, g_rec, g_vec)
    dy[...] = dx.reshape(frames, 16, dmodel)
    d_spec[...] = jnp.zeros_like(d_spec)

    for s in range(slots):
        edge, width = places_s[0, s], places_s[1, s]
        unit, scale, valid, moving, entries = split_rows(spec, edge, width, frames)
        row = v_band[s]
        gain = 1.0 + row[:, :wide]
        z = (unit * gain + row[:, wide : 2 * wide]) * valid
        demb = dy[:, s, :]
        demb_parts = split(demb)
        g_split[s] = dot_parts(split(z), demb_parts, ATB)
        dz = dot_parts(demb_parts, split(w_split[s]), ABT) * valid
        g_band[s, :, :wide] = column_sum(dz * unit)
        g_band[s, :, wide : 2 * wide] = column_sum(dz)
        g_band[s, :, 2 * wide :] = column_sum(demb)
        du = dz * gain
        first = jnp.sum(du, axis=-1, keepdims=True) / entries
        second = jnp.sum(du * unit, axis=-1, keepdims=True) / entries
        dt = scale * (du - first - moving * unit * second) * valid
        base, shift = window_of(edge)
        stacked = jnp.concatenate([dt[:, :LANES], dt[:, LANES:]], axis=0)
        padded = jnp.concatenate([stacked, jnp.zeros_like(stacked)], axis=1)
        d_spec[:, pl.ds(base, 2 * LANES)] += pltpu.roll(padded, shift, 1)


def time_backward(slot_places, clips, dy, spec, saved, w_split, v_band, w_in, w_rec, w_out, vec):
    slots, wide, dmodel = w_split.shape
    hidden = w_rec.shape[1]
    frames = spec.shape[0] // 2
    return pl.pallas_call(
        time_backward_kernel,
        out_shape=[
            f32(spec.shape), f32(w_split.shape), f32((slots, 1, 2 * wide + dmodel)),
            f32(w_in.shape), f32(w_rec.shape), f32(w_out.shape), f32(vec.shape),
        ],
        in_specs=[SMEM, SMEM] + [VMEM] * (3 + 10 + 6),
        out_specs=[VMEM] * 7,
        scratch_shapes=rec_scratch(16 * CLIPS, hidden)
        + [pltpu.VMEM((frames, 16, dmodel), jnp.float32)]
        + [pltpu.VMEM((frames + 1, 16, hidden), jnp.float32)] * 2
        + [pltpu.VMEM((frames + 1, 16, 4 * hidden), jnp.float32)] * 2,
        compiler_params=PARAMS,
        name="time_backward",
    )(slot_places, clips, dy, spec, *saved, w_split, v_band, w_in, w_rec, w_out, vec)


def band_places(bands):
    return lambda e, j: [j if e == 0 else bands - 1 - j]


def band_forward_kernel(
    slot_of, arrived, w_in, w_rec, w_out, vec,
    out, x, act0, act1, tc0, tc1, cp0, cp1, hp0, hp1, h0, h1,
    hi_ref, lo_ref, s0, s1, m0, m1,
):
    bands, unused, dmodel = x.shape

    def fetch(b, carry):
        x[b] = arrived[slot_of[0, b]]
        return carry

    lax.fori_loop(0, bands, fetch, 0)
    act = (act0, act1)

    def x_flat(start, size):
        return x[...].reshape(bands * 16, dmodel)

    gates_forward(x_flat, act, w_in, vec, bands * 16, bands * 16)
    run_forward(
        bands, band_places(bands), act, (tc0, tc1), (cp0, cp1), (hp0, hp1), (h0, h1),
        w_rec, hi_ref, lo_ref, (s0, s1), (m0, m1),
    )
    total = output_forward(bands, (h0, h1), w_out, vec)
    whole = (x[...].reshape(bands * 16, dmodel) + total).reshape(bands, 16, dmodel)
    out[...] = jnp.zeros_like(out)
    for b in range(bands):
        out[slot_of[0, b]] = whole[b]


def band_forward(slot_of, arrived, w_in, w_rec, w_out, vec):
    bands = slot_of.shape[1]
    hidden = w_rec.shape[1]
    dmodel = w_out.shape[1]
    return pl.pallas_call(
        band_forward_kernel,
        out_shape=[f32(arrived.shape), f32((bands, 16, dmodel))] + saved_shapes(bands, hidden),
        in_specs=[SMEM] + [VMEM] * 5,
        out_specs=[VMEM] * 12,
        scratch_shapes=rec_scratch(16, hidden),
        compiler_params=PARAMS,
        name="band_forward",
    )(slot_of, arrived, w_in, w_rec, w_out, vec)


def band_backward_kernel(
    slot_of, arrived, x, act0, act1, tc0, tc1, cp0, cp1, hp0, hp1, h0, h1,
    w_in, w_rec, w_out, vec,
    out, g_in, g_rec, g_out, g_vec,
    hi_ref, lo_ref, s0, s1, m0, m1, dy, dh0, dh1, dz0, dz1,
):
    bands, unused, dmodel = x.shape

    def fetch(b, carry):
        dy[b] = arrived[slot_of[0, b]]
        return carry

    lax.fori_loop(0, bands, fetch, 0)
    states_backward(bands, dy[...].reshape(bands * 16, dmodel), (dh0, dh1), (h0, h1), w_out, g_out)
    run_backward(
        bands, band_places(bands), (act0, act1), (dz0, dz1), (tc0, tc1), (cp0, cp1), (dh0, dh1),
        w_rec, hi_ref, lo_ref, (s0, s1), (m0, m1),
    )
    dx = gates_backward(
        bands, x[...].reshape(bands * 16, dmodel), dy[...].reshape(bands * 16, dmodel),
        (dz0, dz1), (hp0, hp1), w_in, vec, g_in, g_rec, g_vec,
    ).reshape(bands, 16, dmodel)
    out[...] = jnp.zeros_like(out)
    for b in range(bands):
        out[slot_of[0, b]] = dx[b]


def band_backward(slot_of, arrived, saved, w_in, w_rec, w_out, vec):
    bands = slot_of.shape[1]
    hidden = w_rec.shape[1]
    dmodel = w_out.shape[1]
    return pl.pallas_call(
        band_backward_kernel,
        out_shape=[
            f32(arrived.shape), f32(w_in.shape), f32(w_rec.shape), f32(w_out.shape), f32(vec.shape),
        ],
        in_specs=[SMEM] + [VMEM] * (2 + 10 + 4),
        out_specs=[VMEM] * 5,
        scratch_shapes=rec_scratch(16, hidden)
        + [pltpu.VMEM((bands, 16, dmodel), jnp.float32)]
        + [pltpu.VMEM((bands, 16, hidden), jnp.float32)] * 2
        + [pltpu.VMEM((bands, 16, 4 * hidden), jnp.float32)] * 2,
        compiler_params=PARAMS,
        name="band_backward",
    )(slot_of, arrived, *saved, w_in, w_rec, w_out, vec)


def mask_kernel(widths, arrived, cot, w_wide, w_mask, vec, masks, grad, g_wide, g_mask, g_vec):
    s = pl.program_id(0)
    parts, streams, unused, quarter, dmodel = arrived.shape
    mlp = w_wide.shape[2]
    wide = masks.shape[2]
    half = wide // 2
    x = jnp.concatenate(
        [arrived[q, g, 0] for g in range(streams) for q in range(parts)], axis=0
    )
    rows = x.shape[0]
    v = vec[0]
    gain = 1.0 + v[:, :dmodel]
    unit, scale = norm_stats(x)
    p = split(unit * gain + v[:, dmodel : 2 * dmodel])
    wide_parts = split(w_wide[0])
    mask_parts = split(w_mask[0])
    q = jnp.tanh(dot_parts(p, wide_parts, AB) + v[:, 2 * dmodel : 2 * dmodel + mlp])
    q_parts = split(q)
    r = dot_parts(q_parts, mask_parts, AB) + v[:, 2 * dmodel + mlp :]
    lane = lax.broadcasted_iota(jnp.int32, (1, half), 1)
    inside = (lane < widths[0, s]).astype(jnp.float32)
    valid = jnp.concatenate([inside, inside], axis=1)
    value = r[:, :wide]
    gate = sigmoid(r[:, wide:])
    masks[0] = value * gate * valid
    dm = cot[0] * valid
    dr = jnp.concatenate([dm * gate, dm * value * gate * (1.0 - gate)], axis=1)
    dr_parts = split(dr)
    g_mask[0] = dot_parts(q_parts, dr_parts, ATB)
    dq = dot_parts(dr_parts, mask_parts, ABT)
    da = dq * (1.0 - q * q)
    da_parts = split(da)
    g_wide[0] = dot_parts(p, da_parts, ATB)
    dp = dot_parts(da_parts, wide_parts, ABT)
    g_vec[0, :, :dmodel] = column_sum(dp * unit)
    g_vec[0, :, dmodel : 2 * dmodel] = column_sum(dp)
    g_vec[0, :, 2 * dmodel : 2 * dmodel + mlp] = column_sum(da)
    g_vec[0, :, 2 * dmodel + mlp :] = column_sum(dr)
    dx = norm_back(dp * gain, unit, scale)
    k = 0
    for g in range(streams):
        for q_ in range(parts):
            grad[q_, g, 0] = dx[k * quarter : (k + 1) * quarter]
            k += 1


def mask_network(widths, arrived, cot, w_wide, w_mask, vec):
    parts, streams, slots, quarter, dmodel = arrived.shape
    rows, wide = cot.shape[1:]
    mlp = w_wide.shape[2]
    moving = pl.BlockSpec((parts, streams, 1, quarter, dmodel), lambda s: (0, 0, s, 0, 0))

    def lead(shape):
        return pl.BlockSpec((1,) + shape, lambda s: (s,) + (0,) * len(shape))

    return pl.pallas_call(
        mask_kernel,
        grid=(slots,),
        out_shape=[
            f32(cot.shape), f32(arrived.shape), f32(w_wide.shape), f32(w_mask.shape), f32(vec.shape),
        ],
        in_specs=[
            SMEM, moving, lead((rows, wide)), lead(w_wide.shape[1:]), lead(w_mask.shape[1:]),
            lead(vec.shape[1:]),
        ],
        out_specs=[
            lead((rows, wide)), moving, lead(w_wide.shape[1:]), lead(w_mask.shape[1:]),
            lead(vec.shape[1:]),
        ],
        compiler_params=PARAMS,
        name="mask_network",
    )(widths, arrived, cot, w_wide, w_mask, vec)


def groups_of(size, slots):
    outer = math.gcd(size, slots)
    inner = size // outer
    across = [[g * inner + i for g in range(outer)] for i in range(inner)]
    within = [[g * inner + i for i in range(inner)] for g in range(outer)]
    return outer, inner, across, within


def sum_everywhere(values, sizes):
    n = sizes[0] * sizes[1]
    row = jnp.zeros((8, LANES), jnp.float32).at[0, : values.shape[0]].set(values)
    spread = jnp.broadcast_to(row[None], (n, 8, LANES))
    got = lax.all_to_all(spread, ("band", "stream"), 0, 0, tiled=True)
    return jnp.sum(got, axis=0)[0, : values.shape[0]]


def share_slots(shard, outer, across, within, axis):
    slots = shard.shape[0]
    sent = lax.all_to_all(
        shard.reshape((outer, slots // outer) + shard.shape[1:]), "stream", 0, 0,
        axis_index_groups=across, tiled=True,
    )
    inner = len(within[0])
    if inner == 2:
        me = lax.rem(lax.axis_index("stream"), 2)
        count = lax.axis_size("stream")
        other = lax.ppermute(sent, "stream", [(s, s ^ 1) for s in range(count)])
        return jnp.stack([jnp.where(me == 0, sent, other), jnp.where(me == 0, other, sent)])
    return lax.all_gather(sent, "stream", axis_index_groups=within)


def return_slots(grads, outer, inner, across, within):
    if inner == 2:
        me = lax.rem(lax.axis_index("stream"), 2)
        count = lax.axis_size("stream")
        other = lax.ppermute(
            lax.dynamic_index_in_dim(grads, 1 - me, 0, False), "stream",
            [(s, s ^ 1) for s in range(count)],
        )
        mine = lax.dynamic_index_in_dim(grads, me, 0, False) + other
    else:
        mine = lax.psum_scatter(grads, "stream", axis_index_groups=within, tiled=False)
    back = lax.all_to_all(mine, "stream", 0, 0, axis_index_groups=across, tiled=True)
    return back.reshape((-1,) + back.shape[2:])


def lamb_moments(gradient, mean_old, power_old, factor):
    clipped = gradient * factor
    mean_new = BETA_ONE * mean_old + (1.0 - BETA_ONE) * clipped
    power_new = BETA_TWO * power_old + (1.0 - BETA_TWO) * clipped * clipped
    return (mean_new, power_new)


def lamb_direction(weight_matrix, mean_new, power_new, decay):
    corrected = mean_new / (1.0 - BETA_ONE**STEP)
    scale_root = jnp.sqrt(power_new / (1.0 - BETA_TWO**STEP)) + ADAM_EPS
    return corrected / scale_root + decay * weight_matrix


def body(spectrum, segments, widths, groups, cotangent, *state):
    weights, means_old, powers_old = state[:8], state[8:16], state[16:]
    splitter, widener, masker, banding, intake, recurrence, outtake, scalers = weights
    group_count = lax.axis_size("band")
    stream_count = lax.axis_size("stream")
    my_group = lax.axis_index("band")
    my_stream = lax.axis_index("stream")
    slots = splitter.shape[0]
    frames = spectrum.shape[0]
    quarter = frames // group_count
    outer, inner, across, within = groups_of(stream_count, slots)
    share = slots // outer
    my_outer = my_stream // inner
    dmodel = splitter.shape[2]
    wide = splitter.shape[1] * stream_count
    wmax = wide // 2
    mlp = masker.shape[1] * stream_count
    bins = spectrum.shape[2]

    members = (groups[:, None] == jnp.arange(group_count, dtype=jnp.int32)[None, :]).astype(jnp.int32)
    ranking = jnp.sum(jnp.cumsum(members, axis=0) * members, axis=1) - 1
    band_slot_index = groups * slots + ranking
    local_slots = my_group * slots + jnp.arange(slots, dtype=jnp.int32)
    owned = (band_slot_index[None, :] == local_slots[:, None]).astype(jnp.int32)
    edges = jnp.cumsum(widths) - widths
    slot_edges = jnp.sum(owned * edges[None, :], axis=1)
    slot_widths = jnp.sum(owned * widths[None, :], axis=1)
    slot_places = jnp.stack([slot_edges, slot_widths])
    slot_of = band_slot_index[None, :]
    lengths = jnp.sum(
        (segments[0][None, :] == jnp.arange(CLIPS, dtype=jnp.int32)[:, None]).astype(jnp.int32), axis=1
    )
    clips = jnp.stack([jnp.cumsum(lengths) - lengths, lengths])
    share_widths = lax.dynamic_slice(slot_widths, (my_outer * share,), (share,))[None, :]

    w_split = lax.all_gather(splitter, "stream", axis=1, tiled=True)
    v_band = lax.all_gather(banding, "stream", axis=1, tiled=True)
    w_in = lax.all_gather(intake, "stream", axis=3, tiled=True)
    w_rec = lax.all_gather(recurrence, "stream", axis=3, tiled=True)
    w_out = lax.all_gather(outtake, "stream", axis=1, tiled=True)
    v_rnn = lax.all_gather(scalers, "stream", axis=1, tiled=True)

    w_wide = share_slots(widener, outer, across, within, 2)
    w_wide = w_wide.transpose(2, 3, 1, 0, 4).reshape(share, dmodel, mlp)
    w_mask = share_slots(masker, outer, across, within, 1)
    w_mask = w_mask.transpose(2, 1, 0, 3, 4).reshape(share, mlp, 2 * wide)
    cot_parts = cotangent.reshape(frames, outer, share, wide).transpose(1, 2, 0, 3)
    cot = lax.all_to_all(cot_parts, "stream", 0, 0, axis_index_groups=across, tiled=True)
    cot = cot.transpose(1, 0, 2, 3).reshape(share, outer * frames, wide)

    padded = ((bins - 1) // LANES + 2) * LANES
    spec = jnp.pad(
        spectrum.transpose(1, 0, 2).reshape(2 * frames, bins), ((0, 0), (0, padded - bins))
    )
    vec0, vec1 = v_rnn[0:1], v_rnn[1:2]
    v_band = v_band[:, None, :]
    base = 2 * wide + dmodel
    got = time_forward(
        slot_places, clips, spec, w_split, v_band, w_in[0], w_rec[0], w_out[0], vec0, group_count
    )
    time_out, time_saved = got[0], got[1:]
    arrived = lax.all_to_all(time_out, "band", 0, 0, tiled=True)
    got = band_forward(
        slot_of, arrived.reshape(group_count * slots, quarter, dmodel), w_in[1], w_rec[1], w_out[1], vec1
    )
    band_out, band_saved = got[0], got[1:]

    def to_masks(x):
        x = x.reshape(group_count, outer, share, quarter, dmodel)
        x = lax.all_to_all(x, "stream", 1, 1, axis_index_groups=across, tiled=True)
        return lax.all_to_all(x, "band", 0, 0, tiled=True)

    def from_masks(x):
        x = lax.all_to_all(x, "band", 0, 0, tiled=True)
        x = lax.all_to_all(x, "stream", 1, 1, axis_index_groups=across, tiled=True)
        return x.reshape(group_count * slots, quarter, dmodel)

    share_vec = lax.dynamic_slice_in_dim(v_band[:, :, base:], my_outer * share, share, 0)
    mask_parts, grad_mixed, g_wide, g_mask, g_mask_vec = mask_network(
        share_widths, to_masks(band_out), cot, w_wide, w_mask, share_vec
    )
    band_grad, band_gin, band_grec, band_gout, band_gvec = band_backward(
        slot_of, from_masks(grad_mixed), band_saved, w_in[1], w_rec[1], w_out[1], vec1
    )
    grad_time = lax.all_to_all(
        band_grad.reshape(group_count, slots, quarter, dmodel), "band", 0, 0, tiled=True
    )
    d_spec, g_split, g_split_vec, time_gin, time_grec, time_gout, time_gvec = time_backward(
        slot_places, clips, grad_time, spec, time_saved, w_split, v_band, w_in[0], w_rec[0], w_out[0], vec0
    )

    mask_parts = mask_parts.reshape(share, outer, frames, wide).transpose(1, 0, 2, 3)
    mask_parts = lax.all_to_all(mask_parts, "stream", 0, 0, axis_index_groups=across, tiled=True)
    masks = mask_parts.reshape(slots, frames, wide).transpose(1, 0, 2).reshape(cotangent.shape)
    d_spec = lax.psum(d_spec, "band")
    spectrum_grad = d_spec.reshape(2, frames, padded)[:, :, :bins].transpose(1, 0, 2)

    g_wide = g_wide.reshape(share, dmodel, outer, inner, -1).transpose(3, 2, 0, 1, 4)
    widened_reduced = return_slots(g_wide, outer, inner, across, within)
    g_mask = g_mask.reshape(share, outer, inner, -1, 2 * wide).transpose(2, 1, 0, 3, 4)
    mask_reduced = return_slots(g_mask, outer, inner, across, within)
    g_mask_vec = lax.dynamic_update_slice_in_dim(
        jnp.zeros((slots, g_mask_vec.shape[2]), jnp.float32), g_mask_vec[:, 0], my_outer * share, 0
    )
    g_band = jnp.concatenate([g_split_vec[:, 0], g_mask_vec], axis=1)
    rnn_grads = (
        lax.psum_scatter(jnp.stack([time_gin, band_gin]), "stream", scatter_dimension=3, tiled=True),
        lax.psum_scatter(jnp.stack([time_grec, band_grec]), "stream", scatter_dimension=3, tiled=True),
        lax.psum_scatter(jnp.stack([time_gout, band_gout]), "stream", scatter_dimension=1, tiled=True),
        lax.psum_scatter(
            jnp.concatenate([time_gvec, band_gvec], axis=0), "stream", scatter_dimension=1, tiled=True
        ),
    )
    rnn_grads = lax.psum(rnn_grads, "band")
    reduced = (
        lax.psum_scatter(g_split, "stream", scatter_dimension=1, tiled=True),
        widened_reduced,
        mask_reduced,
        lax.psum_scatter(g_band, "stream", scatter_dimension=1, tiled=True),
    ) + tuple(rnn_grads)

    shares = (1.0,) * 4 + (1.0 / group_count,) * 4
    decays = (DECAY_RATE,) * 3 + (0.0,) + (DECAY_RATE,) * 3 + (0.0,)
    sizes = (group_count, stream_count)
    sums = [sum(jnp.sum(g * g) * part for g, part in zip(reduced, shares))]
    sums += [jnp.sum(w * w) * part for w, part in zip(weights, shares)]
    totals = sum_everywhere(jnp.stack(sums), sizes)
    grad_norm = jnp.sqrt(totals[0])
    factor = jnp.minimum(1.0, CLIP_NORM / grad_norm)
    moments = [lamb_moments(g, m, p, factor) for g, m, p in zip(reduced, means_old, powers_old)]
    directions = [lamb_direction(w, m, p, d) for w, (m, p), d in zip(weights, moments, decays)]
    update_totals = sum_everywhere(
        jnp.stack([jnp.sum(d * d) * part for d, part in zip(directions, shares)]), sizes
    )
    ratios = jnp.sqrt(totals[1:]) / jnp.sqrt(update_totals + 1e-12)
    fresh = [w - LEARN_RATE * ratios[k] * d for k, (w, d) in enumerate(zip(weights, directions))]
    return (
        (masks, spectrum_grad, grad_norm)
        + tuple(fresh)
        + tuple(m for m, unused in moments)
        + tuple(p for unused, p in moments)
    )


def solution(mesh):
    stored = (
        P("band", "stream", None),
        P("band", None, "stream"),
        P("band", "stream", None),
        P("band", "stream"),
        P(None, None, None, "stream"),
        P(None, None, None, "stream"),
        P(None, "stream", None),
        P(None, "stream"),
    )
    frames_over = P("stream", None, None)
    mask_over = P("stream", "band", None, None)
    return jax.shard_map(
        body,
        mesh=mesh,
        in_specs=(frames_over, P("stream", None), P(), P(), mask_over) + stored * 3,
        out_specs=(mask_over, frames_over, P()) + stored * 3,
        check_vma=False,
    )
```

```python
from functools import partial
import math

import jax
import jax.numpy as jnp
from jax import lax
from jax.experimental import pallas as pl
from jax.experimental.pallas import tpu as pltpu
from jax.sharding import PartitionSpec as P

STEP = 10
CLIP_NORM = 5.0
LEARN_RATE = 0.5
BETA_ONE = 0.9
BETA_TWO = 0.999
ADAM_EPS = 1e-06
DECAY_RATE = 0.01
NORM_EPS = 1e-05
VAR_FLOOR = 0.25
CLIPS = 3
CLIP_MOST = 32
LANES = 128
VMEM_BYTES = 60 * 1024 * 1024
CORES = 2
MESH = pl.DeviceIdType.MESH

AB = (((1,), (0,)), ((), ()))
ABT = (((1,), (1,)), ((), ()))
ATB = (((0,), (0,)), ((), ()))


def split(x):
    hi = x.astype(jnp.bfloat16)
    lo = (x - hi.astype(jnp.float32)).astype(jnp.bfloat16)
    return hi, lo


def dot1(a, b, dims):
    return lax.dot_general(a, b, dims, preferred_element_type=jnp.float32)


def dot_parts(a, b, dims):
    return dot1(a[0], b[0], dims) + (dot1(a[1], b[0], dims) + dot1(a[0], b[1], dims))


def dot3(a, b, dims):
    return dot_parts(split(a), split(b), dims)


def sigmoid(x):
    return 0.5 * jnp.tanh(0.5 * x) + 0.5


def norm_stats(x):
    center = x - jnp.mean(x, axis=-1, keepdims=True)
    spread = jnp.mean(center * center, axis=-1, keepdims=True)
    scale = lax.rsqrt(spread + NORM_EPS)
    return center * scale, scale


def norm_back(grad_unit, unit, scale):
    first = jnp.mean(grad_unit, axis=-1, keepdims=True)
    second = jnp.mean(grad_unit * unit, axis=-1, keepdims=True)
    return scale * (grad_unit - first - unit * second)


def column_sum(x):
    return jnp.sum(x, axis=0, keepdims=True)


def pack_rows(dmodel, hidden):
    blocks = 4 * hidden // LANES
    out_rows = 2 * hidden // blocks
    weight_rows = 2 * dmodel + 2 * hidden + out_rows
    share = (2 * dmodel + 8 * hidden + dmodel) // blocks
    vec_rows = -(-share // LANES)
    return blocks, out_rows, weight_rows, share, vec_rows, -(-(weight_rows + vec_rows) // 32) * 32


def pack_rnn(w_in, w_rec, w_out, vec, rows, share):
    count = w_in.shape[2] // LANES
    parts = [
        w.reshape(2 * w.shape[1], count, LANES).transpose(1, 0, 2) for w in (w_in, w_rec)
    ] + [w_out.reshape(count, -1, LANES)]
    used = sum(p.shape[1] for p in parts)
    flat = jnp.pad(vec.reshape(count, share), ((0, 0), (0, (rows - used) * LANES - share)))
    return jnp.concatenate(parts + [flat.reshape(count, rows - used, LANES)], axis=1)


def unpack_rnn(pack, dmodel, hidden):
    blocks, out_rows, weight_rows, share, vec_rows, rows = pack_rows(dmodel, hidden)
    count = pack.shape[0]
    cuts = (0, 2 * dmodel, 2 * dmodel + 2 * hidden)
    w_in = pack[:, : cuts[1]].reshape(count, 2, dmodel, LANES).transpose(1, 2, 0, 3)
    w_rec = pack[:, cuts[1] : cuts[2]].reshape(count, 2, hidden, LANES).transpose(1, 2, 0, 3)
    return (
        w_in.reshape(2, dmodel, count * LANES),
        w_rec.reshape(2, hidden, count * LANES),
        pack[:, cuts[2] : weight_rows].reshape(count * out_rows, LANES),
        unpack_vec(pack, weight_rows, vec_rows, share),
    )


def unpack_vec(pack, weight_rows, vec_rows, share):
    count = pack.shape[0]
    flat = pack[:, weight_rows : weight_rows + vec_rows].reshape(count, vec_rows * LANES)
    return flat[:, :share].reshape(1, count * share)


class Pack:
    def __init__(self, ref, dmodel, hidden):
        self.ref, self.dmodel, self.hidden = ref, dmodel, hidden
        self.blocks, self.out_rows = pack_rows(dmodel, hidden)[:2]

    def intake(self, e, first, last):
        rows = slice(e * self.dmodel, (e + 1) * self.dmodel)
        return jnp.concatenate([self.ref[k, rows] for k in range(first, last)], axis=1)

    def recurrence(self, e, k):
        base = 2 * self.dmodel + e * self.hidden
        return self.ref[k, base : base + self.hidden]

    def outtake(self, e):
        base = 2 * self.dmodel + 2 * self.hidden
        half = self.blocks // 2
        return jnp.concatenate(
            [self.ref[k, base : base + self.out_rows] for k in range(half * e, half * (e + 1))], axis=0
        )

    def put(self, k, base, value):
        self.ref[k, base : base + value.shape[0]] = value

    def put_intake(self, e, q, value):
        for h in range(value.shape[1] // LANES):
            self.put(q * value.shape[1] // LANES + h, e * self.dmodel, value[:, h * LANES : (h + 1) * LANES])

    def put_recurrence(self, e, q, value):
        base = 2 * self.dmodel + e * self.hidden
        for h in range(value.shape[1] // LANES):
            self.put(q * value.shape[1] // LANES + h, base, value[:, h * LANES : (h + 1) * LANES])

    def put_outtake(self, e, value):
        base = 2 * self.dmodel + 2 * self.hidden
        for k in range(self.blocks // 2):
            self.put(self.blocks // 2 * e + k, base, value[k * self.out_rows : (k + 1) * self.out_rows])

    def put_vec(self, value):
        unused, unused, base, share, vec_rows, rows = pack_rows(self.dmodel, self.hidden)
        for k in range(self.blocks):
            self.ref[k, base:rows] = jnp.zeros((rows - base, LANES), jnp.float32)
            for r in range(vec_rows):
                width = min(LANES, share - r * LANES)
                at = k * share + r * LANES
                self.ref[k, base + r : base + r + 1, :width] = value[:, at : at + width]


def split_recurrence(pack, hi_ref, lo_ref):
    for e in range(2):
        for k in range(pack.blocks):
            part = slice(k * LANES, (k + 1) * LANES)
            hi_ref[e, :, part], lo_ref[e, :, part] = split(pack.recurrence(e, k))


def gates_forward(x_flat, act, pack, vec, rows, block):
    hidden4 = 4 * pack.hidden
    dmodel = pack.dmodel
    parts = [split(pack.intake(e, 0, pack.blocks)) for e in range(2)]

    def one(r, carry):
        start = pl.multiple_of(r * block, block)
        unit, unused = norm_stats(x_flat(start, block))
        n = split(unit * (1.0 + vec[0:1, :dmodel]) + vec[0:1, dmodel : 2 * dmodel])
        for e in range(2):
            bias = vec[0:1, 2 * dmodel + hidden4 * e : 2 * dmodel + hidden4 * (e + 1)]
            z = dot_parts(n, parts[e], AB) + bias
            act[e][pl.ds(r * (block // 16), block // 16)] = z.reshape(block // 16, 16, hidden4)
        return carry

    lax.fori_loop(0, rows // block, one, 0)


def run_forward(steps, places, act, tc, cp, hp, h, pack, hi_ref, lo_ref, state, memory):
    hidden = pack.hidden
    split_recurrence(pack, hi_ref, lo_ref)
    for e in range(2):
        state[e][...] = jnp.zeros_like(state[e])
        memory[e][...] = jnp.zeros_like(memory[e])

    def step(j, carry):
        work = []
        for e in range(2):
            at = places(e, j)
            prior = state[e][...]
            hi, lo = split(prior)
            rows = prior.shape[0]
            first = dot1(jnp.concatenate([hi, lo], axis=0), hi_ref[e], AB)
            drive = [act[e][p] for p in at]
            drive = drive[0] if len(drive) == 1 else jnp.concatenate(drive, axis=0)
            z = first[:rows] + first[rows:] + dot1(hi, lo_ref[e], AB) + drive
            work.append((at, prior, z))
        for e in range(2):
            at, prior, z = work[e]
            ingate = sigmoid(z[:, :hidden])
            forget = sigmoid(z[:, hidden : 2 * hidden])
            candidate = jnp.tanh(z[:, 2 * hidden : 3 * hidden])
            outgate = sigmoid(z[:, 3 * hidden :])
            before = memory[e][...]
            now = forget * before + ingate * candidate
            squashed = jnp.tanh(now)
            out = outgate * squashed
            memory[e][...] = now
            state[e][...] = out
            for k, p in enumerate(at):
                part = slice(16 * k, 16 * (k + 1))
                act[e][p, :, :hidden] = ingate[part]
                act[e][p, :, hidden : 2 * hidden] = forget[part]
                act[e][p, :, 2 * hidden : 3 * hidden] = candidate[part]
                act[e][p, :, 3 * hidden :] = outgate[part]
                tc[e][p] = squashed[part]
                cp[e][p] = before[part]
                hp[e][p] = prior[part]
                h[e][p] = out[part]
        return carry

    lax.fori_loop(0, steps, step, 0)


def output_forward(count, h, pack, vec):
    hidden = h[0].shape[2]
    dmodel = pack.dmodel
    total = vec[0:1, vec.shape[1] - dmodel :]
    for e in range(2):
        states = h[e][:count].reshape(count * 16, hidden)
        total = total + dot3(states, pack.outtake(e), AB)
    return total


def run_backward(steps, places, act, dz_ref, tc, cp, dh, pack, hi_ref, lo_ref, grad_h, grad_c):
    hidden = pack.hidden
    split_recurrence(pack, hi_ref, lo_ref)
    for e in range(2):
        grad_h[e][...] = jnp.zeros_like(grad_h[e])
        grad_c[e][...] = jnp.zeros_like(grad_c[e])

    def load(ref, at):
        got = [ref[p] for p in at]
        return got[0] if len(got) == 1 else jnp.concatenate(got, axis=0)

    def step(back, carry):
        j = steps - 1 - back
        work = []
        for e in range(2):
            at = places(e, j)
            gates = load(act[e], at)
            ingate = gates[:, :hidden]
            forget = gates[:, hidden : 2 * hidden]
            candidate = gates[:, 2 * hidden : 3 * hidden]
            outgate = gates[:, 3 * hidden :]
            squashed = load(tc[e], at)
            before = load(cp[e], at)
            total_h = load(dh[e], at) + grad_h[e][...]
            total_c = grad_c[e][...] + total_h * outgate * (1.0 - squashed * squashed)
            dz = jnp.concatenate(
                [
                    total_c * candidate * ingate * (1.0 - ingate),
                    total_c * before * forget * (1.0 - forget),
                    total_c * ingate * (1.0 - candidate * candidate),
                    total_h * squashed * outgate * (1.0 - outgate),
                ],
                axis=1,
            )
            grad_c[e][...] = total_c * forget
            for k, p in enumerate(at):
                dz_ref[e][p] = dz[16 * k : 16 * (k + 1)]
            work.append(dz)
        for e in range(2):
            hi, lo = split(work[e])
            rows = hi.shape[0]
            first = dot1(jnp.concatenate([hi, lo], axis=0), hi_ref[e], ABT)
            grad_h[e][...] = first[:rows] + first[rows:] + dot1(hi, lo_ref[e], ABT)
        return carry

    lax.fori_loop(0, steps, step, 0)


def states_backward(count, dy_flat, dh, h, pack, g_pack):
    hidden = h[0].shape[2]
    dy = split(dy_flat)
    for e in range(2):
        dh[e][:count] = dot_parts(dy, split(pack.outtake(e)), ABT).reshape(count, 16, hidden)
        g_pack.put_outtake(e, dot3_parts_first(h[e][:count].reshape(count * 16, hidden), dy))


def dot3_parts_first(a, b_parts):
    return dot_parts(split(a), b_parts, ATB)


def gates_backward(count, x_flat, dy_flat, dz_ref, hp, pack, vec, g_pack, g_vec):
    dmodel = pack.dmodel
    hidden = hp[0].shape[2]
    hidden4 = 4 * hidden
    rows = count * 16
    unit, scale = norm_stats(x_flat)
    gain = 1.0 + vec[0:1, :dmodel]
    n = split(unit * gain + vec[0:1, dmodel : 2 * dmodel])
    dn = jnp.zeros((rows, dmodel), jnp.float32)
    for e in range(2):
        before = split(hp[e][:count].reshape(rows, hidden))
        for q in range(4):
            part = slice(hidden * q, hidden * (q + 1))
            dz_q = dz_ref[e][:count, :, part].reshape(rows, hidden)
            dz = split(dz_q)
            g_pack.put_recurrence(e, q, dot_parts(before, dz, ATB))
            g_pack.put_intake(e, q, dot_parts(n, dz, ATB))
            dn = dn + dot_parts(dz, split(pack.intake(e, q * pack.blocks // 4, (q + 1) * pack.blocks // 4)), ABT)
            base = 2 * dmodel + hidden4 * e + hidden * q
            g_vec[0:1, base : base + hidden] = column_sum(dz_q)
    g_vec[0:1, :dmodel] = column_sum(dn * unit)
    g_vec[0:1, dmodel : 2 * dmodel] = column_sum(dn)
    g_vec[0:1, vec.shape[1] - dmodel :] = column_sum(dy_flat)
    g_pack.put_vec(g_vec[...])
    return dy_flat + norm_back(dn * gain, unit, scale)


def clip_places(clips, spare):
    def places(e, j):
        found = []
        for c in range(CLIPS):
            start, length = clips[0, c], clips[1, c]
            frame = start + j if e == 0 else start + length - 1 - j
            found.append(jnp.where(j < length, frame, spare))
        return found

    return places


def window_of(edge):
    base = pl.multiple_of((edge // LANES) * LANES, LANES)
    return base, lax.rem(edge, LANES)


def split_rows(spec, edge, width, frames):
    wmax = LANES
    base, shift = window_of(edge)
    window = spec[:, pl.ds(base, 2 * LANES)]
    taken = pltpu.roll(window, lax.rem(2 * LANES - shift, 2 * LANES), 1)[:, :wmax]
    taken = jnp.concatenate([taken[:frames], taken[frames:]], axis=1)
    lane = lax.broadcasted_iota(jnp.int32, (frames, wmax), 1)
    inside = (lane < width).astype(jnp.float32)
    valid = jnp.concatenate([inside, inside], axis=1)
    entries = jnp.maximum(2 * width, 1).astype(jnp.float32)
    mean = jnp.sum(taken * valid, axis=-1, keepdims=True) / entries
    center = (taken - mean) * valid
    spread = jnp.sum(center * center, axis=-1, keepdims=True) / entries
    scale = lax.rsqrt(jnp.maximum(spread, VAR_FLOOR))
    moving = jnp.where(spread > VAR_FLOOR, 1.0, jnp.where(spread == VAR_FLOOR, 0.5, 0.0))
    return center * scale, scale, valid, moving, entries


def slot_weights(w_split, s, slot_rows):
    count = w_split.shape[0]
    at = pl.ds(pl.multiple_of(s * slot_rows, slot_rows), slot_rows)
    return jnp.concatenate([w_split[k, at, :] for k in range(count)], axis=0)


def time_forward_kernel(
    slot_rows, places_s, clips, spec, w_split, v_band, rnn, vec,
    out, x, act0, act1, tc0, tc1, cp0, cp1, hp0, hp1, h0, h1,
    hi_ref, lo_ref, s0, s1, m0, m1, y, mixed,
):
    slots = v_band.shape[0]
    frames, unused, dmodel = x.shape
    wide = w_split.shape[0] * slot_rows
    pack = Pack(rnn, dmodel, h0.shape[2])
    x[...] = jnp.zeros_like(x)
    for a in (act0, act1):
        a[frames] = jnp.zeros_like(a[frames])

    def one_slot(s, carry):
        unit, unused, valid, moving, entries = split_rows(spec, places_s[0, s], places_s[1, s], frames)
        row = v_band[s]
        z = (unit * (1.0 + row[:, :wide]) + row[:, wide : 2 * wide]) * valid
        y[s] = dot3(z, slot_weights(w_split, s, slot_rows), AB) + row[:, 2 * wide : 2 * wide + dmodel]
        return carry

    lax.fori_loop(0, slots, one_slot, 0)
    for s in range(slots):
        x[:, s, :] = y[s]
    act = (act0, act1)

    def x_flat(start, size):
        return x[pl.ds(start // 16, size // 16)].reshape(size, dmodel)

    gates_forward(x_flat, act, pack, vec, frames * 16, 256)
    run_forward(
        CLIP_MOST, clip_places(clips, frames), act, (tc0, tc1), (cp0, cp1), (hp0, hp1), (h0, h1),
        pack, hi_ref, lo_ref, (s0, s1), (m0, m1),
    )
    total = output_forward(frames, (h0, h1), pack, vec)
    x_all = x[...].reshape(frames * 16, dmodel)
    mixed[...] = (x_all + total).reshape(frames, 16, dmodel)
    parts, unused_slots, quarter, unused = out.shape
    for s in range(slots):
        for q in range(parts):
            out[q, s] = mixed[q * quarter : (q + 1) * quarter, s, :]


def f32(shape):
    return jax.ShapeDtypeStruct(shape, jnp.float32)


def saved_shapes(count, hidden):
    wide = [f32((count, 16, 4 * hidden))] * 2
    thin = [f32((count, 16, hidden))] * 8
    return wide + thin


def rec_scratch(rows, hidden):
    return [
        pltpu.VMEM((2, hidden, 4 * hidden), jnp.bfloat16),
        pltpu.VMEM((2, hidden, 4 * hidden), jnp.bfloat16),
    ] + [pltpu.VMEM((rows, hidden), jnp.float32)] * 4


SMEM = pl.BlockSpec(memory_space=pltpu.SMEM)
VMEM = pl.BlockSpec(memory_space=pltpu.VMEM)
ANY = pl.BlockSpec(memory_space=pl.ANY)
PARAMS = pltpu.CompilerParams(vmem_limit_bytes=VMEM_BYTES)


def cost(micros):
    return pl.CostEstimate(flops=int(micros * 1.1e9), bytes_accessed=int(micros * 3e6), transcendentals=0)


def time_forward(slot_places, clips, spec, w_split, v_band, rnn, vec, parts, slot_rows, hidden):
    slots = v_band.shape[0]
    dmodel = w_split.shape[2]
    frames = spec.shape[0] // 2
    return pl.pallas_call(
        partial(time_forward_kernel, slot_rows),
        out_shape=[f32((parts, slots, frames // parts, dmodel)), f32((frames, 16, dmodel))]
        + saved_shapes(frames + 1, hidden),
        in_specs=[SMEM, SMEM] + [VMEM] * 5,
        out_specs=[VMEM] * 12,
        scratch_shapes=rec_scratch(16 * CLIPS, hidden)
        + [pltpu.VMEM((slots, frames, dmodel), jnp.float32)]
        + [pltpu.VMEM((frames, 16, dmodel), jnp.float32)],
        compiler_params=PARAMS,
        cost_estimate=cost(35),
        name="time_forward",
    )(slot_places, clips, spec, w_split, v_band, rnn, vec)


def time_backward_kernel(
    slot_rows, places_s, clips, dy_in, spec, x, act0, act1, tc0, tc1, cp0, cp1, hp0, hp1, h0, h1,
    w_split, v_band, rnn, vec,
    d_spec, g_split, g_band, g_rnn,
    hi_ref, lo_ref, s0, s1, m0, m1, dy, g_vec, dh0, dh1, dz0, dz1,
):
    slots = v_band.shape[0]
    frames, unused, dmodel = x.shape
    wide = w_split.shape[0] * slot_rows
    parts, unused_slots, quarter, unused = dy_in.shape
    pack, g_pack = Pack(rnn, dmodel, h0.shape[2]), Pack(g_rnn, dmodel, h0.shape[2])
    dy[...] = jnp.zeros_like(dy)
    for s in range(slots):
        for q in range(parts):
            dy[q * quarter : (q + 1) * quarter, s, :] = dy_in[q, s]
    dy_flat = dy[...].reshape(frames * 16, dmodel)
    states_backward(frames, dy_flat, (dh0, dh1), (h0, h1), pack, g_pack)
    for d in (dh0, dh1):
        d[frames] = jnp.zeros_like(d[frames])
    run_backward(
        CLIP_MOST, clip_places(clips, frames), (act0, act1), (dz0, dz1), (tc0, tc1), (cp0, cp1),
        (dh0, dh1), pack, hi_ref, lo_ref, (s0, s1), (m0, m1),
    )
    x_flat = x[...].reshape(frames * 16, dmodel)
    dx = gates_backward(
        frames, x_flat, dy[...].reshape(frames * 16, dmodel), (dz0, dz1), (hp0, hp1), pack, vec, g_pack, g_vec
    )
    dy[...] = dx.reshape(frames, 16, dmodel)
    d_spec[...] = jnp.zeros_like(d_spec)
    g_split[:, slots * slot_rows :] = jnp.zeros_like(g_split[:, slots * slot_rows :])

    for s in range(slots):
        edge, width = places_s[0, s], places_s[1, s]
        unit, scale, valid, moving, entries = split_rows(spec, edge, width, frames)
        row = v_band[s]
        gain = 1.0 + row[:, :wide]
        z = (unit * gain + row[:, wide : 2 * wide]) * valid
        demb = dy[:, s, :]
        demb_parts = split(demb)
        g_slot = dot_parts(split(z), demb_parts, ATB)
        for k in range(w_split.shape[0]):
            g_split[k, s * slot_rows : (s + 1) * slot_rows] = g_slot[k * slot_rows : (k + 1) * slot_rows]
        dz = dot_parts(demb_parts, split(slot_weights(w_split, s, slot_rows)), ABT) * valid
        g_band[s, :, :wide] = column_sum(dz * unit)
        g_band[s, :, wide : 2 * wide] = column_sum(dz)
        g_band[s, :, 2 * wide :] = column_sum(demb)
        du = dz * gain
        first = jnp.sum(du, axis=-1, keepdims=True) / entries
        second = jnp.sum(du * unit, axis=-1, keepdims=True) / entries
        dt = scale * (du - first - moving * unit * second) * valid
        base, shift = window_of(edge)
        stacked = jnp.concatenate([dt[:, :LANES], dt[:, LANES:]], axis=0)
        padded = jnp.concatenate([stacked, jnp.zeros_like(stacked)], axis=1)
        d_spec[:, pl.ds(base, 2 * LANES)] += pltpu.roll(padded, shift, 1)


def time_backward(slot_places, clips, dy, spec, saved, w_split, v_band, rnn, vec, slot_rows, hidden):
    slots = v_band.shape[0]
    dmodel = w_split.shape[2]
    wide = w_split.shape[0] * slot_rows
    frames = spec.shape[0] // 2
    return pl.pallas_call(
        partial(time_backward_kernel, slot_rows),
        out_shape=[
            f32(spec.shape), f32(w_split.shape), f32((slots, 1, 2 * wide + dmodel)), f32(rnn.shape),
        ],
        in_specs=[SMEM, SMEM] + [VMEM] * (3 + 10 + 4),
        out_specs=[VMEM] * 4,
        scratch_shapes=rec_scratch(16 * CLIPS, hidden)
        + [pltpu.VMEM((frames, 16, dmodel), jnp.float32), pltpu.VMEM(vec.shape, jnp.float32)]
        + [pltpu.VMEM((frames + 1, 16, hidden), jnp.float32)] * 2
        + [pltpu.VMEM((frames + 1, 16, 4 * hidden), jnp.float32)] * 2,
        compiler_params=PARAMS,
        cost_estimate=cost(50),
        name="time_backward",
    )(slot_places, clips, dy, spec, *saved, w_split, v_band, rnn, vec)


def band_places(bands):
    return lambda e, j: [j if e == 0 else bands - 1 - j]


def band_forward_kernel(
    slot_of, arrived, rnn, vec,
    out, x, act0, act1, tc0, tc1, cp0, cp1, hp0, hp1, h0, h1,
    hi_ref, lo_ref, s0, s1, m0, m1,
):
    bands, unused, dmodel = x.shape
    pack = Pack(rnn, dmodel, h0.shape[2])

    def fetch(b, carry):
        x[b] = arrived[slot_of[0, b]]
        return carry

    lax.fori_loop(0, bands, fetch, 0)
    act = (act0, act1)

    def x_flat(start, size):
        return x[...].reshape(bands * 16, dmodel)

    gates_forward(x_flat, act, pack, vec, bands * 16, bands * 16)
    run_forward(
        bands, band_places(bands), act, (tc0, tc1), (cp0, cp1), (hp0, hp1), (h0, h1),
        pack, hi_ref, lo_ref, (s0, s1), (m0, m1),
    )
    total = output_forward(bands, (h0, h1), pack, vec)
    whole = (x[...].reshape(bands * 16, dmodel) + total).reshape(bands, 16, dmodel)
    out[...] = jnp.zeros_like(out)
    for b in range(bands):
        out[slot_of[0, b]] = whole[b]


def band_forward(slot_of, arrived, rnn, vec, hidden):
    bands = slot_of.shape[1]
    dmodel = arrived.shape[2]
    return pl.pallas_call(
        band_forward_kernel,
        out_shape=[f32(arrived.shape), f32((bands, 16, dmodel))] + saved_shapes(bands, hidden),
        in_specs=[SMEM] + [VMEM] * 3,
        out_specs=[VMEM] * 12,
        scratch_shapes=rec_scratch(16, hidden),
        compiler_params=PARAMS,
        cost_estimate=cost(28),
        name="band_forward",
    )(slot_of, arrived, rnn, vec)


def band_backward_kernel(
    slot_of, arrived, x, act0, act1, tc0, tc1, cp0, cp1, hp0, hp1, h0, h1, rnn, vec,
    out, g_rnn,
    hi_ref, lo_ref, s0, s1, m0, m1, dy, g_vec, dh0, dh1, dz0, dz1,
):
    bands, unused, dmodel = x.shape
    pack, g_pack = Pack(rnn, dmodel, h0.shape[2]), Pack(g_rnn, dmodel, h0.shape[2])

    def fetch(b, carry):
        dy[b] = arrived[slot_of[0, b]]
        return carry

    lax.fori_loop(0, bands, fetch, 0)
    states_backward(bands, dy[...].reshape(bands * 16, dmodel), (dh0, dh1), (h0, h1), pack, g_pack)
    run_backward(
        bands, band_places(bands), (act0, act1), (dz0, dz1), (tc0, tc1), (cp0, cp1), (dh0, dh1),
        pack, hi_ref, lo_ref, (s0, s1), (m0, m1),
    )
    dx = gates_backward(
        bands, x[...].reshape(bands * 16, dmodel), dy[...].reshape(bands * 16, dmodel),
        (dz0, dz1), (hp0, hp1), pack, vec, g_pack, g_vec,
    ).reshape(bands, 16, dmodel)
    out[...] = jnp.zeros_like(out)
    for b in range(bands):
        out[slot_of[0, b]] = dx[b]


def band_backward(slot_of, arrived, saved, rnn, vec, hidden):
    bands = slot_of.shape[1]
    dmodel = arrived.shape[2]
    return pl.pallas_call(
        band_backward_kernel,
        out_shape=[f32(arrived.shape), f32(rnn.shape)],
        in_specs=[SMEM] + [VMEM] * (2 + 10 + 2),
        out_specs=[VMEM] * 2,
        scratch_shapes=rec_scratch(16, hidden)
        + [pltpu.VMEM((bands, 16, dmodel), jnp.float32), pltpu.VMEM(vec.shape, jnp.float32)]
        + [pltpu.VMEM((bands, 16, hidden), jnp.float32)] * 2
        + [pltpu.VMEM((bands, 16, 4 * hidden), jnp.float32)] * 2,
        compiler_params=PARAMS,
        cost_estimate=cost(43),
        name="band_backward",
    )(slot_of, arrived, *saved, rnn, vec)


def in_turn(core, mine, other):
    return [jnp.where(core == 0, mine, other), jnp.where(core == 0, other, mine)]


def mask_kernel(
    places, arrived, cot, wide_mine, wide_other, mask_mine, mask_other, vec,
    masks, grad, g_wide_keep, g_wide_send, g_mask_keep, g_mask_send, g_vec,
):
    s = pl.program_id(0)
    parts, streams, unused, quarter, dmodel = arrived.shape
    outer, unused, frames, wide = cot.shape
    half = wide // 2
    core = places[1, 0]
    x = jnp.concatenate([arrived[q, g, 0] for g in range(streams) for q in range(parts)], axis=0)
    w_wide, w_mask = [], []
    for g in range(outer):
        w_wide += in_turn(core, wide_mine[g, 0], wide_other[g, 0])
        w_mask += in_turn(core, mask_mine[g, 0], mask_other[g, 0])
    w_wide, w_mask = jnp.concatenate(w_wide, axis=1), jnp.concatenate(w_mask, axis=0)
    mlp = w_mask.shape[0]
    piece = mlp // (2 * outer)
    v = vec[0]
    gain = 1.0 + v[:, :dmodel]
    unit, scale = norm_stats(x)
    p = split(unit * gain + v[:, dmodel : 2 * dmodel])
    wide_parts = split(w_wide)
    mask_parts = split(w_mask)
    q = jnp.tanh(dot_parts(p, wide_parts, AB) + v[:, 2 * dmodel : 2 * dmodel + mlp])
    q_parts = split(q)
    r = dot_parts(q_parts, mask_parts, AB) + v[:, 2 * dmodel + mlp :]
    lane = lax.broadcasted_iota(jnp.int32, (1, half), 1)
    inside = (lane < places[0, s]).astype(jnp.float32)
    valid = jnp.concatenate([inside, inside], axis=1)
    value = r[:, :wide]
    gate = sigmoid(r[:, wide:])
    masks[...] = (value * gate * valid).reshape(masks.shape)
    dm = cot[...].reshape(outer * frames, wide) * valid
    dr = jnp.concatenate([dm * gate, dm * value * gate * (1.0 - gate)], axis=1)
    dr_parts = split(dr)
    g_mask = dot_parts(q_parts, dr_parts, ATB)
    dq = dot_parts(dr_parts, mask_parts, ABT)
    da = dq * (1.0 - q * q)
    da_parts = split(da)
    g_wide = dot_parts(p, da_parts, ATB)
    for g in range(outer):
        first, second = slice(2 * g * piece, (2 * g + 1) * piece), slice((2 * g + 1) * piece, (2 * g + 2) * piece)
        g_mask_keep[g, 0], g_mask_send[g, 0] = in_turn(core, g_mask[first], g_mask[second])
        g_wide_keep[g, 0], g_wide_send[g, 0] = in_turn(core, g_wide[:, first], g_wide[:, second])
    dp = dot_parts(da_parts, wide_parts, ABT)
    g_vec[0, :, :dmodel] = column_sum(dp * unit)
    g_vec[0, :, dmodel : 2 * dmodel] = column_sum(dp)
    g_vec[0, :, 2 * dmodel : 2 * dmodel + mlp] = column_sum(da)
    g_vec[0, :, 2 * dmodel + mlp :] = column_sum(dr)
    dx = norm_back(dp * gain, unit, scale)
    k = 0
    for g in range(streams):
        for q_ in range(parts):
            grad[q_, g, 0] = dx[k * quarter : (k + 1) * quarter]
            k += 1


def mask_network(places, arrived, cot, w_wide, w_mask, vec):
    parts, streams, slots, quarter, dmodel = arrived.shape

    def second(shape):
        return pl.BlockSpec(
            (shape[0], 1) + shape[2:], lambda s: (0, s) + (0,) * (len(shape) - 2)
        )

    moving = pl.BlockSpec((parts, streams, 1, quarter, dmodel), lambda s: (0, 0, s, 0, 0))
    vector = pl.BlockSpec((1,) + vec.shape[1:], lambda s: (s, 0, 0))
    pieces = [w_wide[0].shape] * 2 + [w_mask[0].shape] * 2
    return pl.pallas_call(
        mask_kernel,
        grid=(slots,),
        out_shape=[f32(cot.shape), f32(arrived.shape)] + [f32(p) for p in pieces] + [f32(vec.shape)],
        in_specs=[SMEM, moving, second(cot.shape)] + [second(p) for p in pieces] + [vector],
        out_specs=[second(cot.shape), moving] + [second(p) for p in pieces] + [vector],
        compiler_params=PARAMS,
        cost_estimate=cost(12),
        name="mask_network",
    )(places, arrived, cot, *w_wide, *w_mask, vec)


class Links:
    def __init__(self, bands, layers, send_sems, recv_sems):
        self.bands, self.layers = bands, layers
        self.band, self.stream = lax.axis_index("band"), lax.axis_index("stream")
        self.layer, self.core = lax.div(self.stream, CORES), lax.rem(self.stream, CORES)
        self.other = self.stream + 1 - 2 * self.core
        self.send_sems, self.recv_sems = send_sems, recv_sems
        self.started = []

    def band_to(self, m):
        return lax.rem(self.band + m, self.bands)

    def band_from(self, m):
        return lax.rem(self.band + self.bands - m, self.bands)

    def layer_to(self, k):
        return lax.rem(self.layer + k, self.layers)

    def layer_from(self, k):
        return lax.rem(self.layer + self.layers - k, self.layers)

    def own(self, layer):
        return layer * CORES + self.core

    def across(self, layer):
        return layer * CORES + 1 - self.core

    def greet(self, partners):
        barrier = pltpu.get_barrier_semaphore()
        for partner in partners:
            pl.semaphore_signal(barrier, inc=1, device_id=partner, device_id_type=MESH)
        pl.semaphore_wait(barrier, len(partners))

    def copy(self, source, target, index, partner):
        return pltpu.make_async_remote_copy(
            src_ref=source, dst_ref=target, send_sem=self.send_sems.at[index],
            recv_sem=self.recv_sems.at[index], device_id=partner, device_id_type=MESH,
        )

    def send(self, source, target, index, partner):
        copy = self.copy(source, target, index, partner)
        copy.start()
        self.started.append(copy)

    def arrive(self, target, index):
        self.copy(target, target, index, (self.band, self.other)).wait_recv()

    def finish(self):
        for copy in self.started:
            copy.wait_send()


def gather_kernel(bands, layers, rnn, own_split, rnn_all, split_all, send_sems, recv_sems, local_sems):
    at = Links(bands, layers, send_sems, recv_sems)
    band, stream, other = at.band, at.stream, at.other
    quarter = rnn.shape[0] // bands
    at.greet(
        [(at.band_to(m), stream) for m in range(1, bands)]
        + [(band, at.own(at.layer_to(k))) for k in range(1, layers)]
        + [(band, other)]
    )
    steps = range(1, layers)
    turns = range(1, bands)

    def rows(b):
        return pl.ds(b * quarter, quarter)

    to_layer, to_layer_split, to_band = 0, layers, 2 * layers
    to_core = to_band + layers * bands
    to_core_split = to_core + layers * bands
    for k in steps:
        at.send(rnn.at[rows(band)], rnn_all.at[stream, rows(band)], to_layer + k, (band, at.own(at.layer_to(k))))
    for k in steps:
        at.send(own_split, split_all.at[stream], to_layer_split + k, (band, at.own(at.layer_to(k))))
    at.send(rnn, rnn_all.at[stream], to_core, (band, other))
    at.send(own_split, split_all.at[stream], to_core_split, (band, other))
    local = [
        pltpu.make_async_copy(rnn, rnn_all.at[stream], local_sems.at[0]),
        pltpu.make_async_copy(own_split, split_all.at[stream], local_sems.at[1]),
    ]
    for copy in local:
        copy.start()
    for k in steps:
        source = at.own(at.layer_from(k))
        piece = rnn_all.at[source, rows(band)]
        at.arrive(piece, to_layer + k)
        for m in turns:
            at.send(piece, piece, to_band + k * bands + m, (at.band_to(m), stream))
        at.send(piece, piece, to_core + k * bands, (band, other))
    for k in steps:
        source = at.own(at.layer_from(k))
        for m in turns:
            piece = rnn_all.at[source, rows(at.band_from(m))]
            at.arrive(piece, to_band + k * bands + m)
            at.send(piece, piece, to_core + k * bands + m, (band, other))
    for k in steps:
        piece = split_all.at[at.own(at.layer_from(k))]
        at.arrive(piece, to_layer_split + k)
        at.send(piece, piece, to_core_split + k, (band, other))
    at.arrive(rnn_all.at[other], to_core)
    at.arrive(split_all.at[other], to_core_split)
    for k in steps:
        source = at.across(at.layer_from(k))
        for m in range(bands):
            at.arrive(rnn_all.at[source, rows(at.band_from(m))], to_core + k * bands + m)
        at.arrive(split_all.at[source], to_core_split + k)
    at.finish()
    for copy in local:
        copy.wait()


def gather_front(rnn, own_split, bands, layers):
    count = 2 * layers + 2 * layers * bands + layers
    return pl.pallas_call(
        partial(gather_kernel, bands, layers),
        out_shape=[f32((layers * CORES,) + rnn.shape), f32((layers * CORES,) + own_split.shape)],
        in_specs=[ANY] * 2,
        out_specs=[ANY] * 2,
        scratch_shapes=[
            pltpu.SemaphoreType.DMA((count,)), pltpu.SemaphoreType.DMA((count,)), pltpu.SemaphoreType.DMA((2,)),
        ],
        compiler_params=pltpu.CompilerParams(collective_id=0, has_side_effects=True),
        cost_estimate=cost(30),
        name="gather_front",
    )(rnn, own_split)


def exchange_kernel(bands, layers, source, target, send_sems, recv_sems, local_sem):
    at = Links(bands, layers, send_sems, recv_sems)
    wide = source.shape[1] == layers
    turns = [(m, k) for k in range(layers if wide else 1) for m in range(bands) if m + k]

    def place(ref, band, layer):
        return ref.at[band, layer] if wide else ref.at[band]

    def stream_of(layer):
        return at.own(layer) if wide else at.stream

    at.greet([(at.band_to(m), stream_of(at.layer_to(k))) for m, k in turns])
    for m, k in turns:
        band, layer = at.band_to(m), at.layer_to(k)
        at.send(
            place(source, band, layer), place(target, at.band, at.layer), k * bands + m, (band, stream_of(layer))
        )
    local = pltpu.make_async_copy(
        place(source, at.band, at.layer), place(target, at.band, at.layer), local_sem
    )
    local.start()
    for m, k in turns:
        at.arrive(place(target, at.band_from(m), at.layer_from(k)), k * bands + m)
    at.finish()
    local.wait()


def exchange(x, bands, layers, number):
    count = bands * layers
    return pl.pallas_call(
        partial(exchange_kernel, bands, layers),
        out_shape=f32(x.shape),
        in_specs=[ANY],
        out_specs=ANY,
        scratch_shapes=[
            pltpu.SemaphoreType.DMA((count,)), pltpu.SemaphoreType.DMA((count,)), pltpu.SemaphoreType.DMA,
        ],
        compiler_params=pltpu.CompilerParams(collective_id=number, has_side_effects=True),
        cost_estimate=cost(8),
        name="exchange",
    )(x)


def reduce_kernel(
    bands, layers, g_rnn, g_split, rnn_out, split_out,
    from_core, from_core_split, from_band, held, from_layer, from_layer_split, send_sems, recv_sems,
):
    at = Links(bands, layers, send_sems, recv_sems)
    band, stream, other = at.band, at.stream, at.other
    quarter = g_rnn.shape[1] // bands
    at.greet(
        [(at.band_to(m), stream) for m in range(1, bands)]
        + [(band, at.own(at.layer_to(k))) for k in range(1, layers)]
        + [(band, other)]
    )
    order = list(range(1, layers)) + [0]
    turns = range(1, bands)

    def rows(b):
        return pl.ds(pl.multiple_of(b * quarter, 8), quarter)

    to_core, to_core_split, to_layer, to_layer_split = 0, layers, 2 * layers, 3 * layers
    to_band = 4 * layers
    to_all = to_band + bands * layers
    for k in order:
        at.send(g_rnn.at[at.across(at.layer_to(k))], from_core.at[k], to_core + k, (band, other))
    for k in order:
        at.send(g_split.at[at.across(at.layer_to(k))], from_core_split.at[k], to_core_split + k, (band, other))
    for k in order:
        at.arrive(from_core.at[k], to_core + k)
        from_core[k] += g_rnn[at.own(at.layer_to(k))]
        for m in turns:
            to = at.band_to(m)
            at.send(
                from_core.at[k, rows(to)], from_band.at[m - 1, k], to_band + m * layers + k, (to, stream)
            )
    for k in order:
        at.arrive(from_core_split.at[k], to_core_split + k)
        from_core_split[k] += g_split[at.own(at.layer_to(k))]
        if k:
            at.send(
                from_core_split.at[k], from_layer_split.at[k - 1], to_layer_split + k,
                (band, at.own(at.layer_to(k))),
            )
    for k in order:
        total = from_core[k, rows(band)]
        for m in turns:
            at.arrive(from_band.at[m - 1, k], to_band + m * layers + k)
            total = total + from_band[m - 1, k]
        held[k] = total
        if k:
            at.send(held.at[k], from_layer.at[k - 1], to_layer + k, (band, at.own(at.layer_to(k))))
    total = held[0]
    for k in range(1, layers):
        at.arrive(from_layer.at[k - 1], to_layer + k)
        total = total + from_layer[k - 1]
    rnn_out[rows(band)] = total
    for m in turns:
        at.send(rnn_out.at[rows(band)], rnn_out.at[rows(band)], to_all + m, (at.band_to(m), stream))
    total = from_core_split[0]
    for k in range(1, layers):
        at.arrive(from_layer_split.at[k - 1], to_layer_split + k)
        total = total + from_layer_split[k - 1]
    split_out[...] = total
    for m in turns:
        at.arrive(rnn_out.at[rows(at.band_from(m))], to_all + m)
    at.finish()


def reduce_back(g_rnn, g_split, bands, layers):
    rows, split_rows_count = g_rnn.shape[1], g_split.shape[1]
    quarter = rows // bands
    count = 4 * layers + bands * layers + bands
    return pl.pallas_call(
        partial(reduce_kernel, bands, layers),
        out_shape=[f32((rows, LANES)), f32((split_rows_count, LANES))],
        in_specs=[VMEM] * 2,
        out_specs=[VMEM] * 2,
        scratch_shapes=[
            pltpu.VMEM((layers, rows, LANES), jnp.float32),
            pltpu.VMEM((layers, split_rows_count, LANES), jnp.float32),
            pltpu.VMEM((bands - 1, layers, quarter, LANES), jnp.float32),
            pltpu.VMEM((layers, quarter, LANES), jnp.float32),
            pltpu.VMEM((layers - 1, quarter, LANES), jnp.float32),
            pltpu.VMEM((layers - 1, split_rows_count, LANES), jnp.float32),
            pltpu.SemaphoreType.DMA((count,)),
            pltpu.SemaphoreType.DMA((count,)),
        ],
        compiler_params=pltpu.CompilerParams(
            collective_id=5, has_side_effects=True, vmem_limit_bytes=VMEM_BYTES
        ),
        cost_estimate=cost(40),
        name="reduce_back",
    )(g_rnn, g_split)


def groups_of(size, slots):
    outer = math.gcd(size, slots)
    inner = size // outer
    across = [[g * inner + i for g in range(outer)] for i in range(inner)]
    within = [[g * inner + i for i in range(inner)] for g in range(outer)]
    return outer, inner, across, within


def sum_everywhere(values, sizes):
    n = sizes[0] * sizes[1]
    row = jnp.zeros((8, LANES), jnp.float32).at[0, : values.shape[0]].set(values)
    spread = jnp.broadcast_to(row[None], (n, 8, LANES))
    got = lax.all_to_all(spread, ("band", "stream"), 0, 0, tiled=True)
    return jnp.sum(got, axis=0)[0, : values.shape[0]]


def swap_cores(x):
    return lax.ppermute(x, "stream", [(s, s ^ 1) for s in range(lax.axis_size("stream"))])


def share_slots(shard, outer, across, within, axis):
    slots = shard.shape[0]
    mine = lax.all_to_all(
        shard.reshape((outer, slots // outer) + shard.shape[1:]), "stream", 0, 0,
        axis_index_groups=across, tiled=True,
    )
    inner = len(within[0])
    if inner == CORES:
        return mine, swap_cores(mine)
    both = lax.all_gather(mine, "stream", axis_index_groups=within)
    both = both.reshape((CORES, inner // CORES) + mine.shape)
    if axis == 1:
        both = both.transpose(0, 2, 3, 1, 4, 5)
        both = both.reshape(both.shape[:3] + (-1, both.shape[5]))
    else:
        both = both.transpose(0, 2, 3, 4, 1, 5)
        both = both.reshape(both.shape[:4] + (-1,))
    return both[0], both[1]


def return_slots(keep, send, outer, inner, across, within, axis):
    if inner == CORES:
        mine = keep + swap_cores(send)
    else:
        both = jnp.stack([keep, send])
        half = inner // CORES
        if axis == 1:
            both = both.reshape(both.shape[:3] + (half, -1, both.shape[4])).transpose(0, 3, 1, 2, 4, 5)
        else:
            both = both.reshape(both.shape[:4] + (half, -1)).transpose(0, 4, 1, 2, 3, 5)
        both = both.reshape((inner,) + both.shape[2:])
        mine = lax.psum_scatter(both, "stream", axis_index_groups=within, tiled=False)
    back = lax.all_to_all(mine, "stream", 0, 0, axis_index_groups=across, tiled=True)
    return back.reshape((-1,) + back.shape[2:])


def lamb_moments(gradient, mean_old, power_old, factor):
    clipped = gradient * factor
    mean_new = BETA_ONE * mean_old + (1.0 - BETA_ONE) * clipped
    power_new = BETA_TWO * power_old + (1.0 - BETA_TWO) * clipped * clipped
    return (mean_new, power_new)


def lamb_direction(weight_matrix, mean_new, power_new, decay):
    corrected = mean_new / (1.0 - BETA_ONE**STEP)
    scale_root = jnp.sqrt(power_new / (1.0 - BETA_TWO**STEP)) + ADAM_EPS
    return corrected / scale_root + decay * weight_matrix


def pack_split(splitter, banding, blocks):
    slots, wide, dmodel = splitter.shape
    columns = banding.shape[1] // blocks
    rows = -(-slots * columns // (8 * LANES)) * 8
    body_rows = splitter.reshape(slots, blocks, wide // blocks, dmodel).transpose(1, 0, 2, 3)
    flat = banding.reshape(slots, blocks, columns).transpose(1, 0, 2).reshape(blocks, slots * columns)
    flat = jnp.pad(flat, ((0, 0), (0, rows * LANES - slots * columns))).reshape(blocks, rows, LANES)
    return jnp.concatenate([body_rows.reshape(blocks, slots * wide // blocks, dmodel), flat], axis=1)


def unpack_banding(pack, start, slots, columns):
    blocks = pack.shape[0]
    flat = pack[:, start:].reshape(blocks, -1)[:, : slots * columns]
    return flat.reshape(blocks, slots, columns).transpose(1, 0, 2).reshape(slots, blocks * columns)


def body(spectrum, segments, widths, groups, cotangent, *state):
    weights, means_old, powers_old = state[:8], state[8:16], state[16:]
    splitter, widener, masker, banding, intake, recurrence, outtake, scalers = weights
    group_count = lax.axis_size("band")
    stream_count = lax.axis_size("stream")
    my_group = lax.axis_index("band")
    my_stream = lax.axis_index("stream")
    slots = splitter.shape[0]
    frames = spectrum.shape[0]
    quarter = frames // group_count
    outer, inner, across, within = groups_of(stream_count, slots)
    share = slots // outer
    my_outer = my_stream // inner
    dmodel = splitter.shape[2]
    hidden = recurrence.shape[2]
    wide = splitter.shape[1] * stream_count
    bins = spectrum.shape[2]
    blocks, out_rows, weight_rows, vec_share, vec_rows, rows = pack_rows(dmodel, hidden)
    slot_rows = wide // blocks
    columns = banding.shape[1] * stream_count // blocks
    direct = stream_count == blocks and inner == CORES

    members = (groups[:, None] == jnp.arange(group_count, dtype=jnp.int32)[None, :]).astype(jnp.int32)
    ranking = jnp.sum(jnp.cumsum(members, axis=0) * members, axis=1) - 1
    band_slot_index = groups * slots + ranking
    local_slots = my_group * slots + jnp.arange(slots, dtype=jnp.int32)
    owned = (band_slot_index[None, :] == local_slots[:, None]).astype(jnp.int32)
    edges = jnp.cumsum(widths) - widths
    slot_edges = jnp.sum(owned * edges[None, :], axis=1)
    slot_widths = jnp.sum(owned * widths[None, :], axis=1)
    slot_places = jnp.stack([slot_edges, slot_widths])
    slot_of = band_slot_index[None, :]
    lengths = jnp.sum(
        (segments[0][None, :] == jnp.arange(CLIPS, dtype=jnp.int32)[:, None]).astype(jnp.int32), axis=1
    )
    clips = jnp.stack([jnp.cumsum(lengths) - lengths, lengths])
    share_widths = lax.dynamic_slice(slot_widths, (my_outer * share,), (share,))
    core = (my_stream % CORES).astype(jnp.int32)
    mask_places = jnp.stack([share_widths, jnp.broadcast_to(core if direct else 0, (share,))]).astype(jnp.int32)

    padded = ((bins - 1) // LANES + 2) * LANES
    spec = jnp.pad(
        spectrum.transpose(1, 0, 2).reshape(2 * frames, bins), ((0, 0), (0, padded - bins))
    )
    cot_parts = cotangent.reshape(frames, outer, share, wide).transpose(1, 2, 0, 3)

    if direct:
        packs = [
            pack_rnn(intake[k], recurrence[k], outtake[k], scalers[k : k + 1], rows, vec_share)[0]
            for k in range(2)
        ]
        rnn0, w_split = gather_front(packs[0], pack_split(splitter, banding, 1)[0], group_count, outer)
        later, w_wide, w_mask, cot_parts, rnn0 = lax.optimization_barrier(
            (packs[1], widener, masker, cot_parts, rnn0)
        )
        rnn1 = lax.all_gather(later, "stream")
    else:
        whole = (
            lax.all_gather(intake, "stream", axis=3, tiled=True),
            lax.all_gather(recurrence, "stream", axis=3, tiled=True),
            lax.all_gather(outtake, "stream", axis=1, tiled=True),
            lax.all_gather(scalers, "stream", axis=1, tiled=True),
        )
        rnn0, rnn1 = (
            pack_rnn(whole[0][k], whole[1][k], whole[2][k], whole[3][k : k + 1], rows, vec_share)
            for k in range(2)
        )
        w_split = pack_split(
            lax.all_gather(splitter, "stream", axis=1, tiled=True),
            lax.all_gather(banding, "stream", axis=1, tiled=True),
            blocks,
        )
        w_wide, w_mask = widener, masker
    vec0, vec1 = (unpack_vec(p, weight_rows, vec_rows, vec_share) for p in (rnn0, rnn1))
    v_band = unpack_banding(w_split, slots * slot_rows, slots, columns)[:, None, :]

    w_mask = share_slots(w_mask, outer, across, within, 1)
    w_wide = share_slots(w_wide, outer, across, within, 2)
    cot = lax.all_to_all(cot_parts, "stream", 0, 0, axis_index_groups=across, tiled=True)

    def by_band(x, number):
        if direct:
            return exchange(x, group_count, outer, number)
        return lax.all_to_all(x, "band", 0, 0, tiled=True)

    def to_masks(x):
        x = x.reshape(group_count, outer, share, quarter, dmodel)
        if direct:
            return exchange(x, group_count, outer, 2)
        x = lax.all_to_all(x, "stream", 1, 1, axis_index_groups=across, tiled=True)
        return lax.all_to_all(x, "band", 0, 0, tiled=True)

    def from_masks(x):
        if direct:
            x = exchange(x, group_count, outer, 3)
        else:
            x = lax.all_to_all(x, "band", 0, 0, tiled=True)
            x = lax.all_to_all(x, "stream", 1, 1, axis_index_groups=across, tiled=True)
        return x.reshape(group_count * slots, quarter, dmodel)

    base = 2 * wide + dmodel
    got = time_forward(
        slot_places, clips, spec, w_split, v_band, rnn0, vec0, group_count, slot_rows, hidden
    )
    time_out, time_saved = got[0], got[1:]
    arrived = by_band(time_out, 1)
    got = band_forward(
        slot_of, arrived.reshape(group_count * slots, quarter, dmodel), rnn1, vec1, hidden
    )
    band_out, band_saved = got[0], got[1:]
    share_vec = lax.dynamic_slice_in_dim(v_band[:, :, base:], my_outer * share, share, 0)
    (
        mask_parts, grad_mixed, g_wide_keep, g_wide_send, g_mask_keep, g_mask_send, g_mask_vec,
    ) = mask_network(mask_places, to_masks(band_out), cot, w_wide, w_mask, share_vec)
    mask_reduced = return_slots(g_mask_keep, g_mask_send, outer, inner, across, within, 1)
    widened_reduced = return_slots(g_wide_keep, g_wide_send, outer, inner, across, within, 2)
    mask_parts = lax.all_to_all(mask_parts, "stream", 0, 0, axis_index_groups=across, tiled=True)
    band_grad, g_rnn1 = band_backward(slot_of, from_masks(grad_mixed), band_saved, rnn1, vec1, hidden)
    grad_time = by_band(band_grad.reshape(group_count, slots, quarter, dmodel), 4)
    if direct:
        g_rnn1 = lax.psum(lax.psum_scatter(g_rnn1, "stream", scatter_dimension=0, tiled=True), "band")
    d_spec, g_split, g_split_vec, g_rnn0 = time_backward(
        slot_places, clips, grad_time, spec, time_saved, w_split, v_band, rnn0, vec0, slot_rows, hidden
    )

    masks = mask_parts.reshape(slots, frames, wide).transpose(1, 0, 2).reshape(cotangent.shape)
    d_spec = lax.psum(d_spec, "band")
    spectrum_grad = d_spec.reshape(2, frames, padded)[:, :, :bins].transpose(1, 0, 2)

    g_mask_vec = lax.dynamic_update_slice_in_dim(
        jnp.zeros((slots, g_mask_vec.shape[2]), jnp.float32), g_mask_vec[:, 0], my_outer * share, 0
    )
    g_band = jnp.concatenate([g_split_vec[:, 0], g_mask_vec], axis=1)
    if direct:
        tail_rows = g_split.shape[1] - slots * slot_rows
        flat = g_band.reshape(slots, blocks, columns).transpose(1, 0, 2).reshape(blocks, slots * columns)
        flat = jnp.pad(flat, ((0, 0), (0, tail_rows * LANES - slots * columns)))
        g_split = lax.dynamic_update_slice_in_dim(
            g_split, flat.reshape(blocks, tail_rows, LANES), slots * slot_rows, 1
        )
        g_rnn0, g_split = reduce_back(g_rnn0, g_split, group_count, outer)
        first = unpack_rnn(g_rnn0[None], dmodel, hidden)
        second = unpack_rnn(g_rnn1, dmodel, hidden)
        rnn_grads = [jnp.stack([a, b]) for a, b in zip(first[:3], second[:3])]
        rnn_grads.append(jnp.concatenate([first[3], second[3]], axis=0))
        split_reduced = g_split[: slots * slot_rows].reshape(splitter.shape)
        band_reduced = unpack_banding(g_split[None], slots * slot_rows, slots, columns)
    else:
        first, second = unpack_rnn(g_rnn0, dmodel, hidden), unpack_rnn(g_rnn1, dmodel, hidden)
        rnn_grads = [jnp.stack([a, b]) for a, b in zip(first[:3], second[:3])]
        rnn_grads.append(jnp.concatenate([first[3], second[3]], axis=0))
        rnn_grads = [
            lax.psum(lax.psum_scatter(g, "stream", scatter_dimension=d, tiled=True), "band")
            for g, d in zip(rnn_grads, (3, 3, 1, 1))
        ]
        g_split = g_split[:, : slots * slot_rows].reshape(blocks, slots, slot_rows, dmodel)
        g_split = g_split.transpose(1, 0, 2, 3).reshape(slots, wide, dmodel)
        split_reduced = lax.psum_scatter(g_split, "stream", scatter_dimension=1, tiled=True)
        band_reduced = lax.psum_scatter(g_band, "stream", scatter_dimension=1, tiled=True)
    reduced = (split_reduced, widened_reduced, mask_reduced, band_reduced) + tuple(rnn_grads)

    shares = (1.0,) * 4 + (1.0 / group_count,) * 4
    decays = (DECAY_RATE,) * 3 + (0.0,) + (DECAY_RATE,) * 3 + (0.0,)
    sizes = (group_count, stream_count)
    sums = [sum(jnp.sum(g * g) * part for g, part in zip(reduced, shares))]
    sums += [jnp.sum(w * w) * part for w, part in zip(weights, shares)]
    totals = sum_everywhere(jnp.stack(sums), sizes)
    grad_norm = jnp.sqrt(totals[0])
    factor = jnp.minimum(1.0, CLIP_NORM / grad_norm)
    moments = [lamb_moments(g, m, p, factor) for g, m, p in zip(reduced, means_old, powers_old)]
    directions = [lamb_direction(w, m, p, d) for w, (m, p), d in zip(weights, moments, decays)]
    update_totals = sum_everywhere(
        jnp.stack([jnp.sum(d * d) * part for d, part in zip(directions, shares)]), sizes
    )
    ratios = jnp.sqrt(totals[1:]) / jnp.sqrt(update_totals + 1e-12)
    fresh = [w - LEARN_RATE * ratios[k] * d for k, (w, d) in enumerate(zip(weights, directions))]
    return (
        (masks, spectrum_grad, grad_norm)
        + tuple(fresh)
        + tuple(m for m, unused in moments)
        + tuple(p for unused, p in moments)
    )


def solution(mesh):
    stored = (
        P("band", "stream", None),
        P("band", None, "stream"),
        P("band", "stream", None),
        P("band", "stream"),
        P(None, None, None, "stream"),
        P(None, None, None, "stream"),
        P(None, "stream", None),
        P(None, "stream"),
    )
    frames_over = P("stream", None, None)
    mask_over = P("stream", "band", None, None)
    return jax.shard_map(
        body,
        mesh=mesh,
        in_specs=(frames_over, P("stream", None), P(), P(), mask_over) + stored * 3,
        out_specs=(mask_over, frames_over, P()) + stored * 3,
        check_vma=False,
    )
```

```python
from functools import partial
import math

import jax
import jax.numpy as jnp
from jax import lax
from jax.experimental import pallas as pl
from jax.experimental.pallas import tpu as pltpu
from jax.sharding import PartitionSpec as P

STEP = 10
CLIP_NORM = 5.0
LEARN_RATE = 0.5
BETA_ONE = 0.9
BETA_TWO = 0.999
ADAM_EPS = 1e-06
DECAY_RATE = 0.01
NORM_EPS = 1e-05
VAR_FLOOR = 0.25
CLIPS = 3
CLIP_MOST = 32
LANES = 128
VMEM_BYTES = 60 * 1024 * 1024
CORES = 2
SLOT_PAD = 16
MESH = pl.DeviceIdType.MESH

AB = (((1,), (0,)), ((), ()))
ABT = (((1,), (1,)), ((), ()))
ATB = (((0,), (0,)), ((), ()))


def split(x):
    hi = x.astype(jnp.bfloat16)
    lo = (x - hi.astype(jnp.float32)).astype(jnp.bfloat16)
    return hi, lo


def dot1(a, b, dims):
    return lax.dot_general(a, b, dims, preferred_element_type=jnp.float32)


def dot_parts(a, b, dims):
    return dot1(a[0], b[0], dims) + (dot1(a[1], b[0], dims) + dot1(a[0], b[1], dims))


def dot3(a, b, dims):
    return dot_parts(split(a), split(b), dims)


def sigmoid(x):
    return 0.5 * jnp.tanh(0.5 * x) + 0.5


def norm_stats(x):
    center = x - jnp.mean(x, axis=-1, keepdims=True)
    spread = jnp.mean(center * center, axis=-1, keepdims=True)
    scale = lax.rsqrt(spread + NORM_EPS)
    return center * scale, scale


def norm_back(grad_unit, unit, scale):
    first = jnp.mean(grad_unit, axis=-1, keepdims=True)
    second = jnp.mean(grad_unit * unit, axis=-1, keepdims=True)
    return scale * (grad_unit - first - unit * second)


def column_sum(x):
    return jnp.sum(x, axis=0, keepdims=True)


def pack_rows(dmodel, hidden):
    blocks = 4 * hidden // LANES
    out_rows = 2 * hidden // blocks
    weight_rows = 2 * dmodel + 2 * hidden + out_rows
    share = (2 * dmodel + 8 * hidden + dmodel) // blocks
    vec_rows = -(-share // LANES)
    return blocks, out_rows, weight_rows, share, vec_rows, -(-(weight_rows + vec_rows) // 32) * 32


def pack_rnn(w_in, w_rec, w_out, vec, rows, share):
    count = w_in.shape[2] // LANES
    parts = [
        w.reshape(2 * w.shape[1], count, LANES).transpose(1, 0, 2) for w in (w_in, w_rec)
    ] + [w_out.reshape(count, -1, LANES)]
    used = sum(p.shape[1] for p in parts)
    flat = jnp.pad(vec.reshape(count, share), ((0, 0), (0, (rows - used) * LANES - share)))
    return jnp.concatenate(parts + [flat.reshape(count, rows - used, LANES)], axis=1)


def unpack_rnn(pack, dmodel, hidden):
    blocks, out_rows, weight_rows, share, vec_rows, rows = pack_rows(dmodel, hidden)
    count = pack.shape[0]
    cuts = (0, 2 * dmodel, 2 * dmodel + 2 * hidden)
    w_in = pack[:, : cuts[1]].reshape(count, 2, dmodel, LANES).transpose(1, 2, 0, 3)
    w_rec = pack[:, cuts[1] : cuts[2]].reshape(count, 2, hidden, LANES).transpose(1, 2, 0, 3)
    return (
        w_in.reshape(2, dmodel, count * LANES),
        w_rec.reshape(2, hidden, count * LANES),
        pack[:, cuts[2] : weight_rows].reshape(count * out_rows, LANES),
        unpack_vec(pack, weight_rows, vec_rows, share),
    )


def unpack_vec(pack, weight_rows, vec_rows, share):
    count = pack.shape[0]
    flat = pack[:, weight_rows : weight_rows + vec_rows].reshape(count, vec_rows * LANES)
    return flat[:, :share].reshape(1, count * share)


class Pack:
    def __init__(self, ref, dmodel, hidden):
        self.ref, self.dmodel, self.hidden = ref, dmodel, hidden
        self.blocks, self.out_rows = pack_rows(dmodel, hidden)[:2]

    def intake(self, e, first, last):
        rows = slice(e * self.dmodel, (e + 1) * self.dmodel)
        return jnp.concatenate([self.ref[k, rows] for k in range(first, last)], axis=1)

    def recurrence(self, e, k):
        base = 2 * self.dmodel + e * self.hidden
        return self.ref[k, base : base + self.hidden]

    def outtake(self, e):
        base = 2 * self.dmodel + 2 * self.hidden
        half = self.blocks // 2
        return jnp.concatenate(
            [self.ref[k, base : base + self.out_rows] for k in range(half * e, half * (e + 1))], axis=0
        )

    def put(self, k, base, value):
        self.ref[k, base : base + value.shape[0]] = value

    def put_intake(self, e, q, value):
        for h in range(value.shape[1] // LANES):
            self.put(q * value.shape[1] // LANES + h, e * self.dmodel, value[:, h * LANES : (h + 1) * LANES])

    def put_recurrence(self, e, q, value):
        base = 2 * self.dmodel + e * self.hidden
        for h in range(value.shape[1] // LANES):
            self.put(q * value.shape[1] // LANES + h, base, value[:, h * LANES : (h + 1) * LANES])

    def put_outtake(self, e, value):
        base = 2 * self.dmodel + 2 * self.hidden
        for k in range(self.blocks // 2):
            self.put(self.blocks // 2 * e + k, base, value[k * self.out_rows : (k + 1) * self.out_rows])

    def put_vec(self, value):
        unused, unused, base, share, vec_rows, rows = pack_rows(self.dmodel, self.hidden)
        for k in range(self.blocks):
            self.ref[k, base:rows] = jnp.zeros((rows - base, LANES), jnp.float32)
            for r in range(vec_rows):
                width = min(LANES, share - r * LANES)
                at = k * share + r * LANES
                self.ref[k, base + r : base + r + 1, :width] = value[:, at : at + width]


def load_vec(pack, vec):
    unused, unused, base, share, vec_rows, unused = pack_rows(pack.dmodel, pack.hidden)
    for k in range(pack.blocks):
        for r in range(vec_rows):
            width = min(LANES, share - r * LANES)
            at = k * share + r * LANES
            vec[0:1, at : at + width] = pack.ref[k, base + r : base + r + 1, :width]


def split_recurrence(pack, hi_ref, lo_ref):
    for e in range(2):
        for k in range(pack.blocks):
            part = slice(k * LANES, (k + 1) * LANES)
            hi_ref[e, :, part], lo_ref[e, :, part] = split(pack.recurrence(e, k))


def gates_forward(x_flat, act, pack, vec, rows, block):
    hidden4 = 4 * pack.hidden
    dmodel = pack.dmodel
    parts = [split(pack.intake(e, 0, pack.blocks)) for e in range(2)]

    def one(r, carry):
        start = pl.multiple_of(r * block, block)
        unit, unused = norm_stats(x_flat(start, block))
        n = split(unit * (1.0 + vec[0:1, :dmodel]) + vec[0:1, dmodel : 2 * dmodel])
        for e in range(2):
            bias = vec[0:1, 2 * dmodel + hidden4 * e : 2 * dmodel + hidden4 * (e + 1)]
            z = dot_parts(n, parts[e], AB) + bias
            act[e][pl.ds(r * (block // 16), block // 16)] = z.reshape(block // 16, 16, hidden4)
        return carry

    lax.fori_loop(0, rows // block, one, 0)


def run_forward(steps, places, act, tc, cp, hp, h, pack, hi_ref, lo_ref, state, memory):
    hidden = pack.hidden
    split_recurrence(pack, hi_ref, lo_ref)
    for e in range(2):
        state[e][...] = jnp.zeros_like(state[e])
        memory[e][...] = jnp.zeros_like(memory[e])

    def step(j, carry):
        work = []
        for e in range(2):
            at = places(e, j)
            prior = state[e][...]
            hi, lo = split(prior)
            rows = prior.shape[0]
            first = dot1(jnp.concatenate([hi, lo], axis=0), hi_ref[e], AB)
            drive = [act[e][p] for p in at]
            drive = drive[0] if len(drive) == 1 else jnp.concatenate(drive, axis=0)
            z = first[:rows] + first[rows:] + dot1(hi, lo_ref[e], AB) + drive
            work.append((at, prior, z))
        for e in range(2):
            at, prior, z = work[e]
            ingate = sigmoid(z[:, :hidden])
            forget = sigmoid(z[:, hidden : 2 * hidden])
            candidate = jnp.tanh(z[:, 2 * hidden : 3 * hidden])
            outgate = sigmoid(z[:, 3 * hidden :])
            before = memory[e][...]
            now = forget * before + ingate * candidate
            squashed = jnp.tanh(now)
            out = outgate * squashed
            memory[e][...] = now
            state[e][...] = out
            for k, p in enumerate(at):
                part = slice(16 * k, 16 * (k + 1))
                act[e][p, :, :hidden] = ingate[part]
                act[e][p, :, hidden : 2 * hidden] = forget[part]
                act[e][p, :, 2 * hidden : 3 * hidden] = candidate[part]
                act[e][p, :, 3 * hidden :] = outgate[part]
                tc[e][p] = squashed[part]
                cp[e][p] = before[part]
                hp[e][p] = prior[part]
                h[e][p] = out[part]
        return carry

    lax.fori_loop(0, steps, step, 0)


def output_forward(count, h, pack, vec):
    hidden = h[0].shape[2]
    dmodel = pack.dmodel
    total = vec[0:1, vec.shape[1] - dmodel :]
    for e in range(2):
        states = h[e][:count].reshape(count * 16, hidden)
        total = total + dot3(states, pack.outtake(e), AB)
    return total


def run_backward(steps, places, act, dz_ref, tc, cp, dh, pack, hi_ref, lo_ref, grad_h, grad_c):
    hidden = pack.hidden
    split_recurrence(pack, hi_ref, lo_ref)
    for e in range(2):
        grad_h[e][...] = jnp.zeros_like(grad_h[e])
        grad_c[e][...] = jnp.zeros_like(grad_c[e])

    def load(ref, at):
        got = [ref[p] for p in at]
        return got[0] if len(got) == 1 else jnp.concatenate(got, axis=0)

    def step(back, carry):
        j = steps - 1 - back
        work = []
        for e in range(2):
            at = places(e, j)
            gates = load(act[e], at)
            ingate = gates[:, :hidden]
            forget = gates[:, hidden : 2 * hidden]
            candidate = gates[:, 2 * hidden : 3 * hidden]
            outgate = gates[:, 3 * hidden :]
            squashed = load(tc[e], at)
            before = load(cp[e], at)
            total_h = load(dh[e], at) + grad_h[e][...]
            total_c = grad_c[e][...] + total_h * outgate * (1.0 - squashed * squashed)
            dz = jnp.concatenate(
                [
                    total_c * candidate * ingate * (1.0 - ingate),
                    total_c * before * forget * (1.0 - forget),
                    total_c * ingate * (1.0 - candidate * candidate),
                    total_h * squashed * outgate * (1.0 - outgate),
                ],
                axis=1,
            )
            grad_c[e][...] = total_c * forget
            for k, p in enumerate(at):
                dz_ref[e][p] = dz[16 * k : 16 * (k + 1)]
            work.append(dz)
        for e in range(2):
            hi, lo = split(work[e])
            rows = hi.shape[0]
            first = dot1(jnp.concatenate([hi, lo], axis=0), hi_ref[e], ABT)
            grad_h[e][...] = first[:rows] + first[rows:] + dot1(hi, lo_ref[e], ABT)
        return carry

    lax.fori_loop(0, steps, step, 0)


def states_backward(count, dy_flat, dh, h, pack, g_pack):
    hidden = h[0].shape[2]
    dy = split(dy_flat)
    for e in range(2):
        dh[e][:count] = dot_parts(dy, split(pack.outtake(e)), ABT).reshape(count, 16, hidden)
        g_pack.put_outtake(e, dot3_parts_first(h[e][:count].reshape(count * 16, hidden), dy))


def dot3_parts_first(a, b_parts):
    return dot_parts(split(a), b_parts, ATB)


def gates_backward(count, x_flat, dy_flat, dz_ref, hp, pack, vec, g_pack, g_vec):
    dmodel = pack.dmodel
    hidden = hp[0].shape[2]
    hidden4 = 4 * hidden
    rows = count * 16
    unit, scale = norm_stats(x_flat)
    gain = 1.0 + vec[0:1, :dmodel]
    n = split(unit * gain + vec[0:1, dmodel : 2 * dmodel])
    dn = jnp.zeros((rows, dmodel), jnp.float32)
    for e in range(2):
        before = split(hp[e][:count].reshape(rows, hidden))
        for q in range(4):
            part = slice(hidden * q, hidden * (q + 1))
            dz_q = dz_ref[e][:count, :, part].reshape(rows, hidden)
            dz = split(dz_q)
            g_pack.put_recurrence(e, q, dot_parts(before, dz, ATB))
            g_pack.put_intake(e, q, dot_parts(n, dz, ATB))
            dn = dn + dot_parts(dz, split(pack.intake(e, q * pack.blocks // 4, (q + 1) * pack.blocks // 4)), ABT)
            base = 2 * dmodel + hidden4 * e + hidden * q
            g_vec[0:1, base : base + hidden] = column_sum(dz_q)
    g_vec[0:1, :dmodel] = column_sum(dn * unit)
    g_vec[0:1, dmodel : 2 * dmodel] = column_sum(dn)
    g_vec[0:1, vec.shape[1] - dmodel :] = column_sum(dy_flat)
    g_pack.put_vec(g_vec[...])
    return dy_flat + norm_back(dn * gain, unit, scale)


def tables_kernel(
    slots, share, inner, direct, segments, widths, groups, places, clips, slot_of, mask_places, counts
):
    band, stream = lax.axis_index("band"), lax.axis_index("stream")
    for s in range(slots):
        places[0, s] = 0
        places[1, s] = 0
    for c in range(CLIPS):
        clips[1, c] = 0
    for g in range(counts.shape[0]):
        counts[g] = 0

    def one_band(b, edge):
        g = groups[0, b]
        rank = counts[g]
        counts[g] = rank + 1
        slot_of[0, b] = g * slots + rank
        width = widths[0, b]

        @pl.when(g == band)
        def mine():
            places[0, rank] = edge
            places[1, rank] = width

        return edge + width

    lax.fori_loop(0, groups.shape[1], one_band, jnp.int32(0))

    def one_frame(t, carry):
        c = segments[0, t]
        clips[1, c] = clips[1, c] + 1
        return carry

    lax.fori_loop(0, segments.shape[1], one_frame, 0)
    start = jnp.int32(0)
    for c in range(CLIPS):
        clips[0, c] = start
        start = start + clips[1, c]
    for j in range(share):
        row = lax.div(stream, inner) * share + j
        mask_places[0, j] = places[1, row]
        mask_places[1, j] = lax.rem(stream, CORES) if direct else jnp.int32(0)
        mask_places[2, j] = row


def tables(segments, widths, groups, slots, share, inner, bands, direct):
    def i32(shape):
        return jax.ShapeDtypeStruct(shape, jnp.int32)

    smem = pl.BlockSpec(memory_space=pltpu.SMEM)
    return pl.pallas_call(
        partial(tables_kernel, slots, share, inner, direct),
        out_shape=[i32((2, slots)), i32((2, CLIPS)), i32(groups.shape), i32((3, share))],
        in_specs=[smem] * 3,
        out_specs=[smem] * 4,
        scratch_shapes=[pltpu.SMEM((bands,), jnp.int32)],
        name="tables",
    )(segments, widths, groups)


def clip_places(clips, spare):
    def places(e, j):
        found = []
        for c in range(CLIPS):
            start, length = clips[0, c], clips[1, c]
            frame = start + j if e == 0 else start + length - 1 - j
            found.append(jnp.where(j < length, frame, spare))
        return found

    return places


def window_of(edge):
    base = pl.multiple_of((edge // LANES) * LANES, LANES)
    return base, lax.rem(edge, LANES)


def split_rows(spec, edge, width, frames):
    wmax = LANES
    base, shift = window_of(edge)
    window = spec[:, pl.ds(base, 2 * LANES)]
    taken = pltpu.roll(window, lax.rem(2 * LANES - shift, 2 * LANES), 1)[:, :wmax]
    taken = jnp.concatenate([taken[:frames], taken[frames:]], axis=1)
    lane = lax.broadcasted_iota(jnp.int32, (frames, wmax), 1)
    inside = (lane < width).astype(jnp.float32)
    valid = jnp.concatenate([inside, inside], axis=1)
    entries = jnp.maximum(2 * width, 1).astype(jnp.float32)
    mean = jnp.sum(taken * valid, axis=-1, keepdims=True) / entries
    center = (taken - mean) * valid
    spread = jnp.sum(center * center, axis=-1, keepdims=True) / entries
    scale = lax.rsqrt(jnp.maximum(spread, VAR_FLOOR))
    moving = jnp.where(spread > VAR_FLOOR, 1.0, jnp.where(spread == VAR_FLOOR, 0.5, 0.0))
    return center * scale, scale, valid, moving, entries


def slot_weights(w_split, s, slot_rows):
    count = w_split.shape[0]
    at = pl.ds(pl.multiple_of(s * slot_rows, slot_rows), slot_rows)
    return jnp.concatenate([w_split[k, at, :] for k in range(count)], axis=0)


def time_forward_kernel(
    slot_rows, places_s, clips, spec, w_split, rnn,
    out, v_band, x, act0, act1, tc0, tc1, cp0, cp1, hp0, hp1, h0, h1,
    hi_ref, lo_ref, s0, s1, m0, m1, y, mixed, vec,
):
    slots = out.shape[1]
    frames, unused, dmodel = x.shape
    wide = w_split.shape[0] * slot_rows
    pack = Pack(rnn, dmodel, h0.shape[2])
    load_vec(pack, vec)
    v_band[...] = jnp.zeros_like(v_band)
    columns = v_band.shape[1] // w_split.shape[0]
    for k in range(w_split.shape[0]):
        for h in range(0, columns, LANES):
            width = min(LANES, columns - h)
            at = slots * slot_rows + SLOT_PAD * (h // LANES)
            v_band[:, k * columns + h : k * columns + h + width] = w_split[k, at : at + SLOT_PAD, :width]
    x[...] = jnp.zeros_like(x)
    for a in (act0, act1):
        a[frames] = jnp.zeros_like(a[frames])

    def one_slot(s, carry):
        unit, unused, valid, moving, entries = split_rows(spec, places_s[0, s], places_s[1, s], frames)
        row = v_band[pl.ds(s, 1), : 2 * wide + dmodel]
        z = (unit * (1.0 + row[:, :wide]) + row[:, wide : 2 * wide]) * valid
        y[s] = dot3(z, slot_weights(w_split, s, slot_rows), AB) + row[:, 2 * wide : 2 * wide + dmodel]
        return carry

    lax.fori_loop(0, slots, one_slot, 0)
    for s in range(slots):
        x[:, s, :] = y[s]
    act = (act0, act1)

    def x_flat(start, size):
        return x[pl.ds(start // 16, size // 16)].reshape(size, dmodel)

    gates_forward(x_flat, act, pack, vec, frames * 16, 256)
    run_forward(
        CLIP_MOST, clip_places(clips, frames), act, (tc0, tc1), (cp0, cp1), (hp0, hp1), (h0, h1),
        pack, hi_ref, lo_ref, (s0, s1), (m0, m1),
    )
    total = output_forward(frames, (h0, h1), pack, vec)
    x_all = x[...].reshape(frames * 16, dmodel)
    mixed[...] = (x_all + total).reshape(frames, 16, dmodel)
    parts, unused_slots, quarter, unused = out.shape
    for s in range(slots):
        for q in range(parts):
            out[q, s] = mixed[q * quarter : (q + 1) * quarter, s, :]


def f32(shape):
    return jax.ShapeDtypeStruct(shape, jnp.float32)


def saved_shapes(count, hidden):
    wide = [f32((count, 16, 4 * hidden))] * 2
    thin = [f32((count, 16, hidden))] * 8
    return wide + thin


def vec_scratch(dmodel, hidden):
    return pltpu.VMEM((1, 3 * dmodel + 8 * hidden), jnp.float32)


def rec_scratch(rows, hidden):
    return [
        pltpu.VMEM((2, hidden, 4 * hidden), jnp.bfloat16),
        pltpu.VMEM((2, hidden, 4 * hidden), jnp.bfloat16),
    ] + [pltpu.VMEM((rows, hidden), jnp.float32)] * 4


SMEM = pl.BlockSpec(memory_space=pltpu.SMEM)
VMEM = pl.BlockSpec(memory_space=pltpu.VMEM)
ANY = pl.BlockSpec(memory_space=pl.ANY)
PARAMS = pltpu.CompilerParams(vmem_limit_bytes=VMEM_BYTES)


def cost(micros):
    return pl.CostEstimate(flops=int(micros * 1.1e9), bytes_accessed=int(micros * 3e6), transcendentals=0)


def time_forward(slot_places, clips, spec, w_split, rnn, parts, slots, band_columns, slot_rows, hidden):
    dmodel = w_split.shape[2]
    frames = spec.shape[0] // 2
    return pl.pallas_call(
        partial(time_forward_kernel, slot_rows),
        out_shape=[
            f32((parts, slots, frames // parts, dmodel)), f32((SLOT_PAD, band_columns)), f32((frames, 16, dmodel)),
        ]
        + saved_shapes(frames + 1, hidden),
        in_specs=[SMEM, SMEM] + [VMEM] * 3,
        out_specs=[VMEM] * 13,
        scratch_shapes=rec_scratch(16 * CLIPS, hidden)
        + [pltpu.VMEM((slots, frames, dmodel), jnp.float32)]
        + [pltpu.VMEM((frames, 16, dmodel), jnp.float32), vec_scratch(dmodel, hidden)],
        compiler_params=PARAMS,
        cost_estimate=cost(35),
        name="time_forward",
    )(slot_places, clips, spec, w_split, rnn)


def time_backward_kernel(
    slot_rows, places_s, clips, my_outer, dy_in, spec, x, act0, act1, tc0, tc1, cp0, cp1, hp0, hp1, h0, h1,
    w_split, v_band, rnn, g_mask_vec,
    d_spec, g_split, g_rnn,
    hi_ref, lo_ref, s0, s1, m0, m1, dy, vec, g_vec, g_band, dh0, dh1, dz0, dz1,
):
    slots = dy_in.shape[1]
    frames, unused, dmodel = x.shape
    wide = w_split.shape[0] * slot_rows
    parts, unused_slots, quarter, unused = dy_in.shape
    pack, g_pack = Pack(rnn, dmodel, h0.shape[2]), Pack(g_rnn, dmodel, h0.shape[2])
    load_vec(pack, vec)
    dy[...] = jnp.zeros_like(dy)
    for s in range(slots):
        for q in range(parts):
            dy[q * quarter : (q + 1) * quarter, s, :] = dy_in[q, s]
    dy_flat = dy[...].reshape(frames * 16, dmodel)
    states_backward(frames, dy_flat, (dh0, dh1), (h0, h1), pack, g_pack)
    for d in (dh0, dh1):
        d[frames] = jnp.zeros_like(d[frames])
    run_backward(
        CLIP_MOST, clip_places(clips, frames), (act0, act1), (dz0, dz1), (tc0, tc1), (cp0, cp1),
        (dh0, dh1), pack, hi_ref, lo_ref, (s0, s1), (m0, m1),
    )
    x_flat = x[...].reshape(frames * 16, dmodel)
    dx = gates_backward(
        frames, x_flat, dy[...].reshape(frames * 16, dmodel), (dz0, dz1), (hp0, hp1), pack, vec, g_pack, g_vec
    )
    dy[...] = dx.reshape(frames, 16, dmodel)
    d_spec[...] = jnp.zeros_like(d_spec)
    g_split[:, slots * slot_rows :] = jnp.zeros_like(g_split[:, slots * slot_rows :])
    g_band[...] = jnp.zeros_like(g_band)

    for s in range(slots):
        edge, width = places_s[0, s], places_s[1, s]
        unit, scale, valid, moving, entries = split_rows(spec, edge, width, frames)
        row = v_band[s : s + 1, : 2 * wide + dmodel]
        gain = 1.0 + row[:, :wide]
        z = (unit * gain + row[:, wide : 2 * wide]) * valid
        demb = dy[:, s, :]
        demb_parts = split(demb)
        g_slot = dot_parts(split(z), demb_parts, ATB)
        for k in range(w_split.shape[0]):
            g_split[k, s * slot_rows : (s + 1) * slot_rows] = g_slot[k * slot_rows : (k + 1) * slot_rows]
        dz = dot_parts(demb_parts, split(slot_weights(w_split, s, slot_rows)), ABT) * valid
        g_band[s : s + 1, :wide] = column_sum(dz * unit)
        g_band[s : s + 1, wide : 2 * wide] = column_sum(dz)
        g_band[s : s + 1, 2 * wide : 2 * wide + dmodel] = column_sum(demb)
        du = dz * gain
        first = jnp.sum(du, axis=-1, keepdims=True) / entries
        second = jnp.sum(du * unit, axis=-1, keepdims=True) / entries
        dt = scale * (du - first - moving * unit * second) * valid
        base, shift = window_of(edge)
        stacked = jnp.concatenate([dt[:, :LANES], dt[:, LANES:]], axis=0)
        padded = jnp.concatenate([stacked, jnp.zeros_like(stacked)], axis=1)
        d_spec[:, pl.ds(base, 2 * LANES)] += pltpu.roll(padded, shift, 1)

    share = g_mask_vec.shape[0]
    for j in range(share):
        g_band[pl.ds(my_outer[0] * share + j, 1), 2 * wide + dmodel :] = g_mask_vec[j]
    gathered = g_band[...]
    blocks = w_split.shape[0]
    columns = gathered.shape[1] // blocks
    for k in range(blocks):
        for h in range(0, columns, LANES):
            width = min(LANES, columns - h)
            at = slots * slot_rows + SLOT_PAD * (h // LANES)
            g_split[k, at : at + SLOT_PAD, :width] = gathered[:, k * columns + h : k * columns + h + width]


def time_backward(
    slot_places, clips, my_outer, dy, spec, saved, w_split, v_band, rnn, g_mask_vec, slot_rows, hidden
):
    band_columns = v_band.shape[1]
    dmodel = w_split.shape[2]
    frames = spec.shape[0] // 2
    return pl.pallas_call(
        partial(time_backward_kernel, slot_rows),
        out_shape=[f32(spec.shape), f32(w_split.shape), f32(rnn.shape)],
        in_specs=[SMEM] * 3 + [VMEM] * (3 + 10 + 4),
        out_specs=[VMEM] * 3,
        scratch_shapes=rec_scratch(16 * CLIPS, hidden)
        + [pltpu.VMEM((frames, 16, dmodel), jnp.float32)] + [vec_scratch(dmodel, hidden)] * 2
        + [pltpu.VMEM((SLOT_PAD, band_columns), jnp.float32)]
        + [pltpu.VMEM((frames + 1, 16, hidden), jnp.float32)] * 2
        + [pltpu.VMEM((frames + 1, 16, 4 * hidden), jnp.float32)] * 2,
        compiler_params=PARAMS,
        cost_estimate=cost(50),
        name="time_backward",
    )(slot_places, clips, my_outer, dy, spec, *saved, w_split, v_band, rnn, g_mask_vec)


def band_places(bands):
    return lambda e, j: [j if e == 0 else bands - 1 - j]


def band_forward_kernel(
    slot_of, arrived, rnn,
    out, x, act0, act1, tc0, tc1, cp0, cp1, hp0, hp1, h0, h1,
    hi_ref, lo_ref, s0, s1, m0, m1, vec,
):
    bands, unused, dmodel = x.shape
    pack = Pack(rnn, dmodel, h0.shape[2])
    load_vec(pack, vec)

    def fetch(b, carry):
        x[b] = arrived[slot_of[0, b]]
        return carry

    lax.fori_loop(0, bands, fetch, 0)
    act = (act0, act1)

    def x_flat(start, size):
        return x[...].reshape(bands * 16, dmodel)

    gates_forward(x_flat, act, pack, vec, bands * 16, bands * 16)
    run_forward(
        bands, band_places(bands), act, (tc0, tc1), (cp0, cp1), (hp0, hp1), (h0, h1),
        pack, hi_ref, lo_ref, (s0, s1), (m0, m1),
    )
    total = output_forward(bands, (h0, h1), pack, vec)
    whole = (x[...].reshape(bands * 16, dmodel) + total).reshape(bands, 16, dmodel)
    out[...] = jnp.zeros_like(out)
    for b in range(bands):
        out[slot_of[0, b]] = whole[b]


def band_forward(slot_of, arrived, rnn, hidden):
    bands = slot_of.shape[1]
    dmodel = arrived.shape[2]
    return pl.pallas_call(
        band_forward_kernel,
        out_shape=[f32(arrived.shape), f32((bands, 16, dmodel))] + saved_shapes(bands, hidden),
        in_specs=[SMEM] + [VMEM] * 2,
        out_specs=[VMEM] * 12,
        scratch_shapes=rec_scratch(16, hidden) + [vec_scratch(dmodel, hidden)],
        compiler_params=PARAMS,
        cost_estimate=cost(28),
        name="band_forward",
    )(slot_of, arrived, rnn)


def band_backward_kernel(
    slot_of, arrived, x, act0, act1, tc0, tc1, cp0, cp1, hp0, hp1, h0, h1, rnn,
    out, g_rnn,
    hi_ref, lo_ref, s0, s1, m0, m1, dy, vec, g_vec, dh0, dh1, dz0, dz1,
):
    bands, unused, dmodel = x.shape
    pack, g_pack = Pack(rnn, dmodel, h0.shape[2]), Pack(g_rnn, dmodel, h0.shape[2])
    load_vec(pack, vec)

    def fetch(b, carry):
        dy[b] = arrived[slot_of[0, b]]
        return carry

    lax.fori_loop(0, bands, fetch, 0)
    states_backward(bands, dy[...].reshape(bands * 16, dmodel), (dh0, dh1), (h0, h1), pack, g_pack)
    run_backward(
        bands, band_places(bands), (act0, act1), (dz0, dz1), (tc0, tc1), (cp0, cp1), (dh0, dh1),
        pack, hi_ref, lo_ref, (s0, s1), (m0, m1),
    )
    dx = gates_backward(
        bands, x[...].reshape(bands * 16, dmodel), dy[...].reshape(bands * 16, dmodel),
        (dz0, dz1), (hp0, hp1), pack, vec, g_pack, g_vec,
    ).reshape(bands, 16, dmodel)
    out[...] = jnp.zeros_like(out)
    for b in range(bands):
        out[slot_of[0, b]] = dx[b]


def band_backward(slot_of, arrived, saved, rnn, hidden):
    bands = slot_of.shape[1]
    dmodel = arrived.shape[2]
    return pl.pallas_call(
        band_backward_kernel,
        out_shape=[f32(arrived.shape), f32(rnn.shape)],
        in_specs=[SMEM] + [VMEM] * (2 + 10 + 1),
        out_specs=[VMEM] * 2,
        scratch_shapes=rec_scratch(16, hidden)
        + [pltpu.VMEM((bands, 16, dmodel), jnp.float32)] + [vec_scratch(dmodel, hidden)] * 2
        + [pltpu.VMEM((bands, 16, hidden), jnp.float32)] * 2
        + [pltpu.VMEM((bands, 16, 4 * hidden), jnp.float32)] * 2,
        compiler_params=PARAMS,
        cost_estimate=cost(43),
        name="band_backward",
    )(slot_of, arrived, *saved, rnn)


def in_turn(core, mine, other):
    return [jnp.where(core == 0, mine, other), jnp.where(core == 0, other, mine)]


def pack_pieces(mask, wide):
    lead, r, w = mask.shape[:2], mask.shape[2], mask.shape[3] // 2
    mask = mask.reshape(lead + (r, 2, w)).transpose(0, 1, 3, 2, 4).reshape(lead + (2 * r, w))
    wide = wide.reshape(lead + (2, r // 2, w // 2)).transpose(0, 1, 3, 2, 4)
    return jnp.concatenate([mask, wide.reshape(lead + (r // 2, w))], axis=2)


def unpack_pieces(pack, r):
    lead, w = pack.shape[:2], pack.shape[3]
    mask = pack[:, :, : 2 * r].reshape(lead + (2, r, w)).transpose(0, 1, 3, 2, 4).reshape(lead + (r, 2 * w))
    wide = pack[:, :, 2 * r :].reshape(lead + (r // 2, 2, w // 2)).transpose(0, 1, 3, 2, 4)
    return mask, wide.reshape(lead + (r, w // 2))


def load_mask_piece(value, r):
    return jnp.concatenate([value[:r], value[r : 2 * r]], axis=1)


def load_wide_piece(value):
    half = value.shape[1] // 2
    return jnp.concatenate([value[:, :half], value[:, half:]], axis=0)


def mask_kernel(base, places, arrived, mine, other, v_band, keep, send, grad, g_vec):
    s = pl.program_id(0)
    parts, streams, unused, quarter, dmodel = arrived.shape
    outer, unused, total_rows, wide = mine.shape
    piece_rows = send.shape[2]
    frames = total_rows - piece_rows
    half = wide // 2
    v = v_band[pl.ds(places[2, s], 1), base:]
    mlp = (v.shape[1] - 2 * dmodel) - 2 * wide
    r = mlp // (2 * outer)
    core = places[1, 0]
    x = jnp.concatenate([arrived[q, g, 0] for g in range(streams) for q in range(parts)], axis=0)
    w_wide, w_mask = [], []
    for g in range(outer):
        w_mask += in_turn(
            core, load_mask_piece(mine[g, 0, : 2 * r], r), load_mask_piece(other[g, 0, : 2 * r], r)
        )
        w_wide += in_turn(
            core, load_wide_piece(mine[g, 0, 2 * r : piece_rows]), load_wide_piece(other[g, 0, 2 * r : piece_rows])
        )
    w_wide, w_mask = jnp.concatenate(w_wide, axis=0), jnp.concatenate(w_mask, axis=0)
    cot = jnp.concatenate([mine[g, 0, piece_rows:] for g in range(outer)], axis=0)
    gain = 1.0 + v[:, :dmodel]
    unit, scale = norm_stats(x)
    p = split(unit * gain + v[:, dmodel : 2 * dmodel])
    wide_parts = split(w_wide)
    mask_parts = split(w_mask)
    q = jnp.tanh(dot_parts(p, wide_parts, ABT) + v[:, 2 * dmodel : 2 * dmodel + mlp])
    q_parts = split(q)
    raw = dot_parts(q_parts, mask_parts, AB) + v[:, 2 * dmodel + mlp :]
    lane = lax.broadcasted_iota(jnp.int32, (1, half), 1)
    inside = (lane < places[0, s]).astype(jnp.float32)
    valid = jnp.concatenate([inside, inside], axis=1)
    value = raw[:, :wide]
    gate = sigmoid(raw[:, wide:])
    masks = value * gate * valid
    dm = cot * valid
    dr = jnp.concatenate([dm * gate, dm * value * gate * (1.0 - gate)], axis=1)
    dr_parts = split(dr)
    g_mask = dot_parts(q_parts, dr_parts, ATB)
    dq = dot_parts(dr_parts, mask_parts, ABT)
    da = dq * (1.0 - q * q)
    da_parts = split(da)
    g_wide = dot_parts(da_parts, p, ATB)
    for g in range(outer):
        first, second = slice(2 * g * r, (2 * g + 1) * r), slice((2 * g + 1) * r, (2 * g + 2) * r)
        for ref, got in zip((keep, send), in_turn(core, g_mask[first], g_mask[second])):
            ref[g, 0, :r] = got[:, :wide]
            ref[g, 0, r : 2 * r] = got[:, wide:]
        for ref, got in zip((keep, send), in_turn(core, g_wide[first], g_wide[second])):
            ref[g, 0, 2 * r : piece_rows, :half] = got[: r // 2]
            ref[g, 0, 2 * r : piece_rows, half:] = got[r // 2 :]
        keep[g, 0, piece_rows:] = masks[g * frames : (g + 1) * frames]
    dp = dot_parts(da_parts, wide_parts, AB)
    g_vec[0, :, :dmodel] = column_sum(dp * unit)
    g_vec[0, :, dmodel : 2 * dmodel] = column_sum(dp)
    g_vec[0, :, 2 * dmodel : 2 * dmodel + mlp] = column_sum(da)
    g_vec[0, :, 2 * dmodel + mlp :] = column_sum(dr)
    dx = norm_back(dp * gain, unit, scale)
    k = 0
    for g in range(streams):
        for q_ in range(parts):
            grad[q_, g, 0] = dx[k * quarter : (k + 1) * quarter]
            k += 1


def mask_network(places, arrived, mine, other, v_band, base, piece_rows):
    parts, streams, slots, quarter, dmodel = arrived.shape
    outer, unused, rows, wide = mine.shape

    def second(count):
        return pl.BlockSpec((outer, 1, count, wide), lambda s: (0, s, 0, 0))

    moving = pl.BlockSpec((parts, streams, 1, quarter, dmodel), lambda s: (0, 0, s, 0, 0))
    columns = v_band.shape[1] - base
    vector = pl.BlockSpec((1, 1, columns), lambda s: (s, 0, 0))
    return pl.pallas_call(
        partial(mask_kernel, base),
        grid=(slots,),
        out_shape=[
            f32(mine.shape), f32((outer, slots, piece_rows, wide)), f32(arrived.shape), f32((slots, 1, columns)),
        ],
        in_specs=[SMEM, moving, second(rows), second(rows), VMEM],
        out_specs=[second(rows), second(piece_rows), moving, vector],
        compiler_params=PARAMS,
        cost_estimate=cost(12),
        name="mask_network",
    )(places, arrived, mine, other, v_band)


class Links:
    def __init__(self, bands, layers, send_sems, recv_sems):
        self.bands, self.layers = bands, layers
        self.band, self.stream = lax.axis_index("band"), lax.axis_index("stream")
        self.layer, self.core = lax.div(self.stream, CORES), lax.rem(self.stream, CORES)
        self.other = self.stream + 1 - 2 * self.core
        self.send_sems, self.recv_sems = send_sems, recv_sems
        self.started = []

    def band_to(self, m):
        return lax.rem(self.band + m, self.bands)

    def band_from(self, m):
        return lax.rem(self.band + self.bands - m, self.bands)

    def layer_to(self, k):
        return lax.rem(self.layer + k, self.layers)

    def layer_from(self, k):
        return lax.rem(self.layer + self.layers - k, self.layers)

    def own(self, layer):
        return layer * CORES + self.core

    def across(self, layer):
        return layer * CORES + 1 - self.core

    def greet(self, partners):
        barrier = pltpu.get_barrier_semaphore()
        for partner in partners:
            pl.semaphore_signal(barrier, inc=1, device_id=partner, device_id_type=MESH)
        pl.semaphore_wait(barrier, len(partners))

    def copy(self, source, target, index, partner):
        return pltpu.make_async_remote_copy(
            src_ref=source, dst_ref=target, send_sem=self.send_sems.at[index],
            recv_sem=self.recv_sems.at[index], device_id=partner, device_id_type=MESH,
        )

    def send(self, source, target, index, partner):
        copy = self.copy(source, target, index, partner)
        copy.start()
        self.started.append(copy)

    def arrive(self, target, index):
        self.copy(target, target, index, (self.band, self.other)).wait_recv()

    def finish(self):
        for copy in self.started:
            copy.wait_send()


def gather_kernel(
    bands, layers, intake, recurrence, outtake, scalers, splitter, banding, masker, widener, cot,
    rnn_all, split_all, rnn_later, pieces,
    vec_rows, band_rows, staged, send_sems, recv_sems, local_sems,
):
    at = Links(bands, layers, send_sems, recv_sems)
    band, stream, other = at.band, at.stream, at.other
    rows_all = rnn_all.shape[1]
    quarter = rows_all // bands
    used = []

    def local(source, target):
        copy = pltpu.make_async_copy(source, target, local_sems.at[len(used)])
        copy.start()
        used.append(copy)
        return copy

    vec_rows[...] = jnp.zeros_like(vec_rows)
    for k in range(2):
        for h in range(0, scalers.shape[1], LANES):
            width = min(LANES, scalers.shape[1] - h)
            vec_rows[k, h // LANES : h // LANES + 1, :width] = scalers[k : k + 1, h : h + width]
    band_rows[...] = jnp.zeros_like(band_rows)
    slots = banding.shape[0]
    for h in range(0, banding.shape[1], LANES):
        width = min(LANES, banding.shape[1] - h)
        base = SLOT_PAD * (h // LANES)
        band_rows[base : base + slots, :width] = banding[:, h : h + width]

    def own_pack(k, target):
        a = intake.shape[1]
        b = a + recurrence.shape[1]
        c = b + outtake.shape[1]
        return [
            local(intake.at[k], target.at[pl.ds(0, a)]),
            local(recurrence.at[k], target.at[pl.ds(a, b - a)]),
            local(outtake.at[k], target.at[pl.ds(b, c - b)]),
            local(vec_rows.at[k], target.at[pl.ds(c, rows_all - c)]),
        ]

    mine, mine_split = rnn_all.at[stream], split_all.at[stream]
    first = own_pack(0, mine)
    split_rows_count = splitter.shape[0]
    second = [
        local(splitter, mine_split.at[pl.ds(0, split_rows_count)]),
        local(band_rows, mine_split.at[pl.ds(split_rows_count, band_rows.shape[0])]),
    ]
    at.greet(
        [(at.band_to(m), stream) for m in range(1, bands)]
        + [(band, at.own(at.layer_to(k))) for k in range(1, layers)]
        + [(band, other)]
    )
    steps = range(1, layers)
    turns = range(1, bands)

    def rows(b):
        return pl.ds(b * quarter, quarter)

    to_layer, to_layer_split, to_band = 0, layers, 2 * layers
    to_core = to_band + layers * bands
    to_core_split = to_core + layers * bands
    for copy in first:
        copy.wait()
    for k in steps:
        piece = rnn_all.at[stream, rows(band)]
        at.send(piece, piece, to_layer + k, (band, at.own(at.layer_to(k))))
    for copy in second:
        copy.wait()
    for k in steps:
        at.send(mine_split, mine_split, to_layer_split + k, (band, at.own(at.layer_to(k))))
    at.send(mine, mine, to_core, (band, other))
    at.send(mine_split, mine_split, to_core_split, (band, other))
    rest = own_pack(1, rnn_later)
    r, wide = masker.shape[1], masker.shape[2] // 2
    half = wide // 2
    rest += [
        local(masker.at[:, :, pl.ds(0, wide)], pieces.at[:, pl.ds(0, r), :]),
        local(masker.at[:, :, pl.ds(wide, wide)], pieces.at[:, pl.ds(r, r), :]),
        local(widener.at[:, pl.ds(0, r // 2), :], pieces.at[:, pl.ds(2 * r, r // 2), pl.ds(0, half)]),
        local(widener.at[:, pl.ds(r // 2, r // 2), :], pieces.at[:, pl.ds(2 * r, r // 2), pl.ds(half, half)]),
    ]
    for s in range(slots):
        for part in range(2):
            staged[s, :, part * half : (part + 1) * half] = cot[:, s, part, :]
    rest.append(local(staged, pieces.at[:, pl.ds(2 * r + r // 2, staged.shape[1]), :]))
    for k in steps:
        source = at.own(at.layer_from(k))
        piece = rnn_all.at[source, rows(band)]
        at.arrive(piece, to_layer + k)
        for m in turns:
            at.send(piece, piece, to_band + k * bands + m, (at.band_to(m), stream))
        at.send(piece, piece, to_core + k * bands, (band, other))
    for k in steps:
        source = at.own(at.layer_from(k))
        for m in turns:
            piece = rnn_all.at[source, rows(at.band_from(m))]
            at.arrive(piece, to_band + k * bands + m)
            at.send(piece, piece, to_core + k * bands + m, (band, other))
    for k in steps:
        piece = split_all.at[at.own(at.layer_from(k))]
        at.arrive(piece, to_layer_split + k)
        at.send(piece, piece, to_core_split + k, (band, other))
    at.arrive(rnn_all.at[other], to_core)
    at.arrive(split_all.at[other], to_core_split)
    for k in steps:
        source = at.across(at.layer_from(k))
        for m in range(bands):
            at.arrive(rnn_all.at[source, rows(at.band_from(m))], to_core + k * bands + m)
        at.arrive(split_all.at[source], to_core_split + k)
    at.finish()
    for copy in rest:
        copy.wait()


def gather_front(intake, recurrence, outtake, scalers, splitter, banding, masker, widener, cot, rows, bands, layers):
    count = 2 * layers + 2 * layers * bands + layers
    streams = layers * CORES
    slots = banding.shape[0]
    strips = -(-banding.shape[1] // LANES)
    r, wide = masker.shape[1], masker.shape[2] // 2
    frames = cot.shape[0]
    weight_rows = intake.shape[1] + recurrence.shape[1] + outtake.shape[1]
    split_rows_count = splitter.shape[0] + SLOT_PAD * strips
    return pl.pallas_call(
        partial(gather_kernel, bands, layers),
        out_shape=[
            f32((streams, rows, LANES)), f32((streams, split_rows_count, LANES)), f32((rows, LANES)),
            f32((slots, 2 * r + r // 2 + frames, wide)),
        ],
        in_specs=[ANY, ANY, ANY, VMEM, ANY, VMEM, ANY, ANY, VMEM],
        out_specs=[ANY] * 4,
        scratch_shapes=[
            pltpu.VMEM((2, rows - weight_rows, LANES), jnp.float32),
            pltpu.VMEM((SLOT_PAD * strips, LANES), jnp.float32),
            pltpu.VMEM((slots, frames, wide), jnp.float32),
            pltpu.SemaphoreType.DMA((count,)), pltpu.SemaphoreType.DMA((count,)), pltpu.SemaphoreType.DMA((16,)),
        ],
        compiler_params=pltpu.CompilerParams(
            collective_id=0, has_side_effects=True, vmem_limit_bytes=32 * 1024 * 1024
        ),
        cost_estimate=cost(30),
        name="gather_front",
    )(intake, recurrence, outtake, scalers, splitter, banding, masker, widener, cot)


def exchange_kernel(bands, layers, source, target, send_sems, recv_sems, local_sem):
    at = Links(bands, layers, send_sems, recv_sems)
    wide = source.shape[1] == layers
    turns = [(m, k) for k in range(layers if wide else 1) for m in range(bands) if m + k]

    def place(ref, band, layer):
        return ref.at[band, layer] if wide else ref.at[band]

    def stream_of(layer):
        return at.own(layer) if wide else at.stream

    at.greet([(at.band_to(m), stream_of(at.layer_to(k))) for m, k in turns])
    for m, k in turns:
        band, layer = at.band_to(m), at.layer_to(k)
        at.send(
            place(source, band, layer), place(target, at.band, at.layer), k * bands + m, (band, stream_of(layer))
        )
    local = pltpu.make_async_copy(
        place(source, at.band, at.layer), place(target, at.band, at.layer), local_sem
    )
    local.start()
    for m, k in turns:
        at.arrive(place(target, at.band_from(m), at.layer_from(k)), k * bands + m)
    at.finish()
    local.wait()


def exchange(x, bands, layers, number):
    count = bands * layers
    return pl.pallas_call(
        partial(exchange_kernel, bands, layers),
        out_shape=f32(x.shape),
        in_specs=[ANY],
        out_specs=ANY,
        scratch_shapes=[
            pltpu.SemaphoreType.DMA((count,)), pltpu.SemaphoreType.DMA((count,)), pltpu.SemaphoreType.DMA,
        ],
        compiler_params=pltpu.CompilerParams(collective_id=number, has_side_effects=True),
        cost_estimate=cost(8),
        name="exchange",
    )(x)


class Grads:
    def __init__(self, pieces, rnn0, rnn1, banded, dims):
        self.pieces, self.rnn, self.banded = pieces, (rnn0, rnn1), banded
        self.slots, self.slot_rows, self.r, self.piece_rows, self.dmodel, self.hidden = dims

    def of_slot(self, s):
        at = pl.ds(pl.multiple_of(s * self.slot_rows, self.slot_rows), self.slot_rows)
        r = self.r
        return [
            (0, (s,), self.banded[at, :]),
            (1, (s,), load_wide_piece(self.pieces[s, 2 * r : self.piece_rows])),
            (2, (s,), load_mask_piece(self.pieces[s, : 2 * r], r)),
        ]

    def rest(self, columns, share):
        found = []
        base = self.slots * self.slot_rows
        strips = []
        for h in range(0, columns, LANES):
            at = base + SLOT_PAD * (h // LANES)
            strips.append(self.banded[at : at + self.slots, : min(LANES, columns - h)])
        found.append((3, (...,), jnp.concatenate(strips, axis=1)))
        unused, out_rows, weight_rows, unused, vec_rows, unused = pack_rows(self.dmodel, self.hidden)
        for k in range(2):
            pack = self.rnn[k]
            at = 0
            for e in range(2):
                found.append((4, (k, e), pack[at : at + self.dmodel]))
                at += self.dmodel
            for e in range(2):
                found.append((5, (k, e), pack[at : at + self.hidden]))
                at += self.hidden
            found.append((6, (k,), pack[at : at + out_rows]))
            at += out_rows
            strips = [
                pack[at + r : at + r + 1, : min(LANES, share - r * LANES)] for r in range(vec_rows)
            ]
            found.append((7, (slice(k, k + 1),), jnp.concatenate(strips, axis=1)))
        return found


DECAYS = (DECAY_RATE,) * 3 + (0.0,) + (DECAY_RATE,) * 3 + (0.0,)


def lamb_moments(gradient, mean_old, power_old, factor):
    clipped = gradient * factor
    mean_new = BETA_ONE * mean_old + (1.0 - BETA_ONE) * clipped
    power_new = BETA_TWO * power_old + (1.0 - BETA_TWO) * clipped * clipped
    return (mean_new, power_new)


def lamb_direction(weight_matrix, mean_new, power_new, decay):
    corrected = mean_new / (1.0 - BETA_ONE**STEP)
    scale_root = jnp.sqrt(power_new / (1.0 - BETA_TWO**STEP)) + ADAM_EPS
    return corrected / scale_root + decay * weight_matrix


def add_up(rows):
    tile = jnp.zeros((16, LANES), jnp.float32)
    line = lax.broadcasted_iota(jnp.int32, (16, LANES), 0)
    for i, row in enumerate(rows):
        tile = jnp.where(line == i, jnp.sum(row, axis=1, keepdims=True), tile)
    return tile


def finish_kernel(bands, layers, dims, g_rnn0, g_split, g_rnn1, d_spec, back, *refs):
    state, refs = refs[:24], refs[24:]
    out, rnn0, rnn1, banded, spec_out = refs[:5]
    pieces, refs = refs[5], refs[6:]
    held_state, refs = refs[:24], refs[24:]
    (
        own0, own_split, parts1, sum1, from_core, from_core_split, from_core1, from_band, held,
        from_layer, from_layer_split, from_layer1, spec_in, spec_own, near, far, tiles,
        local_sems, send_sems, recv_sems,
    ) = refs
    at = Links(bands, layers, send_sems, recv_sems)
    band, stream, other = at.band, at.stream, at.other
    streams = layers * CORES
    quarter = g_rnn0.shape[1] // bands
    spec_rows = d_spec.shape[0] // bands
    order = list(range(1, layers)) + [0]
    turns = range(1, bands)
    taken = [0]

    def take(count):
        taken[0] += count
        return taken[0] - count

    locals_used = []

    def local(source, target):
        copy = pltpu.make_async_copy(source, target, local_sems.at[len(locals_used)])
        copy.start()
        locals_used.append(copy)
        return copy

    def rows(b):
        return pl.ds(pl.multiple_of(b * quarter, 8), quarter)

    def spec_part(b):
        return pl.ds(pl.multiple_of(b * spec_rows, 8), spec_rows)

    def stream_to(k):
        return lax.rem(stream + k, streams)

    at.greet(
        [(band, stream_to(k)) for k in range(1, streams)] + [(at.band_to(m), stream) for m in turns]
    )
    to_core, to_core_split, to_core1 = take(layers), take(layers), take(layers)
    to_layer, to_layer_split, to_layer1 = take(layers), take(layers), take(layers)
    to_band, to_all0, to_all1 = take(bands * layers), take(bands), take(bands)
    to_spec, to_spec_all = take(bands), take(bands)
    for k in order:
        at.send(g_rnn0.at[at.across(at.layer_to(k))], from_core.at[k], to_core + k, (band, other))
    for k in order:
        at.send(g_split.at[at.across(at.layer_to(k))], from_core_split.at[k], to_core_split + k, (band, other))
    load1 = local(g_rnn1, parts1)
    load0 = [local(g_rnn0.at[at.own(at.layer_to(k))], own0.at[k]) for k in range(layers)]
    load_split = [local(g_split.at[at.own(at.layer_to(k))], own_split.at[k]) for k in range(layers)]
    load_spec = local(d_spec.at[spec_part(band)], spec_own)
    load_state = [local(back, pieces)] + [local(a, b) for a, b in zip(state, held_state)]
    load1.wait()

    def block(k, carry):
        total = parts1[0, k]
        for b in range(1, bands):
            total = total + parts1[b, k]
        sum1[k] = total
        return carry

    lax.fori_loop(0, streams, block, 0)
    for k in order:
        at.send(sum1.at[at.across(at.layer_to(k))], from_core1.at[k], to_core1 + k, (band, other))
    for k in order:
        at.arrive(from_core.at[k], to_core + k)
        load0[k].wait()
        from_core[k] += own0[k]
        for m in turns:
            to = at.band_to(m)
            at.send(from_core.at[k, rows(to)], from_band.at[m - 1, k], to_band + m * layers + k, (to, stream))
    for k in order:
        at.arrive(from_core1.at[k], to_core1 + k)
        from_core1[k] += sum1[at.own(at.layer_to(k))]
        if k:
            at.send(from_core1.at[k], from_layer1.at[k - 1], to_layer1 + k, (band, at.own(at.layer_to(k))))
    for k in order:
        at.arrive(from_core_split.at[k], to_core_split + k)
        load_split[k].wait()
        from_core_split[k] += own_split[k]
        if k:
            at.send(
                from_core_split.at[k], from_layer_split.at[k - 1], to_layer_split + k,
                (band, at.own(at.layer_to(k))),
            )
    for m in turns:
        to = at.band_to(m)
        at.send(d_spec.at[spec_part(to)], spec_in.at[m - 1], to_spec + m, (to, stream))
    for k in order:
        total = from_core[k, rows(band)]
        for m in turns:
            at.arrive(from_band.at[m - 1, k], to_band + m * layers + k)
            total = total + from_band[m - 1, k]
        held[k] = total
        if k:
            at.send(held.at[k], from_layer.at[k - 1], to_layer + k, (band, at.own(at.layer_to(k))))

    def gather_quarters(total, target, index):
        target[rows(band)] = total
        for m in turns:
            at.send(target.at[rows(band)], target.at[rows(band)], index + m, (at.band_to(m), stream))

    total = from_core1[0]
    for k in range(1, layers):
        at.arrive(from_layer1.at[k - 1], to_layer1 + k)
        total = total + from_layer1[k - 1]
    gather_quarters(total, rnn1, to_all1)
    total = held[0]
    for k in range(1, layers):
        at.arrive(from_layer.at[k - 1], to_layer + k)
        total = total + from_layer[k - 1]
    gather_quarters(total, rnn0, to_all0)
    total = from_core_split[0]
    for k in range(1, layers):
        at.arrive(from_layer_split.at[k - 1], to_layer_split + k)
        total = total + from_layer_split[k - 1]
    banded[...] = total
    load_spec.wait()
    total = spec_own[...]
    for m in turns:
        at.arrive(spec_in.at[m - 1], to_spec + m)
        total = total + spec_in[m - 1]
    spec_out[spec_part(band)] = total
    for m in turns:
        piece = spec_out.at[spec_part(band)]
        at.send(piece, piece, to_spec_all + m, (at.band_to(m), stream))
    for m in turns:
        at.arrive(rnn1.at[rows(at.band_from(m))], to_all1 + m)
        at.arrive(rnn0.at[rows(at.band_from(m))], to_all0 + m)
    for copy in load_state:
        copy.wait()

    weights, means, powers = held_state[:8], held_state[8:16], held_state[16:]
    grads = Grads(pieces, rnn0, rnn1, banded, dims)
    columns, share = weights[3].shape[1], weights[7].shape[1]
    shares = (1.0,) * 4 + (1.0 / bands,) * 4

    def everywhere(tile, turn):
        to_near, to_far = take(streams), take(bands)
        own, half = tiles.at[turn, 0], tiles.at[turn, 1]
        own[...] = tile
        for k in range(1, streams):
            at.send(own, near.at[turn, k], to_near + k, (band, stream_to(k)))
        total = tile
        for k in range(1, streams):
            at.arrive(near.at[turn, k], to_near + k)
            total = total + near[turn, k]
        half[...] = total
        for m in turns:
            at.send(half, far.at[turn, m], to_far + m, (at.band_to(m), stream))
        for m in turns:
            at.arrive(far.at[turn, m], to_far + m)
            total = total + far[turn, m]
        return total

    def walk(one, count):
        widths = [weights[k].shape[2] for k in range(3)]
        start = tuple(tuple(jnp.zeros((1, w), jnp.float32) for unused in range(count)) for w in widths)

        def slot(s, carry):
            got = []
            for (k, where, g), had in zip(grads.of_slot(s), carry):
                got.append(tuple(a + b for a, b in zip(had, one(k, where, g))))
            return tuple(got)

        total = [list(found) for found in lax.fori_loop(0, dims[0], slot, start)] + [None] * 5
        for k, where, g in grads.rest(columns, share):
            got = one(k, where, g)
            total[k] = list(got) if total[k] is None else [a + b for a, b in zip(total[k], got)]
        return total

    def squares(k, where, g):
        w = weights[k][where]
        return column_sum(g * g), column_sum(w * w)

    first = walk(squares, 2)
    grad_rows = [jnp.sum(t[0], axis=1, keepdims=True) * part for t, part in zip(first, shares)]
    totals = everywhere(add_up([sum(grad_rows)] + [t[1] * part for t, part in zip(first, shares)]), 0)
    grad_norm = jnp.sqrt(totals[0:1])
    factor = jnp.minimum(1.0, CLIP_NORM / grad_norm)[:, 0:1]

    def updates(k, where, g):
        mean, power = lamb_moments(g, means[k][where], powers[k][where], factor)
        direction = lamb_direction(weights[k][where], mean, power, DECAYS[k])
        return (column_sum(direction * direction),)

    second = walk(updates, 1)
    moved = everywhere(add_up([t[0] * part for t, part in zip(second, shares)]), 1)
    out[0:8] = jnp.sqrt(totals[1:9]) / jnp.sqrt(moved[0:8] + 1e-12)
    out[8:9] = jnp.broadcast_to(factor, (1, LANES))
    out[9:10] = grad_norm
    out[10:16] = jnp.zeros((6, LANES), jnp.float32)
    for m in turns:
        at.arrive(spec_out.at[spec_part(at.band_from(m))], to_spec_all + m)
    at.finish()


def finish(g_rnn0, g_split, g_rnn1, d_spec, back, state, bands, layers, dims):
    streams = layers * CORES
    rows, split_count = g_rnn0.shape[1], g_split.shape[1]
    quarter = rows // bands
    spec_shape = (d_spec.shape[0] // bands, d_spec.shape[1])
    count = 6 * layers + bands * layers + 4 * bands + 2 * (streams + bands)
    tile = (16, LANES)

    def vmem(*shape):
        return pltpu.VMEM(shape, jnp.float32)

    return pl.pallas_call(
        partial(finish_kernel, bands, layers, dims),
        out_shape=[
            f32(tile), f32((rows, LANES)), f32((rows, LANES)), f32((split_count, LANES)), f32(d_spec.shape),
        ],
        in_specs=[ANY] * 29,
        out_specs=[VMEM] * 5,
        scratch_shapes=[vmem(*back.shape)]
        + [vmem(*x.shape) for x in state]
        + [
            vmem(layers, rows, LANES),
            vmem(layers, split_count, LANES),
            vmem(*g_rnn1.shape),
            vmem(streams, quarter, LANES),
            vmem(layers, rows, LANES),
            vmem(layers, split_count, LANES),
            vmem(layers, quarter, LANES),
            vmem(bands - 1, layers, quarter, LANES),
            vmem(layers, quarter, LANES),
            vmem(layers - 1, quarter, LANES),
            vmem(layers - 1, split_count, LANES),
            vmem(layers - 1, quarter, LANES),
            vmem(bands - 1, *spec_shape),
            vmem(*spec_shape),
            vmem(2, streams, *tile),
            vmem(2, bands, *tile),
            vmem(2, 2, *tile),
            pltpu.SemaphoreType.DMA((2 * layers + 2 + 25,)),
            pltpu.SemaphoreType.DMA((count,)),
            pltpu.SemaphoreType.DMA((count,)),
        ],
        compiler_params=pltpu.CompilerParams(
            collective_id=5, has_side_effects=True, vmem_limit_bytes=VMEM_BYTES
        ),
        cost_estimate=cost(60),
        name="finish",
    )(g_rnn0, g_split, g_rnn1, d_spec, back, *state)


def update_kernel(dims, scales, pieces, rnn0, rnn1, banded, *refs):
    weights, means, powers = refs[:8], refs[8:16], refs[16:24]
    fresh, new_means, new_powers = refs[24:32], refs[32:40], refs[40:48]
    grads = Grads(pieces, rnn0, rnn1, banded, dims)
    factor = scales[8:9, 0:1]

    def one(k, where, g):
        w = weights[k][where]
        mean, power = lamb_moments(g, means[k][where], powers[k][where], factor)
        direction = lamb_direction(w, mean, power, DECAYS[k])
        fresh[k][where] = w - LEARN_RATE * scales[k : k + 1, 0:1] * direction
        new_means[k][where] = mean
        new_powers[k][where] = power

    def slot(s, carry):
        for part in grads.of_slot(s):
            one(*part)
        return carry

    lax.fori_loop(0, dims[0], slot, 0)
    for part in grads.rest(weights[3].shape[1], weights[7].shape[1]):
        one(*part)


def update(scales, grads, state, dims):
    return pl.pallas_call(
        partial(update_kernel, dims),
        out_shape=[f32(x.shape) for x in state],
        in_specs=[VMEM] * 29,
        out_specs=[VMEM] * 24,
        compiler_params=PARAMS,
        cost_estimate=cost(10),
        name="update",
    )(scales, *grads, *state)


def groups_of(size, slots):
    outer = math.gcd(size, slots)
    inner = size // outer
    across = [[g * inner + i for g in range(outer)] for i in range(inner)]
    within = [[g * inner + i for i in range(inner)] for g in range(outer)]
    return outer, inner, across, within


def sum_everywhere(values, sizes):
    n = sizes[0] * sizes[1]
    row = jnp.zeros((8, LANES), jnp.float32).at[0, : values.shape[0]].set(values)
    spread = jnp.broadcast_to(row[None], (n, 8, LANES))
    got = lax.all_to_all(spread, ("band", "stream"), 0, 0, tiled=True)
    return jnp.sum(got, axis=0)[0, : values.shape[0]]


def swap_cores(x):
    return lax.ppermute(x, "stream", [(s, s ^ 1) for s in range(lax.axis_size("stream"))])


def share_slots(shard, outer, across, within, axis):
    slots = shard.shape[0]
    mine = lax.all_to_all(
        shard.reshape((outer, slots // outer) + shard.shape[1:]), "stream", 0, 0,
        axis_index_groups=across, tiled=True,
    )
    inner = len(within[0])
    if inner == CORES:
        return mine, swap_cores(mine)
    both = lax.all_gather(mine, "stream", axis_index_groups=within)
    both = both.reshape((CORES, inner // CORES) + mine.shape)
    if axis == 1:
        both = both.transpose(0, 2, 3, 1, 4, 5)
        both = both.reshape(both.shape[:3] + (-1, both.shape[5]))
    else:
        both = both.transpose(0, 2, 3, 4, 1, 5)
        both = both.reshape(both.shape[:4] + (-1,))
    return both[0], both[1]


def return_slots(keep, send, outer, inner, across, within, axis):
    if inner == CORES:
        mine = keep + swap_cores(send)
    else:
        both = jnp.stack([keep, send])
        half = inner // CORES
        if axis == 1:
            both = both.reshape(both.shape[:3] + (half, -1, both.shape[4])).transpose(0, 3, 1, 2, 4, 5)
        else:
            both = both.reshape(both.shape[:4] + (half, -1)).transpose(0, 4, 1, 2, 3, 5)
        both = both.reshape((inner,) + both.shape[2:])
        mine = lax.psum_scatter(both, "stream", axis_index_groups=within, tiled=False)
    back = lax.all_to_all(mine, "stream", 0, 0, axis_index_groups=across, tiled=True)
    return back.reshape((-1,) + back.shape[2:])


def pack_split(splitter, banding, blocks):
    slots, wide, dmodel = splitter.shape
    columns = banding.shape[1] // blocks
    strips = -(-columns // LANES)
    main = splitter.reshape(slots, blocks, wide // blocks, dmodel).transpose(1, 0, 2, 3)
    flat = banding.reshape(slots, blocks, columns).transpose(1, 0, 2)
    flat = jnp.pad(flat, ((0, 0), (0, SLOT_PAD - slots), (0, strips * LANES - columns)))
    flat = flat.reshape(blocks, SLOT_PAD, strips, LANES).transpose(0, 2, 1, 3)
    return jnp.concatenate(
        [main.reshape(blocks, slots * wide // blocks, dmodel), flat.reshape(blocks, -1, LANES)], axis=1
    )


def unpack_banding(pack, start, slots, columns):
    blocks = pack.shape[0]
    flat = pack[:, start:].reshape(blocks, -1, SLOT_PAD, LANES)[:, :, :slots].transpose(2, 0, 1, 3)
    return flat.reshape(slots, blocks, -1)[:, :, :columns].reshape(slots, blocks * columns)


def body(spectrum, segments, widths, groups, cotangent, *state):
    weights, means_old, powers_old = state[:8], state[8:16], state[16:]
    splitter, widener, masker, banding, intake, recurrence, outtake, scalers = weights
    group_count = lax.axis_size("band")
    stream_count = lax.axis_size("stream")
    my_stream = lax.axis_index("stream")
    slots = splitter.shape[0]
    frames = spectrum.shape[0]
    quarter = frames // group_count
    outer, inner, across, within = groups_of(stream_count, slots)
    share = slots // outer
    r = masker.shape[1] * stream_count // (2 * outer)
    dmodel = splitter.shape[2]
    hidden = recurrence.shape[2]
    wide = splitter.shape[1] * stream_count
    bins = spectrum.shape[2]
    blocks, out_rows, weight_rows, vec_share, vec_rows, rows = pack_rows(dmodel, hidden)
    slot_rows = wide // blocks
    columns = banding.shape[1] * stream_count // blocks
    direct = stream_count == blocks and inner == CORES

    slot_places, clips, slot_of, mask_places = tables(
        segments, widths[None], groups[None], slots, share, inner, group_count, direct
    )
    padded = ((bins - 1) // LANES + 2) * LANES
    spec = jnp.pad(
        spectrum.transpose(1, 0, 2).reshape(2 * frames, bins), ((0, 0), (0, padded - bins))
    )

    if direct:
        rnn0, w_split, later, pieces = gather_front(
            intake.reshape(2, 2 * dmodel, LANES), recurrence.reshape(2, 2 * hidden, LANES), outtake, scalers,
            splitter.reshape(slots * slot_rows, dmodel), banding, masker, widener.transpose(0, 2, 1), cotangent,
            rows, group_count, outer,
        )
        rnn1 = lax.all_gather(later, "stream")
        pieces = pieces.reshape((outer, share) + pieces.shape[1:])
        mine = lax.all_to_all(pieces, "stream", 0, 0, axis_index_groups=across, tiled=True)
    else:
        whole = (
            lax.all_gather(intake, "stream", axis=3, tiled=True),
            lax.all_gather(recurrence, "stream", axis=3, tiled=True),
            lax.all_gather(outtake, "stream", axis=1, tiled=True),
            lax.all_gather(scalers, "stream", axis=1, tiled=True),
        )
        rnn0, rnn1 = (
            pack_rnn(whole[0][k], whole[1][k], whole[2][k], whole[3][k : k + 1], rows, vec_share)
            for k in range(2)
        )
        w_split = pack_split(
            lax.all_gather(splitter, "stream", axis=1, tiled=True),
            lax.all_gather(banding, "stream", axis=1, tiled=True),
            blocks,
        )
        w_mask = share_slots(masker, outer, across, within, 1)
        w_wide = share_slots(widener.transpose(0, 2, 1), outer, across, within, 1)
        cot_parts = cotangent.reshape(frames, outer, share, wide).transpose(1, 2, 0, 3)
        cot = lax.all_to_all(cot_parts, "stream", 0, 0, axis_index_groups=across, tiled=True)
        mine, other = (
            jnp.concatenate([pack_pieces(w_mask[k], w_wide[k]), cot], axis=2) for k in range(CORES)
        )
    piece_rows = mine.shape[2] - frames
    def by_band(x, number):
        if direct:
            return exchange(x, group_count, outer, number)
        return lax.all_to_all(x, "band", 0, 0, tiled=True)

    def to_masks(x):
        x = x.reshape(group_count, outer, share, quarter, dmodel)
        if direct:
            return exchange(x, group_count, outer, 2)
        x = lax.all_to_all(x, "stream", 1, 1, axis_index_groups=across, tiled=True)
        return lax.all_to_all(x, "band", 0, 0, tiled=True)

    def from_masks(x):
        if direct:
            x = exchange(x, group_count, outer, 3)
        else:
            x = lax.all_to_all(x, "band", 0, 0, tiled=True)
            x = lax.all_to_all(x, "stream", 1, 1, axis_index_groups=across, tiled=True)
        return x.reshape(group_count * slots, quarter, dmodel)

    base = 2 * wide + dmodel
    got = time_forward(
        slot_places, clips, spec, w_split, rnn0, group_count, slots, blocks * columns, slot_rows, hidden
    )
    time_out, v_band, time_saved = got[0], got[1], got[2:]
    arrived = by_band(time_out, 1)
    got = band_forward(slot_of, arrived.reshape(group_count * slots, quarter, dmodel), rnn1, hidden)
    band_out, band_saved = got[0], got[1:]
    if direct:
        mine, band_out = lax.optimization_barrier((mine, band_out))
        other = swap_cores(mine)
    keep, send, grad_mixed, g_mask_vec = mask_network(
        mask_places, to_masks(band_out), mine, other, v_band, base, piece_rows
    )
    r = masker.shape[1] * stream_count // (2 * outer)
    grad_back = from_masks(grad_mixed)
    if direct:
        back = keep.at[:, :, :piece_rows].add(swap_cores(send))
        back, grad_back = lax.optimization_barrier((back, grad_back))
        back = lax.all_to_all(back, "stream", 0, 0, axis_index_groups=across, tiled=True)
        back = back.reshape((slots,) + back.shape[2:])
        mask_parts = back[:, piece_rows:]
    else:
        kept, sent = unpack_pieces(keep[:, :, :piece_rows], r), unpack_pieces(send, r)
        mask_reduced = return_slots(kept[0], sent[0], outer, inner, across, within, 1)
        widened_reduced = return_slots(kept[1], sent[1], outer, inner, across, within, 1).transpose(0, 2, 1)
        mask_parts = keep[:, :, piece_rows:]
        mask_parts = lax.all_to_all(mask_parts, "stream", 0, 0, axis_index_groups=across, tiled=True)
    band_grad, g_rnn1 = band_backward(slot_of, grad_back, band_saved, rnn1, hidden)
    grad_time = by_band(band_grad.reshape(group_count, slots, quarter, dmodel), 4)
    if direct:
        g_rnn1 = g_rnn1.reshape(blocks, group_count, rows // group_count, LANES).transpose(1, 0, 2, 3)
        g_rnn1 = lax.all_to_all(g_rnn1, "band", 0, 0, tiled=True)
    d_spec, g_split, g_rnn0 = time_backward(
        slot_places, clips, (my_stream // inner).astype(jnp.int32)[None], grad_time, spec, time_saved, w_split,
        v_band, rnn0, g_mask_vec, slot_rows, hidden,
    )
    if direct:
        dims = (slots, slot_rows, r, piece_rows, dmodel, hidden)
        state = tuple(x.transpose(0, 2, 1) if k % 8 == 1 else x for k, x in enumerate(state))
        scales, g_rnn0, g_rnn1, g_split, d_spec = finish(
            g_rnn0, g_split, g_rnn1, d_spec, back, state, group_count, outer, dims
        )
    else:
        d_spec = lax.psum(d_spec, "band")

    masks = mask_parts.reshape(slots, frames, wide).transpose(1, 0, 2).reshape(cotangent.shape)
    spectrum_grad = d_spec.reshape(2, frames, padded)[:, :, :bins].transpose(1, 0, 2)

    if direct:
        stepped = update(scales, (back, g_rnn0, g_rnn1, g_split), state, dims)
        stepped = [x.transpose(0, 2, 1) if k % 8 == 1 else x for k, x in enumerate(stepped)]
        return (masks, spectrum_grad, scales[9, 0]) + tuple(stepped)
    first, second = unpack_rnn(g_rnn0, dmodel, hidden), unpack_rnn(g_rnn1, dmodel, hidden)
    rnn_grads = [jnp.stack([a, b]) for a, b in zip(first[:3], second[:3])]
    rnn_grads.append(jnp.concatenate([first[3], second[3]], axis=0))
    rnn_grads = [
        lax.psum(lax.psum_scatter(g, "stream", scatter_dimension=d, tiled=True), "band")
        for g, d in zip(rnn_grads, (3, 3, 1, 1))
    ]
    g_band = unpack_banding(g_split, slots * slot_rows, slots, columns)
    g_split = g_split[:, : slots * slot_rows].reshape(blocks, slots, slot_rows, dmodel)
    g_split = g_split.transpose(1, 0, 2, 3).reshape(slots, wide, dmodel)
    split_reduced = lax.psum_scatter(g_split, "stream", scatter_dimension=1, tiled=True)
    band_reduced = lax.psum_scatter(g_band, "stream", scatter_dimension=1, tiled=True)
    reduced = (split_reduced, widened_reduced, mask_reduced, band_reduced) + tuple(rnn_grads)

    shares = (1.0,) * 4 + (1.0 / group_count,) * 4
    sizes = (group_count, stream_count)
    sums = [sum(jnp.sum(g * g) * part for g, part in zip(reduced, shares))]
    sums += [jnp.sum(w * w) * part for w, part in zip(weights, shares)]
    totals = sum_everywhere(jnp.stack(sums), sizes)
    grad_norm = jnp.sqrt(totals[0])
    factor = jnp.minimum(1.0, CLIP_NORM / grad_norm)
    moments = [lamb_moments(g, m, p, factor) for g, m, p in zip(reduced, means_old, powers_old)]
    directions = [lamb_direction(w, m, p, d) for w, (m, p), d in zip(weights, moments, DECAYS)]
    update_totals = sum_everywhere(
        jnp.stack([jnp.sum(d * d) * part for d, part in zip(directions, shares)]), sizes
    )
    ratios = jnp.sqrt(totals[1:]) / jnp.sqrt(update_totals + 1e-12)
    fresh = [w - LEARN_RATE * ratios[k] * d for k, (w, d) in enumerate(zip(weights, directions))]
    return (
        (masks, spectrum_grad, grad_norm)
        + tuple(fresh)
        + tuple(m for m, unused in moments)
        + tuple(p for unused, p in moments)
    )


def solution(mesh):
    stored = (
        P("band", "stream", None),
        P("band", None, "stream"),
        P("band", "stream", None),
        P("band", "stream"),
        P(None, None, None, "stream"),
        P(None, None, None, "stream"),
        P(None, "stream", None),
        P(None, "stream"),
    )
    frames_over = P("stream", None, None)
    mask_over = P("stream", "band", None, None)
    return jax.shard_map(
        body,
        mesh=mesh,
        in_specs=(frames_over, P("stream", None), P(), P(), mask_over) + stored * 3,
        out_specs=(mask_over, frames_over, P()) + stored * 3,
        check_vma=False,
    )
```

```python
from functools import partial
import math

import jax
import jax.numpy as jnp
from jax import lax
from jax.experimental import pallas as pl
from jax.experimental.pallas import tpu as pltpu
from jax.sharding import PartitionSpec as P

STEP = 10
CLIP_NORM = 5.0
LEARN_RATE = 0.5
BETA_ONE = 0.9
BETA_TWO = 0.999
ADAM_EPS = 1e-06
DECAY_RATE = 0.01
NORM_EPS = 1e-05
VAR_FLOOR = 0.25
CLIPS = 3
CLIP_MOST = 32
LANES = 128
VMEM_BYTES = 60 * 1024 * 1024
CORES = 2
SLOT_PAD = 16
MESH = pl.DeviceIdType.MESH

AB = (((1,), (0,)), ((), ()))
ABT = (((1,), (1,)), ((), ()))
ATB = (((0,), (0,)), ((), ()))


def split(x):
    hi = x.astype(jnp.bfloat16)
    lo = (x - hi.astype(jnp.float32)).astype(jnp.bfloat16)
    return hi, lo


def dot1(a, b, dims):
    return lax.dot_general(a, b, dims, preferred_element_type=jnp.float32)


def dot_parts(a, b, dims):
    return dot1(a[0], b[0], dims) + (dot1(a[1], b[0], dims) + dot1(a[0], b[1], dims))


def dot3(a, b, dims):
    return dot_parts(split(a), split(b), dims)


def sigmoid(x):
    return 0.5 * jnp.tanh(0.5 * x) + 0.5


def norm_stats(x):
    center = x - jnp.mean(x, axis=-1, keepdims=True)
    spread = jnp.mean(center * center, axis=-1, keepdims=True)
    scale = lax.rsqrt(spread + NORM_EPS)
    return center * scale, scale


def norm_back(grad_unit, unit, scale):
    first = jnp.mean(grad_unit, axis=-1, keepdims=True)
    second = jnp.mean(grad_unit * unit, axis=-1, keepdims=True)
    return scale * (grad_unit - first - unit * second)


def column_sum(x):
    return jnp.sum(x, axis=0, keepdims=True)


def pack_rows(dmodel, hidden):
    blocks = 4 * hidden // LANES
    out_rows = 2 * hidden // blocks
    weight_rows = 2 * dmodel + 2 * hidden + out_rows
    share = (2 * dmodel + 8 * hidden + dmodel) // blocks
    vec_rows = -(-share // LANES)
    return blocks, out_rows, weight_rows, share, vec_rows, -(-(weight_rows + vec_rows) // 32) * 32


def pack_rnn(w_in, w_rec, w_out, vec, rows, share):
    count = w_in.shape[2] // LANES
    parts = [
        w.reshape(2 * w.shape[1], count, LANES).transpose(1, 0, 2) for w in (w_in, w_rec)
    ] + [w_out.reshape(count, -1, LANES)]
    used = sum(p.shape[1] for p in parts)
    flat = jnp.pad(vec.reshape(count, share), ((0, 0), (0, (rows - used) * LANES - share)))
    return jnp.concatenate(parts + [flat.reshape(count, rows - used, LANES)], axis=1)


def unpack_rnn(pack, dmodel, hidden):
    blocks, out_rows, weight_rows, share, vec_rows, rows = pack_rows(dmodel, hidden)
    count = pack.shape[0]
    cuts = (0, 2 * dmodel, 2 * dmodel + 2 * hidden)
    w_in = pack[:, : cuts[1]].reshape(count, 2, dmodel, LANES).transpose(1, 2, 0, 3)
    w_rec = pack[:, cuts[1] : cuts[2]].reshape(count, 2, hidden, LANES).transpose(1, 2, 0, 3)
    return (
        w_in.reshape(2, dmodel, count * LANES),
        w_rec.reshape(2, hidden, count * LANES),
        pack[:, cuts[2] : weight_rows].reshape(count * out_rows, LANES),
        unpack_vec(pack, weight_rows, vec_rows, share),
    )


def unpack_vec(pack, weight_rows, vec_rows, share):
    count = pack.shape[0]
    flat = pack[:, weight_rows : weight_rows + vec_rows].reshape(count, vec_rows * LANES)
    return flat[:, :share].reshape(1, count * share)


class Pack:
    def __init__(self, ref, dmodel, hidden):
        self.ref, self.dmodel, self.hidden = ref, dmodel, hidden
        self.blocks, self.out_rows = pack_rows(dmodel, hidden)[:2]

    def intake(self, e, first, last):
        rows = slice(e * self.dmodel, (e + 1) * self.dmodel)
        return jnp.concatenate([self.ref[k, rows] for k in range(first, last)], axis=1)

    def recurrence(self, e, k):
        base = 2 * self.dmodel + e * self.hidden
        return self.ref[k, base : base + self.hidden]

    def outtake(self, e):
        base = 2 * self.dmodel + 2 * self.hidden
        half = self.blocks // 2
        return jnp.concatenate(
            [self.ref[k, base : base + self.out_rows] for k in range(half * e, half * (e + 1))], axis=0
        )

    def put(self, k, base, value):
        if len(self.ref.shape) == 3:
            self.ref[k, base : base + value.shape[0]] = value
            return
        quarter = self.ref.shape[2]
        done = 0
        while done < value.shape[0]:
            part, at = divmod(base + done, quarter)
            count = min(value.shape[0] - done, quarter - at)
            self.ref[part, k, at : at + count] = value[done : done + count]
            done += count

    def put_intake(self, e, q, value):
        for h in range(value.shape[1] // LANES):
            self.put(q * value.shape[1] // LANES + h, e * self.dmodel, value[:, h * LANES : (h + 1) * LANES])

    def put_recurrence(self, e, q, value):
        base = 2 * self.dmodel + e * self.hidden
        for h in range(value.shape[1] // LANES):
            self.put(q * value.shape[1] // LANES + h, base, value[:, h * LANES : (h + 1) * LANES])

    def put_outtake(self, e, value):
        base = 2 * self.dmodel + 2 * self.hidden
        for k in range(self.blocks // 2):
            self.put(self.blocks // 2 * e + k, base, value[k * self.out_rows : (k + 1) * self.out_rows])

    def put_vec(self, value):
        unused, unused, base, share, vec_rows, rows = pack_rows(self.dmodel, self.hidden)
        for k in range(self.blocks):
            block = [
                value[:, k * share + r * LANES : k * share + min(share, (r + 1) * LANES)] for r in range(vec_rows)
            ]
            block[-1] = jnp.concatenate(
                [block[-1], jnp.zeros((1, vec_rows * LANES - share), jnp.float32)], axis=1
            )
            block.append(jnp.zeros((rows - base - vec_rows, LANES), jnp.float32))
            self.put(k, base, jnp.concatenate(block, axis=0))


def load_vec(pack, vec):
    unused, unused, base, share, vec_rows, unused = pack_rows(pack.dmodel, pack.hidden)
    for k in range(pack.blocks):
        for r in range(vec_rows):
            width = min(LANES, share - r * LANES)
            at = k * share + r * LANES
            vec[0:1, at : at + width] = pack.ref[k, base + r : base + r + 1, :width]


def split_recurrence(pack, hi_ref, lo_ref):
    for e in range(2):
        for k in range(pack.blocks):
            part = slice(k * LANES, (k + 1) * LANES)
            hi_ref[e, :, part], lo_ref[e, :, part] = split(pack.recurrence(e, k))


def split_recurrence_turned(pack, hi_ref, lo_ref):
    for e in range(2):
        for k in range(pack.blocks):
            part = slice(k * LANES, (k + 1) * LANES)
            hi_ref[e, part], lo_ref[e, part] = split(pack.recurrence(e, k).T)


def gates_forward(x_flat, act, pack, vec, rows, block):
    hidden4 = 4 * pack.hidden
    dmodel = pack.dmodel
    parts = [split(pack.intake(e, 0, pack.blocks)) for e in range(2)]

    def one(r, carry):
        start = pl.multiple_of(r * block, block)
        unit, unused = norm_stats(x_flat(start, block))
        n = split(unit * (1.0 + vec[0:1, :dmodel]) + vec[0:1, dmodel : 2 * dmodel])
        for e in range(2):
            bias = vec[0:1, 2 * dmodel + hidden4 * e : 2 * dmodel + hidden4 * (e + 1)]
            z = dot_parts(n, parts[e], AB) + bias
            act[e][pl.ds(r * (block // 16), block // 16)] = z.reshape(block // 16, 16, hidden4)
        return carry

    lax.fori_loop(0, rows // block, one, 0)


def run_forward(steps, places, act, c, h, pack, hi_ref, lo_ref, state, memory):
    hidden = pack.hidden
    split_recurrence(pack, hi_ref, lo_ref)
    for e in range(2):
        state[e][...] = jnp.zeros_like(state[e])
        memory[e][...] = jnp.zeros_like(memory[e])

    def step(j, carry):
        work = []
        for e in range(2):
            at = places(e, j)
            prior = state[e][...]
            hi, lo = split(prior)
            rows = prior.shape[0]
            first = dot1(jnp.concatenate([hi, lo], axis=0), hi_ref[e], AB)
            drive = [act[e][p] for p in at]
            drive = drive[0] if len(drive) == 1 else jnp.concatenate(drive, axis=0)
            z = first[:rows] + first[rows:] + dot1(hi, lo_ref[e], AB) + drive
            work.append((at, z))
        for e in range(2):
            at, z = work[e]
            ingate = sigmoid(z[:, :hidden])
            forget = sigmoid(z[:, hidden : 2 * hidden])
            candidate = jnp.tanh(z[:, 2 * hidden : 3 * hidden])
            outgate = sigmoid(z[:, 3 * hidden :])
            before = memory[e][...]
            now = forget * before + ingate * candidate
            squashed = jnp.tanh(now)
            out = outgate * squashed
            memory[e][...] = now
            state[e][...] = out
            for k, p in enumerate(at):
                part = slice(16 * k, 16 * (k + 1))
                act[e][p, :, :hidden] = ingate[part]
                act[e][p, :, hidden : 2 * hidden] = forget[part]
                act[e][p, :, 2 * hidden : 3 * hidden] = candidate[part]
                act[e][p, :, 3 * hidden :] = outgate[part]
                c[e][p] = now[part]
                h[e][p] = out[part]
        return carry

    lax.fori_loop(0, steps, step, 0, unroll=2)


def output_forward(count, h, pack, vec):
    hidden = h[0].shape[2]
    dmodel = pack.dmodel
    total = vec[0:1, vec.shape[1] - dmodel :]
    for e in range(2):
        states = h[e][:count].reshape(count * 16, hidden)
        total = total + dot3(states, pack.outtake(e), AB)
    return total


def run_backward(steps, places, act, dz_ref, c, dh, pack, hi_ref, lo_ref, grad_h, grad_c):
    hidden = pack.hidden
    split_recurrence_turned(pack, hi_ref, lo_ref)
    for e in range(2):
        grad_h[e][...] = jnp.zeros_like(grad_h[e])
        grad_c[e][...] = jnp.zeros_like(grad_c[e])

    def load(ref, at):
        got = [ref[p] for p in at]
        return got[0] if len(got) == 1 else jnp.concatenate(got, axis=0)

    def step(back, carry):
        j = steps - 1 - back
        later = jnp.minimum(j, 1).astype(jnp.float32)
        work = []
        for e in range(2):
            at = places(e, j)
            gates = load(act[e], at)
            ingate = gates[:, :hidden]
            forget = gates[:, hidden : 2 * hidden]
            candidate = gates[:, 2 * hidden : 3 * hidden]
            outgate = gates[:, 3 * hidden :]
            squashed = jnp.tanh(load(c[e], at))
            before = load(c[e], places(e, jnp.maximum(j - 1, 0))) * later
            total_h = load(dh[e], at) + grad_h[e][...]
            total_c = grad_c[e][...] + total_h * outgate * (1.0 - squashed * squashed)
            dz = jnp.concatenate(
                [
                    total_c * candidate * ingate * (1.0 - ingate),
                    total_c * before * forget * (1.0 - forget),
                    total_c * ingate * (1.0 - candidate * candidate),
                    total_h * squashed * outgate * (1.0 - outgate),
                ],
                axis=1,
            )
            grad_c[e][...] = total_c * forget
            for k, p in enumerate(at):
                dz_ref[e][p] = dz[16 * k : 16 * (k + 1)]
            work.append(dz)
        for e in range(2):
            hi, lo = split(work[e])
            rows = hi.shape[0]
            first = dot1(jnp.concatenate([hi, lo], axis=0), hi_ref[e], AB)
            grad_h[e][...] = first[:rows] + first[rows:] + dot1(hi, lo_ref[e], AB)
        return carry

    lax.fori_loop(0, steps, step, 0, unroll=2)


def states_backward(count, dy_flat, dh, h, pack, g_pack):
    hidden = h[0].shape[2]
    dy = split(dy_flat)
    for e in range(2):
        dh[e][:count] = dot_parts(dy, split(pack.outtake(e)), ABT).reshape(count, 16, hidden)
        g_pack.put_outtake(e, dot3_parts_first(h[e][:count].reshape(count * 16, hidden), dy))


def dot3_parts_first(a, b_parts):
    return dot_parts(split(a), b_parts, ATB)


def gates_backward(count, x_flat, dy_flat, dz_ref, before, pack, vec, g_pack, g_vec):
    dmodel, hidden = pack.dmodel, pack.hidden
    hidden4 = 4 * hidden
    rows = count * 16
    unit, scale = norm_stats(x_flat)
    gain = 1.0 + vec[0:1, :dmodel]
    n = unit * gain + vec[0:1, dmodel : 2 * dmodel]
    dn = jnp.zeros((rows, dmodel), jnp.float32)
    for e in range(2):
        left_hi, left_lo = split(jnp.concatenate([n, before(e)], axis=1).T)
        left = jnp.concatenate([left_hi, left_lo], axis=0)
        height = left_hi.shape[0]
        for q in range(4):
            part = slice(hidden * q, hidden * (q + 1))
            dz_q = dz_ref[e][:count, :, part].reshape(rows, hidden)
            dz = split(dz_q)
            first = dot1(left, dz[0], AB)
            got = first[:height] + first[height:] + dot1(left_hi, dz[1], AB)
            g_pack.put_intake(e, q, got[:dmodel])
            g_pack.put_recurrence(e, q, got[dmodel:])
            dn = dn + dot_parts(dz, split(pack.intake(e, q * pack.blocks // 4, (q + 1) * pack.blocks // 4)), ABT)
            base = 2 * dmodel + hidden4 * e + hidden * q
            g_vec[0:1, base : base + hidden] = column_sum(dz_q)
    g_vec[0:1, :dmodel] = column_sum(dn * unit)
    g_vec[0:1, dmodel : 2 * dmodel] = column_sum(dn)
    g_vec[0:1, vec.shape[1] - dmodel :] = column_sum(dy_flat)
    g_pack.put_vec(g_vec[...])
    return dy_flat + norm_back(dn * gain, unit, scale)


def shifted(ref, e, count, hidden, mask):
    rows = (count - 1) * 16
    zero = jnp.zeros((16, hidden), jnp.float32)
    if e == 0:
        kept = ref[: count - 1].reshape(rows, hidden) * mask
        return jnp.concatenate([zero, kept], axis=0)
    kept = ref[1:count].reshape(rows, hidden) * mask
    return jnp.concatenate([kept, zero], axis=0)


def tables_kernel(
    slots, share, inner, direct, segments, widths, groups, places, clips, slot_of, mask_places, counts
):
    band, stream = lax.axis_index("band"), lax.axis_index("stream")
    for s in range(slots):
        places[0, s] = 0
        places[1, s] = 0
    for c in range(CLIPS):
        clips[1, c] = 0
    for g in range(counts.shape[0]):
        counts[g] = 0

    def one_band(b, edge):
        g = groups[0, b]
        rank = counts[g]
        counts[g] = rank + 1
        slot_of[0, b] = g * slots + rank
        width = widths[0, b]

        @pl.when(g == band)
        def mine():
            places[0, rank] = edge
            places[1, rank] = width

        return edge + width

    lax.fori_loop(0, groups.shape[1], one_band, jnp.int32(0))

    def one_frame(t, carry):
        c = segments[0, t]
        clips[1, c] = clips[1, c] + 1
        return carry

    lax.fori_loop(0, segments.shape[1], one_frame, 0)
    start = jnp.int32(0)
    for c in range(CLIPS):
        clips[0, c] = start
        start = start + clips[1, c]
    for j in range(share):
        row = lax.div(stream, inner) * share + j
        mask_places[0, j] = places[1, row]
        mask_places[1, j] = lax.rem(stream, CORES) if direct else jnp.int32(0)
        mask_places[2, j] = row


def tables(segments, widths, groups, slots, share, inner, bands, direct):
    def i32(shape):
        return jax.ShapeDtypeStruct(shape, jnp.int32)

    smem = pl.BlockSpec(memory_space=pltpu.SMEM)
    return pl.pallas_call(
        partial(tables_kernel, slots, share, inner, direct),
        out_shape=[i32((2, slots)), i32((2, CLIPS)), i32(groups.shape), i32((3, share))],
        in_specs=[smem] * 3,
        out_specs=[smem] * 4,
        scratch_shapes=[pltpu.SMEM((bands,), jnp.int32)],
        name="tables",
    )(segments, widths, groups)


def clip_places(clips, spare):
    def places(e, j):
        found = []
        for c in range(CLIPS):
            start, length = clips[0, c], clips[1, c]
            frame = start + j if e == 0 else start + length - 1 - j
            found.append(jnp.where(j < length, frame, spare))
        return found

    return places


def window_of(edge):
    base = pl.multiple_of((edge // LANES) * LANES, LANES)
    return base, lax.rem(edge, LANES)


def split_rows(spec, edge, width, frames):
    wmax = LANES
    base, shift = window_of(edge)
    window = spec[:, pl.ds(base, 2 * LANES)]
    taken = pltpu.roll(window, lax.rem(2 * LANES - shift, 2 * LANES), 1)[:, :wmax]
    taken = jnp.concatenate([taken[:frames], taken[frames:]], axis=1)
    lane = lax.broadcasted_iota(jnp.int32, (frames, wmax), 1)
    inside = (lane < width).astype(jnp.float32)
    valid = jnp.concatenate([inside, inside], axis=1)
    entries = jnp.maximum(2 * width, 1).astype(jnp.float32)
    mean = jnp.sum(taken * valid, axis=-1, keepdims=True) / entries
    center = (taken - mean) * valid
    spread = jnp.sum(center * center, axis=-1, keepdims=True) / entries
    scale = lax.rsqrt(jnp.maximum(spread, VAR_FLOOR))
    moving = jnp.where(spread > VAR_FLOOR, 1.0, jnp.where(spread == VAR_FLOOR, 0.5, 0.0))
    return center * scale, scale, valid, moving, entries


def slot_weights(w_split, s, slot_rows):
    count = w_split.shape[0]
    at = pl.ds(pl.multiple_of(s * slot_rows, slot_rows), slot_rows)
    return jnp.concatenate([w_split[k, at, :] for k in range(count)], axis=0)


def time_forward_kernel(
    slot_rows, places_s, clips, spec, w_split, rnn_in,
    out, v_band, x, *refs,
):
    saved, refs = refs[:6], refs[6:]
    act0, act1, c0, c1, h0, h1, hi_ref, lo_ref, s0, s1, m0, m1, y, mixed, vec, rnn, sems = refs
    slots = out.shape[1]
    frames, unused, dmodel = x.shape
    wide = w_split.shape[0] * slot_rows
    pack = Pack(rnn, dmodel, h0.shape[2])
    load_rnn = pltpu.make_async_copy(rnn_in, rnn, sems.at[0])
    load_rnn.start()
    v_band[...] = jnp.zeros_like(v_band)
    columns = v_band.shape[1] // w_split.shape[0]
    for k in range(w_split.shape[0]):
        for h in range(0, columns, LANES):
            width = min(LANES, columns - h)
            at = slots * slot_rows + SLOT_PAD * (h // LANES)
            v_band[:, k * columns + h : k * columns + h + width] = w_split[k, at : at + SLOT_PAD, :width]
    x[...] = jnp.zeros_like(x)
    for a in (act0, act1):
        a[frames] = jnp.zeros_like(a[frames])

    for s in range(slots):
        unit, unused, valid, moving, entries = split_rows(spec, places_s[0, s], places_s[1, s], frames)
        row = v_band[s : s + 1, : 2 * wide + dmodel]
        z = (unit * (1.0 + row[:, :wide]) + row[:, wide : 2 * wide]) * valid
        y[s] = dot3(z, slot_weights(w_split, s, slot_rows), AB) + row[:, 2 * wide : 2 * wide + dmodel]
    for s in range(slots):
        x[:, s, :] = y[s]
    load_rnn.wait()
    load_vec(pack, vec)
    act = (act0, act1)

    def x_flat(start, size):
        return x[pl.ds(start // 16, size // 16)].reshape(size, dmodel)

    gates_forward(x_flat, act, pack, vec, frames * 16, 256)
    run_forward(
        CLIP_MOST, clip_places(clips, frames), act, (c0, c1), (h0, h1),
        pack, hi_ref, lo_ref, (s0, s1), (m0, m1),
    )
    leaving = [
        pltpu.make_async_copy(a, b, sems.at[1 + k])
        for k, (a, b) in enumerate(zip((act0, act1, c0, c1, h0, h1), saved))
    ]
    for copy in leaving:
        copy.start()
    total = output_forward(frames, (h0, h1), pack, vec)
    x_all = x[...].reshape(frames * 16, dmodel)
    mixed[...] = (x_all + total).reshape(frames, 16, dmodel)
    parts, unused_slots, quarter, unused = out.shape
    for s in range(slots):
        for q in range(parts):
            out[q, s] = mixed[q * quarter : (q + 1) * quarter, s, :]
    for copy in leaving:
        copy.wait()


def f32(shape):
    return jax.ShapeDtypeStruct(shape, jnp.float32)


def saved_shapes(count, hidden):
    return [f32((count, 16, 4 * hidden))] * 2 + [f32((count, 16, hidden))] * 4


def saved_scratch(count, hidden):
    return [pltpu.VMEM(x.shape, jnp.float32) for x in saved_shapes(count, hidden)]


def vec_scratch(dmodel, hidden):
    return pltpu.VMEM((1, 3 * dmodel + 8 * hidden), jnp.float32)


def rec_scratch(rows, hidden, turned=False):
    return [
        pltpu.VMEM((2, 4 * hidden, hidden) if turned else (2, hidden, 4 * hidden), jnp.bfloat16),
        pltpu.VMEM((2, 4 * hidden, hidden) if turned else (2, hidden, 4 * hidden), jnp.bfloat16),
    ] + [pltpu.VMEM((rows, hidden), jnp.float32)] * 4


SMEM = pl.BlockSpec(memory_space=pltpu.SMEM)
VMEM = pl.BlockSpec(memory_space=pltpu.VMEM)
ANY = pl.BlockSpec(memory_space=pl.ANY)
PARAMS = pltpu.CompilerParams(vmem_limit_bytes=VMEM_BYTES)


def cost(micros):
    return pl.CostEstimate(flops=int(micros * 1.1e9), bytes_accessed=int(micros * 3e6), transcendentals=0)


def time_forward(slot_places, clips, spec, w_split, rnn, parts, slots, band_columns, slot_rows, hidden):
    dmodel = w_split.shape[2]
    frames = spec.shape[0] // 2
    return pl.pallas_call(
        partial(time_forward_kernel, slot_rows),
        out_shape=[
            f32((parts, slots, frames // parts, dmodel)), f32((SLOT_PAD, band_columns)), f32((frames, 16, dmodel)),
        ]
        + saved_shapes(frames + 1, hidden),
        in_specs=[SMEM, SMEM, VMEM, VMEM, ANY],
        out_specs=[VMEM] * 3 + [ANY] * 6,
        scratch_shapes=saved_scratch(frames + 1, hidden)
        + rec_scratch(16 * CLIPS, hidden)
        + [pltpu.VMEM((slots, frames, dmodel), jnp.float32)]
        + [pltpu.VMEM((frames, 16, dmodel), jnp.float32), vec_scratch(dmodel, hidden)]
        + [pltpu.VMEM(rnn.shape, jnp.float32), pltpu.SemaphoreType.DMA((7,))],
        compiler_params=PARAMS,
        cost_estimate=cost(35),
        name="time_forward",
    )(slot_places, clips, spec, w_split, rnn)


def time_backward_kernel(
    slot_rows, places_s, clips, my_outer, dy_in, spec_in, x_in, *refs,
):
    saved, refs = refs[:6], refs[6:]
    w_split_in, v_band, rnn_in, g_mask_vec, d_spec, g_split, g_rnn, *refs = refs
    act0, act1, c0, c1, h0, h1, *refs = refs
    hi_ref, lo_ref, s0, s1, m0, m1, dy, vec, g_vec, g_band, dh0, dh1, dz0, dz1, *refs = refs
    rnn, w_split, spec, x, sems = refs
    slots = dy_in.shape[1]
    frames, unused, dmodel = x.shape
    hidden = h0.shape[2]
    wide = w_split.shape[0] * slot_rows
    parts, unused_slots, quarter, unused = dy_in.shape
    pack, g_pack = Pack(rnn, dmodel, hidden), Pack(g_rnn, dmodel, hidden)
    pairs = [(rnn_in, rnn), (saved[4], h0), (saved[5], h1)]
    pairs += list(zip(saved[:4], (act0, act1, c0, c1)))
    pairs += [(w_split_in, w_split), (spec_in, spec), (x_in, x)]
    loads = [pltpu.make_async_copy(a, b, sems.at[k]) for k, (a, b) in enumerate(pairs)]
    for copy in loads:
        copy.start()
    dy[...] = jnp.zeros_like(dy)
    for s in range(slots):
        for q in range(parts):
            dy[q * quarter : (q + 1) * quarter, s, :] = dy_in[q, s]
    for copy in loads[:3]:
        copy.wait()
    load_vec(pack, vec)
    dy_flat = dy[...].reshape(frames * 16, dmodel)
    states_backward(frames, dy_flat, (dh0, dh1), (h0, h1), pack, g_pack)
    for d in (dh0, dh1):
        d[frames] = jnp.zeros_like(d[frames])
    for copy in loads[3:7]:
        copy.wait()
    run_backward(
        CLIP_MOST, clip_places(clips, frames), (act0, act1), (dz0, dz1), (c0, c1),
        (dh0, dh1), pack, hi_ref, lo_ref, (s0, s1), (m0, m1),
    )
    for copy in loads[7:]:
        copy.wait()
    frame = lax.broadcasted_iota(jnp.int32, ((frames - 1) * 16, 1), 0) // 16 + 1
    inside = jnp.ones(frame.shape, jnp.float32)
    for k in range(1, CLIPS):
        inside = jnp.where(frame == clips[0, k], 0.0, inside)
    x_flat = x[...].reshape(frames * 16, dmodel)
    dx = gates_backward(
        frames, x_flat, dy[...].reshape(frames * 16, dmodel), (dz0, dz1),
        lambda e: shifted((h0, h1)[e], e, frames, hidden, inside), pack, vec, g_pack, g_vec,
    )
    dy[...] = dx.reshape(frames, 16, dmodel)
    d_spec[...] = jnp.zeros_like(d_spec)
    g_split[:, slots * slot_rows :] = jnp.zeros_like(g_split[:, slots * slot_rows :])
    g_band[...] = jnp.zeros_like(g_band)

    for s in range(slots):
        edge, width = places_s[0, s], places_s[1, s]
        unit, scale, valid, moving, entries = split_rows(spec, edge, width, frames)
        row = v_band[s : s + 1, : 2 * wide + dmodel]
        gain = 1.0 + row[:, :wide]
        z = (unit * gain + row[:, wide : 2 * wide]) * valid
        demb = dy[:, s, :]
        demb_parts = split(demb)
        g_slot = dot_parts(split(z), demb_parts, ATB)
        for k in range(w_split.shape[0]):
            g_split[k, s * slot_rows : (s + 1) * slot_rows] = g_slot[k * slot_rows : (k + 1) * slot_rows]
        dz = dot_parts(demb_parts, split(slot_weights(w_split, s, slot_rows)), ABT) * valid
        g_band[s : s + 1, :wide] = column_sum(dz * unit)
        g_band[s : s + 1, wide : 2 * wide] = column_sum(dz)
        g_band[s : s + 1, 2 * wide : 2 * wide + dmodel] = column_sum(demb)
        du = dz * gain
        first = jnp.sum(du, axis=-1, keepdims=True) / entries
        second = jnp.sum(du * unit, axis=-1, keepdims=True) / entries
        dt = scale * (du - first - moving * unit * second) * valid
        base, shift = window_of(edge)
        stacked = jnp.concatenate([dt[:, :LANES], dt[:, LANES:]], axis=0)
        padded = jnp.concatenate([stacked, jnp.zeros_like(stacked)], axis=1)
        d_spec[:, pl.ds(base, 2 * LANES)] += pltpu.roll(padded, shift, 1)

    share = g_mask_vec.shape[0]
    for j in range(share):
        g_band[pl.ds(my_outer[0] * share + j, 1), 2 * wide + dmodel :] = g_mask_vec[j]
    gathered = g_band[...]
    blocks = w_split.shape[0]
    columns = gathered.shape[1] // blocks
    for k in range(blocks):
        for h in range(0, columns, LANES):
            width = min(LANES, columns - h)
            at = slots * slot_rows + SLOT_PAD * (h // LANES)
            g_split[k, at : at + SLOT_PAD, :width] = gathered[:, k * columns + h : k * columns + h + width]


def time_backward(
    slot_places, clips, my_outer, dy, spec, saved, w_split, v_band, rnn, g_mask_vec, slot_rows, hidden
):
    band_columns = v_band.shape[1]
    dmodel = w_split.shape[2]
    frames = spec.shape[0] // 2
    return pl.pallas_call(
        partial(time_backward_kernel, slot_rows),
        out_shape=[f32(spec.shape), f32(w_split.shape), f32(rnn.shape)],
        in_specs=[SMEM] * 3 + [VMEM] + [ANY] * (2 + 6 + 1) + [VMEM, ANY, VMEM],
        out_specs=[VMEM] * 3,
        scratch_shapes=saved_scratch(frames + 1, hidden)
        + rec_scratch(16 * CLIPS, hidden, True)
        + [pltpu.VMEM((frames, 16, dmodel), jnp.float32)] + [vec_scratch(dmodel, hidden)] * 2
        + [pltpu.VMEM((SLOT_PAD, band_columns), jnp.float32)]
        + [pltpu.VMEM((frames + 1, 16, hidden), jnp.float32)] * 2
        + [pltpu.VMEM((frames + 1, 16, 4 * hidden), jnp.float32)] * 2
        + [pltpu.VMEM(a.shape, jnp.float32) for a in (rnn, w_split, spec, saved[0])]
        + [pltpu.SemaphoreType.DMA((10,))],
        compiler_params=PARAMS,
        cost_estimate=cost(2),
        name="time_backward",
    )(slot_places, clips, my_outer, dy, spec, *saved, w_split, v_band, rnn, g_mask_vec)


def band_places(bands):
    return lambda e, j: [j if e == 0 else bands - 1 - j]


def place_pack(rnn, pieces, where):
    band, core = where[0], where[1]
    parts = len(pieces) // CORES
    for k, ref in enumerate(pieces):
        kind, m = divmod(k, parts)
        layers, quarter, unused = ref.shape
        at = lax.rem(band + parts - m, parts)
        rows = pl.ds(pl.multiple_of(at * quarter, 8), quarter)
        for layer in range(layers):
            rnn[layer * CORES + lax.rem(core + kind, CORES), rows] = ref[layer]


def arrive_pack(rnn, pieces, where):
    if len(pieces) == 1:
        rnn[...] = pieces[0][...]
    else:
        place_pack(rnn, pieces, where)


def band_forward_kernel(count, slot_of, where, arrived, *refs):
    pieces, refs = refs[:count], refs[count:]
    out, x, *refs = refs
    saved, refs = refs[:6], refs[6:]
    act0, act1, c0, c1, h0, h1, hi_ref, lo_ref, s0, s1, m0, m1, vec, rnn, sems = refs
    bands, unused, dmodel = x.shape
    pack = Pack(rnn, dmodel, h0.shape[2])
    arrive_pack(rnn, pieces, where)
    load_vec(pack, vec)

    def fetch(b, carry):
        x[b] = arrived[slot_of[0, b]]
        return carry

    lax.fori_loop(0, bands, fetch, 0)
    act = (act0, act1)

    def x_flat(start, size):
        return x[...].reshape(bands * 16, dmodel)

    gates_forward(x_flat, act, pack, vec, bands * 16, bands * 16)
    run_forward(
        bands, band_places(bands), act, (c0, c1), (h0, h1), pack, hi_ref, lo_ref, (s0, s1), (m0, m1)
    )
    leaving = [
        pltpu.make_async_copy(a, b, sems.at[k])
        for k, (a, b) in enumerate(zip((act0, act1, c0, c1, h0, h1), saved))
    ]
    for copy in leaving:
        copy.start()
    total = output_forward(bands, (h0, h1), pack, vec)
    whole = (x[...].reshape(bands * 16, dmodel) + total).reshape(bands, 16, dmodel)
    out[...] = jnp.zeros_like(out)
    for b in range(bands):
        out[slot_of[0, b]] = whole[b]
    for copy in leaving:
        copy.wait()


def band_forward(slot_of, where, arrived, pieces, rnn_shape, hidden):
    bands = slot_of.shape[1]
    dmodel = arrived.shape[2]
    return pl.pallas_call(
        partial(band_forward_kernel, len(pieces)),
        out_shape=[f32(arrived.shape), f32((bands, 16, dmodel))] + saved_shapes(bands, hidden),
        in_specs=[SMEM] * 2 + [VMEM] * (1 + len(pieces)),
        out_specs=[VMEM] * 2 + [ANY] * 6,
        scratch_shapes=saved_scratch(bands, hidden)
        + rec_scratch(16, hidden)
        + [vec_scratch(dmodel, hidden), pltpu.VMEM(rnn_shape, jnp.float32), pltpu.SemaphoreType.DMA((6,))],
        compiler_params=PARAMS,
        cost_estimate=cost(28),
        name="band_forward",
    )(slot_of, where, arrived, *pieces)


def band_backward_kernel(count, parts, slot_of, where, arrived, *refs):
    pieces, refs = refs[:count], refs[count:]
    x, *refs = refs
    saved, refs = refs[:6], refs[6:]
    out, outs, refs = refs[0], refs[1 : 1 + parts], refs[1 + parts :]
    act0, act1, c0, c1, h0, h1, *refs = refs
    hi_ref, lo_ref, s0, s1, m0, m1, dy, vec, g_vec, dh0, dh1, dz0, dz1, rnn, g_rnn, sems = refs
    bands, unused, dmodel = x.shape
    hidden = h0.shape[2]
    pack, g_pack = Pack(rnn, dmodel, hidden), Pack(g_rnn, dmodel, hidden)
    pairs = [(saved[4], h0), (saved[5], h1)] + list(zip(saved[:4], (act0, act1, c0, c1)))
    loads = [pltpu.make_async_copy(a, b, sems.at[k]) for k, (a, b) in enumerate(pairs)]
    for copy in loads:
        copy.start()
    arrive_pack(rnn, pieces, where)
    load_vec(pack, vec)

    def fetch(b, carry):
        dy[b] = arrived[slot_of[0, b]]
        return carry

    lax.fori_loop(0, bands, fetch, 0)
    for copy in loads[:2]:
        copy.wait()
    states_backward(bands, dy[...].reshape(bands * 16, dmodel), (dh0, dh1), (h0, h1), pack, g_pack)
    for copy in loads[2:]:
        copy.wait()
    run_backward(
        bands, band_places(bands), (act0, act1), (dz0, dz1), (c0, c1), (dh0, dh1),
        pack, hi_ref, lo_ref, (s0, s1), (m0, m1),
    )
    dx = gates_backward(
        bands, x[...].reshape(bands * 16, dmodel), dy[...].reshape(bands * 16, dmodel), (dz0, dz1),
        lambda e: shifted((h0, h1)[e], e, bands, hidden, 1.0), pack, vec, g_pack, g_vec,
    ).reshape(bands, 16, dmodel)
    out[...] = jnp.zeros_like(out)
    for b in range(bands):
        out[slot_of[0, b]] = dx[b]
    if parts == 1:
        outs[0][...] = g_rnn[...]
    else:
        for m in range(parts):
            outs[m][...] = g_rnn[lax.rem(where[0] + m, parts)]


def band_backward(slot_of, where, arrived, pieces, saved, rnn_shape, parts, hidden):
    bands = slot_of.shape[1]
    dmodel = arrived.shape[2]
    blocks, rows, unused = rnn_shape
    grad_shape = rnn_shape if parts == 1 else (parts, blocks, rows // parts, LANES)
    return pl.pallas_call(
        partial(band_backward_kernel, len(pieces), parts),
        out_shape=[f32(arrived.shape)] + [f32(grad_shape[-3:])] * parts,
        in_specs=[SMEM] * 2 + [VMEM] * (1 + len(pieces) + 1) + [ANY] * 6,
        out_specs=[VMEM] * (1 + parts),
        scratch_shapes=saved_scratch(bands, hidden)
        + rec_scratch(16, hidden, True)
        + [pltpu.VMEM((bands, 16, dmodel), jnp.float32)]
        + [vec_scratch(dmodel, hidden)] * 2
        + [pltpu.VMEM((bands, 16, hidden), jnp.float32)] * 2
        + [pltpu.VMEM((bands, 16, 4 * hidden), jnp.float32)] * 2
        + [pltpu.VMEM(rnn_shape, jnp.float32), pltpu.VMEM(grad_shape, jnp.float32)]
        + [pltpu.SemaphoreType.DMA((6,))],
        compiler_params=PARAMS,
        cost_estimate=cost(34),
        name="band_backward",
    )(slot_of, where, arrived, *pieces, *saved)


def in_turn(core, mine, other):
    return [jnp.where(core == 0, mine, other), jnp.where(core == 0, other, mine)]


def pack_pieces(mask, wide):
    lead, r, w = mask.shape[:2], mask.shape[2], mask.shape[3] // 2
    mask = mask.reshape(lead + (r, 2, w)).transpose(0, 1, 3, 2, 4).reshape(lead + (2 * r, w))
    wide = wide.reshape(lead + (2, r // 2, w // 2)).transpose(0, 1, 3, 2, 4)
    return jnp.concatenate([mask, wide.reshape(lead + (r // 2, w))], axis=2)


def unpack_pieces(pack, r):
    lead, w = pack.shape[:2], pack.shape[3]
    mask = pack[:, :, : 2 * r].reshape(lead + (2, r, w)).transpose(0, 1, 3, 2, 4).reshape(lead + (r, 2 * w))
    wide = pack[:, :, 2 * r :].reshape(lead + (r // 2, 2, w // 2)).transpose(0, 1, 3, 2, 4)
    return mask, wide.reshape(lead + (r, w // 2))


def load_mask_piece(value, r):
    return jnp.concatenate([value[:r], value[r : 2 * r]], axis=1)


def load_wide_piece(value):
    half = value.shape[1] // 2
    return jnp.concatenate([value[:, :half], value[:, half:]], axis=0)


def mask_kernel(base, places, arrived, mine, other, v_band, keep, send, grad, g_vec):
    s = pl.program_id(0)
    parts, streams, unused, quarter, dmodel = arrived.shape
    outer, unused, total_rows, wide = mine.shape
    piece_rows = send.shape[2]
    frames = total_rows - piece_rows
    half = wide // 2
    v = v_band[pl.ds(places[2, s], 1), base:]
    mlp = (v.shape[1] - 2 * dmodel) - 2 * wide
    r = mlp // (2 * outer)
    core = places[1, 0]
    x = jnp.concatenate([arrived[q, g, 0] for g in range(streams) for q in range(parts)], axis=0)
    w_wide, w_mask = [], []
    for g in range(outer):
        w_mask += in_turn(
            core, load_mask_piece(mine[g, 0, : 2 * r], r), load_mask_piece(other[g, 0, : 2 * r], r)
        )
        w_wide += in_turn(
            core, load_wide_piece(mine[g, 0, 2 * r : piece_rows]), load_wide_piece(other[g, 0, 2 * r : piece_rows])
        )
    w_wide, w_mask = jnp.concatenate(w_wide, axis=0), jnp.concatenate(w_mask, axis=0)
    cot = jnp.concatenate([mine[g, 0, piece_rows:] for g in range(outer)], axis=0)
    gain = 1.0 + v[:, :dmodel]
    unit, scale = norm_stats(x)
    p = split(unit * gain + v[:, dmodel : 2 * dmodel])
    wide_parts = split(w_wide)
    mask_parts = split(w_mask)
    q = jnp.tanh(dot_parts(p, wide_parts, ABT) + v[:, 2 * dmodel : 2 * dmodel + mlp])
    q_parts = split(q)
    raw = dot_parts(q_parts, mask_parts, AB) + v[:, 2 * dmodel + mlp :]
    lane = lax.broadcasted_iota(jnp.int32, (1, half), 1)
    inside = (lane < places[0, s]).astype(jnp.float32)
    valid = jnp.concatenate([inside, inside], axis=1)
    value = raw[:, :wide]
    gate = sigmoid(raw[:, wide:])
    masks = value * gate * valid
    dm = cot * valid
    dr = jnp.concatenate([dm * gate, dm * value * gate * (1.0 - gate)], axis=1)
    dr_parts = split(dr)
    g_mask = dot_parts(q_parts, dr_parts, ATB)
    dq = dot_parts(dr_parts, mask_parts, ABT)
    da = dq * (1.0 - q * q)
    da_parts = split(da)
    g_wide = dot_parts(da_parts, p, ATB)
    for g in range(outer):
        first, second = slice(2 * g * r, (2 * g + 1) * r), slice((2 * g + 1) * r, (2 * g + 2) * r)
        for ref, got in zip((keep, send), in_turn(core, g_mask[first], g_mask[second])):
            ref[g, 0, :r] = got[:, :wide]
            ref[g, 0, r : 2 * r] = got[:, wide:]
        for ref, got in zip((keep, send), in_turn(core, g_wide[first], g_wide[second])):
            ref[g, 0, 2 * r : piece_rows, :half] = got[: r // 2]
            ref[g, 0, 2 * r : piece_rows, half:] = got[r // 2 :]
        keep[g, 0, piece_rows:] = masks[g * frames : (g + 1) * frames]
    dp = dot_parts(da_parts, wide_parts, AB)
    g_vec[0, :, :dmodel] = column_sum(dp * unit)
    g_vec[0, :, dmodel : 2 * dmodel] = column_sum(dp)
    g_vec[0, :, 2 * dmodel : 2 * dmodel + mlp] = column_sum(da)
    g_vec[0, :, 2 * dmodel + mlp :] = column_sum(dr)
    dx = norm_back(dp * gain, unit, scale)
    k = 0
    for g in range(streams):
        for q_ in range(parts):
            grad[q_, g, 0] = dx[k * quarter : (k + 1) * quarter]
            k += 1


def mask_network(places, arrived, mine, other, v_band, base, piece_rows):
    parts, streams, slots, quarter, dmodel = arrived.shape
    outer, unused, rows, wide = mine.shape

    def second(count):
        return pl.BlockSpec((outer, 1, count, wide), lambda s: (0, s, 0, 0))

    moving = pl.BlockSpec((parts, streams, 1, quarter, dmodel), lambda s: (0, 0, s, 0, 0))
    columns = v_band.shape[1] - base
    vector = pl.BlockSpec((1, 1, columns), lambda s: (s, 0, 0))
    return pl.pallas_call(
        partial(mask_kernel, base),
        grid=(slots,),
        out_shape=[
            f32(mine.shape), f32((outer, slots, piece_rows, wide)), f32(arrived.shape), f32((slots, 1, columns)),
        ],
        in_specs=[SMEM, moving, second(rows), second(rows), VMEM],
        out_specs=[second(rows), second(piece_rows), moving, vector],
        compiler_params=PARAMS,
        cost_estimate=cost(12),
        name="mask_network",
    )(places, arrived, mine, other, v_band)


class Links:
    def __init__(self, bands, layers, send_sems, recv_sems):
        self.bands, self.layers = bands, layers
        self.band, self.stream = lax.axis_index("band"), lax.axis_index("stream")
        self.layer, self.core = lax.div(self.stream, CORES), lax.rem(self.stream, CORES)
        self.other = self.stream + 1 - 2 * self.core
        self.send_sems, self.recv_sems = send_sems, recv_sems
        self.started = []

    def band_to(self, m):
        return lax.rem(self.band + m, self.bands)

    def band_from(self, m):
        return lax.rem(self.band + self.bands - m, self.bands)

    def layer_to(self, k):
        return lax.rem(self.layer + k, self.layers)

    def layer_from(self, k):
        return lax.rem(self.layer + self.layers - k, self.layers)

    def goal(self, k):
        beside = self.layer + 1 - 2 * lax.rem(self.layer, 2)
        return (beside, 3 - self.layer, lax.rem(self.layer + 2, 4), self.layer)[k]

    def own(self, layer):
        return layer * CORES + self.core

    def across(self, layer):
        return layer * CORES + 1 - self.core

    def greet(self, partners):
        barrier = pltpu.get_barrier_semaphore()
        for partner in partners:
            pl.semaphore_signal(barrier, inc=1, device_id=partner, device_id_type=MESH)
        pl.semaphore_wait(barrier, len(partners))

    def copy(self, source, target, index, partner):
        return pltpu.make_async_remote_copy(
            src_ref=source, dst_ref=target, send_sem=self.send_sems.at[index],
            recv_sem=self.recv_sems.at[index], device_id=partner, device_id_type=MESH,
        )

    def send(self, source, target, index, partner):
        copy = self.copy(source, target, index, partner)
        copy.start()
        self.started.append(copy)

    def arrive(self, target, index):
        self.copy(target, target, index, (self.band, self.other)).wait_recv()

    def finish(self):
        for copy in self.started:
            copy.wait_send()


def gather_kernel(
    bands, layers, intake, recurrence, outtake, scalers, splitter, banding, masker, widener, cot,
    rnn_all, split_all, later, pieces,
    vec_rows, own_later, band_rows, cot_here, staged, send_sems, recv_sems, local_sems,
):
    at = Links(bands, layers, send_sems, recv_sems)
    band, stream, other = at.band, at.stream, at.other
    rows_all = rnn_all.shape[1]
    quarter = rows_all // bands
    used = []

    def local(source, target):
        copy = pltpu.make_async_copy(source, target, local_sems.at[len(used)])
        copy.start()
        used.append(copy)
        return copy

    vec_rows[...] = jnp.zeros_like(vec_rows)
    for k in range(2):
        for h in range(0, scalers.shape[1], LANES):
            width = min(LANES, scalers.shape[1] - h)
            vec_rows[k, h // LANES : h // LANES + 1, :width] = scalers[k : k + 1, h : h + width]
    band_rows[...] = jnp.zeros_like(band_rows)
    slots = banding.shape[0]
    for h in range(0, banding.shape[1], LANES):
        width = min(LANES, banding.shape[1] - h)
        base = SLOT_PAD * (h // LANES)
        band_rows[base : base + slots, :width] = banding[:, h : h + width]

    def own_pack(k, target):
        a = intake.shape[1]
        b = a + recurrence.shape[1]
        c = b + outtake.shape[1]
        return [
            local(intake.at[k], target.at[pl.ds(0, a)]),
            local(recurrence.at[k], target.at[pl.ds(a, b - a)]),
            local(outtake.at[k], target.at[pl.ds(b, c - b)]),
            local(vec_rows.at[k], target.at[pl.ds(c, rows_all - c)]),
        ]

    mine, mine_split = rnn_all.at[stream], split_all.at[stream]
    first = own_pack(0, mine)
    split_rows_count = splitter.shape[0]
    second = [
        local(splitter, mine_split.at[pl.ds(0, split_rows_count)]),
        local(band_rows, mine_split.at[pl.ds(split_rows_count, band_rows.shape[0])]),
    ]
    at.greet(
        [(at.band_to(m), stream) for m in range(1, bands)]
        + [(band, at.own(at.layer_to(k))) for k in range(1, layers)]
        + [(band, other)]
    )
    steps = range(1, layers)
    turns = range(1, bands)

    def rows(b):
        return pl.ds(b * quarter, quarter)

    to_layer, to_layer_split, to_band = 0, layers, 2 * layers
    to_core = to_band + layers * bands
    to_core_split = to_core + layers * bands
    to_layer_later = to_core_split + layers
    for copy in first:
        copy.wait()
    for k in steps:
        piece = rnn_all.at[stream, rows(band)]
        at.send(piece, piece, to_layer + k, (band, at.own(at.layer_to(k))))
    for copy in second:
        copy.wait()
    for k in steps:
        at.send(mine_split, mine_split, to_layer_split + k, (band, at.own(at.layer_to(k))))
    at.send(mine, mine, to_core, (band, other))
    at.send(mine_split, mine_split, to_core_split, (band, other))
    third = own_pack(1, own_later)
    for copy in third:
        copy.wait()
    piece = own_later.at[rows(band)]
    for k in steps:
        at.send(piece, later.at[at.layer], to_layer_later + k, (band, at.own(at.layer_to(k))))
    later[at.layer] = own_later[rows(band), :]
    load_cot = local(cot, cot_here)
    r, wide = masker.shape[1], masker.shape[2] // 2
    half = wide // 2
    base = 2 * r + r // 2
    fill = [
        local(masker.at[:, :, pl.ds(0, wide)], staged.at[:, pl.ds(0, r), :]),
        local(masker.at[:, :, pl.ds(wide, wide)], staged.at[:, pl.ds(r, r), :]),
        local(widener.at[:, pl.ds(0, r // 2), :], staged.at[:, pl.ds(2 * r, r // 2), pl.ds(0, half)]),
        local(widener.at[:, pl.ds(r // 2, r // 2), :], staged.at[:, pl.ds(2 * r, r // 2), pl.ds(half, half)]),
    ]
    for k in steps:
        source = at.own(at.layer_from(k))
        piece = rnn_all.at[source, rows(band)]
        at.arrive(piece, to_layer + k)
        for m in turns:
            at.send(piece, piece, to_band + k * bands + m, (at.band_to(m), stream))
        at.send(piece, piece, to_core + k * bands, (band, other))
    load_cot.wait()
    for s in range(slots):
        for part in range(2):
            staged[s, base:, part * half : (part + 1) * half] = cot_here[:, s, part, :]
    for copy in fill:
        copy.wait()
    rest = [local(staged, pieces)]
    for k in steps:
        source = at.own(at.layer_from(k))
        for m in turns:
            piece = rnn_all.at[source, rows(at.band_from(m))]
            at.arrive(piece, to_band + k * bands + m)
            at.send(piece, piece, to_core + k * bands + m, (band, other))
    for k in steps:
        piece = split_all.at[at.own(at.layer_from(k))]
        at.arrive(piece, to_layer_split + k)
        at.send(piece, piece, to_core_split + k, (band, other))
    at.arrive(rnn_all.at[other], to_core)
    at.arrive(split_all.at[other], to_core_split)
    for k in steps:
        source = at.across(at.layer_from(k))
        for m in range(bands):
            at.arrive(rnn_all.at[source, rows(at.band_from(m))], to_core + k * bands + m)
        at.arrive(split_all.at[source], to_core_split + k)
        at.arrive(later.at[at.layer_from(k)], to_layer_later + k)
    at.finish()
    for copy in rest:
        copy.wait()


def gather_front(intake, recurrence, outtake, scalers, splitter, banding, masker, widener, cot, rows, bands, layers):
    count = 4 * layers + 2 * layers * bands
    streams = layers * CORES
    slots = banding.shape[0]
    strips = -(-banding.shape[1] // LANES)
    r, wide = masker.shape[1], masker.shape[2] // 2
    frames = cot.shape[0]
    weight_rows = intake.shape[1] + recurrence.shape[1] + outtake.shape[1]
    split_rows_count = splitter.shape[0] + SLOT_PAD * strips
    return pl.pallas_call(
        partial(gather_kernel, bands, layers),
        out_shape=[
            f32((streams, rows, LANES)), f32((streams, split_rows_count, LANES)), f32((layers, rows // bands, LANES)),
            f32((slots, 2 * r + r // 2 + frames, wide)),
        ],
        in_specs=[ANY, ANY, ANY, VMEM, ANY, VMEM, ANY, ANY, ANY],
        out_specs=[VMEM] * 3 + [ANY],
        scratch_shapes=[
            pltpu.VMEM((2, rows - weight_rows, LANES), jnp.float32),
            pltpu.VMEM((rows, LANES), jnp.float32),
            pltpu.VMEM((SLOT_PAD * strips, LANES), jnp.float32),
            pltpu.VMEM(cot.shape, jnp.float32),
            pltpu.VMEM((slots, 2 * r + r // 2 + frames, wide), jnp.float32),
            pltpu.SemaphoreType.DMA((count,)), pltpu.SemaphoreType.DMA((count,)), pltpu.SemaphoreType.DMA((20,)),
        ],
        compiler_params=pltpu.CompilerParams(
            collective_id=0, has_side_effects=True, vmem_limit_bytes=VMEM_BYTES
        ),
        cost_estimate=cost(30),
        name="gather_front",
    )(intake, recurrence, outtake, scalers, splitter, banding, masker, widener, cot)


def exchange_kernel(bands, layers, source, target, send_sems, recv_sems, local_sem):
    at = Links(bands, layers, send_sems, recv_sems)
    wide = source.shape[1] == layers
    turns = [(m, k) for k in range(layers if wide else 1) for m in range(bands) if m + k]

    def place(ref, band, layer):
        return ref.at[band, layer] if wide else ref.at[band]

    def stream_of(layer):
        return at.own(layer) if wide else at.stream

    at.greet([(at.band_to(m), stream_of(at.layer_to(k))) for m, k in turns])
    for m, k in turns:
        band, layer = at.band_to(m), at.layer_to(k)
        at.send(
            place(source, band, layer), place(target, at.band, at.layer), k * bands + m, (band, stream_of(layer))
        )
    local = pltpu.make_async_copy(
        place(source, at.band, at.layer), place(target, at.band, at.layer), local_sem
    )
    local.start()
    for m, k in turns:
        at.arrive(place(target, at.band_from(m), at.layer_from(k)), k * bands + m)
    at.finish()
    local.wait()


def exchange(x, bands, layers, number):
    count = bands * layers
    return pl.pallas_call(
        partial(exchange_kernel, bands, layers),
        out_shape=f32(x.shape),
        in_specs=[ANY],
        out_specs=ANY,
        scratch_shapes=[
            pltpu.SemaphoreType.DMA((count,)), pltpu.SemaphoreType.DMA((count,)), pltpu.SemaphoreType.DMA,
        ],
        compiler_params=pltpu.CompilerParams(collective_id=number, has_side_effects=True),
        cost_estimate=cost(8),
        name="exchange",
    )(x)


class Grads:
    def __init__(self, pieces, rnn0, rnn1, banded, dims):
        self.pieces, self.rnn, self.banded = pieces, (rnn0, rnn1), banded
        self.slots, self.slot_rows, self.r, self.piece_rows, self.dmodel, self.hidden = dims

    def of_slot(self, s):
        at = pl.ds(pl.multiple_of(s * self.slot_rows, self.slot_rows), self.slot_rows)
        r = self.r
        return [
            (0, (s,), self.banded[at, :]),
            (1, (s,), load_wide_piece(self.pieces[s, 2 * r : self.piece_rows])),
            (2, (s,), load_mask_piece(self.pieces[s, : 2 * r], r)),
        ]

    def rest(self, columns, share):
        found = []
        base = self.slots * self.slot_rows
        strips = []
        for h in range(0, columns, LANES):
            at = base + SLOT_PAD * (h // LANES)
            strips.append(self.banded[at : at + self.slots, : min(LANES, columns - h)])
        found.append((3, (...,), jnp.concatenate(strips, axis=1)))
        unused, out_rows, weight_rows, unused, vec_rows, unused = pack_rows(self.dmodel, self.hidden)
        for k in range(2):
            pack = self.rnn[k]
            at = 0
            for e in range(2):
                found.append((4, (k, e), pack[at : at + self.dmodel]))
                at += self.dmodel
            for e in range(2):
                found.append((5, (k, e), pack[at : at + self.hidden]))
                at += self.hidden
            found.append((6, (k,), pack[at : at + out_rows]))
            at += out_rows
            strips = [
                pack[at + r : at + r + 1, : min(LANES, share - r * LANES)] for r in range(vec_rows)
            ]
            found.append((7, (slice(k, k + 1),), jnp.concatenate(strips, axis=1)))
        return found


DECAYS = (DECAY_RATE,) * 3 + (0.0,) + (DECAY_RATE,) * 3 + (0.0,)


def lamb_moments(gradient, mean_old, power_old, factor):
    clipped = gradient * factor
    mean_new = BETA_ONE * mean_old + (1.0 - BETA_ONE) * clipped
    power_new = BETA_TWO * power_old + (1.0 - BETA_TWO) * clipped * clipped
    return (mean_new, power_new)


def lamb_direction(weight_matrix, mean_new, power_new, decay):
    corrected = mean_new / (1.0 - BETA_ONE**STEP)
    scale_root = jnp.sqrt(power_new / (1.0 - BETA_TWO**STEP)) + ADAM_EPS
    return corrected / scale_root + decay * weight_matrix


def add_up(rows):
    tile = jnp.zeros((16, LANES), jnp.float32)
    line = lax.broadcasted_iota(jnp.int32, (16, LANES), 0)
    for i, row in enumerate(rows):
        tile = jnp.where(line == i, jnp.sum(row, axis=1, keepdims=True), tile)
    return tile


def finish_kernel(bands, layers, dims, g_rnn0, g_split, d_spec, back, *refs):
    g_rnn1, refs = refs[:bands], refs[bands:]
    state, refs = refs[:24], refs[24:]
    out, rnn0, rnn1, banded, spec_out = refs[:5]
    pieces, refs = refs[5], refs[6:]
    held_state, refs = refs[:24], refs[24:]
    (
        own0, own_split, parts1, sum1, from_core, from_core_split, from_core1, from_band, held,
        from_layer, from_layer_split, from_layer1, spec_in, spec_own, near, far, tiles,
        local_sems, send_sems, recv_sems,
    ) = refs
    at = Links(bands, layers, send_sems, recv_sems)
    band, stream, other = at.band, at.stream, at.other
    streams = layers * CORES
    quarter = g_rnn0.shape[1] // bands
    spec_rows = d_spec.shape[0] // bands
    order = range(layers)
    turns = range(1, bands)
    taken = [0]

    def take(count):
        taken[0] += count
        return taken[0] - count

    locals_used = []

    def local(source, target):
        copy = pltpu.make_async_copy(source, target, local_sems.at[len(locals_used)])
        copy.start()
        locals_used.append(copy)
        return copy

    def rows(b):
        return pl.ds(pl.multiple_of(b * quarter, 8), quarter)

    def spec_part(b):
        return pl.ds(pl.multiple_of(b * spec_rows, 8), spec_rows)

    def stream_to(k):
        return lax.rem(stream + k, streams)

    at.greet(
        [(band, stream_to(k)) for k in range(1, streams)] + [(at.band_to(m), stream) for m in turns]
    )
    to_core, to_core_split, to_core1 = take(layers), take(layers), take(layers)
    to_layer, to_layer_split, to_layer1 = take(layers), take(layers), take(layers)
    to_band, to_all0, to_all1 = take(bands * layers), take(bands), take(bands)
    to_spec, to_spec_all = take(bands), take(bands)
    for k in order:
        at.send(g_rnn0.at[at.across(at.goal(k))], from_core.at[k], to_core + k, (band, other))
    for k in order:
        at.send(g_split.at[at.across(at.goal(k))], from_core_split.at[k], to_core_split + k, (band, other))
    load1 = [local(g, parts1.at[k]) for k, g in enumerate(g_rnn1)]
    load0 = [local(g_rnn0.at[at.own(at.goal(k))], own0.at[k]) for k in range(layers)]
    load_split = [local(g_split.at[at.own(at.goal(k))], own_split.at[k]) for k in range(layers)]
    load_spec = local(d_spec.at[spec_part(band)], spec_own)
    load_state = [local(back, pieces)] + [local(a, b) for a, b in zip(state, held_state)]
    for copy in load1:
        copy.wait()

    def block(k, carry):
        total = parts1[0, k]
        for b in range(1, bands):
            total = total + parts1[b, k]
        sum1[k] = total
        return carry

    lax.fori_loop(0, streams, block, 0)
    for k in order:
        at.send(sum1.at[at.across(at.goal(k))], from_core1.at[k], to_core1 + k, (band, other))

    def first_turn(acc, far, index, k):
        if k < 2:
            at.send(acc.at[k], far.at[k], index + k, (band, at.own(at.goal(0))))

    def second_turn(acc, far, index):
        at.arrive(far.at[1], index + 1)
        acc[2] += far[1]
        at.send(acc.at[2], far.at[2], index + 2, (band, at.own(at.goal(2))))

    def own_total(acc, far, index):
        at.arrive(far.at[0], index)
        at.arrive(far.at[2], index + 2)
        return acc[3] + far[0] + far[2]

    for k in order:
        at.arrive(from_core.at[k], to_core + k)
        load0[k].wait()
        from_core[k] += own0[k]
        for m in turns:
            to = at.band_to(m)
            at.send(from_core.at[k, rows(to)], from_band.at[m - 1, k], to_band + m * layers + k, (to, stream))
    for k in order:
        at.arrive(from_core_split.at[k], to_core_split + k)
        load_split[k].wait()
        from_core_split[k] += own_split[k]
        first_turn(from_core_split, from_layer_split, to_layer_split, k)
    for k in order:
        at.arrive(from_core1.at[k], to_core1 + k)
        from_core1[k] += sum1[at.own(at.goal(k))]
        first_turn(from_core1, from_layer1, to_layer1, k)
    for m in turns:
        to = at.band_to(m)
        at.send(d_spec.at[spec_part(to)], spec_in.at[m - 1], to_spec + m, (to, stream))
    second_turn(from_core_split, from_layer_split, to_layer_split)
    second_turn(from_core1, from_layer1, to_layer1)
    for k in order:
        total = from_core[k, rows(band)]
        for m in turns:
            at.arrive(from_band.at[m - 1, k], to_band + m * layers + k)
            total = total + from_band[m - 1, k]
        held[k] = total
        first_turn(held, from_layer, to_layer, k)
    second_turn(held, from_layer, to_layer)

    def gather_quarters(total, target, index):
        target[rows(band)] = total
        for m in turns:
            at.send(target.at[rows(band)], target.at[rows(band)], index + m, (at.band_to(m), stream))

    gather_quarters(own_total(from_core1, from_layer1, to_layer1), rnn1, to_all1)
    banded[...] = own_total(from_core_split, from_layer_split, to_layer_split)
    gather_quarters(own_total(held, from_layer, to_layer), rnn0, to_all0)
    load_spec.wait()
    total = spec_own[...]
    for m in turns:
        at.arrive(spec_in.at[m - 1], to_spec + m)
        total = total + spec_in[m - 1]
    spec_out[spec_part(band)] = total
    for m in turns:
        piece = spec_out.at[spec_part(band)]
        at.send(piece, piece, to_spec_all + m, (at.band_to(m), stream))
    for m in turns:
        at.arrive(rnn1.at[rows(at.band_from(m))], to_all1 + m)
        at.arrive(rnn0.at[rows(at.band_from(m))], to_all0 + m)
    for copy in load_state:
        copy.wait()

    weights, means, powers = held_state[:8], held_state[8:16], held_state[16:]
    grads = Grads(pieces, rnn0, rnn1, banded, dims)
    columns, share = weights[3].shape[1], weights[7].shape[1]
    shares = (1.0,) * 4 + (1.0 / bands,) * 4

    def everywhere(tile, turn):
        to_near, to_far = take(streams), take(bands)
        own, half = tiles.at[turn, 0], tiles.at[turn, 1]
        own[...] = tile
        for k in range(1, streams):
            at.send(own, near.at[turn, k], to_near + k, (band, stream_to(k)))
        total = tile
        for k in range(1, streams):
            at.arrive(near.at[turn, k], to_near + k)
            total = total + near[turn, k]
        half[...] = total
        for m in turns:
            at.send(half, far.at[turn, m], to_far + m, (at.band_to(m), stream))
        for m in turns:
            at.arrive(far.at[turn, m], to_far + m)
            total = total + far[turn, m]
        return total

    def walk(one, count):
        widths = [weights[k].shape[2] for k in range(3)]
        start = tuple(tuple(jnp.zeros((1, w), jnp.float32) for unused in range(count)) for w in widths)

        def slot(s, carry):
            got = []
            for (k, where, g), had in zip(grads.of_slot(s), carry):
                got.append(tuple(a + b for a, b in zip(had, one(k, where, g))))
            return tuple(got)

        total = [list(found) for found in lax.fori_loop(0, dims[0], slot, start)] + [None] * 5
        for k, where, g in grads.rest(columns, share):
            got = one(k, where, g)
            total[k] = list(got) if total[k] is None else [a + b for a, b in zip(total[k], got)]
        return total

    def squares(k, where, g):
        w = weights[k][where]
        return column_sum(g * g), column_sum(w * w)

    first = walk(squares, 2)
    grad_rows = [jnp.sum(t[0], axis=1, keepdims=True) * part for t, part in zip(first, shares)]
    totals = everywhere(add_up([sum(grad_rows)] + [t[1] * part for t, part in zip(first, shares)]), 0)
    grad_norm = jnp.sqrt(totals[0:1])
    factor = jnp.minimum(1.0, CLIP_NORM / grad_norm)[:, 0:1]

    def updates(k, where, g):
        mean, power = lamb_moments(g, means[k][where], powers[k][where], factor)
        direction = lamb_direction(weights[k][where], mean, power, DECAYS[k])
        return (column_sum(direction * direction),)

    second = walk(updates, 1)
    moved = everywhere(add_up([t[0] * part for t, part in zip(second, shares)]), 1)
    out[0:8] = jnp.sqrt(totals[1:9]) / jnp.sqrt(moved[0:8] + 1e-12)
    out[8:9] = jnp.broadcast_to(factor, (1, LANES))
    out[9:10] = grad_norm
    out[10:16] = jnp.zeros((6, LANES), jnp.float32)
    for m in turns:
        at.arrive(spec_out.at[spec_part(at.band_from(m))], to_spec_all + m)
    at.finish()


def finish(g_rnn0, g_split, g_rnn1, d_spec, back, state, bands, layers, dims):
    streams = layers * CORES
    rows, split_count = g_rnn0.shape[1], g_split.shape[1]
    quarter = rows // bands
    spec_shape = (d_spec.shape[0] // bands, d_spec.shape[1])
    count = 6 * layers + bands * layers + 4 * bands + 2 * (streams + bands)
    tile = (16, LANES)

    def vmem(*shape):
        return pltpu.VMEM(shape, jnp.float32)

    return pl.pallas_call(
        partial(finish_kernel, bands, layers, dims),
        out_shape=[
            f32(tile), f32((rows, LANES)), f32((rows, LANES)), f32((split_count, LANES)), f32(d_spec.shape),
        ],
        in_specs=[ANY] * (28 + bands),
        out_specs=[VMEM] * 5,
        scratch_shapes=[vmem(*back.shape)]
        + [vmem(*x.shape) for x in state]
        + [
            vmem(layers, rows, LANES),
            vmem(layers, split_count, LANES),
            vmem(bands, *g_rnn1[0].shape),
            vmem(streams, quarter, LANES),
            vmem(layers, rows, LANES),
            vmem(layers, split_count, LANES),
            vmem(layers, quarter, LANES),
            vmem(bands - 1, layers, quarter, LANES),
            vmem(layers, quarter, LANES),
            vmem(layers - 1, quarter, LANES),
            vmem(layers - 1, split_count, LANES),
            vmem(layers - 1, quarter, LANES),
            vmem(bands - 1, *spec_shape),
            vmem(*spec_shape),
            vmem(2, streams, *tile),
            vmem(2, bands, *tile),
            vmem(2, 2, *tile),
            pltpu.SemaphoreType.DMA((2 * layers + bands + 1 + 25,)),
            pltpu.SemaphoreType.DMA((count,)),
            pltpu.SemaphoreType.DMA((count,)),
        ],
        compiler_params=pltpu.CompilerParams(
            collective_id=5, has_side_effects=True, vmem_limit_bytes=VMEM_BYTES
        ),
        cost_estimate=cost(60),
        name="finish",
    )(g_rnn0, g_split, d_spec, back, *g_rnn1, *state)


def update_kernel(dims, scales, pieces, rnn0, rnn1, banded, *refs):
    weights, means, powers = refs[:8], refs[8:16], refs[16:24]
    fresh, new_means, new_powers = refs[24:32], refs[32:40], refs[40:48]
    grads = Grads(pieces, rnn0, rnn1, banded, dims)
    factor = scales[8:9, 0:1]

    def one(k, where, g):
        w = weights[k][where]
        mean, power = lamb_moments(g, means[k][where], powers[k][where], factor)
        direction = lamb_direction(w, mean, power, DECAYS[k])
        fresh[k][where] = w - LEARN_RATE * scales[k : k + 1, 0:1] * direction
        new_means[k][where] = mean
        new_powers[k][where] = power

    def slot(s, carry):
        for part in grads.of_slot(s):
            one(*part)
        return carry

    lax.fori_loop(0, dims[0], slot, 0)
    for part in grads.rest(weights[3].shape[1], weights[7].shape[1]):
        one(*part)


def update(scales, grads, state, dims):
    return pl.pallas_call(
        partial(update_kernel, dims),
        out_shape=[f32(x.shape) for x in state],
        in_specs=[VMEM] * 29,
        out_specs=[VMEM] * 24,
        compiler_params=PARAMS,
        cost_estimate=cost(10),
        name="update",
    )(scales, *grads, *state)


def groups_of(size, slots):
    outer = math.gcd(size, slots)
    inner = size // outer
    across = [[g * inner + i for g in range(outer)] for i in range(inner)]
    within = [[g * inner + i for i in range(inner)] for g in range(outer)]
    return outer, inner, across, within


def sum_everywhere(values, sizes):
    n = sizes[0] * sizes[1]
    row = jnp.zeros((8, LANES), jnp.float32).at[0, : values.shape[0]].set(values)
    spread = jnp.broadcast_to(row[None], (n, 8, LANES))
    got = lax.all_to_all(spread, ("band", "stream"), 0, 0, tiled=True)
    return jnp.sum(got, axis=0)[0, : values.shape[0]]


def pass_along(x, axis, by):
    size = lax.axis_size(axis)
    return lax.ppermute(x, axis, [(k, (k + by) % size) for k in range(size)])


def swap_cores(x):
    return lax.ppermute(x, "stream", [(s, s ^ 1) for s in range(lax.axis_size("stream"))])


def share_slots(shard, outer, across, within, axis):
    slots = shard.shape[0]
    mine = lax.all_to_all(
        shard.reshape((outer, slots // outer) + shard.shape[1:]), "stream", 0, 0,
        axis_index_groups=across, tiled=True,
    )
    inner = len(within[0])
    if inner == CORES:
        return mine, swap_cores(mine)
    both = lax.all_gather(mine, "stream", axis_index_groups=within)
    both = both.reshape((CORES, inner // CORES) + mine.shape)
    if axis == 1:
        both = both.transpose(0, 2, 3, 1, 4, 5)
        both = both.reshape(both.shape[:3] + (-1, both.shape[5]))
    else:
        both = both.transpose(0, 2, 3, 4, 1, 5)
        both = both.reshape(both.shape[:4] + (-1,))
    return both[0], both[1]


def return_slots(keep, send, outer, inner, across, within, axis):
    if inner == CORES:
        mine = keep + swap_cores(send)
    else:
        both = jnp.stack([keep, send])
        half = inner // CORES
        if axis == 1:
            both = both.reshape(both.shape[:3] + (half, -1, both.shape[4])).transpose(0, 3, 1, 2, 4, 5)
        else:
            both = both.reshape(both.shape[:4] + (half, -1)).transpose(0, 4, 1, 2, 3, 5)
        both = both.reshape((inner,) + both.shape[2:])
        mine = lax.psum_scatter(both, "stream", axis_index_groups=within, tiled=False)
    back = lax.all_to_all(mine, "stream", 0, 0, axis_index_groups=across, tiled=True)
    return back.reshape((-1,) + back.shape[2:])


def pack_split(splitter, banding, blocks):
    slots, wide, dmodel = splitter.shape
    columns = banding.shape[1] // blocks
    strips = -(-columns // LANES)
    main = splitter.reshape(slots, blocks, wide // blocks, dmodel).transpose(1, 0, 2, 3)
    flat = banding.reshape(slots, blocks, columns).transpose(1, 0, 2)
    flat = jnp.pad(flat, ((0, 0), (0, SLOT_PAD - slots), (0, strips * LANES - columns)))
    flat = flat.reshape(blocks, SLOT_PAD, strips, LANES).transpose(0, 2, 1, 3)
    return jnp.concatenate(
        [main.reshape(blocks, slots * wide // blocks, dmodel), flat.reshape(blocks, -1, LANES)], axis=1
    )


def unpack_banding(pack, start, slots, columns):
    blocks = pack.shape[0]
    flat = pack[:, start:].reshape(blocks, -1, SLOT_PAD, LANES)[:, :, :slots].transpose(2, 0, 1, 3)
    return flat.reshape(slots, blocks, -1)[:, :, :columns].reshape(slots, blocks * columns)


def body(spectrum, segments, widths, groups, cotangent, *state):
    weights, means_old, powers_old = state[:8], state[8:16], state[16:]
    splitter, widener, masker, banding, intake, recurrence, outtake, scalers = weights
    group_count = lax.axis_size("band")
    stream_count = lax.axis_size("stream")
    my_stream = lax.axis_index("stream")
    slots = splitter.shape[0]
    frames = spectrum.shape[0]
    quarter = frames // group_count
    outer, inner, across, within = groups_of(stream_count, slots)
    share = slots // outer
    r = masker.shape[1] * stream_count // (2 * outer)
    dmodel = splitter.shape[2]
    hidden = recurrence.shape[2]
    wide = splitter.shape[1] * stream_count
    bins = spectrum.shape[2]
    blocks, out_rows, weight_rows, vec_share, vec_rows, rows = pack_rows(dmodel, hidden)
    slot_rows = wide // blocks
    columns = banding.shape[1] * stream_count // blocks
    direct = stream_count == blocks and inner == CORES and outer == 4 and group_count == 4

    slot_places, clips, slot_of, mask_places = tables(
        segments, widths[None], groups[None], slots, share, inner, group_count, direct
    )
    padded = ((bins - 1) // LANES + 2) * LANES
    spec = jnp.pad(
        spectrum.transpose(1, 0, 2).reshape(2 * frames, bins), ((0, 0), (0, padded - bins))
    )

    if direct:
        rnn0, w_split, later, pieces = gather_front(
            intake.reshape(2, 2 * dmodel, LANES), recurrence.reshape(2, 2 * hidden, LANES), outtake, scalers,
            splitter.reshape(slots * slot_rows, dmodel), banding, masker, widener.transpose(0, 2, 1), cotangent,
            rows, group_count, outer,
        )
        near = [later] + [pass_along(later, "band", m) for m in range(1, group_count)]
        pieces = pieces.reshape((outer, share) + pieces.shape[1:])
        mine = lax.all_to_all(pieces, "stream", 0, 0, axis_index_groups=across, tiled=True)
    else:
        whole = (
            lax.all_gather(intake, "stream", axis=3, tiled=True),
            lax.all_gather(recurrence, "stream", axis=3, tiled=True),
            lax.all_gather(outtake, "stream", axis=1, tiled=True),
            lax.all_gather(scalers, "stream", axis=1, tiled=True),
        )
        rnn0, rnn1 = (
            pack_rnn(whole[0][k], whole[1][k], whole[2][k], whole[3][k : k + 1], rows, vec_share)
            for k in range(2)
        )
        w_split = pack_split(
            lax.all_gather(splitter, "stream", axis=1, tiled=True),
            lax.all_gather(banding, "stream", axis=1, tiled=True),
            blocks,
        )
        w_mask = share_slots(masker, outer, across, within, 1)
        w_wide = share_slots(widener.transpose(0, 2, 1), outer, across, within, 1)
        cot_parts = cotangent.reshape(frames, outer, share, wide).transpose(1, 2, 0, 3)
        cot = lax.all_to_all(cot_parts, "stream", 0, 0, axis_index_groups=across, tiled=True)
        mine, other = (
            jnp.concatenate([pack_pieces(w_mask[k], w_wide[k]), cot], axis=2) for k in range(CORES)
        )
    piece_rows = mine.shape[2] - frames
    def by_band(x, number):
        if direct:
            return exchange(x, group_count, outer, number)
        return lax.all_to_all(x, "band", 0, 0, tiled=True)

    def to_masks(x):
        x = x.reshape(group_count, outer, share, quarter, dmodel)
        if direct:
            return exchange(x, group_count, outer, 2)
        x = lax.all_to_all(x, "stream", 1, 1, axis_index_groups=across, tiled=True)
        return lax.all_to_all(x, "band", 0, 0, tiled=True)

    def from_masks(x):
        if direct:
            x = exchange(x, group_count, outer, 3)
        else:
            x = lax.all_to_all(x, "band", 0, 0, tiled=True)
            x = lax.all_to_all(x, "stream", 1, 1, axis_index_groups=across, tiled=True)
        return x.reshape(group_count * slots, quarter, dmodel)

    base = 2 * wide + dmodel
    got = time_forward(
        slot_places, clips, spec, w_split, rnn0, group_count, slots, blocks * columns, slot_rows, hidden
    )
    time_out, v_band, time_saved = got[0], got[1], got[2:]
    if direct:
        time_out, near = lax.optimization_barrier((time_out, near))
        rnn1 = near + [swap_cores(x) for x in near]
    else:
        rnn1 = [rnn1]
    arrived = by_band(time_out, 1)
    pack_shape = (blocks, rows, LANES)
    where = jnp.stack([lax.axis_index("band"), my_stream % CORES]).astype(jnp.int32)
    got = band_forward(
        slot_of, where, arrived.reshape(group_count * slots, quarter, dmodel), rnn1, pack_shape, hidden
    )
    band_out, band_saved = got[0], got[1:]
    if direct:
        mine, band_out = lax.optimization_barrier((mine, band_out))
        other = swap_cores(mine)
    keep, send, grad_mixed, g_mask_vec = mask_network(
        mask_places, to_masks(band_out), mine, other, v_band, base, piece_rows
    )
    r = masker.shape[1] * stream_count // (2 * outer)
    grad_back = from_masks(grad_mixed)
    if direct:
        back = keep.at[:, :, :piece_rows].add(swap_cores(send))
        back, grad_back = lax.optimization_barrier((back, grad_back))
        back = lax.all_to_all(back, "stream", 0, 0, axis_index_groups=across, tiled=True)
        back = back.reshape((slots,) + back.shape[2:])
        mask_parts = back[:, piece_rows:]
    else:
        kept, sent = unpack_pieces(keep[:, :, :piece_rows], r), unpack_pieces(send, r)
        mask_reduced = return_slots(kept[0], sent[0], outer, inner, across, within, 1)
        widened_reduced = return_slots(kept[1], sent[1], outer, inner, across, within, 1).transpose(0, 2, 1)
        mask_parts = keep[:, :, piece_rows:]
        mask_parts = lax.all_to_all(mask_parts, "stream", 0, 0, axis_index_groups=across, tiled=True)
    band_grad, *g_rnn1 = band_backward(
        slot_of, where, grad_back, rnn1, band_saved, pack_shape, group_count if direct else 1, hidden
    )
    grad_time = by_band(band_grad.reshape(group_count, slots, quarter, dmodel), 4)
    if direct:
        grad_time, g_rnn1 = lax.optimization_barrier((grad_time, g_rnn1))
        g_rnn1 = g_rnn1[:1] + [pass_along(g, "band", m) for m, g in enumerate(g_rnn1) if m]
    d_spec, g_split, g_rnn0 = time_backward(
        slot_places, clips, (my_stream // inner).astype(jnp.int32)[None], grad_time, spec, time_saved, w_split,
        v_band, rnn0, g_mask_vec, slot_rows, hidden,
    )
    if direct:
        dims = (slots, slot_rows, r, piece_rows, dmodel, hidden)
        state = tuple(x.transpose(0, 2, 1) if k % 8 == 1 else x for k, x in enumerate(state))
        scales, g_rnn0, g_rnn1, g_split, d_spec = finish(
            g_rnn0, g_split, g_rnn1, d_spec, back, state, group_count, outer, dims
        )
    else:
        d_spec = lax.psum(d_spec, "band")

    masks = mask_parts.reshape(slots, frames, wide).transpose(1, 0, 2).reshape(cotangent.shape)
    spectrum_grad = d_spec.reshape(2, frames, padded)[:, :, :bins].transpose(1, 0, 2)

    if direct:
        stepped = update(scales, (back, g_rnn0, g_rnn1, g_split), state, dims)
        stepped = [x.transpose(0, 2, 1) if k % 8 == 1 else x for k, x in enumerate(stepped)]
        return (masks, spectrum_grad, scales[9, 0]) + tuple(stepped)
    first, second = unpack_rnn(g_rnn0, dmodel, hidden), unpack_rnn(g_rnn1[0], dmodel, hidden)
    rnn_grads = [jnp.stack([a, b]) for a, b in zip(first[:3], second[:3])]
    rnn_grads.append(jnp.concatenate([first[3], second[3]], axis=0))
    rnn_grads = [
        lax.psum(lax.psum_scatter(g, "stream", scatter_dimension=d, tiled=True), "band")
        for g, d in zip(rnn_grads, (3, 3, 1, 1))
    ]
    g_band = unpack_banding(g_split, slots * slot_rows, slots, columns)
    g_split = g_split[:, : slots * slot_rows].reshape(blocks, slots, slot_rows, dmodel)
    g_split = g_split.transpose(1, 0, 2, 3).reshape(slots, wide, dmodel)
    split_reduced = lax.psum_scatter(g_split, "stream", scatter_dimension=1, tiled=True)
    band_reduced = lax.psum_scatter(g_band, "stream", scatter_dimension=1, tiled=True)
    reduced = (split_reduced, widened_reduced, mask_reduced, band_reduced) + tuple(rnn_grads)

    shares = (1.0,) * 4 + (1.0 / group_count,) * 4
    sizes = (group_count, stream_count)
    sums = [sum(jnp.sum(g * g) * part for g, part in zip(reduced, shares))]
    sums += [jnp.sum(w * w) * part for w, part in zip(weights, shares)]
    totals = sum_everywhere(jnp.stack(sums), sizes)
    grad_norm = jnp.sqrt(totals[0])
    factor = jnp.minimum(1.0, CLIP_NORM / grad_norm)
    moments = [lamb_moments(g, m, p, factor) for g, m, p in zip(reduced, means_old, powers_old)]
    directions = [lamb_direction(w, m, p, d) for w, (m, p), d in zip(weights, moments, DECAYS)]
    update_totals = sum_everywhere(
        jnp.stack([jnp.sum(d * d) * part for d, part in zip(directions, shares)]), sizes
    )
    ratios = jnp.sqrt(totals[1:]) / jnp.sqrt(update_totals + 1e-12)
    fresh = [w - LEARN_RATE * ratios[k] * d for k, (w, d) in enumerate(zip(weights, directions))]
    return (
        (masks, spectrum_grad, grad_norm)
        + tuple(fresh)
        + tuple(m for m, unused in moments)
        + tuple(p for unused, p in moments)
    )


def solution(mesh):
    stored = (
        P("band", "stream", None),
        P("band", None, "stream"),
        P("band", "stream", None),
        P("band", "stream"),
        P(None, None, None, "stream"),
        P(None, None, None, "stream"),
        P(None, "stream", None),
        P(None, "stream"),
    )
    frames_over = P("stream", None, None)
    mask_over = P("stream", "band", None, None)
    return jax.shard_map(
        body,
        mesh=mesh,
        in_specs=(frames_over, P("stream", None), P(), P(), mask_over) + stored * 3,
        out_specs=(mask_over, frames_over, P()) + stored * 3,
        check_vma=False,
    )
```

```python
from functools import partial
import math

import jax
import jax.numpy as jnp
from jax import lax
from jax.experimental import pallas as pl
from jax.experimental.pallas import tpu as pltpu
from jax.sharding import PartitionSpec as P

STEP = 10
CLIP_NORM = 5.0
LEARN_RATE = 0.5
BETA_ONE = 0.9
BETA_TWO = 0.999
ADAM_EPS = 1e-06
DECAY_RATE = 0.01
NORM_EPS = 1e-05
VAR_FLOOR = 0.25
CLIPS = 3
CLIP_MOST = 32
LANES = 128
VMEM_BYTES = 60 * 1024 * 1024
CORES = 2
SLOT_PAD = 16
MESH = pl.DeviceIdType.MESH

AB = (((1,), (0,)), ((), ()))
ABT = (((1,), (1,)), ((), ()))
ATB = (((0,), (0,)), ((), ()))


def split(x):
    hi = x.astype(jnp.bfloat16)
    lo = (x - hi.astype(jnp.float32)).astype(jnp.bfloat16)
    return hi, lo


def dot1(a, b, dims):
    return lax.dot_general(a, b, dims, preferred_element_type=jnp.float32)


def dot_parts(a, b, dims):
    return dot1(a[0], b[0], dims) + (dot1(a[1], b[0], dims) + dot1(a[0], b[1], dims))


def dot3(a, b, dims):
    return dot_parts(split(a), split(b), dims)


def sigmoid(x):
    return 0.5 * jnp.tanh(0.5 * x) + 0.5


def norm_stats(x):
    center = x - jnp.mean(x, axis=-1, keepdims=True)
    spread = jnp.mean(center * center, axis=-1, keepdims=True)
    scale = lax.rsqrt(spread + NORM_EPS)
    return center * scale, scale


def norm_back(grad_unit, unit, scale):
    first = jnp.mean(grad_unit, axis=-1, keepdims=True)
    second = jnp.mean(grad_unit * unit, axis=-1, keepdims=True)
    return scale * (grad_unit - first - unit * second)


def column_sum(x):
    return jnp.sum(x, axis=0, keepdims=True)


def pack_rows(dmodel, hidden):
    blocks = 4 * hidden // LANES
    out_rows = 2 * hidden // blocks
    weight_rows = 2 * dmodel + 2 * hidden + out_rows
    share = (2 * dmodel + 8 * hidden + dmodel) // blocks
    vec_rows = -(-share // LANES)
    return blocks, out_rows, weight_rows, share, vec_rows, -(-(weight_rows + vec_rows) // 32) * 32


def pack_rnn(w_in, w_rec, w_out, vec, rows, share):
    count = w_in.shape[2] // LANES
    parts = [
        w.reshape(2 * w.shape[1], count, LANES).transpose(1, 0, 2) for w in (w_in, w_rec)
    ] + [w_out.reshape(count, -1, LANES)]
    used = sum(p.shape[1] for p in parts)
    flat = jnp.pad(vec.reshape(count, share), ((0, 0), (0, (rows - used) * LANES - share)))
    return jnp.concatenate(parts + [flat.reshape(count, rows - used, LANES)], axis=1)


def unpack_rnn(pack, dmodel, hidden):
    blocks, out_rows, weight_rows, share, vec_rows, rows = pack_rows(dmodel, hidden)
    count = pack.shape[0]
    cuts = (0, 2 * dmodel, 2 * dmodel + 2 * hidden)
    w_in = pack[:, : cuts[1]].reshape(count, 2, dmodel, LANES).transpose(1, 2, 0, 3)
    w_rec = pack[:, cuts[1] : cuts[2]].reshape(count, 2, hidden, LANES).transpose(1, 2, 0, 3)
    return (
        w_in.reshape(2, dmodel, count * LANES),
        w_rec.reshape(2, hidden, count * LANES),
        pack[:, cuts[2] : weight_rows].reshape(count * out_rows, LANES),
        unpack_vec(pack, weight_rows, vec_rows, share),
    )


def unpack_vec(pack, weight_rows, vec_rows, share):
    count = pack.shape[0]
    flat = pack[:, weight_rows : weight_rows + vec_rows].reshape(count, vec_rows * LANES)
    return flat[:, :share].reshape(1, count * share)


class Pack:
    def __init__(self, ref, dmodel, hidden):
        self.ref, self.dmodel, self.hidden = ref, dmodel, hidden
        self.blocks, self.out_rows = pack_rows(dmodel, hidden)[:2]

    def intake(self, e, first, last):
        rows = slice(e * self.dmodel, (e + 1) * self.dmodel)
        return jnp.concatenate([self.ref[k, rows] for k in range(first, last)], axis=1)

    def recurrence(self, e, k):
        base = 2 * self.dmodel + e * self.hidden
        return self.ref[k, base : base + self.hidden]

    def outtake(self, e):
        base = 2 * self.dmodel + 2 * self.hidden
        half = self.blocks // 2
        return jnp.concatenate(
            [self.ref[k, base : base + self.out_rows] for k in range(half * e, half * (e + 1))], axis=0
        )

    def put(self, k, base, value):
        if len(self.ref.shape) == 3:
            self.ref[k, base : base + value.shape[0]] = value
            return
        quarter = self.ref.shape[2]
        done = 0
        while done < value.shape[0]:
            part, at = divmod(base + done, quarter)
            count = min(value.shape[0] - done, quarter - at)
            self.ref[part, k, at : at + count] = value[done : done + count]
            done += count

    def put_intake(self, e, q, value):
        for h in range(value.shape[1] // LANES):
            self.put(q * value.shape[1] // LANES + h, e * self.dmodel, value[:, h * LANES : (h + 1) * LANES])

    def put_recurrence(self, e, q, value):
        base = 2 * self.dmodel + e * self.hidden
        for h in range(value.shape[1] // LANES):
            self.put(q * value.shape[1] // LANES + h, base, value[:, h * LANES : (h + 1) * LANES])

    def put_outtake(self, e, value):
        base = 2 * self.dmodel + 2 * self.hidden
        for k in range(self.blocks // 2):
            self.put(self.blocks // 2 * e + k, base, value[k * self.out_rows : (k + 1) * self.out_rows])

    def put_vec(self, value):
        unused, unused, base, share, vec_rows, rows = pack_rows(self.dmodel, self.hidden)
        for k in range(self.blocks):
            block = [
                value[:, k * share + r * LANES : k * share + min(share, (r + 1) * LANES)] for r in range(vec_rows)
            ]
            block[-1] = jnp.concatenate(
                [block[-1], jnp.zeros((1, vec_rows * LANES - share), jnp.float32)], axis=1
            )
            block.append(jnp.zeros((rows - base - vec_rows, LANES), jnp.float32))
            self.put(k, base, jnp.concatenate(block, axis=0))


def load_vec(pack, vec):
    unused, unused, base, share, vec_rows, unused = pack_rows(pack.dmodel, pack.hidden)
    for k in range(pack.blocks):
        for r in range(vec_rows):
            width = min(LANES, share - r * LANES)
            at = k * share + r * LANES
            vec[0:1, at : at + width] = pack.ref[k, base + r : base + r + 1, :width]


def split_recurrence(pack, hi_ref, lo_ref):
    for e in range(2):
        for k in range(pack.blocks):
            part = slice(k * LANES, (k + 1) * LANES)
            hi_ref[e, :, part], lo_ref[e, :, part] = split(pack.recurrence(e, k))


def split_recurrence_turned(pack, hi_ref, lo_ref):
    for e in range(2):
        for k in range(pack.blocks):
            part = slice(k * LANES, (k + 1) * LANES)
            hi_ref[e, part], lo_ref[e, part] = split(pack.recurrence(e, k).T)


def gates_forward(x_flat, act, pack, vec, rows, block):
    hidden4 = 4 * pack.hidden
    dmodel = pack.dmodel
    parts = [split(pack.intake(e, 0, pack.blocks)) for e in range(2)]

    def one(r, carry):
        start = pl.multiple_of(r * block, block)
        unit, unused = norm_stats(x_flat(start, block))
        n = split(unit * (1.0 + vec[0:1, :dmodel]) + vec[0:1, dmodel : 2 * dmodel])
        for e in range(2):
            bias = vec[0:1, 2 * dmodel + hidden4 * e : 2 * dmodel + hidden4 * (e + 1)]
            z = dot_parts(n, parts[e], AB) + bias
            act[e][pl.ds(r * (block // 16), block // 16)] = z.reshape(block // 16, 16, hidden4)
        return carry

    lax.fori_loop(0, rows // block, one, 0)


def run_forward(steps, places, act, c, h, pack, hi_ref, lo_ref, state, memory):
    hidden = pack.hidden
    split_recurrence(pack, hi_ref, lo_ref)
    for e in range(2):
        state[e][...] = jnp.zeros_like(state[e])
        memory[e][...] = jnp.zeros_like(memory[e])

    def step(j, carry):
        work = []
        for e in range(2):
            at = places(e, j)
            prior = state[e][...]
            hi, lo = split(prior)
            rows = prior.shape[0]
            first = dot1(jnp.concatenate([hi, lo], axis=0), hi_ref[e], AB)
            drive = [act[e][p] for p in at]
            drive = drive[0] if len(drive) == 1 else jnp.concatenate(drive, axis=0)
            z = first[:rows] + first[rows:] + dot1(hi, lo_ref[e], AB) + drive
            work.append((at, z))
        for e in range(2):
            at, z = work[e]
            ingate = sigmoid(z[:, :hidden])
            forget = sigmoid(z[:, hidden : 2 * hidden])
            candidate = jnp.tanh(z[:, 2 * hidden : 3 * hidden])
            outgate = sigmoid(z[:, 3 * hidden :])
            before = memory[e][...]
            now = forget * before + ingate * candidate
            squashed = jnp.tanh(now)
            out = outgate * squashed
            memory[e][...] = now
            state[e][...] = out
            for k, p in enumerate(at):
                part = slice(16 * k, 16 * (k + 1))
                act[e][p, :, :hidden] = ingate[part]
                act[e][p, :, hidden : 2 * hidden] = forget[part]
                act[e][p, :, 2 * hidden : 3 * hidden] = candidate[part]
                act[e][p, :, 3 * hidden :] = outgate[part]
                c[e][p] = now[part]
                h[e][p] = out[part]
        return carry

    lax.fori_loop(0, steps, step, 0, unroll=2)


def output_forward(count, h, pack, vec):
    hidden = h[0].shape[2]
    dmodel = pack.dmodel
    total = vec[0:1, vec.shape[1] - dmodel :]
    for e in range(2):
        states = h[e][:count].reshape(count * 16, hidden)
        total = total + dot3(states, pack.outtake(e), AB)
    return total


def run_backward(steps, places, act, dz_ref, c, dh, pack, hi_ref, lo_ref, grad_h, grad_c):
    hidden = pack.hidden
    split_recurrence_turned(pack, hi_ref, lo_ref)
    for e in range(2):
        grad_h[e][...] = jnp.zeros_like(grad_h[e])
        grad_c[e][...] = jnp.zeros_like(grad_c[e])

    def load(ref, at):
        got = [ref[p] for p in at]
        return got[0] if len(got) == 1 else jnp.concatenate(got, axis=0)

    def step(back, carry):
        j = steps - 1 - back
        later = jnp.minimum(j, 1).astype(jnp.float32)
        work = []
        for e in range(2):
            at = places(e, j)
            gates = load(act[e], at)
            ingate = gates[:, :hidden]
            forget = gates[:, hidden : 2 * hidden]
            candidate = gates[:, 2 * hidden : 3 * hidden]
            outgate = gates[:, 3 * hidden :]
            squashed = jnp.tanh(load(c[e], at))
            before = load(c[e], places(e, jnp.maximum(j - 1, 0))) * later
            total_h = load(dh[e], at) + grad_h[e][...]
            total_c = grad_c[e][...] + total_h * outgate * (1.0 - squashed * squashed)
            dz = jnp.concatenate(
                [
                    total_c * candidate * ingate * (1.0 - ingate),
                    total_c * before * forget * (1.0 - forget),
                    total_c * ingate * (1.0 - candidate * candidate),
                    total_h * squashed * outgate * (1.0 - outgate),
                ],
                axis=1,
            )
            grad_c[e][...] = total_c * forget
            for k, p in enumerate(at):
                dz_ref[e][p] = dz[16 * k : 16 * (k + 1)]
            work.append(dz)
        for e in range(2):
            hi, lo = split(work[e])
            rows = hi.shape[0]
            first = dot1(jnp.concatenate([hi, lo], axis=0), hi_ref[e], AB)
            grad_h[e][...] = first[:rows] + first[rows:] + dot1(hi, lo_ref[e], AB)
        return carry

    lax.fori_loop(0, steps, step, 0, unroll=2)


def states_backward(count, dy_flat, dh, h, pack, g_pack):
    hidden = h[0].shape[2]
    dy = split(dy_flat)
    for e in range(2):
        dh[e][:count] = dot_parts(dy, split(pack.outtake(e)), ABT).reshape(count, 16, hidden)
        g_pack.put_outtake(e, dot3_parts_first(h[e][:count].reshape(count * 16, hidden), dy))


def dot3_parts_first(a, b_parts):
    return dot_parts(split(a), b_parts, ATB)


def gates_backward(count, x_flat, dy_flat, dz_ref, before, pack, vec, g_pack, g_vec):
    dmodel, hidden = pack.dmodel, pack.hidden
    hidden4 = 4 * hidden
    rows = count * 16
    unit, scale = norm_stats(x_flat)
    gain = 1.0 + vec[0:1, :dmodel]
    n = unit * gain + vec[0:1, dmodel : 2 * dmodel]
    dn = jnp.zeros((rows, dmodel), jnp.float32)
    for e in range(2):
        left_hi, left_lo = split(jnp.concatenate([n, before(e)], axis=1).T)
        left = jnp.concatenate([left_hi, left_lo], axis=0)
        height = left_hi.shape[0]
        for q in range(4):
            part = slice(hidden * q, hidden * (q + 1))
            dz_q = dz_ref[e][:count, :, part].reshape(rows, hidden)
            dz = split(dz_q)
            first = dot1(left, dz[0], AB)
            got = first[:height] + first[height:] + dot1(left_hi, dz[1], AB)
            g_pack.put_intake(e, q, got[:dmodel])
            g_pack.put_recurrence(e, q, got[dmodel:])
            dn = dn + dot_parts(dz, split(pack.intake(e, q * pack.blocks // 4, (q + 1) * pack.blocks // 4)), ABT)
            base = 2 * dmodel + hidden4 * e + hidden * q
            g_vec[0:1, base : base + hidden] = column_sum(dz_q)
    g_vec[0:1, :dmodel] = column_sum(dn * unit)
    g_vec[0:1, dmodel : 2 * dmodel] = column_sum(dn)
    g_vec[0:1, vec.shape[1] - dmodel :] = column_sum(dy_flat)
    g_pack.put_vec(g_vec[...])
    return dy_flat + norm_back(dn * gain, unit, scale)


def shifted(ref, e, count, hidden, mask):
    rows = (count - 1) * 16
    zero = jnp.zeros((16, hidden), jnp.float32)
    if e == 0:
        kept = ref[: count - 1].reshape(rows, hidden) * mask
        return jnp.concatenate([zero, kept], axis=0)
    kept = ref[1:count].reshape(rows, hidden) * mask
    return jnp.concatenate([kept, zero], axis=0)


def tables_kernel(
    slots, share, inner, direct, segments, widths, groups, places, clips, slot_of, mask_places, counts
):
    band, stream = lax.axis_index("band"), lax.axis_index("stream")
    for s in range(slots):
        places[0, s] = 0
        places[1, s] = 0
    for c in range(CLIPS):
        clips[1, c] = 0
    for g in range(counts.shape[0]):
        counts[g] = 0

    def one_band(b, edge):
        g = groups[0, b]
        rank = counts[g]
        counts[g] = rank + 1
        slot_of[0, b] = g * slots + rank
        width = widths[0, b]

        @pl.when(g == band)
        def mine():
            places[0, rank] = edge
            places[1, rank] = width

        return edge + width

    lax.fori_loop(0, groups.shape[1], one_band, jnp.int32(0))

    def one_frame(t, carry):
        c = segments[0, t]
        clips[1, c] = clips[1, c] + 1
        return carry

    lax.fori_loop(0, segments.shape[1], one_frame, 0)
    start = jnp.int32(0)
    for c in range(CLIPS):
        clips[0, c] = start
        start = start + clips[1, c]
    for j in range(share):
        row = lax.div(stream, inner) * share + j
        mask_places[0, j] = places[1, row]
        mask_places[1, j] = lax.rem(stream, CORES) if direct else jnp.int32(0)
        mask_places[2, j] = row


def tables(segments, widths, groups, slots, share, inner, bands, direct):
    def i32(shape):
        return jax.ShapeDtypeStruct(shape, jnp.int32)

    smem = pl.BlockSpec(memory_space=pltpu.SMEM)
    return pl.pallas_call(
        partial(tables_kernel, slots, share, inner, direct),
        out_shape=[i32((2, slots)), i32((2, CLIPS)), i32(groups.shape), i32((3, share))],
        in_specs=[smem] * 3,
        out_specs=[smem] * 4,
        scratch_shapes=[pltpu.SMEM((bands,), jnp.int32)],
        name="tables",
    )(segments, widths, groups)


def clip_places(clips, spare):
    def places(e, j):
        found = []
        for c in range(CLIPS):
            start, length = clips[0, c], clips[1, c]
            frame = start + j if e == 0 else start + length - 1 - j
            found.append(jnp.where(j < length, frame, spare))
        return found

    return places


def window_of(edge):
    base = pl.multiple_of((edge // LANES) * LANES, LANES)
    return base, lax.rem(edge, LANES)


def split_rows(spec, edge, width, frames):
    wmax = LANES
    base, shift = window_of(edge)
    window = spec[:, pl.ds(base, 2 * LANES)]
    taken = pltpu.roll(window, lax.rem(2 * LANES - shift, 2 * LANES), 1)[:, :wmax]
    taken = jnp.concatenate([taken[:frames], taken[frames:]], axis=1)
    lane = lax.broadcasted_iota(jnp.int32, (frames, wmax), 1)
    inside = (lane < width).astype(jnp.float32)
    valid = jnp.concatenate([inside, inside], axis=1)
    entries = jnp.maximum(2 * width, 1).astype(jnp.float32)
    mean = jnp.sum(taken * valid, axis=-1, keepdims=True) / entries
    center = (taken - mean) * valid
    spread = jnp.sum(center * center, axis=-1, keepdims=True) / entries
    scale = lax.rsqrt(jnp.maximum(spread, VAR_FLOOR))
    moving = jnp.where(spread > VAR_FLOOR, 1.0, jnp.where(spread == VAR_FLOOR, 0.5, 0.0))
    return center * scale, scale, valid, moving, entries


def slot_weights(w_split, s, slot_rows):
    count = w_split.shape[0]
    at = pl.ds(pl.multiple_of(s * slot_rows, slot_rows), slot_rows)
    return jnp.concatenate([w_split[k, at, :] for k in range(count)], axis=0)


def time_forward_kernel(
    slot_rows, places_s, clips, spec, w_split, rnn_in,
    out, v_band, x, *refs,
):
    saved, refs = refs[:6], refs[6:]
    act0, act1, c0, c1, h0, h1, hi_ref, lo_ref, s0, s1, m0, m1, y, mixed, vec, rnn, sems = refs
    slots = out.shape[1]
    frames, unused, dmodel = x.shape
    wide = w_split.shape[0] * slot_rows
    pack = Pack(rnn, dmodel, h0.shape[2])
    load_rnn = pltpu.make_async_copy(rnn_in, rnn, sems.at[0])
    load_rnn.start()
    v_band[...] = jnp.zeros_like(v_band)
    columns = v_band.shape[1] // w_split.shape[0]
    for k in range(w_split.shape[0]):
        for h in range(0, columns, LANES):
            width = min(LANES, columns - h)
            at = slots * slot_rows + SLOT_PAD * (h // LANES)
            v_band[:, k * columns + h : k * columns + h + width] = w_split[k, at : at + SLOT_PAD, :width]
    x[...] = jnp.zeros_like(x)
    for a in (act0, act1):
        a[frames] = jnp.zeros_like(a[frames])

    for s in range(slots):
        unit, unused, valid, moving, entries = split_rows(spec, places_s[0, s], places_s[1, s], frames)
        row = v_band[s : s + 1, : 2 * wide + dmodel]
        z = (unit * (1.0 + row[:, :wide]) + row[:, wide : 2 * wide]) * valid
        y[s] = dot3(z, slot_weights(w_split, s, slot_rows), AB) + row[:, 2 * wide : 2 * wide + dmodel]
    for s in range(slots):
        x[:, s, :] = y[s]
    load_rnn.wait()
    load_vec(pack, vec)
    act = (act0, act1)

    def x_flat(start, size):
        return x[pl.ds(start // 16, size // 16)].reshape(size, dmodel)

    gates_forward(x_flat, act, pack, vec, frames * 16, 256)
    run_forward(
        CLIP_MOST, clip_places(clips, frames), act, (c0, c1), (h0, h1),
        pack, hi_ref, lo_ref, (s0, s1), (m0, m1),
    )
    leaving = [
        pltpu.make_async_copy(a, b, sems.at[1 + k])
        for k, (a, b) in enumerate(zip((act0, act1, c0, c1, h0, h1), saved))
    ]
    for copy in leaving:
        copy.start()
    total = output_forward(frames, (h0, h1), pack, vec)
    x_all = x[...].reshape(frames * 16, dmodel)
    mixed[...] = (x_all + total).reshape(frames, 16, dmodel)
    parts, unused_slots, quarter, unused = out.shape
    for s in range(slots):
        for q in range(parts):
            out[q, s] = mixed[q * quarter : (q + 1) * quarter, s, :]
    for copy in leaving:
        copy.wait()


def f32(shape):
    return jax.ShapeDtypeStruct(shape, jnp.float32)


def saved_shapes(count, hidden):
    return [f32((count, 16, 4 * hidden))] * 2 + [f32((count, 16, hidden))] * 4


def saved_scratch(count, hidden):
    return [pltpu.VMEM(x.shape, jnp.float32) for x in saved_shapes(count, hidden)]


def vec_scratch(dmodel, hidden):
    return pltpu.VMEM((1, 3 * dmodel + 8 * hidden), jnp.float32)


def rec_scratch(rows, hidden, turned=False):
    return [
        pltpu.VMEM((2, 4 * hidden, hidden) if turned else (2, hidden, 4 * hidden), jnp.bfloat16),
        pltpu.VMEM((2, 4 * hidden, hidden) if turned else (2, hidden, 4 * hidden), jnp.bfloat16),
    ] + [pltpu.VMEM((rows, hidden), jnp.float32)] * 4


SMEM = pl.BlockSpec(memory_space=pltpu.SMEM)
VMEM = pl.BlockSpec(memory_space=pltpu.VMEM)
ANY = pl.BlockSpec(memory_space=pl.ANY)
PARAMS = pltpu.CompilerParams(vmem_limit_bytes=VMEM_BYTES)


def cost(micros):
    return pl.CostEstimate(flops=int(micros * 1.1e9), bytes_accessed=int(micros * 3e6), transcendentals=0)


def time_forward(slot_places, clips, spec, w_split, rnn, parts, slots, band_columns, slot_rows, hidden):
    dmodel = w_split.shape[2]
    frames = spec.shape[0] // 2
    return pl.pallas_call(
        partial(time_forward_kernel, slot_rows),
        out_shape=[
            f32((parts, slots, frames // parts, dmodel)), f32((SLOT_PAD, band_columns)), f32((frames, 16, dmodel)),
        ]
        + saved_shapes(frames + 1, hidden),
        in_specs=[SMEM, SMEM, VMEM, VMEM, ANY],
        out_specs=[VMEM] * 3 + [ANY] * 6,
        scratch_shapes=saved_scratch(frames + 1, hidden)
        + rec_scratch(16 * CLIPS, hidden)
        + [pltpu.VMEM((slots, frames, dmodel), jnp.float32)]
        + [pltpu.VMEM((frames, 16, dmodel), jnp.float32), vec_scratch(dmodel, hidden)]
        + [pltpu.VMEM(rnn.shape, jnp.float32), pltpu.SemaphoreType.DMA((7,))],
        compiler_params=PARAMS,
        cost_estimate=cost(35),
        name="time_forward",
    )(slot_places, clips, spec, w_split, rnn)


def time_backward_kernel(
    slot_rows, places_s, clips, my_outer, dy_in, spec_in, x_in, *refs,
):
    saved, refs = refs[:6], refs[6:]
    w_split_in, v_band, rnn_in, g_mask_vec, d_spec, g_split, g_rnn, *refs = refs
    act0, act1, c0, c1, h0, h1, *refs = refs
    hi_ref, lo_ref, s0, s1, m0, m1, dy, vec, g_vec, g_band, dh0, dh1, dz0, dz1, *refs = refs
    rnn, w_split, spec, x, sems = refs
    slots = dy_in.shape[1]
    frames, unused, dmodel = x.shape
    hidden = h0.shape[2]
    wide = w_split.shape[0] * slot_rows
    parts, unused_slots, quarter, unused = dy_in.shape
    pack, g_pack = Pack(rnn, dmodel, hidden), Pack(g_rnn, dmodel, hidden)
    pairs = [(rnn_in, rnn), (saved[4], h0), (saved[5], h1)]
    pairs += list(zip(saved[:4], (act0, act1, c0, c1)))
    pairs += [(w_split_in, w_split), (spec_in, spec), (x_in, x)]
    loads = [pltpu.make_async_copy(a, b, sems.at[k]) for k, (a, b) in enumerate(pairs)]
    for copy in loads:
        copy.start()
    dy[...] = jnp.zeros_like(dy)
    for s in range(slots):
        for q in range(parts):
            dy[q * quarter : (q + 1) * quarter, s, :] = dy_in[q, s]
    for copy in loads[:3]:
        copy.wait()
    load_vec(pack, vec)
    dy_flat = dy[...].reshape(frames * 16, dmodel)
    states_backward(frames, dy_flat, (dh0, dh1), (h0, h1), pack, g_pack)
    for d in (dh0, dh1):
        d[frames] = jnp.zeros_like(d[frames])
    for copy in loads[3:7]:
        copy.wait()
    run_backward(
        CLIP_MOST, clip_places(clips, frames), (act0, act1), (dz0, dz1), (c0, c1),
        (dh0, dh1), pack, hi_ref, lo_ref, (s0, s1), (m0, m1),
    )
    for copy in loads[7:]:
        copy.wait()
    frame = lax.broadcasted_iota(jnp.int32, ((frames - 1) * 16, 1), 0) // 16 + 1
    inside = jnp.ones(frame.shape, jnp.float32)
    for k in range(1, CLIPS):
        inside = jnp.where(frame == clips[0, k], 0.0, inside)
    x_flat = x[...].reshape(frames * 16, dmodel)
    dx = gates_backward(
        frames, x_flat, dy[...].reshape(frames * 16, dmodel), (dz0, dz1),
        lambda e: shifted((h0, h1)[e], e, frames, hidden, inside), pack, vec, g_pack, g_vec,
    )
    dy[...] = dx.reshape(frames, 16, dmodel)
    d_spec[...] = jnp.zeros_like(d_spec)
    g_split[:, slots * slot_rows :] = jnp.zeros_like(g_split[:, slots * slot_rows :])
    g_band[...] = jnp.zeros_like(g_band)

    for s in range(slots):
        edge, width = places_s[0, s], places_s[1, s]
        unit, scale, valid, moving, entries = split_rows(spec, edge, width, frames)
        row = v_band[s : s + 1, : 2 * wide + dmodel]
        gain = 1.0 + row[:, :wide]
        z = (unit * gain + row[:, wide : 2 * wide]) * valid
        demb = dy[:, s, :]
        demb_parts = split(demb)
        g_slot = dot_parts(split(z), demb_parts, ATB)
        for k in range(w_split.shape[0]):
            g_split[k, s * slot_rows : (s + 1) * slot_rows] = g_slot[k * slot_rows : (k + 1) * slot_rows]
        dz = dot_parts(demb_parts, split(slot_weights(w_split, s, slot_rows)), ABT) * valid
        g_band[s : s + 1, :wide] = column_sum(dz * unit)
        g_band[s : s + 1, wide : 2 * wide] = column_sum(dz)
        g_band[s : s + 1, 2 * wide : 2 * wide + dmodel] = column_sum(demb)
        du = dz * gain
        first = jnp.sum(du, axis=-1, keepdims=True) / entries
        second = jnp.sum(du * unit, axis=-1, keepdims=True) / entries
        dt = scale * (du - first - moving * unit * second) * valid
        base, shift = window_of(edge)
        stacked = jnp.concatenate([dt[:, :LANES], dt[:, LANES:]], axis=0)
        padded = jnp.concatenate([stacked, jnp.zeros_like(stacked)], axis=1)
        d_spec[:, pl.ds(base, 2 * LANES)] += pltpu.roll(padded, shift, 1)

    share = g_mask_vec.shape[0]
    for j in range(share):
        g_band[pl.ds(my_outer[0] * share + j, 1), 2 * wide + dmodel :] = g_mask_vec[j]
    gathered = g_band[...]
    blocks = w_split.shape[0]
    columns = gathered.shape[1] // blocks
    for k in range(blocks):
        for h in range(0, columns, LANES):
            width = min(LANES, columns - h)
            at = slots * slot_rows + SLOT_PAD * (h // LANES)
            g_split[k, at : at + SLOT_PAD, :width] = gathered[:, k * columns + h : k * columns + h + width]


def time_backward(
    slot_places, clips, my_outer, dy, spec, saved, w_split, v_band, rnn, g_mask_vec, slot_rows, hidden
):
    band_columns = v_band.shape[1]
    dmodel = w_split.shape[2]
    frames = spec.shape[0] // 2
    return pl.pallas_call(
        partial(time_backward_kernel, slot_rows),
        out_shape=[f32(spec.shape), f32(w_split.shape), f32(rnn.shape)],
        in_specs=[SMEM] * 3 + [VMEM] + [ANY] * (2 + 6 + 1) + [VMEM, ANY, VMEM],
        out_specs=[VMEM] * 3,
        scratch_shapes=saved_scratch(frames + 1, hidden)
        + rec_scratch(16 * CLIPS, hidden, True)
        + [pltpu.VMEM((frames, 16, dmodel), jnp.float32)] + [vec_scratch(dmodel, hidden)] * 2
        + [pltpu.VMEM((SLOT_PAD, band_columns), jnp.float32)]
        + [pltpu.VMEM((frames + 1, 16, hidden), jnp.float32)] * 2
        + [pltpu.VMEM((frames + 1, 16, 4 * hidden), jnp.float32)] * 2
        + [pltpu.VMEM(a.shape, jnp.float32) for a in (rnn, w_split, spec, saved[0])]
        + [pltpu.SemaphoreType.DMA((10,))],
        compiler_params=PARAMS,
        cost_estimate=cost(2),
        name="time_backward",
    )(slot_places, clips, my_outer, dy, spec, *saved, w_split, v_band, rnn, g_mask_vec)


def band_places(bands):
    return lambda e, j: [j if e == 0 else bands - 1 - j]


def place_pack(rnn, pieces, where):
    band, core = where[0], where[1]
    parts = len(pieces) // CORES
    for k, ref in enumerate(pieces):
        kind, m = divmod(k, parts)
        layers, quarter, unused = ref.shape
        at = lax.rem(band + parts - m, parts)
        rows = pl.ds(pl.multiple_of(at * quarter, 8), quarter)
        for layer in range(layers):
            rnn[layer * CORES + lax.rem(core + kind, CORES), rows] = ref[layer]


def arrive_pack(rnn, pieces, where):
    if len(pieces) == 1:
        rnn[...] = pieces[0][...]
    else:
        place_pack(rnn, pieces, where)


def band_forward_kernel(count, slot_of, where, arrived, *refs):
    pieces, refs = refs[:count], refs[count:]
    out, x, *refs = refs
    saved, refs = refs[:6], refs[6:]
    act0, act1, c0, c1, h0, h1, hi_ref, lo_ref, s0, s1, m0, m1, vec, rnn, sems = refs
    bands, unused, dmodel = x.shape
    pack = Pack(rnn, dmodel, h0.shape[2])
    arrive_pack(rnn, pieces, where)
    load_vec(pack, vec)

    def fetch(b, carry):
        x[b] = arrived[slot_of[0, b]]
        return carry

    lax.fori_loop(0, bands, fetch, 0)
    act = (act0, act1)

    def x_flat(start, size):
        return x[...].reshape(bands * 16, dmodel)

    gates_forward(x_flat, act, pack, vec, bands * 16, bands * 16)
    run_forward(
        bands, band_places(bands), act, (c0, c1), (h0, h1), pack, hi_ref, lo_ref, (s0, s1), (m0, m1)
    )
    leaving = [
        pltpu.make_async_copy(a, b, sems.at[k])
        for k, (a, b) in enumerate(zip((act0, act1, c0, c1, h0, h1), saved))
    ]
    for copy in leaving:
        copy.start()
    total = output_forward(bands, (h0, h1), pack, vec)
    whole = (x[...].reshape(bands * 16, dmodel) + total).reshape(bands, 16, dmodel)
    out[...] = jnp.zeros_like(out)
    for b in range(bands):
        out[slot_of[0, b]] = whole[b]
    for copy in leaving:
        copy.wait()


def band_forward(slot_of, where, arrived, pieces, rnn_shape, hidden):
    bands = slot_of.shape[1]
    dmodel = arrived.shape[2]
    return pl.pallas_call(
        partial(band_forward_kernel, len(pieces)),
        out_shape=[f32(arrived.shape), f32((bands, 16, dmodel))] + saved_shapes(bands, hidden),
        in_specs=[SMEM] * 2 + [VMEM] * (1 + len(pieces)),
        out_specs=[VMEM] * 2 + [ANY] * 6,
        scratch_shapes=saved_scratch(bands, hidden)
        + rec_scratch(16, hidden)
        + [vec_scratch(dmodel, hidden), pltpu.VMEM(rnn_shape, jnp.float32), pltpu.SemaphoreType.DMA((6,))],
        compiler_params=PARAMS,
        cost_estimate=cost(28),
        name="band_forward",
    )(slot_of, where, arrived, *pieces)


def band_backward_kernel(count, parts, slot_of, where, arrived, *refs):
    pieces, refs = refs[:count], refs[count:]
    x, *refs = refs
    saved, refs = refs[:6], refs[6:]
    out, outs, refs = refs[0], refs[1 : 1 + parts], refs[1 + parts :]
    act0, act1, c0, c1, h0, h1, *refs = refs
    hi_ref, lo_ref, s0, s1, m0, m1, dy, vec, g_vec, dh0, dh1, dz0, dz1, rnn, g_rnn, sems = refs
    bands, unused, dmodel = x.shape
    hidden = h0.shape[2]
    pack, g_pack = Pack(rnn, dmodel, hidden), Pack(g_rnn, dmodel, hidden)
    pairs = [(saved[4], h0), (saved[5], h1)] + list(zip(saved[:4], (act0, act1, c0, c1)))
    loads = [pltpu.make_async_copy(a, b, sems.at[k]) for k, (a, b) in enumerate(pairs)]
    for copy in loads:
        copy.start()
    arrive_pack(rnn, pieces, where)
    load_vec(pack, vec)

    def fetch(b, carry):
        dy[b] = arrived[slot_of[0, b]]
        return carry

    lax.fori_loop(0, bands, fetch, 0)
    for copy in loads[:2]:
        copy.wait()
    states_backward(bands, dy[...].reshape(bands * 16, dmodel), (dh0, dh1), (h0, h1), pack, g_pack)
    for copy in loads[2:]:
        copy.wait()
    run_backward(
        bands, band_places(bands), (act0, act1), (dz0, dz1), (c0, c1), (dh0, dh1),
        pack, hi_ref, lo_ref, (s0, s1), (m0, m1),
    )
    dx = gates_backward(
        bands, x[...].reshape(bands * 16, dmodel), dy[...].reshape(bands * 16, dmodel), (dz0, dz1),
        lambda e: shifted((h0, h1)[e], e, bands, hidden, 1.0), pack, vec, g_pack, g_vec,
    ).reshape(bands, 16, dmodel)
    out[...] = jnp.zeros_like(out)
    for b in range(bands):
        out[slot_of[0, b]] = dx[b]
    if parts == 1:
        outs[0][...] = g_rnn[...]
    else:
        for m in range(parts):
            outs[m][...] = g_rnn[lax.rem(where[0] + m, parts)]


def band_backward(slot_of, where, arrived, pieces, saved, rnn_shape, parts, hidden):
    bands = slot_of.shape[1]
    dmodel = arrived.shape[2]
    blocks, rows, unused = rnn_shape
    grad_shape = rnn_shape if parts == 1 else (parts, blocks, rows // parts, LANES)
    return pl.pallas_call(
        partial(band_backward_kernel, len(pieces), parts),
        out_shape=[f32(arrived.shape)] + [f32(grad_shape[-3:])] * parts,
        in_specs=[SMEM] * 2 + [VMEM] * (1 + len(pieces) + 1) + [ANY] * 6,
        out_specs=[VMEM] * (1 + parts),
        scratch_shapes=saved_scratch(bands, hidden)
        + rec_scratch(16, hidden, True)
        + [pltpu.VMEM((bands, 16, dmodel), jnp.float32)]
        + [vec_scratch(dmodel, hidden)] * 2
        + [pltpu.VMEM((bands, 16, hidden), jnp.float32)] * 2
        + [pltpu.VMEM((bands, 16, 4 * hidden), jnp.float32)] * 2
        + [pltpu.VMEM(rnn_shape, jnp.float32), pltpu.VMEM(grad_shape, jnp.float32)]
        + [pltpu.SemaphoreType.DMA((6,))],
        compiler_params=PARAMS,
        cost_estimate=cost(34),
        name="band_backward",
    )(slot_of, where, arrived, *pieces, *saved)


def in_turn(core, mine, other):
    return [jnp.where(core == 0, mine, other), jnp.where(core == 0, other, mine)]


def pack_pieces(mask, wide):
    lead, r, w = mask.shape[:2], mask.shape[2], mask.shape[3] // 2
    mask = mask.reshape(lead + (r, 2, w)).transpose(0, 1, 3, 2, 4).reshape(lead + (2 * r, w))
    wide = wide.reshape(lead + (2, r // 2, w // 2)).transpose(0, 1, 3, 2, 4)
    return jnp.concatenate([mask, wide.reshape(lead + (r // 2, w))], axis=2)


def unpack_pieces(pack, r):
    lead, w = pack.shape[:2], pack.shape[3]
    mask = pack[:, :, : 2 * r].reshape(lead + (2, r, w)).transpose(0, 1, 3, 2, 4).reshape(lead + (r, 2 * w))
    wide = pack[:, :, 2 * r :].reshape(lead + (r // 2, 2, w // 2)).transpose(0, 1, 3, 2, 4)
    return mask, wide.reshape(lead + (r, w // 2))


def load_mask_piece(value, r):
    return jnp.concatenate([value[:r], value[r : 2 * r]], axis=1)


def load_wide_piece(value):
    half = value.shape[1] // 2
    return jnp.concatenate([value[:, :half], value[:, half:]], axis=0)


def mask_slot(core, width, v, x, mine, other, keep, send, g_vec):
    outer, total_rows, wide = mine.shape
    piece_rows = send.shape[1]
    frames = total_rows - piece_rows
    dmodel = x.shape[1]
    half = wide // 2
    mlp = (v.shape[1] - 2 * dmodel) - 2 * wide
    r = mlp // (2 * outer)
    w_wide, w_mask = [], []
    for g in range(outer):
        w_mask += in_turn(core, load_mask_piece(mine[g, : 2 * r], r), load_mask_piece(other[g, : 2 * r], r))
        w_wide += in_turn(
            core, load_wide_piece(mine[g, 2 * r : piece_rows]), load_wide_piece(other[g, 2 * r : piece_rows])
        )
    w_wide, w_mask = jnp.concatenate(w_wide, axis=0), jnp.concatenate(w_mask, axis=0)
    cot = jnp.concatenate([mine[g, piece_rows:] for g in range(outer)], axis=0)
    gain = 1.0 + v[:, :dmodel]
    unit, scale = norm_stats(x)
    p = split(unit * gain + v[:, dmodel : 2 * dmodel])
    wide_parts = split(w_wide)
    mask_parts = split(w_mask)
    q = jnp.tanh(dot_parts(p, wide_parts, ABT) + v[:, 2 * dmodel : 2 * dmodel + mlp])
    q_parts = split(q)
    raw = dot_parts(q_parts, mask_parts, AB) + v[:, 2 * dmodel + mlp :]
    lane = lax.broadcasted_iota(jnp.int32, (1, half), 1)
    inside = (lane < width).astype(jnp.float32)
    valid = jnp.concatenate([inside, inside], axis=1)
    value = raw[:, :wide]
    gate = sigmoid(raw[:, wide:])
    masks = value * gate * valid
    dm = cot * valid
    dr = jnp.concatenate([dm * gate, dm * value * gate * (1.0 - gate)], axis=1)
    dr_parts = split(dr)
    g_mask = dot_parts(q_parts, dr_parts, ATB)
    dq = dot_parts(dr_parts, mask_parts, ABT)
    da = dq * (1.0 - q * q)
    da_parts = split(da)
    g_wide = dot_parts(da_parts, p, ATB)
    for g in range(outer):
        first, second = slice(2 * g * r, (2 * g + 1) * r), slice((2 * g + 1) * r, (2 * g + 2) * r)
        for ref, got in zip((keep, send), in_turn(core, g_mask[first], g_mask[second])):
            ref[g, :r] = got[:, :wide]
            ref[g, r : 2 * r] = got[:, wide:]
        for ref, got in zip((keep, send), in_turn(core, g_wide[first], g_wide[second])):
            ref[g, 2 * r : piece_rows, :half] = got[: r // 2]
            ref[g, 2 * r : piece_rows, half:] = got[r // 2 :]
        keep[g, piece_rows:] = masks[g * frames : (g + 1) * frames]
    dp = dot_parts(da_parts, wide_parts, AB)
    g_vec[:, :dmodel] = column_sum(dp * unit)
    g_vec[:, dmodel : 2 * dmodel] = column_sum(dp)
    g_vec[:, 2 * dmodel : 2 * dmodel + mlp] = column_sum(da)
    g_vec[:, 2 * dmodel + mlp :] = column_sum(dr)
    return norm_back(dp * gain, unit, scale)


def mask_kernel(base, places, arrived, mine, other, v_band, keep, send, grad, g_vec):
    s = pl.program_id(0)
    parts, streams, unused, quarter, dmodel = arrived.shape
    order = [(q, g) for g in range(streams) for q in range(parts)]
    x = jnp.concatenate([arrived[q, g, 0] for q, g in order], axis=0)
    dx = mask_slot(
        places[1, 0], places[0, s], v_band[pl.ds(places[2, s], 1), base:], x,
        mine.at[:, 0], other.at[:, 0], keep.at[:, 0], send.at[:, 0], g_vec.at[0],
    )
    for k, (q, g) in enumerate(order):
        grad[q, g, 0] = dx[k * quarter : (k + 1) * quarter]


def mask_network(places, arrived, mine, other, v_band, base, piece_rows):
    parts, streams, slots, quarter, dmodel = arrived.shape
    outer, unused, rows, wide = mine.shape

    def second(count):
        return pl.BlockSpec((outer, 1, count, wide), lambda s: (0, s, 0, 0))

    moving = pl.BlockSpec((parts, streams, 1, quarter, dmodel), lambda s: (0, 0, s, 0, 0))
    columns = v_band.shape[1] - base
    vector = pl.BlockSpec((1, 1, columns), lambda s: (s, 0, 0))
    return pl.pallas_call(
        partial(mask_kernel, base),
        grid=(slots,),
        out_shape=[
            f32(mine.shape), f32((outer, slots, piece_rows, wide)), f32(arrived.shape), f32((slots, 1, columns)),
        ],
        in_specs=[SMEM, moving, second(rows), second(rows), VMEM],
        out_specs=[second(rows), second(piece_rows), moving, vector],
        compiler_params=PARAMS,
        cost_estimate=cost(12),
        name="mask_network",
    )(places, arrived, mine, other, v_band)


class Links:
    def __init__(self, bands, layers, send_sems, recv_sems):
        self.bands, self.layers = bands, layers
        self.band, self.stream = lax.axis_index("band"), lax.axis_index("stream")
        self.layer, self.core = lax.div(self.stream, CORES), lax.rem(self.stream, CORES)
        self.other = self.stream + 1 - 2 * self.core
        self.send_sems, self.recv_sems = send_sems, recv_sems
        self.started = []

    def band_to(self, m):
        return lax.rem(self.band + m, self.bands)

    def band_from(self, m):
        return lax.rem(self.band + self.bands - m, self.bands)

    def layer_to(self, k):
        return lax.rem(self.layer + k, self.layers)

    def layer_from(self, k):
        return lax.rem(self.layer + self.layers - k, self.layers)

    def goal(self, k):
        beside = self.layer + 1 - 2 * lax.rem(self.layer, 2)
        return (beside, 3 - self.layer, lax.rem(self.layer + 2, 4), self.layer)[k]

    def own(self, layer):
        return layer * CORES + self.core

    def across(self, layer):
        return layer * CORES + 1 - self.core

    def greet(self, partners):
        barrier = pltpu.get_barrier_semaphore()
        for partner in partners:
            pl.semaphore_signal(barrier, inc=1, device_id=partner, device_id_type=MESH)
        pl.semaphore_wait(barrier, len(partners))

    def copy(self, source, target, index, partner):
        return pltpu.make_async_remote_copy(
            src_ref=source, dst_ref=target, send_sem=self.send_sems.at[index],
            recv_sem=self.recv_sems.at[index], device_id=partner, device_id_type=MESH,
        )

    def send(self, source, target, index, partner):
        copy = self.copy(source, target, index, partner)
        copy.start()
        self.started.append(copy)

    def arrive(self, target, index):
        self.copy(target, target, index, (self.band, self.other)).wait_recv()

    def finish(self):
        for copy in self.started:
            copy.wait_send()


def gather_kernel(
    bands, layers, intake, recurrence, outtake, scalers, splitter, banding, masker, widener, cot,
    rnn_all, split_all, later, pieces,
    vec_rows, own_later, band_rows, cot_here, staged, send_sems, recv_sems, local_sems,
):
    at = Links(bands, layers, send_sems, recv_sems)
    band, stream, other = at.band, at.stream, at.other
    rows_all = rnn_all.shape[1]
    quarter = rows_all // bands
    used = []

    def local(source, target):
        copy = pltpu.make_async_copy(source, target, local_sems.at[len(used)])
        copy.start()
        used.append(copy)
        return copy

    vec_rows[...] = jnp.zeros_like(vec_rows)
    for k in range(2):
        for h in range(0, scalers.shape[1], LANES):
            width = min(LANES, scalers.shape[1] - h)
            vec_rows[k, h // LANES : h // LANES + 1, :width] = scalers[k : k + 1, h : h + width]
    band_rows[...] = jnp.zeros_like(band_rows)
    slots = banding.shape[0]
    for h in range(0, banding.shape[1], LANES):
        width = min(LANES, banding.shape[1] - h)
        base = SLOT_PAD * (h // LANES)
        band_rows[base : base + slots, :width] = banding[:, h : h + width]

    def own_pack(k, target):
        a = intake.shape[1]
        b = a + recurrence.shape[1]
        c = b + outtake.shape[1]
        return [
            local(intake.at[k], target.at[pl.ds(0, a)]),
            local(recurrence.at[k], target.at[pl.ds(a, b - a)]),
            local(outtake.at[k], target.at[pl.ds(b, c - b)]),
            local(vec_rows.at[k], target.at[pl.ds(c, rows_all - c)]),
        ]

    mine, mine_split = rnn_all.at[stream], split_all.at[stream]
    first = own_pack(0, mine)
    split_rows_count = splitter.shape[0]
    second = [
        local(splitter, mine_split.at[pl.ds(0, split_rows_count)]),
        local(band_rows, mine_split.at[pl.ds(split_rows_count, band_rows.shape[0])]),
    ]
    at.greet(
        [(at.band_to(m), stream) for m in range(1, bands)]
        + [(band, at.own(at.layer_to(k))) for k in range(1, layers)]
        + [(band, other)]
    )
    steps = (2, 0, 1)
    turns = range(1, bands)

    def rows(b):
        return pl.ds(b * quarter, quarter)

    to_layer, to_layer_split, to_band = 0, layers, 2 * layers
    to_core = to_band + layers * bands
    to_core_split = to_core + layers * bands
    to_layer_later = to_core_split + layers

    def spread(piece, index):
        for k in (2, 0):
            at.send(piece, piece, index + k, (band, at.own(at.goal(k))))

    def relay(piece, index):
        at.send(piece, piece, index + 1, (band, at.own(at.goal(0))))

    def rnn_piece(k):
        return rnn_all.at[at.own(at.goal(k)), rows(band)]

    def split_piece(k):
        return split_all.at[at.own(at.goal(k))]

    def later_piece(k):
        return later.at[at.goal(k)]

    def hand_on(k):
        piece = rnn_piece(k)
        for m in turns:
            at.send(piece, piece, to_band + k * bands + m, (at.band_to(m), stream))
        at.send(piece, piece, to_core + k * bands, (band, other))

    for copy in first:
        copy.wait()
    spread(rnn_piece(3), to_layer)
    for copy in second:
        copy.wait()
    spread(mine_split, to_layer_split)
    at.send(mine, mine, to_core + 3 * bands, (band, other))
    at.send(mine_split, mine_split, to_core_split + 3, (band, other))
    third = own_pack(1, own_later)
    load_cot = local(cot, cot_here)
    r, wide = masker.shape[1], masker.shape[2] // 2
    half = wide // 2
    base = 2 * r + r // 2
    fill = [
        local(masker.at[:, :, pl.ds(0, wide)], staged.at[:, pl.ds(0, r), :]),
        local(masker.at[:, :, pl.ds(wide, wide)], staged.at[:, pl.ds(r, r), :]),
        local(widener.at[:, pl.ds(0, r // 2), :], staged.at[:, pl.ds(2 * r, r // 2), pl.ds(0, half)]),
        local(widener.at[:, pl.ds(r // 2, r // 2), :], staged.at[:, pl.ds(2 * r, r // 2), pl.ds(half, half)]),
    ]
    at.arrive(rnn_piece(2), to_layer + 2)
    relay(rnn_piece(2), to_layer)
    hand_on(2)
    for copy in third:
        copy.wait()
    later[at.layer] = own_later[rows(band), :]
    spread(later_piece(3), to_layer_later)
    at.arrive(rnn_piece(0), to_layer)
    hand_on(0)
    at.arrive(split_piece(2), to_layer_split + 2)
    relay(split_piece(2), to_layer_split)
    at.send(split_piece(2), split_piece(2), to_core_split + 2, (band, other))
    at.arrive(rnn_piece(1), to_layer + 1)
    hand_on(1)
    at.arrive(later_piece(2), to_layer_later + 2)
    relay(later_piece(2), to_layer_later)
    load_cot.wait()
    for s in range(slots):
        for part in range(2):
            staged[s, base:, part * half : (part + 1) * half] = cot_here[:, s, part, :]
    for copy in fill:
        copy.wait()
    rest = [local(staged, pieces)]
    for k in (0, 1):
        at.arrive(split_piece(k), to_layer_split + k)
        at.send(split_piece(k), split_piece(k), to_core_split + k, (band, other))
    for k in steps:
        for m in turns:
            piece = rnn_all.at[at.own(at.goal(k)), rows(at.band_from(m))]
            at.arrive(piece, to_band + k * bands + m)
            at.send(piece, piece, to_core + k * bands + m, (band, other))
    at.arrive(rnn_all.at[other], to_core + 3 * bands)
    at.arrive(split_all.at[other], to_core_split + 3)
    for k in steps:
        source = at.across(at.goal(k))
        for m in range(bands):
            at.arrive(rnn_all.at[source, rows(at.band_from(m))], to_core + k * bands + m)
        at.arrive(split_all.at[source], to_core_split + k)
    for k in (0, 1):
        at.arrive(later_piece(k), to_layer_later + k)
    at.finish()
    for copy in rest:
        copy.wait()


def gather_front(intake, recurrence, outtake, scalers, splitter, banding, masker, widener, cot, rows, bands, layers):
    count = 4 * layers + 2 * layers * bands
    streams = layers * CORES
    slots = banding.shape[0]
    strips = -(-banding.shape[1] // LANES)
    r, wide = masker.shape[1], masker.shape[2] // 2
    frames = cot.shape[0]
    weight_rows = intake.shape[1] + recurrence.shape[1] + outtake.shape[1]
    split_rows_count = splitter.shape[0] + SLOT_PAD * strips
    return pl.pallas_call(
        partial(gather_kernel, bands, layers),
        out_shape=[
            f32((streams, rows, LANES)), f32((streams, split_rows_count, LANES)), f32((layers, rows // bands, LANES)),
            f32((slots, 2 * r + r // 2 + frames, wide)),
        ],
        in_specs=[ANY, ANY, ANY, VMEM, ANY, VMEM, ANY, ANY, ANY],
        out_specs=[VMEM] * 3 + [ANY],
        scratch_shapes=[
            pltpu.VMEM((2, rows - weight_rows, LANES), jnp.float32),
            pltpu.VMEM((rows, LANES), jnp.float32),
            pltpu.VMEM((SLOT_PAD * strips, LANES), jnp.float32),
            pltpu.VMEM(cot.shape, jnp.float32),
            pltpu.VMEM((slots, 2 * r + r // 2 + frames, wide), jnp.float32),
            pltpu.SemaphoreType.DMA((count,)), pltpu.SemaphoreType.DMA((count,)), pltpu.SemaphoreType.DMA((20,)),
        ],
        compiler_params=pltpu.CompilerParams(
            collective_id=0, has_side_effects=True, vmem_limit_bytes=VMEM_BYTES
        ),
        cost_estimate=cost(30),
        name="gather_front",
    )(intake, recurrence, outtake, scalers, splitter, banding, masker, widener, cot)


def exchange_kernel(bands, layers, source, target, send_sems, recv_sems, local_sem):
    at = Links(bands, layers, send_sems, recv_sems)
    wide = source.shape[1] == layers
    turns = [(m, k) for k in range(layers if wide else 1) for m in range(bands) if m + k]

    def place(ref, band, layer):
        return ref.at[band, layer] if wide else ref.at[band]

    def stream_of(layer):
        return at.own(layer) if wide else at.stream

    at.greet([(at.band_to(m), stream_of(at.layer_to(k))) for m, k in turns])
    for m, k in turns:
        band, layer = at.band_to(m), at.layer_to(k)
        at.send(
            place(source, band, layer), place(target, at.band, at.layer), k * bands + m, (band, stream_of(layer))
        )
    local = pltpu.make_async_copy(
        place(source, at.band, at.layer), place(target, at.band, at.layer), local_sem
    )
    local.start()
    for m, k in turns:
        at.arrive(place(target, at.band_from(m), at.layer_from(k)), k * bands + m)
    at.finish()
    local.wait()


def exchange(x, bands, layers, number):
    count = bands * layers
    return pl.pallas_call(
        partial(exchange_kernel, bands, layers),
        out_shape=f32(x.shape),
        in_specs=[ANY],
        out_specs=ANY,
        scratch_shapes=[
            pltpu.SemaphoreType.DMA((count,)), pltpu.SemaphoreType.DMA((count,)), pltpu.SemaphoreType.DMA,
        ],
        compiler_params=pltpu.CompilerParams(collective_id=number, has_side_effects=True),
        cost_estimate=cost(8),
        name="exchange",
    )(x)


def mask_exchange_kernel(
    base, bands, layers, places, source, mine_in, v_band,
    back, grad_back, g_vec,
    arrived, grad, mine, other, send, received, send_sems, recv_sems, local_sems,
):
    at = Links(bands, layers, send_sems, recv_sems)
    share, outer, piece_rows, wide = other.shape
    quarter = arrived.shape[3]
    partner = (at.band, at.other)
    turns = [(m, k) for k in range(layers) for m in range(bands) if m + k]
    stride = bands * layers
    to_back, to_core, to_core_back = share * stride, 2 * share * stride, 2 * share * stride + share
    at.greet([(at.band_to(m), at.own(at.layer_to(k))) for m, k in turns] + [partner])
    loads = []
    for j in range(share):
        loads.append(
            [
                pltpu.make_async_copy(mine_in.at[:, j], mine.at[j], local_sems.at[2 * j]),
                pltpu.make_async_copy(
                    source.at[at.band, at.layer, j], arrived.at[j, at.band, at.layer], local_sems.at[2 * j + 1]
                ),
            ]
        )
        for copy in loads[-1]:
            copy.start()
    for j in range(share):
        at.send(mine_in.at[:, j, pl.ds(0, piece_rows)], other.at[j], to_core + j, partner)
        for m, k in turns:
            band, layer = at.band_to(m), at.layer_to(k)
            at.send(
                source.at[band, layer, j], arrived.at[j, at.band, at.layer], j * stride + k * bands + m,
                (band, at.own(layer)),
            )
    order = [(q, g) for g in range(layers) for q in range(bands)]
    for j in range(share):
        for copy in loads[j]:
            copy.wait()
        at.arrive(other.at[j], to_core + j)
        for m, k in turns:
            at.arrive(arrived.at[j, at.band_from(m), at.layer_from(k)], j * stride + k * bands + m)
        x = jnp.concatenate([arrived[j, q, g] for q, g in order], axis=0)
        dx = mask_slot(
            at.core, places[0, j], v_band[pl.ds(at.layer * share + j, 1), base:], x,
            mine.at[j], other.at[j], back.at[:, j], send.at[j], g_vec.at[j],
        )
        for i, (q, g) in enumerate(order):
            grad[j, q, g] = dx[i * quarter : (i + 1) * quarter]
        for m, k in turns:
            band, layer = at.band_to(m), at.layer_to(k)
            at.send(
                grad.at[j, band, layer], grad_back.at[at.band, at.layer, j], to_back + j * stride + k * bands + m,
                (band, at.own(layer)),
            )
        at.send(send.at[j], received.at[j], to_core_back + j, partner)
        grad_back[at.band, at.layer, j] = grad[j, at.band, at.layer]
    for j in range(share):
        at.arrive(received.at[j], to_core_back + j)
        for g in range(outer):
            back[g, j, :piece_rows] += received[j, g]
    for j in range(share):
        for m, k in turns:
            at.arrive(grad_back.at[at.band_from(m), at.layer_from(k), j], to_back + j * stride + k * bands + m)
    at.finish()


def mask_exchange(places, source, mine, v_band, base, piece_rows):
    bands, layers, share, quarter, dmodel = source.shape
    outer, unused, rows, wide = mine.shape
    columns = v_band.shape[1] - base
    count = 2 * share * bands * layers + 2 * share

    def vmem(*shape):
        return pltpu.VMEM(shape, jnp.float32)

    return pl.pallas_call(
        partial(mask_exchange_kernel, base, bands, layers),
        out_shape=[f32(mine.shape), f32(source.shape), f32((share, 1, columns))],
        in_specs=[SMEM, ANY, ANY, VMEM],
        out_specs=[VMEM] * 3,
        scratch_shapes=[
            vmem(share, bands, layers, quarter, dmodel),
            vmem(share, bands, layers, quarter, dmodel),
            vmem(share, outer, rows, wide),
            vmem(share, outer, piece_rows, wide),
            vmem(share, outer, piece_rows, wide),
            vmem(share, outer, piece_rows, wide),
            pltpu.SemaphoreType.DMA((count,)),
            pltpu.SemaphoreType.DMA((count,)),
            pltpu.SemaphoreType.DMA((2 * share,)),
        ],
        compiler_params=pltpu.CompilerParams(
            collective_id=2, has_side_effects=True, vmem_limit_bytes=VMEM_BYTES
        ),
        cost_estimate=cost(28),
        name="mask_exchange",
    )(places, source, mine, v_band)


class Grads:
    def __init__(self, pieces, rnn0, rnn1, banded, dims):
        self.pieces, self.rnn, self.banded = pieces, (rnn0, rnn1), banded
        self.slots, self.slot_rows, self.r, self.piece_rows, self.dmodel, self.hidden = dims

    def of_slot(self, s):
        at = pl.ds(pl.multiple_of(s * self.slot_rows, self.slot_rows), self.slot_rows)
        r = self.r
        return [
            (0, (s,), self.banded[at, :]),
            (1, (s,), load_wide_piece(self.pieces[s, 2 * r : self.piece_rows])),
            (2, (s,), load_mask_piece(self.pieces[s, : 2 * r], r)),
        ]

    def rest(self, columns, share):
        found = []
        base = self.slots * self.slot_rows
        strips = []
        for h in range(0, columns, LANES):
            at = base + SLOT_PAD * (h // LANES)
            strips.append(self.banded[at : at + self.slots, : min(LANES, columns - h)])
        found.append((3, (...,), jnp.concatenate(strips, axis=1)))
        unused, out_rows, weight_rows, unused, vec_rows, unused = pack_rows(self.dmodel, self.hidden)
        for k in range(2):
            pack = self.rnn[k]
            at = 0
            for e in range(2):
                found.append((4, (k, e), pack[at : at + self.dmodel]))
                at += self.dmodel
            for e in range(2):
                found.append((5, (k, e), pack[at : at + self.hidden]))
                at += self.hidden
            found.append((6, (k,), pack[at : at + out_rows]))
            at += out_rows
            strips = [
                pack[at + r : at + r + 1, : min(LANES, share - r * LANES)] for r in range(vec_rows)
            ]
            found.append((7, (slice(k, k + 1),), jnp.concatenate(strips, axis=1)))
        return found


DECAYS = (DECAY_RATE,) * 3 + (0.0,) + (DECAY_RATE,) * 3 + (0.0,)


def lamb_moments(gradient, mean_old, power_old, factor):
    clipped = gradient * factor
    mean_new = BETA_ONE * mean_old + (1.0 - BETA_ONE) * clipped
    power_new = BETA_TWO * power_old + (1.0 - BETA_TWO) * clipped * clipped
    return (mean_new, power_new)


def lamb_direction(weight_matrix, mean_new, power_new, decay):
    corrected = mean_new / (1.0 - BETA_ONE**STEP)
    scale_root = jnp.sqrt(power_new / (1.0 - BETA_TWO**STEP)) + ADAM_EPS
    return corrected / scale_root + decay * weight_matrix


def add_up(rows):
    tile = jnp.zeros((16, LANES), jnp.float32)
    line = lax.broadcasted_iota(jnp.int32, (16, LANES), 0)
    for i, row in enumerate(rows):
        tile = jnp.where(line == i, jnp.sum(row, axis=1, keepdims=True), tile)
    return tile


def finish_kernel(bands, layers, dims, g_rnn0, g_split, d_spec, back, *refs):
    g_rnn1, refs = refs[:bands], refs[bands:]
    state, refs = refs[:24], refs[24:]
    out, rnn0, rnn1, banded, spec_out = refs[:5]
    pieces, refs = refs[5], refs[6:]
    held_state, refs = refs[:24], refs[24:]
    (
        own0, own_split, parts1, sum1, from_core, from_core_split, from_core1, from_band, held,
        from_layer, from_layer_split, from_layer1, spec_in, spec_own, near, far, tiles,
        local_sems, send_sems, recv_sems,
    ) = refs
    at = Links(bands, layers, send_sems, recv_sems)
    band, stream, other = at.band, at.stream, at.other
    streams = layers * CORES
    quarter = g_rnn0.shape[1] // bands
    spec_rows = d_spec.shape[0] // bands
    order = range(layers)
    turns = range(1, bands)
    taken = [0]

    def take(count):
        taken[0] += count
        return taken[0] - count

    locals_used = []

    def local(source, target):
        copy = pltpu.make_async_copy(source, target, local_sems.at[len(locals_used)])
        copy.start()
        locals_used.append(copy)
        return copy

    def rows(b):
        return pl.ds(pl.multiple_of(b * quarter, 8), quarter)

    def spec_part(b):
        return pl.ds(pl.multiple_of(b * spec_rows, 8), spec_rows)

    def stream_to(k):
        return lax.rem(stream + k, streams)

    at.greet(
        [(band, stream_to(k)) for k in range(1, streams)] + [(at.band_to(m), stream) for m in turns]
    )
    to_core, to_core_split, to_core1 = take(layers), take(layers), take(layers)
    to_layer, to_layer_split, to_layer1 = take(layers), take(layers), take(layers)
    to_band, to_all0, to_all1 = take(bands * layers), take(bands), take(bands)
    to_spec, to_spec_all = take(bands), take(bands)
    for k in order:
        at.send(g_rnn0.at[at.across(at.goal(k))], from_core.at[k], to_core + k, (band, other))
    for k in order:
        at.send(g_split.at[at.across(at.goal(k))], from_core_split.at[k], to_core_split + k, (band, other))
    load1 = [local(g, parts1.at[k]) for k, g in enumerate(g_rnn1)]
    load0 = [local(g_rnn0.at[at.own(at.goal(k))], own0.at[k]) for k in range(layers)]
    load_split = [local(g_split.at[at.own(at.goal(k))], own_split.at[k]) for k in range(layers)]
    load_spec = local(d_spec.at[spec_part(band)], spec_own)
    load_state = [local(back, pieces)] + [local(a, b) for a, b in zip(state, held_state)]
    for copy in load1:
        copy.wait()

    def block(k, carry):
        total = parts1[0, k]
        for b in range(1, bands):
            total = total + parts1[b, k]
        sum1[k] = total
        return carry

    lax.fori_loop(0, streams, block, 0)
    for k in order:
        at.send(sum1.at[at.across(at.goal(k))], from_core1.at[k], to_core1 + k, (band, other))

    def first_turn(acc, far, index, k):
        if k < 2:
            at.send(acc.at[k], far.at[k], index + k, (band, at.own(at.goal(0))))

    def second_turn(acc, far, index):
        at.arrive(far.at[1], index + 1)
        acc[2] += far[1]
        at.send(acc.at[2], far.at[2], index + 2, (band, at.own(at.goal(2))))

    def own_total(acc, far, index):
        at.arrive(far.at[0], index)
        at.arrive(far.at[2], index + 2)
        return acc[3] + far[0] + far[2]

    for k in order:
        at.arrive(from_core.at[k], to_core + k)
        load0[k].wait()
        from_core[k] += own0[k]
        for m in turns:
            to = at.band_to(m)
            at.send(from_core.at[k, rows(to)], from_band.at[m - 1, k], to_band + m * layers + k, (to, stream))
    for k in order:
        at.arrive(from_core_split.at[k], to_core_split + k)
        load_split[k].wait()
        from_core_split[k] += own_split[k]
        first_turn(from_core_split, from_layer_split, to_layer_split, k)
    for k in order:
        at.arrive(from_core1.at[k], to_core1 + k)
        from_core1[k] += sum1[at.own(at.goal(k))]
        first_turn(from_core1, from_layer1, to_layer1, k)
    second_turn(from_core_split, from_layer_split, to_layer_split)
    second_turn(from_core1, from_layer1, to_layer1)
    for k in order:
        total = from_core[k, rows(band)]
        for m in turns:
            at.arrive(from_band.at[m - 1, k], to_band + m * layers + k)
            total = total + from_band[m - 1, k]
        held[k] = total
        first_turn(held, from_layer, to_layer, k)
    for m in turns:
        to = at.band_to(m)
        at.send(d_spec.at[spec_part(to)], spec_in.at[m - 1], to_spec + m, (to, stream))
    second_turn(held, from_layer, to_layer)

    def gather_quarters(total, target, index):
        target[rows(band)] = total
        for m in turns:
            at.send(target.at[rows(band)], target.at[rows(band)], index + m, (at.band_to(m), stream))

    gather_quarters(own_total(from_core1, from_layer1, to_layer1), rnn1, to_all1)
    banded[...] = own_total(from_core_split, from_layer_split, to_layer_split)
    gather_quarters(own_total(held, from_layer, to_layer), rnn0, to_all0)
    load_spec.wait()
    total = spec_own[...]
    for m in turns:
        at.arrive(spec_in.at[m - 1], to_spec + m)
        total = total + spec_in[m - 1]
    spec_out[spec_part(band)] = total
    for m in turns:
        piece = spec_out.at[spec_part(band)]
        at.send(piece, piece, to_spec_all + m, (at.band_to(m), stream))
    for m in turns:
        at.arrive(rnn1.at[rows(at.band_from(m))], to_all1 + m)
        at.arrive(rnn0.at[rows(at.band_from(m))], to_all0 + m)
    for copy in load_state:
        copy.wait()

    weights, means, powers = held_state[:8], held_state[8:16], held_state[16:]
    grads = Grads(pieces, rnn0, rnn1, banded, dims)
    columns, share = weights[3].shape[1], weights[7].shape[1]
    shares = (1.0,) * 4 + (1.0 / bands,) * 4

    def everywhere(tile, turn):
        to_near, to_far = take(streams), take(bands)
        own, half = tiles.at[turn, 0], tiles.at[turn, 1]
        own[...] = tile
        for k in range(1, streams):
            at.send(own, near.at[turn, k], to_near + k, (band, stream_to(k)))
        total = tile
        for k in range(1, streams):
            at.arrive(near.at[turn, k], to_near + k)
            total = total + near[turn, k]
        half[...] = total
        for m in turns:
            at.send(half, far.at[turn, m], to_far + m, (at.band_to(m), stream))
        for m in turns:
            at.arrive(far.at[turn, m], to_far + m)
            total = total + far[turn, m]
        return total

    def walk(one, count):
        widths = [weights[k].shape[2] for k in range(3)]
        start = tuple(tuple(jnp.zeros((1, w), jnp.float32) for unused in range(count)) for w in widths)

        def slot(s, carry):
            got = []
            for (k, where, g), had in zip(grads.of_slot(s), carry):
                got.append(tuple(a + b for a, b in zip(had, one(k, where, g))))
            return tuple(got)

        total = [list(found) for found in lax.fori_loop(0, dims[0], slot, start)] + [None] * 5
        for k, where, g in grads.rest(columns, share):
            got = one(k, where, g)
            total[k] = list(got) if total[k] is None else [a + b for a, b in zip(total[k], got)]
        return total

    def squares(k, where, g):
        w = weights[k][where]
        return column_sum(g * g), column_sum(w * w)

    first = walk(squares, 2)
    grad_rows = [jnp.sum(t[0], axis=1, keepdims=True) * part for t, part in zip(first, shares)]
    totals = everywhere(add_up([sum(grad_rows)] + [t[1] * part for t, part in zip(first, shares)]), 0)
    grad_norm = jnp.sqrt(totals[0:1])
    factor = jnp.minimum(1.0, CLIP_NORM / grad_norm)[:, 0:1]

    def updates(k, where, g):
        mean, power = lamb_moments(g, means[k][where], powers[k][where], factor)
        direction = lamb_direction(weights[k][where], mean, power, DECAYS[k])
        return (column_sum(direction * direction),)

    second = walk(updates, 1)
    moved = everywhere(add_up([t[0] * part for t, part in zip(second, shares)]), 1)
    out[0:8] = jnp.sqrt(totals[1:9]) / jnp.sqrt(moved[0:8] + 1e-12)
    out[8:9] = jnp.broadcast_to(factor, (1, LANES))
    out[9:10] = grad_norm
    out[10:16] = jnp.zeros((6, LANES), jnp.float32)
    for m in turns:
        at.arrive(spec_out.at[spec_part(at.band_from(m))], to_spec_all + m)
    at.finish()


def finish(g_rnn0, g_split, g_rnn1, d_spec, back, state, bands, layers, dims):
    streams = layers * CORES
    rows, split_count = g_rnn0.shape[1], g_split.shape[1]
    quarter = rows // bands
    spec_shape = (d_spec.shape[0] // bands, d_spec.shape[1])
    count = 6 * layers + bands * layers + 4 * bands + 2 * (streams + bands)
    tile = (16, LANES)

    def vmem(*shape):
        return pltpu.VMEM(shape, jnp.float32)

    return pl.pallas_call(
        partial(finish_kernel, bands, layers, dims),
        out_shape=[
            f32(tile), f32((rows, LANES)), f32((rows, LANES)), f32((split_count, LANES)), f32(d_spec.shape),
        ],
        in_specs=[ANY] * (28 + bands),
        out_specs=[VMEM] * 5,
        scratch_shapes=[vmem(*back.shape)]
        + [vmem(*x.shape) for x in state]
        + [
            vmem(layers, rows, LANES),
            vmem(layers, split_count, LANES),
            vmem(bands, *g_rnn1[0].shape),
            vmem(streams, quarter, LANES),
            vmem(layers, rows, LANES),
            vmem(layers, split_count, LANES),
            vmem(layers, quarter, LANES),
            vmem(bands - 1, layers, quarter, LANES),
            vmem(layers, quarter, LANES),
            vmem(layers - 1, quarter, LANES),
            vmem(layers - 1, split_count, LANES),
            vmem(layers - 1, quarter, LANES),
            vmem(bands - 1, *spec_shape),
            vmem(*spec_shape),
            vmem(2, streams, *tile),
            vmem(2, bands, *tile),
            vmem(2, 2, *tile),
            pltpu.SemaphoreType.DMA((2 * layers + bands + 1 + 25,)),
            pltpu.SemaphoreType.DMA((count,)),
            pltpu.SemaphoreType.DMA((count,)),
        ],
        compiler_params=pltpu.CompilerParams(
            collective_id=5, has_side_effects=True, vmem_limit_bytes=VMEM_BYTES
        ),
        cost_estimate=cost(60),
        name="finish",
    )(g_rnn0, g_split, d_spec, back, *g_rnn1, *state)


CHUNK = 4


def update_kernel(dims, scales, d_spec, pieces_in, rnn0_in, rnn1_in, banded_in, *refs):
    state, refs = refs[:24], refs[24:]
    results, masks_out, spec_out, refs = refs[:24], refs[24], refs[25], refs[26:]
    pieces, rnn0, rnn1, banded, refs = *refs[:4], refs[4:]
    here, refs = refs[:24], refs[24:]
    made, refs = refs[:24], refs[24:]
    masks, load_sems, store_sems = refs
    weights, means, powers = here[:8], here[8:16], here[16:]
    fresh, new_means, new_powers = made[:8], made[8:16], made[16:]
    slots, piece_rows = dims[0], dims[3]
    grads = Grads(pieces, rnn0, rnn1, banded, dims)
    factor = scales[8:9, 0:1]
    used = [0, 0]

    def copy(pair, which):
        sems = (load_sems, store_sems)[which]
        made_copy = pltpu.make_async_copy(*pair, sems.at[used[which]])
        used[which] += 1
        made_copy.start()
        return made_copy

    def arrays(numbers, sources, targets):
        return [(sources[8 * t + k], targets[8 * t + k]) for k in numbers for t in range(3)]

    def cut(pair, c):
        part = pl.ds(c * CHUNK, CHUNK)
        return pair[0].at[part], pair[1].at[part]

    small = [copy(p, 0) for p in [(rnn0_in, rnn0), (rnn1_in, rnn1), (banded_in, banded)] + arrays(range(3, 8), state, here)]
    chunks = [
        [copy(cut(p, c), 0) for p in [(pieces_in, pieces)] + arrays(range(3), state, here)]
        for c in range(slots // CHUNK)
    ]
    half_rows = d_spec.shape[0] // 2
    for part in range(2):
        spec_out[:, part, :] = d_spec[part * half_rows : (part + 1) * half_rows, : spec_out.shape[2]]

    def one(k, where, g):
        w = weights[k][where]
        mean, power = lamb_moments(g, means[k][where], powers[k][where], factor)
        direction = lamb_direction(w, mean, power, DECAYS[k])
        fresh[k][where] = w - LEARN_RATE * scales[k : k + 1, 0:1] * direction
        new_means[k][where] = mean
        new_powers[k][where] = power

    for got in small:
        got.wait()
    for part in grads.rest(weights[3].shape[1], weights[7].shape[1]):
        one(*part)
    stores = [copy(p, 1) for p in arrays(range(3, 8), made, results)]
    half = pieces.shape[2] // 2
    for c in range(slots // CHUNK):
        for got in chunks[c]:
            got.wait()

        def slot(s, carry):
            for part in grads.of_slot(s):
                one(*part)
            return carry

        lax.fori_loop(c * CHUNK, (c + 1) * CHUNK, slot, 0)
        stores += [copy(cut(p, c), 1) for p in arrays(range(3), made, results)]
    for s in range(slots):
        for part in range(2):
            masks[:, s, part, :] = pieces[s, piece_rows:, part * half : (part + 1) * half]
    stores.append(copy((masks, masks_out), 1))
    for sent in stores:
        sent.wait()


def update(scales, d_spec, grads, state, dims, bins):
    slots, rows, wide = grads[0].shape
    frames = rows - dims[3]
    masks_shape = (frames, slots, 2, wide // 2)
    loads = 18 + 10 * (slots // CHUNK)
    stores = 16 + 9 * (slots // CHUNK)
    return pl.pallas_call(
        partial(update_kernel, dims),
        out_shape=[f32(x.shape) for x in state] + [f32(masks_shape), f32((frames, 2, bins))],
        in_specs=[VMEM] * 2 + [ANY] * 28,
        out_specs=[ANY] * 25 + [VMEM],
        scratch_shapes=[pltpu.VMEM(x.shape, jnp.float32) for x in tuple(grads) + tuple(state) * 2]
        + [pltpu.VMEM(masks_shape, jnp.float32)]
        + [pltpu.SemaphoreType.DMA((loads,)), pltpu.SemaphoreType.DMA((stores,))],
        compiler_params=PARAMS,
        cost_estimate=cost(10),
        name="update",
    )(scales, d_spec, *grads, *state)


def groups_of(size, slots):
    outer = math.gcd(size, slots)
    inner = size // outer
    across = [[g * inner + i for g in range(outer)] for i in range(inner)]
    within = [[g * inner + i for i in range(inner)] for g in range(outer)]
    return outer, inner, across, within


def sum_everywhere(values, sizes):
    n = sizes[0] * sizes[1]
    row = jnp.zeros((8, LANES), jnp.float32).at[0, : values.shape[0]].set(values)
    spread = jnp.broadcast_to(row[None], (n, 8, LANES))
    got = lax.all_to_all(spread, ("band", "stream"), 0, 0, tiled=True)
    return jnp.sum(got, axis=0)[0, : values.shape[0]]


def pass_along(x, axis, by):
    size = lax.axis_size(axis)
    return lax.ppermute(x, axis, [(k, (k + by) % size) for k in range(size)])


def swap_cores(x):
    return lax.ppermute(x, "stream", [(s, s ^ 1) for s in range(lax.axis_size("stream"))])


def share_slots(shard, outer, across, within, axis):
    slots = shard.shape[0]
    mine = lax.all_to_all(
        shard.reshape((outer, slots // outer) + shard.shape[1:]), "stream", 0, 0,
        axis_index_groups=across, tiled=True,
    )
    inner = len(within[0])
    if inner == CORES:
        return mine, swap_cores(mine)
    both = lax.all_gather(mine, "stream", axis_index_groups=within)
    both = both.reshape((CORES, inner // CORES) + mine.shape)
    if axis == 1:
        both = both.transpose(0, 2, 3, 1, 4, 5)
        both = both.reshape(both.shape[:3] + (-1, both.shape[5]))
    else:
        both = both.transpose(0, 2, 3, 4, 1, 5)
        both = both.reshape(both.shape[:4] + (-1,))
    return both[0], both[1]


def return_slots(keep, send, outer, inner, across, within, axis):
    if inner == CORES:
        mine = keep + swap_cores(send)
    else:
        both = jnp.stack([keep, send])
        half = inner // CORES
        if axis == 1:
            both = both.reshape(both.shape[:3] + (half, -1, both.shape[4])).transpose(0, 3, 1, 2, 4, 5)
        else:
            both = both.reshape(both.shape[:4] + (half, -1)).transpose(0, 4, 1, 2, 3, 5)
        both = both.reshape((inner,) + both.shape[2:])
        mine = lax.psum_scatter(both, "stream", axis_index_groups=within, tiled=False)
    back = lax.all_to_all(mine, "stream", 0, 0, axis_index_groups=across, tiled=True)
    return back.reshape((-1,) + back.shape[2:])


def pack_split(splitter, banding, blocks):
    slots, wide, dmodel = splitter.shape
    columns = banding.shape[1] // blocks
    strips = -(-columns // LANES)
    main = splitter.reshape(slots, blocks, wide // blocks, dmodel).transpose(1, 0, 2, 3)
    flat = banding.reshape(slots, blocks, columns).transpose(1, 0, 2)
    flat = jnp.pad(flat, ((0, 0), (0, SLOT_PAD - slots), (0, strips * LANES - columns)))
    flat = flat.reshape(blocks, SLOT_PAD, strips, LANES).transpose(0, 2, 1, 3)
    return jnp.concatenate(
        [main.reshape(blocks, slots * wide // blocks, dmodel), flat.reshape(blocks, -1, LANES)], axis=1
    )


def unpack_banding(pack, start, slots, columns):
    blocks = pack.shape[0]
    flat = pack[:, start:].reshape(blocks, -1, SLOT_PAD, LANES)[:, :, :slots].transpose(2, 0, 1, 3)
    return flat.reshape(slots, blocks, -1)[:, :, :columns].reshape(slots, blocks * columns)


def body(spectrum, segments, widths, groups, cotangent, *state):
    weights, means_old, powers_old = state[:8], state[8:16], state[16:]
    splitter, widener, masker, banding, intake, recurrence, outtake, scalers = weights
    group_count = lax.axis_size("band")
    stream_count = lax.axis_size("stream")
    my_stream = lax.axis_index("stream")
    slots = splitter.shape[0]
    frames = spectrum.shape[0]
    quarter = frames // group_count
    outer, inner, across, within = groups_of(stream_count, slots)
    share = slots // outer
    r = masker.shape[1] * stream_count // (2 * outer)
    dmodel = splitter.shape[2]
    hidden = recurrence.shape[2]
    wide = splitter.shape[1] * stream_count
    bins = spectrum.shape[2]
    blocks, out_rows, weight_rows, vec_share, vec_rows, rows = pack_rows(dmodel, hidden)
    slot_rows = wide // blocks
    columns = banding.shape[1] * stream_count // blocks
    direct = stream_count == blocks and inner == CORES and outer == 4 and group_count == 4

    slot_places, clips, slot_of, mask_places = tables(
        segments, widths[None], groups[None], slots, share, inner, group_count, direct
    )
    padded = ((bins - 1) // LANES + 2) * LANES
    spec = jnp.pad(
        spectrum.transpose(1, 0, 2).reshape(2 * frames, bins), ((0, 0), (0, padded - bins))
    )

    if direct:
        rnn0, w_split, later, pieces = gather_front(
            intake.reshape(2, 2 * dmodel, LANES), recurrence.reshape(2, 2 * hidden, LANES), outtake, scalers,
            splitter.reshape(slots * slot_rows, dmodel), banding, masker, widener.transpose(0, 2, 1), cotangent,
            rows, group_count, outer,
        )
        near = [later] + [pass_along(later, "band", m) for m in range(1, group_count)]
        pieces = pieces.reshape((outer, share) + pieces.shape[1:])
        mine = lax.all_to_all(pieces, "stream", 0, 0, axis_index_groups=across, tiled=True)
    else:
        whole = (
            lax.all_gather(intake, "stream", axis=3, tiled=True),
            lax.all_gather(recurrence, "stream", axis=3, tiled=True),
            lax.all_gather(outtake, "stream", axis=1, tiled=True),
            lax.all_gather(scalers, "stream", axis=1, tiled=True),
        )
        rnn0, rnn1 = (
            pack_rnn(whole[0][k], whole[1][k], whole[2][k], whole[3][k : k + 1], rows, vec_share)
            for k in range(2)
        )
        w_split = pack_split(
            lax.all_gather(splitter, "stream", axis=1, tiled=True),
            lax.all_gather(banding, "stream", axis=1, tiled=True),
            blocks,
        )
        w_mask = share_slots(masker, outer, across, within, 1)
        w_wide = share_slots(widener.transpose(0, 2, 1), outer, across, within, 1)
        cot_parts = cotangent.reshape(frames, outer, share, wide).transpose(1, 2, 0, 3)
        cot = lax.all_to_all(cot_parts, "stream", 0, 0, axis_index_groups=across, tiled=True)
        mine, other = (
            jnp.concatenate([pack_pieces(w_mask[k], w_wide[k]), cot], axis=2) for k in range(CORES)
        )
    piece_rows = mine.shape[2] - frames
    def by_band(x, number):
        if direct:
            return exchange(x, group_count, outer, number)
        return lax.all_to_all(x, "band", 0, 0, tiled=True)

    base = 2 * wide + dmodel
    got = time_forward(
        slot_places, clips, spec, w_split, rnn0, group_count, slots, blocks * columns, slot_rows, hidden
    )
    time_out, v_band, time_saved = got[0], got[1], got[2:]
    if direct:
        time_out, near = lax.optimization_barrier((time_out, near))
        rnn1 = near + [swap_cores(x) for x in near]
    else:
        rnn1 = [rnn1]
    arrived = by_band(time_out, 1)
    pack_shape = (blocks, rows, LANES)
    where = jnp.stack([lax.axis_index("band"), my_stream % CORES]).astype(jnp.int32)
    got = band_forward(
        slot_of, where, arrived.reshape(group_count * slots, quarter, dmodel), rnn1, pack_shape, hidden
    )
    band_out, band_saved = got[0], got[1:]
    band_out = band_out.reshape(group_count, outer, share, quarter, dmodel)
    if direct:
        back, grad_back, g_mask_vec = mask_exchange(mask_places, band_out, mine, v_band, base, piece_rows)
        back = lax.all_to_all(back, "stream", 0, 0, axis_index_groups=across, tiled=True)
        back = back.reshape((slots,) + back.shape[2:])
    else:
        band_out = lax.all_to_all(band_out, "stream", 1, 1, axis_index_groups=across, tiled=True)
        band_out = lax.all_to_all(band_out, "band", 0, 0, tiled=True)
        keep, send, grad_back, g_mask_vec = mask_network(
            mask_places, band_out, mine, other, v_band, base, piece_rows
        )
        grad_back = lax.all_to_all(grad_back, "band", 0, 0, tiled=True)
        grad_back = lax.all_to_all(grad_back, "stream", 1, 1, axis_index_groups=across, tiled=True)
        kept, sent = unpack_pieces(keep[:, :, :piece_rows], r), unpack_pieces(send, r)
        mask_reduced = return_slots(kept[0], sent[0], outer, inner, across, within, 1)
        widened_reduced = return_slots(kept[1], sent[1], outer, inner, across, within, 1).transpose(0, 2, 1)
        mask_parts = keep[:, :, piece_rows:]
        mask_parts = lax.all_to_all(mask_parts, "stream", 0, 0, axis_index_groups=across, tiled=True)
    grad_back = grad_back.reshape(group_count * slots, quarter, dmodel)
    band_grad, *g_rnn1 = band_backward(
        slot_of, where, grad_back, rnn1, band_saved, pack_shape, group_count if direct else 1, hidden
    )
    grad_time = by_band(band_grad.reshape(group_count, slots, quarter, dmodel), 4)
    if direct:
        grad_time, g_rnn1 = lax.optimization_barrier((grad_time, g_rnn1))
        g_rnn1 = g_rnn1[:1] + [pass_along(g, "band", m) for m, g in enumerate(g_rnn1) if m]
    d_spec, g_split, g_rnn0 = time_backward(
        slot_places, clips, (my_stream // inner).astype(jnp.int32)[None], grad_time, spec, time_saved, w_split,
        v_band, rnn0, g_mask_vec, slot_rows, hidden,
    )
    if direct:
        dims = (slots, slot_rows, r, piece_rows, dmodel, hidden)
        state = tuple(x.transpose(0, 2, 1) if k % 8 == 1 else x for k, x in enumerate(state))
        scales, g_rnn0, g_rnn1, g_split, d_spec = finish(
            g_rnn0, g_split, g_rnn1, d_spec, back, state, group_count, outer, dims
        )
    else:
        d_spec = lax.psum(d_spec, "band")

    if not direct:
        masks = mask_parts.reshape(slots, frames, wide).transpose(1, 0, 2).reshape(cotangent.shape)
        spectrum_grad = d_spec.reshape(2, frames, padded)[:, :, :bins].transpose(1, 0, 2)

    if direct:
        *stepped, masks, spectrum_grad = update(scales, d_spec, (back, g_rnn0, g_rnn1, g_split), state, dims, bins)
        stepped = [x.transpose(0, 2, 1) if k % 8 == 1 else x for k, x in enumerate(stepped)]
        return (masks, spectrum_grad, scales[9, 0]) + tuple(stepped)
    first, second = unpack_rnn(g_rnn0, dmodel, hidden), unpack_rnn(g_rnn1[0], dmodel, hidden)
    rnn_grads = [jnp.stack([a, b]) for a, b in zip(first[:3], second[:3])]
    rnn_grads.append(jnp.concatenate([first[3], second[3]], axis=0))
    rnn_grads = [
        lax.psum(lax.psum_scatter(g, "stream", scatter_dimension=d, tiled=True), "band")
        for g, d in zip(rnn_grads, (3, 3, 1, 1))
    ]
    g_band = unpack_banding(g_split, slots * slot_rows, slots, columns)
    g_split = g_split[:, : slots * slot_rows].reshape(blocks, slots, slot_rows, dmodel)
    g_split = g_split.transpose(1, 0, 2, 3).reshape(slots, wide, dmodel)
    split_reduced = lax.psum_scatter(g_split, "stream", scatter_dimension=1, tiled=True)
    band_reduced = lax.psum_scatter(g_band, "stream", scatter_dimension=1, tiled=True)
    reduced = (split_reduced, widened_reduced, mask_reduced, band_reduced) + tuple(rnn_grads)

    shares = (1.0,) * 4 + (1.0 / group_count,) * 4
    sizes = (group_count, stream_count)
    sums = [sum(jnp.sum(g * g) * part for g, part in zip(reduced, shares))]
    sums += [jnp.sum(w * w) * part for w, part in zip(weights, shares)]
    totals = sum_everywhere(jnp.stack(sums), sizes)
    grad_norm = jnp.sqrt(totals[0])
    factor = jnp.minimum(1.0, CLIP_NORM / grad_norm)
    moments = [lamb_moments(g, m, p, factor) for g, m, p in zip(reduced, means_old, powers_old)]
    directions = [lamb_direction(w, m, p, d) for w, (m, p), d in zip(weights, moments, DECAYS)]
    update_totals = sum_everywhere(
        jnp.stack([jnp.sum(d * d) * part for d, part in zip(directions, shares)]), sizes
    )
    ratios = jnp.sqrt(totals[1:]) / jnp.sqrt(update_totals + 1e-12)
    fresh = [w - LEARN_RATE * ratios[k] * d for k, (w, d) in enumerate(zip(weights, directions))]
    return (
        (masks, spectrum_grad, grad_norm)
        + tuple(fresh)
        + tuple(m for m, unused in moments)
        + tuple(p for unused, p in moments)
    )


def solution(mesh):
    stored = (
        P("band", "stream", None),
        P("band", None, "stream"),
        P("band", "stream", None),
        P("band", "stream"),
        P(None, None, None, "stream"),
        P(None, None, None, "stream"),
        P(None, "stream", None),
        P(None, "stream"),
    )
    frames_over = P("stream", None, None)
    mask_over = P("stream", "band", None, None)
    return jax.shard_map(
        body,
        mesh=mesh,
        in_specs=(frames_over, P("stream", None), P(), P(), mask_over) + stored * 3,
        out_specs=(mask_over, frames_over, P()) + stored * 3,
        check_vma=False,
    )
```

```python
from functools import partial
import math

import jax
import jax.numpy as jnp
from jax import lax
from jax.experimental import pallas as pl
from jax.experimental.pallas import tpu as pltpu
from jax.sharding import PartitionSpec as P

STEP = 10
CLIP_NORM = 5.0
LEARN_RATE = 0.5
BETA_ONE = 0.9
BETA_TWO = 0.999
ADAM_EPS = 1e-06
DECAY_RATE = 0.01
NORM_EPS = 1e-05
VAR_FLOOR = 0.25
CLIPS = 3
CLIP_MOST = 32
LANES = 128
VMEM_BYTES = 60 * 1024 * 1024
CORES = 2
SLOT_PAD = 16
MESH = pl.DeviceIdType.MESH

AB = (((1,), (0,)), ((), ()))
ABT = (((1,), (1,)), ((), ()))
ATB = (((0,), (0,)), ((), ()))


def split(x):
    hi = x.astype(jnp.bfloat16)
    lo = (x - hi.astype(jnp.float32)).astype(jnp.bfloat16)
    return hi, lo


def dot1(a, b, dims):
    return lax.dot_general(a, b, dims, preferred_element_type=jnp.float32)


def dot_parts(a, b, dims):
    return dot1(a[0], b[0], dims) + (dot1(a[1], b[0], dims) + dot1(a[0], b[1], dims))


def dot3(a, b, dims):
    return dot_parts(split(a), split(b), dims)


def sigmoid(x):
    return 0.5 * jnp.tanh(0.5 * x) + 0.5


def norm_stats(x):
    center = x - jnp.mean(x, axis=-1, keepdims=True)
    spread = jnp.mean(center * center, axis=-1, keepdims=True)
    scale = lax.rsqrt(spread + NORM_EPS)
    return center * scale, scale


def norm_back(grad_unit, unit, scale):
    first = jnp.mean(grad_unit, axis=-1, keepdims=True)
    second = jnp.mean(grad_unit * unit, axis=-1, keepdims=True)
    return scale * (grad_unit - first - unit * second)


def column_sum(x):
    return jnp.sum(x, axis=0, keepdims=True)


def pack_rows(dmodel, hidden):
    blocks = 4 * hidden // LANES
    out_rows = 2 * hidden // blocks
    weight_rows = 2 * dmodel + 2 * hidden + out_rows
    share = (2 * dmodel + 8 * hidden + dmodel) // blocks
    vec_rows = -(-share // LANES)
    return blocks, out_rows, weight_rows, share, vec_rows, -(-(weight_rows + vec_rows) // 32) * 32


def pack_rnn(w_in, w_rec, w_out, vec, rows, share):
    count = w_in.shape[2] // LANES
    parts = [
        w.reshape(2 * w.shape[1], count, LANES).transpose(1, 0, 2) for w in (w_in, w_rec)
    ] + [w_out.reshape(count, -1, LANES)]
    used = sum(p.shape[1] for p in parts)
    flat = jnp.pad(vec.reshape(count, share), ((0, 0), (0, (rows - used) * LANES - share)))
    return jnp.concatenate(parts + [flat.reshape(count, rows - used, LANES)], axis=1)


def unpack_rnn(pack, dmodel, hidden):
    blocks, out_rows, weight_rows, share, vec_rows, rows = pack_rows(dmodel, hidden)
    count = pack.shape[0]
    cuts = (0, 2 * dmodel, 2 * dmodel + 2 * hidden)
    w_in = pack[:, : cuts[1]].reshape(count, 2, dmodel, LANES).transpose(1, 2, 0, 3)
    w_rec = pack[:, cuts[1] : cuts[2]].reshape(count, 2, hidden, LANES).transpose(1, 2, 0, 3)
    return (
        w_in.reshape(2, dmodel, count * LANES),
        w_rec.reshape(2, hidden, count * LANES),
        pack[:, cuts[2] : weight_rows].reshape(count * out_rows, LANES),
        unpack_vec(pack, weight_rows, vec_rows, share),
    )


def unpack_vec(pack, weight_rows, vec_rows, share):
    count = pack.shape[0]
    flat = pack[:, weight_rows : weight_rows + vec_rows].reshape(count, vec_rows * LANES)
    return flat[:, :share].reshape(1, count * share)


class Pack:
    def __init__(self, ref, dmodel, hidden):
        self.ref, self.dmodel, self.hidden = ref, dmodel, hidden
        self.blocks, self.out_rows = pack_rows(dmodel, hidden)[:2]

    def intake(self, e, first, last):
        rows = slice(e * self.dmodel, (e + 1) * self.dmodel)
        return jnp.concatenate([self.ref[k, rows] for k in range(first, last)], axis=1)

    def recurrence(self, e, k):
        base = 2 * self.dmodel + e * self.hidden
        return self.ref[k, base : base + self.hidden]

    def outtake(self, e):
        base = 2 * self.dmodel + 2 * self.hidden
        half = self.blocks // 2
        return jnp.concatenate(
            [self.ref[k, base : base + self.out_rows] for k in range(half * e, half * (e + 1))], axis=0
        )

    def put(self, k, base, value):
        if len(self.ref.shape) == 3:
            self.ref[k, base : base + value.shape[0]] = value
            return
        quarter = self.ref.shape[2]
        done = 0
        while done < value.shape[0]:
            part, at = divmod(base + done, quarter)
            count = min(value.shape[0] - done, quarter - at)
            self.ref[part, k, at : at + count] = value[done : done + count]
            done += count

    def put_intake(self, e, q, value):
        for h in range(value.shape[1] // LANES):
            self.put(q * value.shape[1] // LANES + h, e * self.dmodel, value[:, h * LANES : (h + 1) * LANES])

    def put_recurrence(self, e, q, value):
        base = 2 * self.dmodel + e * self.hidden
        for h in range(value.shape[1] // LANES):
            self.put(q * value.shape[1] // LANES + h, base, value[:, h * LANES : (h + 1) * LANES])

    def put_outtake(self, e, value):
        base = 2 * self.dmodel + 2 * self.hidden
        for k in range(self.blocks // 2):
            self.put(self.blocks // 2 * e + k, base, value[k * self.out_rows : (k + 1) * self.out_rows])

    def put_vec(self, value):
        unused, unused, base, share, vec_rows, rows = pack_rows(self.dmodel, self.hidden)
        for k in range(self.blocks):
            block = [
                value[:, k * share + r * LANES : k * share + min(share, (r + 1) * LANES)] for r in range(vec_rows)
            ]
            block[-1] = jnp.concatenate(
                [block[-1], jnp.zeros((1, vec_rows * LANES - share), jnp.float32)], axis=1
            )
            block.append(jnp.zeros((rows - base - vec_rows, LANES), jnp.float32))
            self.put(k, base, jnp.concatenate(block, axis=0))


def load_vec(pack, vec):
    unused, unused, base, share, vec_rows, unused = pack_rows(pack.dmodel, pack.hidden)
    for k in range(pack.blocks):
        for r in range(vec_rows):
            width = min(LANES, share - r * LANES)
            at = k * share + r * LANES
            vec[0:1, at : at + width] = pack.ref[k, base + r : base + r + 1, :width]


def split_recurrence(pack, hi_ref, lo_ref):
    for e in range(2):
        for k in range(pack.blocks):
            part = slice(k * LANES, (k + 1) * LANES)
            hi_ref[e, :, part], lo_ref[e, :, part] = split(pack.recurrence(e, k))


def split_recurrence_turned(pack, hi_ref, lo_ref):
    for e in range(2):
        for k in range(pack.blocks):
            part = slice(k * LANES, (k + 1) * LANES)
            hi_ref[e, part], lo_ref[e, part] = split(pack.recurrence(e, k).T)


def gates_forward(x_flat, act, pack, vec, rows, block):
    hidden4 = 4 * pack.hidden
    dmodel = pack.dmodel
    parts = [split(pack.intake(e, 0, pack.blocks)) for e in range(2)]

    def one(r, carry):
        start = pl.multiple_of(r * block, block)
        unit, unused = norm_stats(x_flat(start, block))
        n = split(unit * (1.0 + vec[0:1, :dmodel]) + vec[0:1, dmodel : 2 * dmodel])
        for e in range(2):
            bias = vec[0:1, 2 * dmodel + hidden4 * e : 2 * dmodel + hidden4 * (e + 1)]
            z = dot_parts(n, parts[e], AB) + bias
            act[e][pl.ds(r * (block // 16), block // 16)] = z.reshape(block // 16, 16, hidden4)
        return carry

    lax.fori_loop(0, rows // block, one, 0)


def run_forward(steps, places, act, c, h, pack, hi_ref, lo_ref, state, memory):
    hidden = pack.hidden
    for e in range(2):
        state[e][...] = jnp.zeros_like(state[e])
        memory[e][...] = jnp.zeros_like(memory[e])

    def step(j, carry):
        work = []
        for e in range(2):
            at = places(e, j)
            prior = state[e][...]
            hi, lo = split(prior)
            rows = prior.shape[0]
            first = dot1(jnp.concatenate([hi, lo], axis=0), hi_ref[e], AB)
            drive = [act[e][p] for p in at]
            drive = drive[0] if len(drive) == 1 else jnp.concatenate(drive, axis=0)
            z = first[:rows] + first[rows:] + dot1(hi, lo_ref[e], AB) + drive
            work.append((at, z))
        for e in range(2):
            at, z = work[e]
            ingate = sigmoid(z[:, :hidden])
            forget = sigmoid(z[:, hidden : 2 * hidden])
            candidate = jnp.tanh(z[:, 2 * hidden : 3 * hidden])
            outgate = sigmoid(z[:, 3 * hidden :])
            before = memory[e][...]
            now = forget * before + ingate * candidate
            squashed = jnp.tanh(now)
            out = outgate * squashed
            memory[e][...] = now
            state[e][...] = out
            for k, p in enumerate(at):
                part = slice(16 * k, 16 * (k + 1))
                act[e][p, :, :hidden] = ingate[part]
                act[e][p, :, hidden : 2 * hidden] = forget[part]
                act[e][p, :, 2 * hidden : 3 * hidden] = candidate[part]
                act[e][p, :, 3 * hidden :] = outgate[part]
                c[e][p] = now[part]
                h[e][p] = out[part]
        return carry

    lax.fori_loop(0, steps, step, 0, unroll=4)


def output_forward(count, h, pack, vec):
    hidden = h[0].shape[2]
    dmodel = pack.dmodel
    total = vec[0:1, vec.shape[1] - dmodel :]
    for e in range(2):
        states = h[e][:count].reshape(count * 16, hidden)
        total = total + dot3(states, pack.outtake(e), AB)
    return total


def run_backward(steps, places, act, dz_ref, c, dh, pack, hi_ref, lo_ref, grad_h, grad_c):
    hidden = pack.hidden
    split_recurrence_turned(pack, hi_ref, lo_ref)
    for e in range(2):
        grad_h[e][...] = jnp.zeros_like(grad_h[e])
        grad_c[e][...] = jnp.zeros_like(grad_c[e])

    def load(ref, at):
        got = [ref[p] for p in at]
        return got[0] if len(got) == 1 else jnp.concatenate(got, axis=0)

    def step(back, carry):
        j = steps - 1 - back
        later = jnp.minimum(j, 1).astype(jnp.float32)
        work = []
        for e in range(2):
            at = places(e, j)
            gates = load(act[e], at)
            ingate = gates[:, :hidden]
            forget = gates[:, hidden : 2 * hidden]
            candidate = gates[:, 2 * hidden : 3 * hidden]
            outgate = gates[:, 3 * hidden :]
            squashed = jnp.tanh(load(c[e], at))
            before = load(c[e], places(e, jnp.maximum(j - 1, 0))) * later
            total_h = load(dh[e], at) + grad_h[e][...]
            total_c = grad_c[e][...] + total_h * outgate * (1.0 - squashed * squashed)
            dz = jnp.concatenate(
                [
                    total_c * candidate * ingate * (1.0 - ingate),
                    total_c * before * forget * (1.0 - forget),
                    total_c * ingate * (1.0 - candidate * candidate),
                    total_h * squashed * outgate * (1.0 - outgate),
                ],
                axis=1,
            )
            grad_c[e][...] = total_c * forget
            for k, p in enumerate(at):
                dz_ref[e][p] = dz[16 * k : 16 * (k + 1)]
            work.append(dz)
        for e in range(2):
            hi, lo = split(work[e])
            rows = hi.shape[0]
            first = dot1(jnp.concatenate([hi, lo], axis=0), hi_ref[e], AB)
            grad_h[e][...] = first[:rows] + first[rows:] + dot1(hi, lo_ref[e], AB)
        return carry

    lax.fori_loop(0, steps, step, 0, unroll=4)


def states_backward(count, dy_flat, dh, h, pack, g_pack):
    hidden = h[0].shape[2]
    dy = split(dy_flat)
    for e in range(2):
        dh[e][:count] = dot_parts(dy, split(pack.outtake(e)), ABT).reshape(count, 16, hidden)
        g_pack.put_outtake(e, dot3_parts_first(h[e][:count].reshape(count * 16, hidden), dy))


def dot3_parts_first(a, b_parts):
    return dot_parts(split(a), b_parts, ATB)


def gates_backward(count, x_flat, dy_flat, dz_ref, before, pack, vec, g_pack, g_vec):
    dmodel, hidden = pack.dmodel, pack.hidden
    hidden4 = 4 * hidden
    rows = count * 16
    unit, scale = norm_stats(x_flat)
    gain = 1.0 + vec[0:1, :dmodel]
    n = unit * gain + vec[0:1, dmodel : 2 * dmodel]
    dn = jnp.zeros((rows, dmodel), jnp.float32)
    for e in range(2):
        left_hi, left_lo = split(jnp.concatenate([n, before(e)], axis=1).T)
        left = jnp.concatenate([left_hi, left_lo], axis=0)
        height = left_hi.shape[0]
        for q in range(4):
            part = slice(hidden * q, hidden * (q + 1))
            dz_q = dz_ref[e][:count, :, part].reshape(rows, hidden)
            dz = split(dz_q)
            first = dot1(left, dz[0], AB)
            got = first[:height] + first[height:] + dot1(left_hi, dz[1], AB)
            g_pack.put_intake(e, q, got[:dmodel])
            g_pack.put_recurrence(e, q, got[dmodel:])
            dn = dn + dot_parts(dz, split(pack.intake(e, q * pack.blocks // 4, (q + 1) * pack.blocks // 4)), ABT)
            base = 2 * dmodel + hidden4 * e + hidden * q
            g_vec[0:1, base : base + hidden] = column_sum(dz_q)
    g_vec[0:1, :dmodel] = column_sum(dn * unit)
    g_vec[0:1, dmodel : 2 * dmodel] = column_sum(dn)
    g_vec[0:1, vec.shape[1] - dmodel :] = column_sum(dy_flat)
    g_pack.put_vec(g_vec[...])
    return dy_flat + norm_back(dn * gain, unit, scale)


def input_backward(count, x_flat, dy_flat, dz_ref, pack, vec, g_vec):
    dmodel, hidden = pack.dmodel, pack.hidden
    rows = count * 16
    unit, scale = norm_stats(x_flat)
    gain = 1.0 + vec[0:1, :dmodel]
    dn = jnp.zeros((rows, dmodel), jnp.float32)
    for e in range(2):
        for q in range(4):
            part = slice(hidden * q, hidden * (q + 1))
            dz = split(dz_ref[e][:count, :, part].reshape(rows, hidden))
            dn = dn + dot_parts(dz, split(pack.intake(e, q * pack.blocks // 4, (q + 1) * pack.blocks // 4)), ABT)
    g_vec[0:1, :dmodel] = column_sum(dn * unit)
    g_vec[0:1, dmodel : 2 * dmodel] = column_sum(dn)
    g_vec[0:1, vec.shape[1] - dmodel :] = column_sum(dy_flat)
    return dy_flat + norm_back(dn * gain, unit, scale)


def weights_backward(count, x_flat, dz_ref, before, pack, vec, g_pack, g_vec):
    dmodel, hidden = pack.dmodel, pack.hidden
    rows = count * 16
    unit, unused = norm_stats(x_flat)
    n = unit * (1.0 + vec[0:1, :dmodel]) + vec[0:1, dmodel : 2 * dmodel]
    for e in range(2):
        left_hi, left_lo = split(jnp.concatenate([n, before(e)], axis=1).T)
        left = jnp.concatenate([left_hi, left_lo], axis=0)
        height = left_hi.shape[0]
        for q in range(4):
            part = slice(hidden * q, hidden * (q + 1))
            dz_q = dz_ref[e][:count, :, part].reshape(rows, hidden)
            dz = split(dz_q)
            first = dot1(left, dz[0], AB)
            got = first[:height] + first[height:] + dot1(left_hi, dz[1], AB)
            g_pack.put_intake(e, q, got[:dmodel])
            g_pack.put_recurrence(e, q, got[dmodel:])
            base = 2 * dmodel + 4 * hidden * e + hidden * q
            g_vec[0:1, base : base + hidden] = column_sum(dz_q)
    g_pack.put_vec(g_vec[...])


def shifted(ref, e, count, hidden, mask):
    rows = (count - 1) * 16
    zero = jnp.zeros((16, hidden), jnp.float32)
    if e == 0:
        kept = ref[: count - 1].reshape(rows, hidden) * mask
        return jnp.concatenate([zero, kept], axis=0)
    kept = ref[1:count].reshape(rows, hidden) * mask
    return jnp.concatenate([kept, zero], axis=0)


def tables_kernel(
    slots, share, inner, direct, segments, widths, groups, places, clips, slot_of, band_of, mask_places, counts
):
    band, stream = lax.axis_index("band"), lax.axis_index("stream")
    for s in range(slots):
        places[0, s] = 0
        places[1, s] = 0
    for s in range(band_of.shape[1]):
        band_of[0, s] = 0
        band_of[1, s] = 0
    for c in range(CLIPS):
        clips[1, c] = 0
    for g in range(counts.shape[0]):
        counts[g] = 0

    def one_band(b, edge):
        g = groups[0, b]
        rank = counts[g]
        counts[g] = rank + 1
        slot_of[0, b] = g * slots + rank
        band_of[0, g * slots + rank] = b
        band_of[1, g * slots + rank] = 1
        width = widths[0, b]

        @pl.when(g == band)
        def mine():
            places[0, rank] = edge
            places[1, rank] = width

        return edge + width

    lax.fori_loop(0, groups.shape[1], one_band, jnp.int32(0))

    def one_frame(t, carry):
        c = segments[0, t]
        clips[1, c] = clips[1, c] + 1
        return carry

    lax.fori_loop(0, segments.shape[1], one_frame, 0)
    start = jnp.int32(0)
    for c in range(CLIPS):
        clips[0, c] = start
        start = start + clips[1, c]
    for j in range(share):
        row = lax.div(stream, inner) * share + j
        mask_places[0, j] = places[1, row]
        mask_places[1, j] = lax.rem(stream, CORES) if direct else jnp.int32(0)
        mask_places[2, j] = row


def table_shapes(slots, share, bands, parts):
    shapes = ((2, slots), (2, CLIPS), (1, bands), (2, parts * slots), (3, share))
    return [jax.ShapeDtypeStruct(x, jnp.int32) for x in shapes]


def clip_places(clips, spare):
    def places(e, j):
        found = []
        for c in range(CLIPS):
            start, length = clips[0, c], clips[1, c]
            frame = start + j if e == 0 else start + length - 1 - j
            found.append(jnp.where(j < length, frame, spare))
        return found

    return places


def window_of(edge):
    base = pl.multiple_of((edge // LANES) * LANES, LANES)
    return base, lax.rem(edge, LANES)


def split_rows(spec, edge, width, frames):
    wmax = LANES
    base, shift = window_of(edge)
    window = spec[:, pl.ds(base, 2 * LANES)]
    taken = pltpu.roll(window, lax.rem(2 * LANES - shift, 2 * LANES), 1)[:, :wmax]
    taken = jnp.concatenate([taken[:frames], taken[frames:]], axis=1)
    lane = lax.broadcasted_iota(jnp.int32, (frames, wmax), 1)
    inside = (lane < width).astype(jnp.float32)
    valid = jnp.concatenate([inside, inside], axis=1)
    entries = jnp.maximum(2 * width, 1).astype(jnp.float32)
    mean = jnp.sum(taken * valid, axis=-1, keepdims=True) / entries
    center = (taken - mean) * valid
    spread = jnp.sum(center * center, axis=-1, keepdims=True) / entries
    scale = lax.rsqrt(jnp.maximum(spread, VAR_FLOOR))
    moving = jnp.where(spread > VAR_FLOOR, 1.0, jnp.where(spread == VAR_FLOOR, 0.5, 0.0))
    return center * scale, scale, valid, moving, entries


def slot_weights(w_split, s, slot_rows):
    count = w_split.shape[0]
    at = pl.ds(pl.multiple_of(s * slot_rows, slot_rows), slot_rows)
    return jnp.concatenate([w_split[k, at, :] for k in range(count)], axis=0)


def time_forward_kernel(
    slot_rows, share, inner, direct, segments, widths, groups, spec_in, w_split_in, rnn_in,
    places_s, clips, slot_of, band_of, mask_places, out, v_band, x, *refs,
):
    saved, refs = refs[:6], refs[6:]
    act0, act1, c0, c1, h0, h1, hi_ref, lo_ref, s0, s1, m0, m1, y, mixed, vec, rnn, w_split, spec, *refs = refs
    counts, sems = refs
    slots = out.shape[1]
    frames, unused, dmodel = x.shape
    wide = w_split.shape[0] * slot_rows
    pack = Pack(rnn, dmodel, h0.shape[2])
    load_split = pltpu.make_async_copy(w_split_in, w_split, sems.at[7])
    load_spec = pltpu.make_async_copy(spec_in, spec, sems.at[8])
    load_rnn = pltpu.make_async_copy(rnn_in, rnn, sems.at[0])
    for copy in (load_split, load_spec, load_rnn):
        copy.start()
    tables_kernel(
        slots, share, inner, direct, segments, widths, groups, places_s, clips, slot_of, band_of, mask_places, counts
    )
    load_split.wait()
    load_spec.wait()
    v_band[...] = jnp.zeros_like(v_band)
    columns = v_band.shape[1] // w_split.shape[0]
    for k in range(w_split.shape[0]):
        for h in range(0, columns, LANES):
            width = min(LANES, columns - h)
            at = slots * slot_rows + SLOT_PAD * (h // LANES)
            v_band[:, k * columns + h : k * columns + h + width] = w_split[k, at : at + SLOT_PAD, :width]
    x[...] = jnp.zeros_like(x)
    for a in (act0, act1):
        a[frames] = jnp.zeros_like(a[frames])

    for s in range(slots):
        unit, unused, valid, moving, entries = split_rows(spec, places_s[0, s], places_s[1, s], frames)
        row = v_band[s : s + 1, : 2 * wide + dmodel]
        z = (unit * (1.0 + row[:, :wide]) + row[:, wide : 2 * wide]) * valid
        y[s] = dot3(z, slot_weights(w_split, s, slot_rows), AB) + row[:, 2 * wide : 2 * wide + dmodel]
    for s in range(slots):
        x[:, s, :] = y[s]
    load_rnn.wait()
    load_vec(pack, vec)
    split_recurrence(pack, hi_ref, lo_ref)
    act = (act0, act1)

    def x_flat(start, size):
        return x[pl.ds(start // 16, size // 16)].reshape(size, dmodel)

    gates_forward(x_flat, act, pack, vec, frames * 16, 256)
    run_forward(
        CLIP_MOST, clip_places(clips, frames), act, (c0, c1), (h0, h1),
        pack, hi_ref, lo_ref, (s0, s1), (m0, m1),
    )
    leaving = [
        pltpu.make_async_copy(a, b, sems.at[1 + k])
        for k, (a, b) in enumerate(zip((act0, act1, c0, c1, h0, h1), saved))
    ]
    for copy in leaving:
        copy.start()
    total = output_forward(frames, (h0, h1), pack, vec)
    x_all = x[...].reshape(frames * 16, dmodel)
    mixed[...] = (x_all + total).reshape(frames, 16, dmodel)
    parts, unused_slots, quarter, unused = out.shape
    for s in range(slots):
        for q in range(parts):
            out[q, s] = mixed[q * quarter : (q + 1) * quarter, s, :]
    for copy in leaving:
        copy.wait()


def f32(shape):
    return jax.ShapeDtypeStruct(shape, jnp.float32)


def saved_shapes(count, hidden):
    return [f32((count, 16, 4 * hidden))] * 2 + [f32((count, 16, hidden))] * 4


def saved_scratch(count, hidden):
    return [pltpu.VMEM(x.shape, jnp.float32) for x in saved_shapes(count, hidden)]


def vec_scratch(dmodel, hidden):
    return pltpu.VMEM((1, 3 * dmodel + 8 * hidden), jnp.float32)


def rec_scratch(rows, hidden, turned=False):
    return [
        pltpu.VMEM((2, 4 * hidden, hidden) if turned else (2, hidden, 4 * hidden), jnp.bfloat16),
        pltpu.VMEM((2, 4 * hidden, hidden) if turned else (2, hidden, 4 * hidden), jnp.bfloat16),
    ] + [pltpu.VMEM((rows, hidden), jnp.float32)] * 4


SMEM = pl.BlockSpec(memory_space=pltpu.SMEM)
VMEM = pl.BlockSpec(memory_space=pltpu.VMEM)
ANY = pl.BlockSpec(memory_space=pl.ANY)
PARAMS = pltpu.CompilerParams(vmem_limit_bytes=VMEM_BYTES)


def cost(micros):
    return pl.CostEstimate(flops=int(micros * 1.1e9), bytes_accessed=int(micros * 3e6), transcendentals=0)


def time_forward(segments, widths, groups, spec, w_split, rnn, sizes):
    parts, slots, share, inner, direct, band_columns, slot_rows, hidden = sizes
    dmodel = w_split.shape[2]
    frames = spec.shape[0] // 2
    return pl.pallas_call(
        partial(time_forward_kernel, slot_rows, share, inner, direct),
        out_shape=table_shapes(slots, share, widths.shape[1], parts)
        + [
            f32((parts, slots, frames // parts, dmodel)), f32((SLOT_PAD, band_columns)), f32((frames, 16, dmodel)),
        ]
        + saved_shapes(frames + 1, hidden),
        in_specs=[SMEM] * 3 + [ANY] * 3,
        out_specs=[SMEM] * 5 + [VMEM] * 3 + [ANY] * 6,
        scratch_shapes=saved_scratch(frames + 1, hidden)
        + rec_scratch(16 * CLIPS, hidden)
        + [pltpu.VMEM((slots, frames, dmodel), jnp.float32)]
        + [pltpu.VMEM((frames, 16, dmodel), jnp.float32), vec_scratch(dmodel, hidden)]
        + [pltpu.VMEM(a.shape, jnp.float32) for a in (rnn, w_split, spec)]
        + [pltpu.SMEM((parts,), jnp.int32), pltpu.SemaphoreType.DMA((9,))],
        compiler_params=PARAMS,
        cost_estimate=cost(35),
        name="time_forward",
    )(segments, widths, groups, spec, w_split, rnn)


def time_backward_kernel(
    slot_rows, places_s, clips, my_outer, dy_in, spec_in, x_in, *refs,
):
    saved, refs = refs[:6], refs[6:]
    w_split_in, v_band, rnn_in, g_mask_vec, d_spec, g_split, g_rnn, *refs = refs
    act0, act1, c0, c1, h0, h1, *refs = refs
    hi_ref, lo_ref, s0, s1, m0, m1, dy, vec, g_vec, g_band, dh0, dh1, dz0, dz1, *refs = refs
    rnn, w_split, spec, x, sems = refs
    slots = dy_in.shape[1]
    frames, unused, dmodel = x.shape
    hidden = h0.shape[2]
    wide = w_split.shape[0] * slot_rows
    parts, unused_slots, quarter, unused = dy_in.shape
    pack, g_pack = Pack(rnn, dmodel, hidden), Pack(g_rnn, dmodel, hidden)
    pairs = [(rnn_in, rnn), (saved[4], h0), (saved[5], h1)]
    pairs += list(zip(saved[:4], (act0, act1, c0, c1)))
    pairs += [(w_split_in, w_split), (spec_in, spec), (x_in, x)]
    loads = [pltpu.make_async_copy(a, b, sems.at[k]) for k, (a, b) in enumerate(pairs)]
    for copy in loads:
        copy.start()
    dy[...] = jnp.zeros_like(dy)
    for s in range(slots):
        for q in range(parts):
            dy[q * quarter : (q + 1) * quarter, s, :] = dy_in[q, s]
    for copy in loads[:3]:
        copy.wait()
    load_vec(pack, vec)
    dy_flat = dy[...].reshape(frames * 16, dmodel)
    states_backward(frames, dy_flat, (dh0, dh1), (h0, h1), pack, g_pack)
    for d in (dh0, dh1):
        d[frames] = jnp.zeros_like(d[frames])
    for copy in loads[3:7]:
        copy.wait()
    run_backward(
        CLIP_MOST, clip_places(clips, frames), (act0, act1), (dz0, dz1), (c0, c1),
        (dh0, dh1), pack, hi_ref, lo_ref, (s0, s1), (m0, m1),
    )
    for copy in loads[7:]:
        copy.wait()
    frame = lax.broadcasted_iota(jnp.int32, ((frames - 1) * 16, 1), 0) // 16 + 1
    inside = jnp.ones(frame.shape, jnp.float32)
    for k in range(1, CLIPS):
        inside = jnp.where(frame == clips[0, k], 0.0, inside)
    x_flat = x[...].reshape(frames * 16, dmodel)
    dx = gates_backward(
        frames, x_flat, dy[...].reshape(frames * 16, dmodel), (dz0, dz1),
        lambda e: shifted((h0, h1)[e], e, frames, hidden, inside), pack, vec, g_pack, g_vec,
    )
    dy[...] = dx.reshape(frames, 16, dmodel)
    d_spec[...] = jnp.zeros_like(d_spec)
    g_split[:, slots * slot_rows :] = jnp.zeros_like(g_split[:, slots * slot_rows :])
    g_band[...] = jnp.zeros_like(g_band)

    for s in range(slots):
        edge, width = places_s[0, s], places_s[1, s]
        unit, scale, valid, moving, entries = split_rows(spec, edge, width, frames)
        row = v_band[s : s + 1, : 2 * wide + dmodel]
        gain = 1.0 + row[:, :wide]
        z = (unit * gain + row[:, wide : 2 * wide]) * valid
        demb = dy[:, s, :]
        demb_parts = split(demb)
        g_slot = dot_parts(split(z), demb_parts, ATB)
        for k in range(w_split.shape[0]):
            g_split[k, s * slot_rows : (s + 1) * slot_rows] = g_slot[k * slot_rows : (k + 1) * slot_rows]
        dz = dot_parts(demb_parts, split(slot_weights(w_split, s, slot_rows)), ABT) * valid
        g_band[s : s + 1, :wide] = column_sum(dz * unit)
        g_band[s : s + 1, wide : 2 * wide] = column_sum(dz)
        g_band[s : s + 1, 2 * wide : 2 * wide + dmodel] = column_sum(demb)
        du = dz * gain
        first = jnp.sum(du, axis=-1, keepdims=True) / entries
        second = jnp.sum(du * unit, axis=-1, keepdims=True) / entries
        dt = scale * (du - first - moving * unit * second) * valid
        base, shift = window_of(edge)
        stacked = jnp.concatenate([dt[:, :LANES], dt[:, LANES:]], axis=0)
        padded = jnp.concatenate([stacked, jnp.zeros_like(stacked)], axis=1)
        d_spec[:, pl.ds(base, 2 * LANES)] += pltpu.roll(padded, shift, 1)

    share = g_mask_vec.shape[0]
    for j in range(share):
        g_band[pl.ds(my_outer[0] * share + j, 1), 2 * wide + dmodel :] = g_mask_vec[j]
    gathered = g_band[...]
    blocks = w_split.shape[0]
    columns = gathered.shape[1] // blocks
    for k in range(blocks):
        for h in range(0, columns, LANES):
            width = min(LANES, columns - h)
            at = slots * slot_rows + SLOT_PAD * (h // LANES)
            g_split[k, at : at + SLOT_PAD, :width] = gathered[:, k * columns + h : k * columns + h + width]


def time_backward(
    slot_places, clips, my_outer, dy, spec, saved, w_split, v_band, rnn, g_mask_vec, slot_rows, hidden
):
    band_columns = v_band.shape[1]
    dmodel = w_split.shape[2]
    frames = spec.shape[0] // 2
    return pl.pallas_call(
        partial(time_backward_kernel, slot_rows),
        out_shape=[f32(spec.shape), f32(w_split.shape), f32(rnn.shape)],
        in_specs=[SMEM] * 3 + [VMEM] + [ANY] * (2 + 6 + 1) + [VMEM, ANY, VMEM],
        out_specs=[VMEM] * 3,
        scratch_shapes=saved_scratch(frames + 1, hidden)
        + rec_scratch(16 * CLIPS, hidden, True)
        + [pltpu.VMEM((frames, 16, dmodel), jnp.float32)] + [vec_scratch(dmodel, hidden)] * 2
        + [pltpu.VMEM((SLOT_PAD, band_columns), jnp.float32)]
        + [pltpu.VMEM((frames + 1, 16, hidden), jnp.float32)] * 2
        + [pltpu.VMEM((frames + 1, 16, 4 * hidden), jnp.float32)] * 2
        + [pltpu.VMEM(a.shape, jnp.float32) for a in (rnn, w_split, spec, saved[0])]
        + [pltpu.SemaphoreType.DMA((10,))],
        compiler_params=PARAMS,
        cost_estimate=cost(2),
        name="time_backward",
    )(slot_places, clips, my_outer, dy, spec, *saved, w_split, v_band, rnn, g_mask_vec)


def in_turn(core, mine, other):
    return [jnp.where(core == 0, mine, other), jnp.where(core == 0, other, mine)]


def pack_pieces(mask, wide):
    lead, r, w = mask.shape[:2], mask.shape[2], mask.shape[3] // 2
    mask = mask.reshape(lead + (r, 2, w)).transpose(0, 1, 3, 2, 4).reshape(lead + (2 * r, w))
    wide = wide.reshape(lead + (2, r // 2, w // 2)).transpose(0, 1, 3, 2, 4)
    return jnp.concatenate([mask, wide.reshape(lead + (r // 2, w))], axis=2)


def unpack_pieces(pack, r):
    lead, w = pack.shape[:2], pack.shape[3]
    mask = pack[:, :, : 2 * r].reshape(lead + (2, r, w)).transpose(0, 1, 3, 2, 4).reshape(lead + (r, 2 * w))
    wide = pack[:, :, 2 * r :].reshape(lead + (r // 2, 2, w // 2)).transpose(0, 1, 3, 2, 4)
    return mask, wide.reshape(lead + (r, w // 2))


def load_mask_piece(value, r):
    return jnp.concatenate([value[:r], value[r : 2 * r]], axis=1)


def load_wide_piece(value):
    half = value.shape[1] // 2
    return jnp.concatenate([value[:, :half], value[:, half:]], axis=0)


def mask_slot(core, width, v, x, mine, other, keep, send, g_vec):
    outer, total_rows, wide = mine.shape
    piece_rows = send.shape[1]
    frames = total_rows - piece_rows
    dmodel = x.shape[1]
    half = wide // 2
    mlp = (v.shape[1] - 2 * dmodel) - 2 * wide
    r = mlp // (2 * outer)
    w_wide, w_mask = [], []
    for g in range(outer):
        w_mask += in_turn(core, load_mask_piece(mine[g, : 2 * r], r), load_mask_piece(other[g, : 2 * r], r))
        w_wide += in_turn(
            core, load_wide_piece(mine[g, 2 * r : piece_rows]), load_wide_piece(other[g, 2 * r : piece_rows])
        )
    w_wide, w_mask = jnp.concatenate(w_wide, axis=0), jnp.concatenate(w_mask, axis=0)
    cot = jnp.concatenate([mine[g, piece_rows:] for g in range(outer)], axis=0)
    gain = 1.0 + v[:, :dmodel]
    unit, scale = norm_stats(x)
    p = split(unit * gain + v[:, dmodel : 2 * dmodel])
    wide_parts = split(w_wide)
    mask_parts = split(w_mask)
    q = jnp.tanh(dot_parts(p, wide_parts, ABT) + v[:, 2 * dmodel : 2 * dmodel + mlp])
    q_parts = split(q)
    raw = dot_parts(q_parts, mask_parts, AB) + v[:, 2 * dmodel + mlp :]
    lane = lax.broadcasted_iota(jnp.int32, (1, half), 1)
    inside = (lane < width).astype(jnp.float32)
    valid = jnp.concatenate([inside, inside], axis=1)
    value = raw[:, :wide]
    gate = sigmoid(raw[:, wide:])
    masks = value * gate * valid
    dm = cot * valid
    dr = jnp.concatenate([dm * gate, dm * value * gate * (1.0 - gate)], axis=1)
    dr_parts = split(dr)
    g_mask = dot_parts(q_parts, dr_parts, ATB)
    dq = dot_parts(dr_parts, mask_parts, ABT)
    da = dq * (1.0 - q * q)
    da_parts = split(da)
    g_wide = dot_parts(da_parts, p, ATB)
    for g in range(outer):
        first, second = slice(2 * g * r, (2 * g + 1) * r), slice((2 * g + 1) * r, (2 * g + 2) * r)
        for ref, got in zip((keep, send), in_turn(core, g_mask[first], g_mask[second])):
            ref[g, :r] = got[:, :wide]
            ref[g, r : 2 * r] = got[:, wide:]
        for ref, got in zip((keep, send), in_turn(core, g_wide[first], g_wide[second])):
            ref[g, 2 * r : piece_rows, :half] = got[: r // 2]
            ref[g, 2 * r : piece_rows, half:] = got[r // 2 :]
        keep[g, piece_rows:] = masks[g * frames : (g + 1) * frames]
    dp = dot_parts(da_parts, wide_parts, AB)
    g_vec[:, :dmodel] = column_sum(dp * unit)
    g_vec[:, dmodel : 2 * dmodel] = column_sum(dp)
    g_vec[:, 2 * dmodel : 2 * dmodel + mlp] = column_sum(da)
    g_vec[:, 2 * dmodel + mlp :] = column_sum(dr)
    return norm_back(dp * gain, unit, scale)


def mask_kernel(base, places, arrived, mine, other, v_band, keep, send, grad, g_vec):
    s = pl.program_id(0)
    parts, streams, unused, quarter, dmodel = arrived.shape
    order = [(q, g) for g in range(streams) for q in range(parts)]
    x = jnp.concatenate([arrived[q, g, 0] for q, g in order], axis=0)
    dx = mask_slot(
        places[1, 0], places[0, s], v_band[pl.ds(places[2, s], 1), base:], x,
        mine.at[:, 0], other.at[:, 0], keep.at[:, 0], send.at[:, 0], g_vec.at[0],
    )
    for k, (q, g) in enumerate(order):
        grad[q, g, 0] = dx[k * quarter : (k + 1) * quarter]


def mask_network(places, arrived, mine, other, v_band, base, piece_rows):
    parts, streams, slots, quarter, dmodel = arrived.shape
    outer, unused, rows, wide = mine.shape

    def second(count):
        return pl.BlockSpec((outer, 1, count, wide), lambda s: (0, s, 0, 0))

    moving = pl.BlockSpec((parts, streams, 1, quarter, dmodel), lambda s: (0, 0, s, 0, 0))
    columns = v_band.shape[1] - base
    vector = pl.BlockSpec((1, 1, columns), lambda s: (s, 0, 0))
    return pl.pallas_call(
        partial(mask_kernel, base),
        grid=(slots,),
        out_shape=[
            f32(mine.shape), f32((outer, slots, piece_rows, wide)), f32(arrived.shape), f32((slots, 1, columns)),
        ],
        in_specs=[SMEM, moving, second(rows), second(rows), VMEM],
        out_specs=[second(rows), second(piece_rows), moving, vector],
        compiler_params=PARAMS,
        cost_estimate=cost(12),
        name="mask_network",
    )(places, arrived, mine, other, v_band)


class Links:
    def __init__(self, bands, layers, send_sems, recv_sems):
        self.bands, self.layers = bands, layers
        self.band, self.stream = lax.axis_index("band"), lax.axis_index("stream")
        self.layer, self.core = lax.div(self.stream, CORES), lax.rem(self.stream, CORES)
        self.other = self.stream + 1 - 2 * self.core
        self.send_sems, self.recv_sems = send_sems, recv_sems
        self.started = []

    def band_to(self, m):
        return lax.rem(self.band + m, self.bands)

    def band_from(self, m):
        return lax.rem(self.band + self.bands - m, self.bands)

    def layer_to(self, k):
        return lax.rem(self.layer + k, self.layers)

    def layer_from(self, k):
        return lax.rem(self.layer + self.layers - k, self.layers)

    def goal(self, k):
        beside = self.layer + 1 - 2 * lax.rem(self.layer, 2)
        return (beside, 3 - self.layer, lax.rem(self.layer + 2, 4), self.layer)[k]

    def own(self, layer):
        return layer * CORES + self.core

    def across(self, layer):
        return layer * CORES + 1 - self.core

    def greet(self, partners):
        barrier = pltpu.get_barrier_semaphore()
        for partner in partners:
            pl.semaphore_signal(barrier, inc=1, device_id=partner, device_id_type=MESH)
        pl.semaphore_wait(barrier, len(partners))

    def copy(self, source, target, index, partner):
        return pltpu.make_async_remote_copy(
            src_ref=source, dst_ref=target, send_sem=self.send_sems.at[index],
            recv_sem=self.recv_sems.at[index], device_id=partner, device_id_type=MESH,
        )

    def send(self, source, target, index, partner):
        copy = self.copy(source, target, index, partner)
        copy.start()
        self.started.append(copy)

    def arrive(self, target, index):
        self.copy(target, target, index, (self.band, self.other)).wait_recv()

    def finish(self):
        for copy in self.started:
            copy.wait_send()


def gather_kernel(
    bands, layers, intake, recurrence, outtake, scalers, splitter, banding, masker, widener, cot,
    rnn_all, split_all, later, pieces,
    vec_rows, own_later, band_rows, cot_here, staged, send_sems, recv_sems, local_sems,
):
    at = Links(bands, layers, send_sems, recv_sems)
    band, stream, other = at.band, at.stream, at.other
    rows_all = rnn_all.shape[1]
    quarter = rows_all // bands
    used = []

    def local(source, target):
        copy = pltpu.make_async_copy(source, target, local_sems.at[len(used)])
        copy.start()
        used.append(copy)
        return copy

    vec_rows[...] = jnp.zeros_like(vec_rows)
    for k in range(2):
        for h in range(0, scalers.shape[1], LANES):
            width = min(LANES, scalers.shape[1] - h)
            vec_rows[k, h // LANES : h // LANES + 1, :width] = scalers[k : k + 1, h : h + width]
    band_rows[...] = jnp.zeros_like(band_rows)
    slots = banding.shape[0]
    for h in range(0, banding.shape[1], LANES):
        width = min(LANES, banding.shape[1] - h)
        base = SLOT_PAD * (h // LANES)
        band_rows[base : base + slots, :width] = banding[:, h : h + width]

    def own_pack(k, target):
        a = intake.shape[1]
        b = a + recurrence.shape[1]
        c = b + outtake.shape[1]
        return [
            local(intake.at[k], target.at[pl.ds(0, a)]),
            local(recurrence.at[k], target.at[pl.ds(a, b - a)]),
            local(outtake.at[k], target.at[pl.ds(b, c - b)]),
            local(vec_rows.at[k], target.at[pl.ds(c, rows_all - c)]),
        ]

    mine, mine_split = rnn_all.at[stream], split_all.at[stream]
    first = own_pack(0, mine)
    split_rows_count = splitter.shape[0]
    second = [
        local(splitter, mine_split.at[pl.ds(0, split_rows_count)]),
        local(band_rows, mine_split.at[pl.ds(split_rows_count, band_rows.shape[0])]),
    ]
    at.greet(
        [(at.band_to(m), stream) for m in range(1, bands)]
        + [(band, at.own(at.layer_to(k))) for k in range(1, layers)]
        + [(band, other)]
    )
    steps = (2, 0, 1)
    turns = range(1, bands)

    def rows(b):
        return pl.ds(b * quarter, quarter)

    to_layer, to_layer_split, to_band = 0, layers, 2 * layers
    to_core = to_band + layers * bands
    to_core_split = to_core + layers * bands
    to_layer_later = to_core_split + layers

    def spread(piece, index):
        for k in (2, 0):
            at.send(piece, piece, index + k, (band, at.own(at.goal(k))))

    def relay(piece, index):
        at.send(piece, piece, index + 1, (band, at.own(at.goal(0))))

    def rnn_piece(k):
        return rnn_all.at[at.own(at.goal(k)), rows(band)]

    def split_piece(k):
        return split_all.at[at.own(at.goal(k))]

    def later_piece(k):
        return later.at[at.goal(k)]

    def hand_on(k):
        piece = rnn_piece(k)
        for m in turns:
            at.send(piece, piece, to_band + k * bands + m, (at.band_to(m), stream))
        at.send(piece, piece, to_core + k * bands, (band, other))

    for copy in first:
        copy.wait()
    spread(rnn_piece(3), to_layer)
    for copy in second:
        copy.wait()
    spread(mine_split, to_layer_split)
    at.send(mine, mine, to_core + 3 * bands, (band, other))
    at.send(mine_split, mine_split, to_core_split + 3, (band, other))
    third = own_pack(1, own_later)
    load_cot = local(cot, cot_here)
    r, wide = masker.shape[1], masker.shape[2] // 2
    half = wide // 2
    base = 2 * r + r // 2
    fill = [
        local(masker.at[:, :, pl.ds(0, wide)], staged.at[:, pl.ds(0, r), :]),
        local(masker.at[:, :, pl.ds(wide, wide)], staged.at[:, pl.ds(r, r), :]),
        local(widener.at[:, pl.ds(0, r // 2), :], staged.at[:, pl.ds(2 * r, r // 2), pl.ds(0, half)]),
        local(widener.at[:, pl.ds(r // 2, r // 2), :], staged.at[:, pl.ds(2 * r, r // 2), pl.ds(half, half)]),
    ]
    at.arrive(rnn_piece(2), to_layer + 2)
    relay(rnn_piece(2), to_layer)
    hand_on(2)
    for copy in third:
        copy.wait()
    later[at.layer] = own_later[rows(band), :]
    spread(later_piece(3), to_layer_later)
    at.arrive(rnn_piece(0), to_layer)
    hand_on(0)
    at.arrive(split_piece(2), to_layer_split + 2)
    relay(split_piece(2), to_layer_split)
    at.send(split_piece(2), split_piece(2), to_core_split + 2, (band, other))
    at.arrive(rnn_piece(1), to_layer + 1)
    hand_on(1)
    at.arrive(later_piece(2), to_layer_later + 2)
    relay(later_piece(2), to_layer_later)
    load_cot.wait()
    for s in range(slots):
        for part in range(2):
            staged[s, base:, part * half : (part + 1) * half] = cot_here[:, s, part, :]
    for copy in fill:
        copy.wait()
    rest = [local(staged, pieces)]
    for k in (0, 1):
        at.arrive(split_piece(k), to_layer_split + k)
        at.send(split_piece(k), split_piece(k), to_core_split + k, (band, other))
    for k in steps:
        for m in turns:
            piece = rnn_all.at[at.own(at.goal(k)), rows(at.band_from(m))]
            at.arrive(piece, to_band + k * bands + m)
            at.send(piece, piece, to_core + k * bands + m, (band, other))
    at.arrive(rnn_all.at[other], to_core + 3 * bands)
    at.arrive(split_all.at[other], to_core_split + 3)
    for k in steps:
        source = at.across(at.goal(k))
        for m in range(bands):
            at.arrive(rnn_all.at[source, rows(at.band_from(m))], to_core + k * bands + m)
        at.arrive(split_all.at[source], to_core_split + k)
    for k in (0, 1):
        at.arrive(later_piece(k), to_layer_later + k)
    at.finish()
    for copy in rest:
        copy.wait()


def gather_front(intake, recurrence, outtake, scalers, splitter, banding, masker, widener, cot, rows, bands, layers):
    count = 4 * layers + 2 * layers * bands
    streams = layers * CORES
    slots = banding.shape[0]
    strips = -(-banding.shape[1] // LANES)
    r, wide = masker.shape[1], masker.shape[2] // 2
    frames = cot.shape[0]
    weight_rows = intake.shape[1] + recurrence.shape[1] + outtake.shape[1]
    split_rows_count = splitter.shape[0] + SLOT_PAD * strips
    return pl.pallas_call(
        partial(gather_kernel, bands, layers),
        out_shape=[
            f32((streams, rows, LANES)), f32((streams, split_rows_count, LANES)), f32((layers, rows // bands, LANES)),
            f32((slots, 2 * r + r // 2 + frames, wide)),
        ],
        in_specs=[ANY, ANY, ANY, VMEM, ANY, VMEM, ANY, ANY, ANY],
        out_specs=[VMEM] * 3 + [ANY],
        scratch_shapes=[
            pltpu.VMEM((2, rows - weight_rows, LANES), jnp.float32),
            pltpu.VMEM((rows, LANES), jnp.float32),
            pltpu.VMEM((SLOT_PAD * strips, LANES), jnp.float32),
            pltpu.VMEM(cot.shape, jnp.float32),
            pltpu.VMEM((slots, 2 * r + r // 2 + frames, wide), jnp.float32),
            pltpu.SemaphoreType.DMA((count,)), pltpu.SemaphoreType.DMA((count,)), pltpu.SemaphoreType.DMA((20,)),
        ],
        compiler_params=pltpu.CompilerParams(
            collective_id=0, has_side_effects=True, vmem_limit_bytes=VMEM_BYTES
        ),
        cost_estimate=cost(30),
        name="gather_front",
    )(intake, recurrence, outtake, scalers, splitter, banding, masker, widener, cot)


def mask_exchange_kernel(
    base, bands, layers, places, source, mine_in, v_band,
    back, grad_back, g_vec,
    arrived, grad, mine, other, send, received, send_sems, recv_sems, local_sems,
):
    at = Links(bands, layers, send_sems, recv_sems)
    share, outer, piece_rows, wide = other.shape
    quarter = arrived.shape[3]
    partner = (at.band, at.other)
    turns = [(m, k) for k in range(layers) for m in range(bands) if m + k]
    stride = bands * layers
    to_back, to_core, to_core_back = share * stride, 2 * share * stride, 2 * share * stride + share
    at.greet([(at.band_to(m), at.own(at.layer_to(k))) for m, k in turns] + [partner])
    loads = []
    for j in range(share):
        loads.append(
            [
                pltpu.make_async_copy(mine_in.at[:, j], mine.at[j], local_sems.at[2 * j]),
                pltpu.make_async_copy(
                    source.at[at.band, at.layer, j], arrived.at[j, at.band, at.layer], local_sems.at[2 * j + 1]
                ),
            ]
        )
        for copy in loads[-1]:
            copy.start()
    for j in range(share):
        at.send(mine_in.at[:, j, pl.ds(0, piece_rows)], other.at[j], to_core + j, partner)
        for m, k in turns:
            band, layer = at.band_to(m), at.layer_to(k)
            at.send(
                source.at[band, layer, j], arrived.at[j, at.band, at.layer], j * stride + k * bands + m,
                (band, at.own(layer)),
            )
    order = [(q, g) for g in range(layers) for q in range(bands)]
    for j in range(share):
        for copy in loads[j]:
            copy.wait()
        at.arrive(other.at[j], to_core + j)
        for m, k in turns:
            at.arrive(arrived.at[j, at.band_from(m), at.layer_from(k)], j * stride + k * bands + m)
        x = jnp.concatenate([arrived[j, q, g] for q, g in order], axis=0)
        dx = mask_slot(
            at.core, places[0, j], v_band[pl.ds(at.layer * share + j, 1), base:], x,
            mine.at[j], other.at[j], back.at[:, j], send.at[j], g_vec.at[j],
        )
        for i, (q, g) in enumerate(order):
            grad[j, q, g] = dx[i * quarter : (i + 1) * quarter]
        for m, k in turns:
            band, layer = at.band_to(m), at.layer_to(k)
            at.send(
                grad.at[j, band, layer], grad_back.at[at.band, at.layer, j], to_back + j * stride + k * bands + m,
                (band, at.own(layer)),
            )
        at.send(send.at[j], received.at[j], to_core_back + j, partner)
        grad_back[at.band, at.layer, j] = grad[j, at.band, at.layer]
    for j in range(share):
        at.arrive(received.at[j], to_core_back + j)
        for g in range(outer):
            back[g, j, :piece_rows] += received[j, g]
    for j in range(share):
        for m, k in turns:
            at.arrive(grad_back.at[at.band_from(m), at.layer_from(k), j], to_back + j * stride + k * bands + m)
    at.finish()


def mask_exchange(places, source, mine, v_band, base, piece_rows):
    bands, layers, share, quarter, dmodel = source.shape
    outer, unused, rows, wide = mine.shape
    columns = v_band.shape[1] - base
    count = 2 * share * bands * layers + 2 * share

    def vmem(*shape):
        return pltpu.VMEM(shape, jnp.float32)

    return pl.pallas_call(
        partial(mask_exchange_kernel, base, bands, layers),
        out_shape=[f32(mine.shape), f32(source.shape), f32((share, 1, columns))],
        in_specs=[SMEM, ANY, ANY, VMEM],
        out_specs=[VMEM] * 3,
        scratch_shapes=[
            vmem(share, bands, layers, quarter, dmodel),
            vmem(share, bands, layers, quarter, dmodel),
            vmem(share, outer, rows, wide),
            vmem(share, outer, piece_rows, wide),
            vmem(share, outer, piece_rows, wide),
            vmem(share, outer, piece_rows, wide),
            pltpu.SemaphoreType.DMA((count,)),
            pltpu.SemaphoreType.DMA((count,)),
            pltpu.SemaphoreType.DMA((2 * share,)),
        ],
        compiler_params=pltpu.CompilerParams(
            collective_id=2, has_side_effects=True, vmem_limit_bytes=VMEM_BYTES
        ),
        cost_estimate=cost(28),
        name="mask_exchange",
    )(places, source, mine, v_band)


def band_places(bands):
    return lambda e, j: [j if e == 0 else bands - 1 - j]


def load_pack(rnn, pieces, sems):
    if len(pieces) == 1:
        copies = [pltpu.make_async_copy(pieces[0], rnn, sems.at[0])]
    else:
        band, core = lax.axis_index("band"), lax.rem(lax.axis_index("stream"), CORES)
        parts = len(pieces) // CORES
        copies = []
        for k, ref in enumerate(pieces):
            kind, m = divmod(k, parts)
            layers, quarter, unused = ref.shape
            rows = pl.ds(pl.multiple_of(lax.rem(band + parts - m, parts) * quarter, 8), quarter)
            for layer in range(layers):
                target = rnn.at[layer * CORES + lax.rem(core + kind, CORES), rows]
                copies.append(pltpu.make_async_copy(ref.at[layer], target, sems.at[len(copies)]))
    for copy in copies:
        copy.start()
    return copies


def pack_loads(pieces):
    return 1 if len(pieces) == 1 else sum(x.shape[0] for x in pieces)


def to_slots(target, source, band_of):
    for s in range(target.shape[0]):
        target[s] = source[band_of[0, s]] * band_of[1, s].astype(jnp.float32)


def band_forward_kernel(count, parts, slot_of, band_of, arrived_in, *refs):
    pieces, refs = refs[:count], refs[count:]
    out, x, *refs = refs
    saved, refs = refs[:6], refs[6:]
    act0, act1, c0, c1, h0, h1, hi_ref, lo_ref, s0, s1, m0, m1, vec, rnn, arrived, mixed, *refs = refs
    send_sems, recv_sems, pack_sems, sems = refs
    bands, unused, dmodel = x.shape
    pack = Pack(rnn, dmodel, h0.shape[2])
    at, come = swap_bands(parts, arrived_in, arrived, send_sems, recv_sems, sems.at[6])
    for copy in load_pack(rnn, pieces, pack_sems):
        copy.wait()
    load_vec(pack, vec)
    split_recurrence(pack, hi_ref, lo_ref)
    come()

    def fetch(b, carry):
        x[b] = arrived[slot_of[0, b]]
        return carry

    lax.fori_loop(0, bands, fetch, 0)
    act = (act0, act1)

    def x_flat(start, size):
        return x[...].reshape(bands * 16, dmodel)

    gates_forward(x_flat, act, pack, vec, bands * 16, bands * 16)
    run_forward(
        bands, band_places(bands), act, (c0, c1), (h0, h1), pack, hi_ref, lo_ref, (s0, s1), (m0, m1)
    )
    leaving = [
        pltpu.make_async_copy(a, b, sems.at[k])
        for k, (a, b) in enumerate(zip((act0, act1, c0, c1, h0, h1), saved))
    ]
    for copy in leaving:
        copy.start()
    total = output_forward(bands, (h0, h1), pack, vec)
    mixed[...] = (x[...].reshape(bands * 16, dmodel) + total).reshape(bands, 16, dmodel)
    to_slots(out, mixed, band_of)
    at.finish()
    for copy in leaving:
        copy.wait()


def swap_bands(parts, source, target, send_sems, recv_sems, local_sem):
    at = Links(parts, 1, send_sems, recv_sems)
    slots = target.shape[0] // parts
    if parts == 1:
        local = pltpu.make_async_copy(source, target, local_sem)
        local.start()
        return at, local.wait
    at.greet([(at.band_to(m), at.stream) for m in range(1, parts)])

    def part(ref, b):
        return ref.at[pl.ds(b * slots, slots)]

    for m in range(1, parts):
        at.send(part(source, at.band_to(m)), part(target, at.band), m, (at.band_to(m), at.stream))
    local = pltpu.make_async_copy(part(source, at.band), part(target, at.band), local_sem)
    local.start()

    def come():
        for m in range(1, parts):
            at.arrive(part(target, at.band_from(m)), m)
        local.wait()

    return at, come


def swap_scratch(parts):
    return [pltpu.SemaphoreType.DMA((parts,)), pltpu.SemaphoreType.DMA((parts,))]


def remote(parts, number):
    if parts == 1:
        return PARAMS
    return pltpu.CompilerParams(collective_id=number, has_side_effects=True, vmem_limit_bytes=VMEM_BYTES)


def band_forward(slot_of, band_of, arrived, pieces, rnn_shape, parts, hidden):
    bands = slot_of.shape[1]
    dmodel = arrived.shape[2]
    return pl.pallas_call(
        partial(band_forward_kernel, len(pieces), parts),
        out_shape=[f32(arrived.shape), f32((bands, 16, dmodel))] + saved_shapes(bands, hidden),
        in_specs=[SMEM] * 2 + [ANY] * (1 + len(pieces)),
        out_specs=[VMEM] * 2 + [ANY] * 6,
        scratch_shapes=saved_scratch(bands, hidden)
        + rec_scratch(16, hidden)
        + [vec_scratch(dmodel, hidden), pltpu.VMEM(rnn_shape, jnp.float32)]
        + [pltpu.VMEM(arrived.shape, jnp.float32), pltpu.VMEM((bands, 16, dmodel), jnp.float32)]
        + swap_scratch(parts)
        + [pltpu.SemaphoreType.DMA((pack_loads(pieces),)), pltpu.SemaphoreType.DMA((7,))],
        compiler_params=remote(parts, 1),
        cost_estimate=cost(35),
        name="band_forward",
    )(slot_of, band_of, arrived, *pieces)


def band_backward_kernel(count, parts, slot_of, band_of, arrived, *refs):
    pieces, refs = refs[:count], refs[count:]
    x, *refs = refs
    saved, refs = refs[:6], refs[6:]
    out, outs, refs = refs[0], refs[1 : 1 + parts], refs[1 + parts :]
    act0, act1, c0, c1, h0, h1, *refs = refs
    hi_ref, lo_ref, s0, s1, m0, m1, dy, vec, g_vec, dh0, dh1, dz0, dz1, rnn, g_rnn, *refs = refs
    leaving, send_sems, recv_sems, pack_sems, sems = refs
    bands, unused, dmodel = x.shape
    hidden = h0.shape[2]
    pack, g_pack = Pack(rnn, dmodel, hidden), Pack(g_rnn, dmodel, hidden)
    pack_copies = load_pack(rnn, pieces, pack_sems)
    pairs = [(saved[4], h0), (saved[5], h1)] + list(zip(saved[:4], (act0, act1, c0, c1)))
    loads = [pltpu.make_async_copy(a, b, sems.at[k]) for k, (a, b) in enumerate(pairs)]
    for copy in loads:
        copy.start()

    def fetch(b, carry):
        dy[b] = arrived[slot_of[0, b]]
        return carry

    lax.fori_loop(0, bands, fetch, 0)
    for copy in pack_copies:
        copy.wait()
    load_vec(pack, vec)
    for copy in loads[:2]:
        copy.wait()
    states_backward(bands, dy[...].reshape(bands * 16, dmodel), (dh0, dh1), (h0, h1), pack, g_pack)
    for copy in loads[2:]:
        copy.wait()
    run_backward(
        bands, band_places(bands), (act0, act1), (dz0, dz1), (c0, c1), (dh0, dh1),
        pack, hi_ref, lo_ref, (s0, s1), (m0, m1),
    )
    x_all, dy_all = x[...].reshape(bands * 16, dmodel), dy[...].reshape(bands * 16, dmodel)
    dx = input_backward(bands, x_all, dy_all, (dz0, dz1), pack, vec, g_vec)
    dy[...] = dx.reshape(bands, 16, dmodel)
    to_slots(leaving, dy, band_of)
    at, come = swap_bands(parts, leaving, out, send_sems, recv_sems, sems.at[6])
    weights_backward(
        bands, x_all, (dz0, dz1), lambda e: shifted((h0, h1)[e], e, bands, hidden, 1.0), pack, vec, g_pack, g_vec
    )
    if parts == 1:
        outs[0][...] = g_rnn[...]
    else:
        for m in range(parts):
            outs[m][...] = g_rnn[at.band_to(m)]
    come()
    at.finish()


def band_backward(slot_of, band_of, arrived, pieces, saved, rnn_shape, parts, hidden):
    bands = slot_of.shape[1]
    dmodel = arrived.shape[2]
    blocks, rows, unused = rnn_shape
    grad_shape = rnn_shape if parts == 1 else (parts, blocks, rows // parts, LANES)
    return pl.pallas_call(
        partial(band_backward_kernel, len(pieces), parts),
        out_shape=[f32(arrived.shape)] + [f32(grad_shape[-3:])] * parts,
        in_specs=[SMEM] * 2 + [VMEM] + [ANY] * len(pieces) + [VMEM] + [ANY] * 6,
        out_specs=[VMEM] * (1 + parts),
        scratch_shapes=saved_scratch(bands, hidden)
        + rec_scratch(16, hidden, True)
        + [pltpu.VMEM((bands, 16, dmodel), jnp.float32)]
        + [vec_scratch(dmodel, hidden)] * 2
        + [pltpu.VMEM((bands, 16, hidden), jnp.float32)] * 2
        + [pltpu.VMEM((bands, 16, 4 * hidden), jnp.float32)] * 2
        + [pltpu.VMEM(rnn_shape, jnp.float32), pltpu.VMEM(grad_shape, jnp.float32)]
        + [pltpu.VMEM(arrived.shape, jnp.float32)]
        + swap_scratch(parts)
        + [pltpu.SemaphoreType.DMA((pack_loads(pieces),)), pltpu.SemaphoreType.DMA((7,))],
        compiler_params=remote(parts, 3),
        cost_estimate=cost(38),
        name="band_backward",
    )(slot_of, band_of, arrived, *pieces, *saved)


class Grads:
    def __init__(self, pieces, rnn0, rnn1, banded, dims):
        self.pieces, self.rnn, self.banded = pieces, (rnn0, rnn1), banded
        self.slots, self.slot_rows, self.r, self.piece_rows, self.dmodel, self.hidden = dims

    def piece(self, k, s):
        if k == 0:
            at = pl.ds(pl.multiple_of(s * self.slot_rows, self.slot_rows), self.slot_rows)
            return self.banded[at, :]
        if k == 1:
            return load_wide_piece(self.pieces[s, 2 * self.r : self.piece_rows])
        return load_mask_piece(self.pieces[s, : 2 * self.r], self.r)

    def of_slot(self, s):
        return [(k, (s,), self.piece(k, s)) for k in range(3)]

    def banding(self, columns):
        base = self.slots * self.slot_rows
        strips = []
        for h in range(0, columns, LANES):
            at = base + SLOT_PAD * (h // LANES)
            strips.append(self.banded[at : at + self.slots, : min(LANES, columns - h)])
        return jnp.concatenate(strips, axis=1)

    def rest(self, columns, share):
        found = [(3, (...,), self.banding(columns))]
        unused, out_rows, weight_rows, unused, vec_rows, unused = pack_rows(self.dmodel, self.hidden)
        for k in range(2):
            pack = self.rnn[k]
            at = 0
            for e in range(2):
                found.append((4, (k, e), pack[at : at + self.dmodel]))
                at += self.dmodel
            for e in range(2):
                found.append((5, (k, e), pack[at : at + self.hidden]))
                at += self.hidden
            found.append((6, (k,), pack[at : at + out_rows]))
            at += out_rows
            strips = [
                pack[at + r : at + r + 1, : min(LANES, share - r * LANES)] for r in range(vec_rows)
            ]
            found.append((7, (slice(k, k + 1),), jnp.concatenate(strips, axis=1)))
        return found


DECAYS = (DECAY_RATE,) * 3 + (0.0,) + (DECAY_RATE,) * 3 + (0.0,)


def lamb_moments(gradient, mean_old, power_old, factor):
    clipped = gradient * factor
    mean_new = BETA_ONE * mean_old + (1.0 - BETA_ONE) * clipped
    power_new = BETA_TWO * power_old + (1.0 - BETA_TWO) * clipped * clipped
    return (mean_new, power_new)


def lamb_direction(weight_matrix, mean_new, power_new, decay):
    corrected = mean_new / (1.0 - BETA_ONE**STEP)
    scale_root = jnp.sqrt(power_new / (1.0 - BETA_TWO**STEP)) + ADAM_EPS
    return corrected / scale_root + decay * weight_matrix


def add_up(rows):
    tile = jnp.zeros((16, LANES), jnp.float32)
    line = lax.broadcasted_iota(jnp.int32, (16, LANES), 0)
    for i, row in enumerate(rows):
        tile = jnp.where(line == i, jnp.sum(row, axis=1, keepdims=True), tile)
    return tile


def finish_kernel(bands, layers, dims, g_rnn0, g_split, d_spec, back, *refs):
    g_rnn1, refs = refs[:bands], refs[bands:]
    state, refs = refs[:24], refs[24:]
    out, rnn0, rnn1, banded, spec_out = refs[:5]
    pieces, refs = refs[5], refs[6:]
    held_state, packs, refs = refs[:12], refs[12], refs[13:]
    (
        own0, own_split, parts1, sum1, from_core, from_core_split, from_core1, from_band, held,
        from_layer, from_layer_split, from_layer1, spec_in, spec_own, near, far, tiles,
        local_sems, send_sems, recv_sems,
    ) = refs
    at = Links(bands, layers, send_sems, recv_sems)
    band, stream, other = at.band, at.stream, at.other
    streams = layers * CORES
    quarter = g_rnn0.shape[1] // bands
    spec_rows = d_spec.shape[0] // bands
    order = range(layers)
    turns = range(1, bands)
    taken = [0]

    def take(count):
        taken[0] += count
        return taken[0] - count

    locals_used = []

    def local(source, target):
        copy = pltpu.make_async_copy(source, target, local_sems.at[len(locals_used)])
        copy.start()
        locals_used.append(copy)
        return copy

    def rows(b):
        return pl.ds(pl.multiple_of(b * quarter, 8), quarter)

    def spec_part(b):
        return pl.ds(pl.multiple_of(b * spec_rows, 8), spec_rows)

    def stream_to(k):
        return lax.rem(stream + k, streams)

    at.greet(
        [(band, stream_to(k)) for k in range(1, streams)] + [(at.band_to(m), stream) for m in turns]
    )
    to_core, to_core_split, to_core1 = take(layers), take(layers), take(layers)
    to_layer, to_layer_split, to_layer1 = take(layers), take(layers), take(layers)
    to_band, to_all0, to_all1 = take(bands * layers), take(bands), take(bands)
    to_spec, to_spec_all = take(bands), take(bands)
    for k in order:
        at.send(g_rnn0.at[at.across(at.goal(k))], from_core.at[k], to_core + k, (band, other))
    for k in order:
        at.send(g_split.at[at.across(at.goal(k))], from_core_split.at[k], to_core_split + k, (band, other))
    load1 = [local(g, parts1.at[k]) for k, g in enumerate(g_rnn1)]
    load0 = [local(g_rnn0.at[at.own(at.goal(k))], own0.at[k]) for k in range(layers)]
    load_split = [local(g_split.at[at.own(at.goal(k))], own_split.at[k]) for k in range(layers)]
    load_spec = local(d_spec.at[spec_part(band)], spec_own)
    load_state = [local(back, pieces)]
    pack_base = sum(state[k].shape[1] for k in range(4, 7))
    for t in range(3):
        kind = state[8 * t : 8 * t + 8]
        load_state += [local(a, b) for a, b in zip(kind[:4], held_state[4 * t : 4 * t + 4])]
        for k in range(2):
            base = 0
            for a in kind[4:7]:
                load_state.append(local(a.at[k], packs.at[t, k, pl.ds(base, a.shape[1])]))
                base += a.shape[1]
            packs[t, k, base:] = jnp.zeros_like(packs[t, k, base:])
            length = kind[7].shape[1]
            for h in range(0, length, LANES):
                width = min(LANES, length - h)
                row = base + h // LANES
                packs[t, k, row : row + 1, :width] = kind[7][k : k + 1, h : h + width]
    for copy in load1:
        copy.wait()

    def block(k, carry):
        total = parts1[0, k]
        for b in range(1, bands):
            total = total + parts1[b, k]
        sum1[k] = total
        return carry

    lax.fori_loop(0, streams, block, 0)
    for k in order:
        at.send(sum1.at[at.across(at.goal(k))], from_core1.at[k], to_core1 + k, (band, other))

    def first_turn(acc, far, index, k):
        if k < 2:
            at.send(acc.at[k], far.at[k], index + k, (band, at.own(at.goal(0))))

    def second_turn(acc, far, index):
        at.arrive(far.at[1], index + 1)
        acc[2] += far[1]
        at.send(acc.at[2], far.at[2], index + 2, (band, at.own(at.goal(2))))

    def own_total(acc, far, index):
        at.arrive(far.at[0], index)
        at.arrive(far.at[2], index + 2)
        return acc[3] + far[0] + far[2]

    for k in order:
        at.arrive(from_core.at[k], to_core + k)
        load0[k].wait()
        from_core[k] += own0[k]
        for m in turns:
            to = at.band_to(m)
            at.send(from_core.at[k, rows(to)], from_band.at[m - 1, k], to_band + m * layers + k, (to, stream))
    for k in order:
        at.arrive(from_core_split.at[k], to_core_split + k)
        load_split[k].wait()
        from_core_split[k] += own_split[k]
        first_turn(from_core_split, from_layer_split, to_layer_split, k)
    for k in order:
        at.arrive(from_core1.at[k], to_core1 + k)
        from_core1[k] += sum1[at.own(at.goal(k))]
        first_turn(from_core1, from_layer1, to_layer1, k)
    weights, means, powers = held_state[:4], held_state[4:8], held_state[8:]
    grads = Grads(pieces, rnn0, rnn1, banded, dims)
    slots = dims[0]
    for copy in load_state:
        copy.wait()

    def add_squares(pairs, had):
        return tuple(a + column_sum(b * b) for a, b in zip(had, pairs))

    def early_slot(s, had):
        return add_squares(
            [weights[0][s], weights[1][s], weights[2][s], grads.piece(1, s), grads.piece(2, s)], had
        )

    early = lax.fori_loop(
        0, slots, early_slot, tuple(jnp.zeros((1, weights[k].shape[2]), jnp.float32) for k in (0, 1, 2, 1, 2))
    )
    row = lax.broadcasted_iota(jnp.int32, (quarter, LANES), 0) + band * quarter
    edges = [0]
    for a in state[4:7]:
        edges.append(edges[-1] + a.shape[1])

    def by_array(values):
        edge = edges + [bands * quarter]
        return [
            column_sum(jnp.where((row >= edge[i]) & (row < edge[i + 1]), values, 0.0)) for i in range(4)
        ]

    def both_modules(one):
        found = [by_array(one(k, rows(band))) for k in range(2)]
        return [a + b for a, b in zip(*found)]

    weight_rows = list(early[:3]) + [column_sum(weights[3][...] * weights[3][...])]
    weight_rows += both_modules(lambda k, q: packs[0, k, q] * packs[0, k, q])
    second_turn(from_core_split, from_layer_split, to_layer_split)
    second_turn(from_core1, from_layer1, to_layer1)
    for k in order:
        total = from_core[k, rows(band)]
        for m in turns:
            at.arrive(from_band.at[m - 1, k], to_band + m * layers + k)
            total = total + from_band[m - 1, k]
        held[k] = total
        first_turn(held, from_layer, to_layer, k)
    for m in turns:
        to = at.band_to(m)
        at.send(d_spec.at[spec_part(to)], spec_in.at[m - 1], to_spec + m, (to, stream))
    second_turn(held, from_layer, to_layer)

    def gather_quarters(total, target, index):
        target[rows(band)] = total
        for m in turns:
            at.send(target.at[rows(band)], target.at[rows(band)], index + m, (at.band_to(m), stream))

    gather_quarters(own_total(from_core1, from_layer1, to_layer1), rnn1, to_all1)
    banded[...] = own_total(from_core_split, from_layer_split, to_layer_split)
    gather_quarters(own_total(held, from_layer, to_layer), rnn0, to_all0)
    load_spec.wait()
    total = spec_own[...]
    for m in turns:
        at.arrive(spec_in.at[m - 1], to_spec + m)
        total = total + spec_in[m - 1]
    spec_out[spec_part(band)] = total
    for m in turns:
        piece = spec_out.at[spec_part(band)]
        at.send(piece, piece, to_spec_all + m, (at.band_to(m), stream))
    def everywhere(tile, turn):
        to_near, to_far = take(streams), take(bands)
        own, half = tiles.at[turn, 0], tiles.at[turn, 1]
        own[...] = tile
        for k in range(1, streams):
            at.send(own, near.at[turn, k], to_near + k, (band, stream_to(k)))
        total = tile
        for k in range(1, streams):
            at.arrive(near.at[turn, k], to_near + k)
            total = total + near[turn, k]
        half[...] = total
        for m in turns:
            at.send(half, far.at[turn, m], to_far + m, (at.band_to(m), stream))
        for m in turns:
            at.arrive(far.at[turn, m], to_far + m)
            total = total + far[turn, m]
        return total

    main = banded[: slots * dims[1]]
    band_grad = grads.banding(weights[3].shape[1])
    module_rows = both_modules(lambda k, q: (rnn0, rnn1)[k][q] * (rnn0, rnn1)[k][q])
    found = [column_sum(main * main), early[3], early[4], column_sum(band_grad * band_grad)] + module_rows
    grad_total = sum(jnp.sum(x, axis=1, keepdims=True) for x in found)
    totals = everywhere(add_up([grad_total] + weight_rows), 0)
    grad_norm = jnp.sqrt(totals[0:1])
    factor = jnp.minimum(1.0, CLIP_NORM / grad_norm)[:, 0:1]

    def direction(w, mean_old, power_old, g, decay):
        mean, power = lamb_moments(g, mean_old, power_old, factor)
        return lamb_direction(w, mean, power, decay)

    def slot(s, had):
        return add_squares(
            [
                direction(weights[k][s], means[k][s], powers[k][s], grads.piece(k, s), DECAYS[k])
                for k in range(3)
            ],
            had,
        )

    moved_rows = list(
        lax.fori_loop(0, slots, slot, tuple(jnp.zeros((1, weights[k].shape[2]), jnp.float32) for k in range(3)))
    )
    moved = direction(weights[3][...], means[3][...], powers[3][...], band_grad, DECAYS[3])
    moved_rows.append(column_sum(moved * moved))
    decay = jnp.where(row < edges[3], DECAYS[4], DECAYS[7])

    def module(k, q):
        got = direction(packs[0, k, q], packs[1, k, q], packs[2, k, q], (rnn0, rnn1)[k][q], decay)
        return got * got

    moved_rows += both_modules(module)
    moved = everywhere(add_up(moved_rows), 1)
    out[0:8] = jnp.sqrt(totals[1:9]) / jnp.sqrt(moved[0:8] + 1e-12)
    out[8:9] = jnp.broadcast_to(factor, (1, LANES))
    out[9:10] = grad_norm
    out[10:16] = jnp.zeros((6, LANES), jnp.float32)
    for m in turns:
        at.arrive(rnn1.at[rows(at.band_from(m))], to_all1 + m)
        at.arrive(rnn0.at[rows(at.band_from(m))], to_all0 + m)
        at.arrive(spec_out.at[spec_part(at.band_from(m))], to_spec_all + m)
    at.finish()


def finish(g_rnn0, g_split, g_rnn1, d_spec, back, state, bands, layers, dims):
    streams = layers * CORES
    rows, split_count = g_rnn0.shape[1], g_split.shape[1]
    quarter = rows // bands
    spec_shape = (d_spec.shape[0] // bands, d_spec.shape[1])
    count = 6 * layers + bands * layers + 4 * bands + 2 * (streams + bands)
    tile = (16, LANES)

    def vmem(*shape):
        return pltpu.VMEM(shape, jnp.float32)

    return pl.pallas_call(
        partial(finish_kernel, bands, layers, dims),
        out_shape=[
            f32(tile), f32((rows, LANES)), f32((rows, LANES)), f32((split_count, LANES)), f32(d_spec.shape),
        ],
        in_specs=[ANY] * (4 + bands) + ([ANY] * 7 + [VMEM]) * 3,
        out_specs=[VMEM] * 5,
        scratch_shapes=[vmem(*back.shape)]
        + [vmem(*x.shape) for k, x in enumerate(state) if k % 8 < 4]
        + [vmem(3, 2, rows, LANES)]
        + [
            vmem(layers, rows, LANES),
            vmem(layers, split_count, LANES),
            vmem(bands, *g_rnn1[0].shape),
            vmem(streams, quarter, LANES),
            vmem(layers, rows, LANES),
            vmem(layers, split_count, LANES),
            vmem(layers, quarter, LANES),
            vmem(bands - 1, layers, quarter, LANES),
            vmem(layers, quarter, LANES),
            vmem(layers - 1, quarter, LANES),
            vmem(layers - 1, split_count, LANES),
            vmem(layers - 1, quarter, LANES),
            vmem(bands - 1, *spec_shape),
            vmem(*spec_shape),
            vmem(2, streams, *tile),
            vmem(2, bands, *tile),
            vmem(2, 2, *tile),
            pltpu.SemaphoreType.DMA((2 * layers + bands + 2 + 12 + 18,)),
            pltpu.SemaphoreType.DMA((count,)),
            pltpu.SemaphoreType.DMA((count,)),
        ],
        compiler_params=pltpu.CompilerParams(
            collective_id=5, has_side_effects=True, vmem_limit_bytes=VMEM_BYTES
        ),
        cost_estimate=cost(60),
        name="finish",
    )(g_rnn0, g_split, d_spec, back, *g_rnn1, *state)


CHUNK = 4


def update_kernel(dims, scales, d_spec, pieces_in, rnn0_in, rnn1_in, banded_in, *refs):
    state, refs = refs[:24], refs[24:]
    results, masks_out, spec_out, norm_out, refs = refs[:24], refs[24], refs[25], refs[26], refs[27:]
    norm_out[...] = scales[9:10, 0:1]
    pieces, rnn0, rnn1, banded, refs = *refs[:4], refs[4:]
    here, refs = refs[:24], refs[24:]
    made, refs = refs[:24], refs[24:]
    masks, load_sems, store_sems = refs
    weights, means, powers = here[:8], here[8:16], here[16:]
    fresh, new_means, new_powers = made[:8], made[8:16], made[16:]
    slots, piece_rows = dims[0], dims[3]
    grads = Grads(pieces, rnn0, rnn1, banded, dims)
    factor = scales[8:9, 0:1]
    used = [0, 0]

    def copy(pair, which):
        sems = (load_sems, store_sems)[which]
        made_copy = pltpu.make_async_copy(*pair, sems.at[used[which]])
        used[which] += 1
        made_copy.start()
        return made_copy

    def arrays(numbers, sources, targets):
        return [(sources[8 * t + k], targets[8 * t + k]) for k in numbers for t in range(3)]

    def cut(pair, c):
        part = pl.ds(c * CHUNK, CHUNK)
        return pair[0].at[part], pair[1].at[part]

    small = [copy(p, 0) for p in [(rnn0_in, rnn0), (rnn1_in, rnn1), (banded_in, banded)] + arrays(range(3, 8), state, here)]
    chunks = [
        [copy(cut(p, c), 0) for p in [(pieces_in, pieces)] + arrays(range(3), state, here)]
        for c in range(slots // CHUNK)
    ]
    half_rows = d_spec.shape[0] // 2
    for part in range(2):
        spec_out[:, part, :] = d_spec[part * half_rows : (part + 1) * half_rows, : spec_out.shape[2]]

    def one(k, where, g):
        w = weights[k][where]
        mean, power = lamb_moments(g, means[k][where], powers[k][where], factor)
        direction = lamb_direction(w, mean, power, DECAYS[k])
        fresh[k][where] = w - LEARN_RATE * scales[k : k + 1, 0:1] * direction
        new_means[k][where] = mean
        new_powers[k][where] = power

    for got in small:
        got.wait()
    for part in grads.rest(weights[3].shape[1], weights[7].shape[1]):
        one(*part)
    stores = [copy(p, 1) for p in arrays(range(3, 8), made, results)]
    half = pieces.shape[2] // 2
    for c in range(slots // CHUNK):
        for got in chunks[c]:
            got.wait()

        def slot(s, carry):
            for part in grads.of_slot(s):
                one(*part)
            return carry

        lax.fori_loop(c * CHUNK, (c + 1) * CHUNK, slot, 0)
        stores += [copy(cut(p, c), 1) for p in arrays(range(3), made, results)]
    for s in range(slots):
        for part in range(2):
            masks[:, s, part, :] = pieces[s, piece_rows:, part * half : (part + 1) * half]
    stores.append(copy((masks, masks_out), 1))
    for sent in stores:
        sent.wait()


def update(scales, d_spec, grads, state, dims, bins):
    slots, rows, wide = grads[0].shape
    frames = rows - dims[3]
    masks_shape = (frames, slots, 2, wide // 2)
    loads = 18 + 10 * (slots // CHUNK)
    stores = 16 + 9 * (slots // CHUNK)
    return pl.pallas_call(
        partial(update_kernel, dims),
        out_shape=[f32(x.shape) for x in state] + [f32(masks_shape), f32((frames, 2, bins)), f32((1, 1))],
        in_specs=[VMEM] * 2 + [ANY] * 28,
        out_specs=[ANY] * 25 + [VMEM] * 2,
        scratch_shapes=[pltpu.VMEM(x.shape, jnp.float32) for x in tuple(grads) + tuple(state) * 2]
        + [pltpu.VMEM(masks_shape, jnp.float32)]
        + [pltpu.SemaphoreType.DMA((loads,)), pltpu.SemaphoreType.DMA((stores,))],
        compiler_params=PARAMS,
        cost_estimate=cost(10),
        name="update",
    )(scales, d_spec, *grads, *state)


def groups_of(size, slots):
    outer = math.gcd(size, slots)
    inner = size // outer
    across = [[g * inner + i for g in range(outer)] for i in range(inner)]
    within = [[g * inner + i for i in range(inner)] for g in range(outer)]
    return outer, inner, across, within


def sum_everywhere(values, sizes):
    n = sizes[0] * sizes[1]
    row = jnp.zeros((8, LANES), jnp.float32).at[0, : values.shape[0]].set(values)
    spread = jnp.broadcast_to(row[None], (n, 8, LANES))
    got = lax.all_to_all(spread, ("band", "stream"), 0, 0, tiled=True)
    return jnp.sum(got, axis=0)[0, : values.shape[0]]


def pass_along(x, axis, by):
    size = lax.axis_size(axis)
    return lax.ppermute(x, axis, [(k, (k + by) % size) for k in range(size)])


def swap_cores(x):
    return lax.ppermute(x, "stream", [(s, s ^ 1) for s in range(lax.axis_size("stream"))])


def share_slots(shard, outer, across, within, axis):
    slots = shard.shape[0]
    mine = lax.all_to_all(
        shard.reshape((outer, slots // outer) + shard.shape[1:]), "stream", 0, 0,
        axis_index_groups=across, tiled=True,
    )
    inner = len(within[0])
    if inner == CORES:
        return mine, swap_cores(mine)
    both = lax.all_gather(mine, "stream", axis_index_groups=within)
    both = both.reshape((CORES, inner // CORES) + mine.shape)
    if axis == 1:
        both = both.transpose(0, 2, 3, 1, 4, 5)
        both = both.reshape(both.shape[:3] + (-1, both.shape[5]))
    else:
        both = both.transpose(0, 2, 3, 4, 1, 5)
        both = both.reshape(both.shape[:4] + (-1,))
    return both[0], both[1]


def return_slots(keep, send, outer, inner, across, within, axis):
    if inner == CORES:
        mine = keep + swap_cores(send)
    else:
        both = jnp.stack([keep, send])
        half = inner // CORES
        if axis == 1:
            both = both.reshape(both.shape[:3] + (half, -1, both.shape[4])).transpose(0, 3, 1, 2, 4, 5)
        else:
            both = both.reshape(both.shape[:4] + (half, -1)).transpose(0, 4, 1, 2, 3, 5)
        both = both.reshape((inner,) + both.shape[2:])
        mine = lax.psum_scatter(both, "stream", axis_index_groups=within, tiled=False)
    back = lax.all_to_all(mine, "stream", 0, 0, axis_index_groups=across, tiled=True)
    return back.reshape((-1,) + back.shape[2:])


def pack_split(splitter, banding, blocks):
    slots, wide, dmodel = splitter.shape
    columns = banding.shape[1] // blocks
    strips = -(-columns // LANES)
    main = splitter.reshape(slots, blocks, wide // blocks, dmodel).transpose(1, 0, 2, 3)
    flat = banding.reshape(slots, blocks, columns).transpose(1, 0, 2)
    flat = jnp.pad(flat, ((0, 0), (0, SLOT_PAD - slots), (0, strips * LANES - columns)))
    flat = flat.reshape(blocks, SLOT_PAD, strips, LANES).transpose(0, 2, 1, 3)
    return jnp.concatenate(
        [main.reshape(blocks, slots * wide // blocks, dmodel), flat.reshape(blocks, -1, LANES)], axis=1
    )


def unpack_banding(pack, start, slots, columns):
    blocks = pack.shape[0]
    flat = pack[:, start:].reshape(blocks, -1, SLOT_PAD, LANES)[:, :, :slots].transpose(2, 0, 1, 3)
    return flat.reshape(slots, blocks, -1)[:, :, :columns].reshape(slots, blocks * columns)


def body(spectrum, segments, widths, groups, cotangent, *state):
    weights, means_old, powers_old = state[:8], state[8:16], state[16:]
    splitter, widener, masker, banding, intake, recurrence, outtake, scalers = weights
    group_count = lax.axis_size("band")
    stream_count = lax.axis_size("stream")
    my_stream = lax.axis_index("stream")
    slots = splitter.shape[0]
    frames = spectrum.shape[0]
    quarter = frames // group_count
    outer, inner, across, within = groups_of(stream_count, slots)
    share = slots // outer
    r = masker.shape[1] * stream_count // (2 * outer)
    dmodel = splitter.shape[2]
    hidden = recurrence.shape[2]
    wide = splitter.shape[1] * stream_count
    bins = spectrum.shape[2]
    blocks, out_rows, weight_rows, vec_share, vec_rows, rows = pack_rows(dmodel, hidden)
    slot_rows = wide // blocks
    columns = banding.shape[1] * stream_count // blocks
    direct = stream_count == blocks and inner == CORES and outer == 4 and group_count == 4

    padded = ((bins - 1) // LANES + 2) * LANES
    spec = jnp.pad(
        spectrum.transpose(1, 0, 2).reshape(2 * frames, bins), ((0, 0), (0, padded - bins))
    )

    if direct:
        rnn0, w_split, later, pieces = gather_front(
            intake.reshape(2, 2 * dmodel, LANES), recurrence.reshape(2, 2 * hidden, LANES), outtake, scalers,
            splitter.reshape(slots * slot_rows, dmodel), banding, masker, widener.transpose(0, 2, 1), cotangent,
            rows, group_count, outer,
        )
        near = [later] + [pass_along(later, "band", m) for m in range(1, group_count)]
        pieces = pieces.reshape((outer, share) + pieces.shape[1:])
        mine = lax.all_to_all(pieces, "stream", 0, 0, axis_index_groups=across, tiled=True)
    else:
        whole = (
            lax.all_gather(intake, "stream", axis=3, tiled=True),
            lax.all_gather(recurrence, "stream", axis=3, tiled=True),
            lax.all_gather(outtake, "stream", axis=1, tiled=True),
            lax.all_gather(scalers, "stream", axis=1, tiled=True),
        )
        rnn0, rnn1 = (
            pack_rnn(whole[0][k], whole[1][k], whole[2][k], whole[3][k : k + 1], rows, vec_share)
            for k in range(2)
        )
        w_split = pack_split(
            lax.all_gather(splitter, "stream", axis=1, tiled=True),
            lax.all_gather(banding, "stream", axis=1, tiled=True),
            blocks,
        )
        w_mask = share_slots(masker, outer, across, within, 1)
        w_wide = share_slots(widener.transpose(0, 2, 1), outer, across, within, 1)
        cot_parts = cotangent.reshape(frames, outer, share, wide).transpose(1, 2, 0, 3)
        cot = lax.all_to_all(cot_parts, "stream", 0, 0, axis_index_groups=across, tiled=True)
        mine, other = (
            jnp.concatenate([pack_pieces(w_mask[k], w_wide[k]), cot], axis=2) for k in range(CORES)
        )
    piece_rows = mine.shape[2] - frames
    base = 2 * wide + dmodel
    sizes = (group_count, slots, share, inner, direct, blocks * columns, slot_rows, hidden)
    got = time_forward(segments, widths[None], groups[None], spec, w_split, rnn0, sizes)
    slot_places, clips, slot_of, band_of, mask_places = got[:5]
    time_out, v_band, time_saved = got[5], got[6], got[7:]
    parts = group_count if direct else 1
    if direct:
        time_out, near = lax.optimization_barrier((time_out, near))
        rnn1 = near + [swap_cores(x) for x in near]
    else:
        rnn1 = [rnn1]
        time_out = lax.all_to_all(time_out, "band", 0, 0, tiled=True)
    pack_shape = (blocks, rows, LANES)
    got = band_forward(
        slot_of, band_of, time_out.reshape(group_count * slots, quarter, dmodel), rnn1, pack_shape, parts, hidden
    )
    band_out, band_saved = got[0], got[1:]
    band_out = band_out.reshape(group_count, outer, share, quarter, dmodel)
    if direct:
        back, grad_back, g_mask_vec = mask_exchange(mask_places, band_out, mine, v_band, base, piece_rows)
        back = lax.all_to_all(back, "stream", 0, 0, axis_index_groups=across, tiled=True)
        back = back.reshape((slots,) + back.shape[2:])
    else:
        band_out = lax.all_to_all(band_out, "stream", 1, 1, axis_index_groups=across, tiled=True)
        band_out = lax.all_to_all(band_out, "band", 0, 0, tiled=True)
        keep, send, grad_back, g_mask_vec = mask_network(
            mask_places, band_out, mine, other, v_band, base, piece_rows
        )
        grad_back = lax.all_to_all(grad_back, "band", 0, 0, tiled=True)
        grad_back = lax.all_to_all(grad_back, "stream", 1, 1, axis_index_groups=across, tiled=True)
        kept, sent = unpack_pieces(keep[:, :, :piece_rows], r), unpack_pieces(send, r)
        mask_reduced = return_slots(kept[0], sent[0], outer, inner, across, within, 1)
        widened_reduced = return_slots(kept[1], sent[1], outer, inner, across, within, 1).transpose(0, 2, 1)
        mask_parts = keep[:, :, piece_rows:]
        mask_parts = lax.all_to_all(mask_parts, "stream", 0, 0, axis_index_groups=across, tiled=True)
    grad_back = grad_back.reshape(group_count * slots, quarter, dmodel)
    band_grad, *g_rnn1 = band_backward(
        slot_of, band_of, grad_back, rnn1, band_saved, pack_shape, parts, hidden
    )
    grad_time = band_grad.reshape(group_count, slots, quarter, dmodel)
    if not direct:
        grad_time = lax.all_to_all(grad_time, "band", 0, 0, tiled=True)
    if direct:
        g_rnn1 = g_rnn1[:1] + [pass_along(g, "band", m) for m, g in enumerate(g_rnn1) if m]
    d_spec, g_split, g_rnn0 = time_backward(
        slot_places, clips, (my_stream // inner).astype(jnp.int32)[None], grad_time, spec, time_saved, w_split,
        v_band, rnn0, g_mask_vec, slot_rows, hidden,
    )
    if direct:
        dims = (slots, slot_rows, r, piece_rows, dmodel, hidden)
        state = tuple(x.transpose(0, 2, 1) if k % 8 == 1 else x for k, x in enumerate(state))
        scales, g_rnn0, g_rnn1, g_split, d_spec = finish(
            g_rnn0, g_split, g_rnn1, d_spec, back,
            tuple(x.reshape(2, -1, LANES) if k % 8 in (4, 5) else x for k, x in enumerate(state)),
            group_count, outer, dims,
        )
    else:
        d_spec = lax.psum(d_spec, "band")

    if not direct:
        masks = mask_parts.reshape(slots, frames, wide).transpose(1, 0, 2).reshape(cotangent.shape)
        spectrum_grad = d_spec.reshape(2, frames, padded)[:, :, :bins].transpose(1, 0, 2)

    if direct:
        *stepped, masks, spectrum_grad, grad_norm = update(scales, d_spec, (back, g_rnn0, g_rnn1, g_split), state, dims, bins)
        stepped = [x.transpose(0, 2, 1) if k % 8 == 1 else x for k, x in enumerate(stepped)]
        return (masks, spectrum_grad, grad_norm.reshape(())) + tuple(stepped)
    first, second = unpack_rnn(g_rnn0, dmodel, hidden), unpack_rnn(g_rnn1[0], dmodel, hidden)
    rnn_grads = [jnp.stack([a, b]) for a, b in zip(first[:3], second[:3])]
    rnn_grads.append(jnp.concatenate([first[3], second[3]], axis=0))
    rnn_grads = [
        lax.psum(lax.psum_scatter(g, "stream", scatter_dimension=d, tiled=True), "band")
        for g, d in zip(rnn_grads, (3, 3, 1, 1))
    ]
    g_band = unpack_banding(g_split, slots * slot_rows, slots, columns)
    g_split = g_split[:, : slots * slot_rows].reshape(blocks, slots, slot_rows, dmodel)
    g_split = g_split.transpose(1, 0, 2, 3).reshape(slots, wide, dmodel)
    split_reduced = lax.psum_scatter(g_split, "stream", scatter_dimension=1, tiled=True)
    band_reduced = lax.psum_scatter(g_band, "stream", scatter_dimension=1, tiled=True)
    reduced = (split_reduced, widened_reduced, mask_reduced, band_reduced) + tuple(rnn_grads)

    shares = (1.0,) * 4 + (1.0 / group_count,) * 4
    sizes = (group_count, stream_count)
    sums = [sum(jnp.sum(g * g) * part for g, part in zip(reduced, shares))]
    sums += [jnp.sum(w * w) * part for w, part in zip(weights, shares)]
    totals = sum_everywhere(jnp.stack(sums), sizes)
    grad_norm = jnp.sqrt(totals[0])
    factor = jnp.minimum(1.0, CLIP_NORM / grad_norm)
    moments = [lamb_moments(g, m, p, factor) for g, m, p in zip(reduced, means_old, powers_old)]
    directions = [lamb_direction(w, m, p, d) for w, (m, p), d in zip(weights, moments, DECAYS)]
    update_totals = sum_everywhere(
        jnp.stack([jnp.sum(d * d) * part for d, part in zip(directions, shares)]), sizes
    )
    ratios = jnp.sqrt(totals[1:]) / jnp.sqrt(update_totals + 1e-12)
    fresh = [w - LEARN_RATE * ratios[k] * d for k, (w, d) in enumerate(zip(weights, directions))]
    return (
        (masks, spectrum_grad, grad_norm)
        + tuple(fresh)
        + tuple(m for m, unused in moments)
        + tuple(p for unused, p in moments)
    )


def solution(mesh):
    stored = (
        P("band", "stream", None),
        P("band", None, "stream"),
        P("band", "stream", None),
        P("band", "stream"),
        P(None, None, None, "stream"),
        P(None, None, None, "stream"),
        P(None, "stream", None),
        P(None, "stream"),
    )
    frames_over = P("stream", None, None)
    mask_over = P("stream", "band", None, None)
    return jax.shard_map(
        body,
        mesh=mesh,
        in_specs=(frames_over, P("stream", None), P(), P(), mask_over) + stored * 3,
        out_specs=(mask_over, frames_over, P()) + stored * 3,
        check_vma=False,
    )
```

```python
from functools import partial
import math

import jax
import jax.numpy as jnp
from jax import lax
from jax.experimental import pallas as pl
from jax.experimental.pallas import tpu as pltpu
from jax.sharding import PartitionSpec as P

STEP = 10
CLIP_NORM = 5.0
LEARN_RATE = 0.5
BETA_ONE = 0.9
BETA_TWO = 0.999
ADAM_EPS = 1e-06
DECAY_RATE = 0.01
NORM_EPS = 1e-05
VAR_FLOOR = 0.25
CLIPS = 3
CLIP_MOST = 32
LANES = 128
VMEM_BYTES = 60 * 1024 * 1024
CORES = 2
SLOT_PAD = 16
MESH = pl.DeviceIdType.MESH

AB = (((1,), (0,)), ((), ()))
ABT = (((1,), (1,)), ((), ()))
ATB = (((0,), (0,)), ((), ()))


def split(x):
    hi = x.astype(jnp.bfloat16)
    lo = (x - hi.astype(jnp.float32)).astype(jnp.bfloat16)
    return hi, lo


def dot1(a, b, dims):
    return lax.dot_general(a, b, dims, preferred_element_type=jnp.float32)


def dot_parts(a, b, dims):
    return dot1(a[0], b[0], dims) + (dot1(a[1], b[0], dims) + dot1(a[0], b[1], dims))


def dot3(a, b, dims):
    return dot_parts(split(a), split(b), dims)


def sigmoid(x):
    return 0.5 * jnp.tanh(0.5 * x) + 0.5


def norm_stats(x):
    center = x - jnp.mean(x, axis=-1, keepdims=True)
    spread = jnp.mean(center * center, axis=-1, keepdims=True)
    scale = lax.rsqrt(spread + NORM_EPS)
    return center * scale, scale


def norm_back(grad_unit, unit, scale):
    first = jnp.mean(grad_unit, axis=-1, keepdims=True)
    second = jnp.mean(grad_unit * unit, axis=-1, keepdims=True)
    return scale * (grad_unit - first - unit * second)


def column_sum(x):
    return jnp.sum(x, axis=0, keepdims=True)


def pack_rows(dmodel, hidden):
    blocks = 4 * hidden // LANES
    out_rows = 2 * hidden // blocks
    weight_rows = 2 * dmodel + 2 * hidden + out_rows
    share = (2 * dmodel + 8 * hidden + dmodel) // blocks
    vec_rows = -(-share // LANES)
    return blocks, out_rows, weight_rows, share, vec_rows, -(-(weight_rows + vec_rows) // 32) * 32


def pack_rnn(w_in, w_rec, w_out, vec, rows, share):
    count = w_in.shape[2] // LANES
    parts = [
        w.reshape(2 * w.shape[1], count, LANES).transpose(1, 0, 2) for w in (w_in, w_rec)
    ] + [w_out.reshape(count, -1, LANES)]
    used = sum(p.shape[1] for p in parts)
    flat = jnp.pad(vec.reshape(count, share), ((0, 0), (0, (rows - used) * LANES - share)))
    return jnp.concatenate(parts + [flat.reshape(count, rows - used, LANES)], axis=1)


def unpack_rnn(pack, dmodel, hidden):
    blocks, out_rows, weight_rows, share, vec_rows, rows = pack_rows(dmodel, hidden)
    count = pack.shape[0]
    cuts = (0, 2 * dmodel, 2 * dmodel + 2 * hidden)
    w_in = pack[:, : cuts[1]].reshape(count, 2, dmodel, LANES).transpose(1, 2, 0, 3)
    w_rec = pack[:, cuts[1] : cuts[2]].reshape(count, 2, hidden, LANES).transpose(1, 2, 0, 3)
    return (
        w_in.reshape(2, dmodel, count * LANES),
        w_rec.reshape(2, hidden, count * LANES),
        pack[:, cuts[2] : weight_rows].reshape(count * out_rows, LANES),
        unpack_vec(pack, weight_rows, vec_rows, share),
    )


def unpack_vec(pack, weight_rows, vec_rows, share):
    count = pack.shape[0]
    flat = pack[:, weight_rows : weight_rows + vec_rows].reshape(count, vec_rows * LANES)
    return flat[:, :share].reshape(1, count * share)


class Pack:
    def __init__(self, ref, dmodel, hidden):
        self.ref, self.dmodel, self.hidden = ref, dmodel, hidden
        self.blocks, self.out_rows = pack_rows(dmodel, hidden)[:2]

    def intake(self, e, first, last):
        rows = slice(e * self.dmodel, (e + 1) * self.dmodel)
        return jnp.concatenate([self.ref[k, rows] for k in range(first, last)], axis=1)

    def recurrence(self, e, k):
        base = 2 * self.dmodel + e * self.hidden
        return self.ref[k, base : base + self.hidden]

    def outtake(self, e):
        base = 2 * self.dmodel + 2 * self.hidden
        half = self.blocks // 2
        return jnp.concatenate(
            [self.ref[k, base : base + self.out_rows] for k in range(half * e, half * (e + 1))], axis=0
        )

    def put(self, k, base, value):
        if len(self.ref.shape) == 3:
            self.ref[k, base : base + value.shape[0]] = value
            return
        quarter = self.ref.shape[2]
        done = 0
        while done < value.shape[0]:
            part, at = divmod(base + done, quarter)
            count = min(value.shape[0] - done, quarter - at)
            self.ref[part, k, at : at + count] = value[done : done + count]
            done += count

    def put_intake(self, e, q, value):
        for h in range(value.shape[1] // LANES):
            self.put(q * value.shape[1] // LANES + h, e * self.dmodel, value[:, h * LANES : (h + 1) * LANES])

    def put_recurrence(self, e, q, value):
        base = 2 * self.dmodel + e * self.hidden
        for h in range(value.shape[1] // LANES):
            self.put(q * value.shape[1] // LANES + h, base, value[:, h * LANES : (h + 1) * LANES])

    def put_outtake(self, e, value):
        base = 2 * self.dmodel + 2 * self.hidden
        for k in range(self.blocks // 2):
            self.put(self.blocks // 2 * e + k, base, value[k * self.out_rows : (k + 1) * self.out_rows])

    def put_vec(self, value):
        unused, unused, base, share, vec_rows, rows = pack_rows(self.dmodel, self.hidden)
        for k in range(self.blocks):
            block = [
                value[:, k * share + r * LANES : k * share + min(share, (r + 1) * LANES)] for r in range(vec_rows)
            ]
            block[-1] = jnp.concatenate(
                [block[-1], jnp.zeros((1, vec_rows * LANES - share), jnp.float32)], axis=1
            )
            block.append(jnp.zeros((rows - base - vec_rows, LANES), jnp.float32))
            self.put(k, base, jnp.concatenate(block, axis=0))


def load_vec(pack, vec):
    unused, unused, base, share, vec_rows, unused = pack_rows(pack.dmodel, pack.hidden)
    for k in range(pack.blocks):
        for r in range(vec_rows):
            width = min(LANES, share - r * LANES)
            at = k * share + r * LANES
            vec[0:1, at : at + width] = pack.ref[k, base + r : base + r + 1, :width]


def split_recurrence(pack, hi_ref, lo_ref):
    for e in range(2):
        for k in range(pack.blocks):
            part = slice(k * LANES, (k + 1) * LANES)
            hi_ref[e, :, part], lo_ref[e, :, part] = split(pack.recurrence(e, k))


def split_recurrence_turned(pack, hi_ref, lo_ref):
    for e in range(2):
        for k in range(pack.blocks):
            part = slice(k * LANES, (k + 1) * LANES)
            hi_ref[e, part], lo_ref[e, part] = split(pack.recurrence(e, k).T)


def gates_forward(x_flat, act, pack, vec, rows, block):
    hidden4 = 4 * pack.hidden
    dmodel = pack.dmodel
    parts = [split(pack.intake(e, 0, pack.blocks)) for e in range(2)]

    def one(r, carry):
        start = pl.multiple_of(r * block, block)
        unit, unused = norm_stats(x_flat(start, block))
        n = split(unit * (1.0 + vec[0:1, :dmodel]) + vec[0:1, dmodel : 2 * dmodel])
        for e in range(2):
            bias = vec[0:1, 2 * dmodel + hidden4 * e : 2 * dmodel + hidden4 * (e + 1)]
            z = dot_parts(n, parts[e], AB) + bias
            act[e][pl.ds(r * (block // 16), block // 16)] = z.reshape(block // 16, 16, hidden4)
        return carry

    lax.fori_loop(0, rows // block, one, 0)


def run_forward(steps, places, act, c, h, pack, hi_ref, lo_ref, state, memory):
    hidden = pack.hidden
    for e in range(2):
        state[e][...] = jnp.zeros_like(state[e])
        memory[e][...] = jnp.zeros_like(memory[e])

    def step(j, carry):
        work = []
        for e in range(2):
            at = places(e, j)
            prior = state[e][...]
            hi, lo = split(prior)
            rows = prior.shape[0]
            first = dot1(jnp.concatenate([hi, lo], axis=0), hi_ref[e], AB)
            drive = [act[e][p] for p in at]
            drive = drive[0] if len(drive) == 1 else jnp.concatenate(drive, axis=0)
            z = first[:rows] + first[rows:] + dot1(hi, lo_ref[e], AB) + drive
            work.append((at, z))
        for e in range(2):
            at, z = work[e]
            ingate = sigmoid(z[:, :hidden])
            forget = sigmoid(z[:, hidden : 2 * hidden])
            candidate = jnp.tanh(z[:, 2 * hidden : 3 * hidden])
            outgate = sigmoid(z[:, 3 * hidden :])
            before = memory[e][...]
            now = forget * before + ingate * candidate
            squashed = jnp.tanh(now)
            out = outgate * squashed
            memory[e][...] = now
            state[e][...] = out
            for k, p in enumerate(at):
                part = slice(16 * k, 16 * (k + 1))
                act[e][p, :, :hidden] = ingate[part]
                act[e][p, :, hidden : 2 * hidden] = forget[part]
                act[e][p, :, 2 * hidden : 3 * hidden] = candidate[part]
                act[e][p, :, 3 * hidden :] = outgate[part]
                c[e][p] = now[part]
                h[e][p] = out[part]
        return carry

    lax.fori_loop(0, steps, step, 0, unroll=4)


def output_forward(count, h, pack, vec):
    hidden = h[0].shape[2]
    dmodel = pack.dmodel
    total = vec[0:1, vec.shape[1] - dmodel :]
    for e in range(2):
        states = h[e][:count].reshape(count * 16, hidden)
        total = total + dot3(states, pack.outtake(e), AB)
    return total


def run_backward(steps, places, act, dz_ref, c, dh, pack, hi_ref, lo_ref, grad_h, grad_c):
    hidden = pack.hidden
    split_recurrence_turned(pack, hi_ref, lo_ref)
    for e in range(2):
        grad_h[e][...] = jnp.zeros_like(grad_h[e])
        grad_c[e][...] = jnp.zeros_like(grad_c[e])

    def load(ref, at):
        got = [ref[p] for p in at]
        return got[0] if len(got) == 1 else jnp.concatenate(got, axis=0)

    def step(back, carry):
        j = steps - 1 - back
        later = jnp.minimum(j, 1).astype(jnp.float32)
        work = []
        for e in range(2):
            at = places(e, j)
            gates = load(act[e], at)
            ingate = gates[:, :hidden]
            forget = gates[:, hidden : 2 * hidden]
            candidate = gates[:, 2 * hidden : 3 * hidden]
            outgate = gates[:, 3 * hidden :]
            squashed = jnp.tanh(load(c[e], at))
            before = load(c[e], places(e, jnp.maximum(j - 1, 0))) * later
            total_h = load(dh[e], at) + grad_h[e][...]
            total_c = grad_c[e][...] + total_h * outgate * (1.0 - squashed * squashed)
            dz = jnp.concatenate(
                [
                    total_c * candidate * ingate * (1.0 - ingate),
                    total_c * before * forget * (1.0 - forget),
                    total_c * ingate * (1.0 - candidate * candidate),
                    total_h * squashed * outgate * (1.0 - outgate),
                ],
                axis=1,
            )
            grad_c[e][...] = total_c * forget
            for k, p in enumerate(at):
                dz_ref[e][p] = dz[16 * k : 16 * (k + 1)]
            work.append(dz)
        for e in range(2):
            hi, lo = split(work[e])
            rows = hi.shape[0]
            first = dot1(jnp.concatenate([hi, lo], axis=0), hi_ref[e], AB)
            grad_h[e][...] = first[:rows] + first[rows:] + dot1(hi, lo_ref[e], AB)
        return carry

    lax.fori_loop(0, steps, step, 0, unroll=4)


def states_backward(count, dy_flat, dh, h, pack, g_pack):
    hidden = h[0].shape[2]
    dy = split(dy_flat)
    for e in range(2):
        dh[e][:count] = dot_parts(dy, split(pack.outtake(e)), ABT).reshape(count, 16, hidden)
        g_pack.put_outtake(e, dot3_parts_first(h[e][:count].reshape(count * 16, hidden), dy))


def dot3_parts_first(a, b_parts):
    return dot_parts(split(a), b_parts, ATB)


def gates_backward(count, x_flat, dy_flat, dz_ref, before, pack, vec, g_pack, g_vec):
    dmodel, hidden = pack.dmodel, pack.hidden
    hidden4 = 4 * hidden
    rows = count * 16
    unit, scale = norm_stats(x_flat)
    gain = 1.0 + vec[0:1, :dmodel]
    n = unit * gain + vec[0:1, dmodel : 2 * dmodel]
    dn = jnp.zeros((rows, dmodel), jnp.float32)
    for e in range(2):
        left_hi, left_lo = split(jnp.concatenate([n, before(e)], axis=1).T)
        left = jnp.concatenate([left_hi, left_lo], axis=0)
        height = left_hi.shape[0]
        for q in range(4):
            part = slice(hidden * q, hidden * (q + 1))
            dz_q = dz_ref[e][:count, :, part].reshape(rows, hidden)
            dz = split(dz_q)
            first = dot1(left, dz[0], AB)
            got = first[:height] + first[height:] + dot1(left_hi, dz[1], AB)
            g_pack.put_intake(e, q, got[:dmodel])
            g_pack.put_recurrence(e, q, got[dmodel:])
            dn = dn + dot_parts(dz, split(pack.intake(e, q * pack.blocks // 4, (q + 1) * pack.blocks // 4)), ABT)
            base = 2 * dmodel + hidden4 * e + hidden * q
            g_vec[0:1, base : base + hidden] = column_sum(dz_q)
    g_vec[0:1, :dmodel] = column_sum(dn * unit)
    g_vec[0:1, dmodel : 2 * dmodel] = column_sum(dn)
    g_vec[0:1, vec.shape[1] - dmodel :] = column_sum(dy_flat)
    g_pack.put_vec(g_vec[...])
    return dy_flat + norm_back(dn * gain, unit, scale)


def input_backward(count, x_flat, dy_flat, dz_ref, pack, vec, g_vec):
    dmodel, hidden = pack.dmodel, pack.hidden
    rows = count * 16
    unit, scale = norm_stats(x_flat)
    gain = 1.0 + vec[0:1, :dmodel]
    dn = jnp.zeros((rows, dmodel), jnp.float32)
    for e in range(2):
        for q in range(4):
            part = slice(hidden * q, hidden * (q + 1))
            dz = split(dz_ref[e][:count, :, part].reshape(rows, hidden))
            dn = dn + dot_parts(dz, split(pack.intake(e, q * pack.blocks // 4, (q + 1) * pack.blocks // 4)), ABT)
    g_vec[0:1, :dmodel] = column_sum(dn * unit)
    g_vec[0:1, dmodel : 2 * dmodel] = column_sum(dn)
    g_vec[0:1, vec.shape[1] - dmodel :] = column_sum(dy_flat)
    return dy_flat + norm_back(dn * gain, unit, scale)


def weights_backward(count, x_flat, dz_ref, before, pack, vec, g_pack, g_vec):
    dmodel, hidden = pack.dmodel, pack.hidden
    rows = count * 16
    unit, unused = norm_stats(x_flat)
    n = unit * (1.0 + vec[0:1, :dmodel]) + vec[0:1, dmodel : 2 * dmodel]
    for e in range(2):
        left_hi, left_lo = split(jnp.concatenate([n, before(e)], axis=1).T)
        left = jnp.concatenate([left_hi, left_lo], axis=0)
        height = left_hi.shape[0]
        for q in range(4):
            part = slice(hidden * q, hidden * (q + 1))
            dz_q = dz_ref[e][:count, :, part].reshape(rows, hidden)
            dz = split(dz_q)
            first = dot1(left, dz[0], AB)
            got = first[:height] + first[height:] + dot1(left_hi, dz[1], AB)
            g_pack.put_intake(e, q, got[:dmodel])
            g_pack.put_recurrence(e, q, got[dmodel:])
            base = 2 * dmodel + 4 * hidden * e + hidden * q
            g_vec[0:1, base : base + hidden] = column_sum(dz_q)
    g_pack.put_vec(g_vec[...])


def shifted(ref, e, count, hidden, mask):
    rows = (count - 1) * 16
    zero = jnp.zeros((16, hidden), jnp.float32)
    if e == 0:
        kept = ref[: count - 1].reshape(rows, hidden) * mask
        return jnp.concatenate([zero, kept], axis=0)
    kept = ref[1:count].reshape(rows, hidden) * mask
    return jnp.concatenate([kept, zero], axis=0)


def tables_kernel(
    slots, share, inner, direct, segments, widths, groups, places, clips, slot_of, band_of, mask_places, counts
):
    band, stream = lax.axis_index("band"), lax.axis_index("stream")
    for s in range(slots):
        places[0, s] = 0
        places[1, s] = 0
    for s in range(band_of.shape[1]):
        band_of[0, s] = 0
        band_of[1, s] = 0
    for c in range(CLIPS):
        clips[1, c] = 0
    for g in range(counts.shape[0]):
        counts[g] = 0

    def one_band(b, edge):
        g = groups[0, b]
        rank = counts[g]
        counts[g] = rank + 1
        slot_of[0, b] = g * slots + rank
        band_of[0, g * slots + rank] = b
        band_of[1, g * slots + rank] = 1
        width = widths[0, b]

        @pl.when(g == band)
        def mine():
            places[0, rank] = edge
            places[1, rank] = width

        return edge + width

    lax.fori_loop(0, groups.shape[1], one_band, jnp.int32(0))

    def one_frame(t, carry):
        c = segments[0, t]
        clips[1, c] = clips[1, c] + 1
        return carry

    lax.fori_loop(0, segments.shape[1], one_frame, 0)
    start = jnp.int32(0)
    for c in range(CLIPS):
        clips[0, c] = start
        start = start + clips[1, c]
    for j in range(share):
        row = lax.div(stream, inner) * share + j
        mask_places[0, j] = places[1, row]
        mask_places[1, j] = lax.rem(stream, CORES) if direct else jnp.int32(0)
        mask_places[2, j] = row


def table_shapes(slots, share, bands, parts):
    shapes = ((2, slots), (2, CLIPS), (1, bands), (2, parts * slots), (3, share))
    return [jax.ShapeDtypeStruct(x, jnp.int32) for x in shapes]


def clip_places(clips, spare):
    def places(e, j):
        found = []
        for c in range(CLIPS):
            start, length = clips[0, c], clips[1, c]
            frame = start + j if e == 0 else start + length - 1 - j
            found.append(jnp.where(j < length, frame, spare))
        return found

    return places


def window_of(edge):
    base = pl.multiple_of((edge // LANES) * LANES, LANES)
    return base, lax.rem(edge, LANES)


def split_rows(spec, edge, width, frames):
    wmax = LANES
    base, shift = window_of(edge)
    window = spec[:, pl.ds(base, 2 * LANES)]
    taken = pltpu.roll(window, lax.rem(2 * LANES - shift, 2 * LANES), 1)[:, :wmax]
    taken = jnp.concatenate([taken[:frames], taken[frames:]], axis=1)
    lane = lax.broadcasted_iota(jnp.int32, (frames, wmax), 1)
    inside = (lane < width).astype(jnp.float32)
    valid = jnp.concatenate([inside, inside], axis=1)
    entries = jnp.maximum(2 * width, 1).astype(jnp.float32)
    mean = jnp.sum(taken * valid, axis=-1, keepdims=True) / entries
    center = (taken - mean) * valid
    spread = jnp.sum(center * center, axis=-1, keepdims=True) / entries
    scale = lax.rsqrt(jnp.maximum(spread, VAR_FLOOR))
    moving = jnp.where(spread > VAR_FLOOR, 1.0, jnp.where(spread == VAR_FLOOR, 0.5, 0.0))
    return center * scale, scale, valid, moving, entries


def slot_weights(w_split, s, slot_rows):
    count = w_split.shape[0]
    at = pl.ds(pl.multiple_of(s * slot_rows, slot_rows), slot_rows)
    return jnp.concatenate([w_split[k, at, :] for k in range(count)], axis=0)


def time_forward_kernel(
    slot_rows, share, inner, direct, segments, widths, groups, spec_in, w_split_in, rnn_in,
    places_s, clips, slot_of, band_of, mask_places, out, v_band, x, *refs,
):
    saved, refs = refs[:6], refs[6:]
    act0, act1, c0, c1, h0, h1, hi_ref, lo_ref, s0, s1, m0, m1, y, mixed, vec, rnn, w_split, spec, *refs = refs
    counts, sems = refs
    slots = out.shape[1]
    frames, unused, dmodel = x.shape
    wide = w_split.shape[0] * slot_rows
    pack = Pack(rnn, dmodel, h0.shape[2])
    load_split = pltpu.make_async_copy(w_split_in, w_split, sems.at[7])
    load_spec = pltpu.make_async_copy(spec_in, spec, sems.at[8])
    load_rnn = pltpu.make_async_copy(rnn_in, rnn, sems.at[0])
    for copy in (load_split, load_spec, load_rnn):
        copy.start()
    tables_kernel(
        slots, share, inner, direct, segments, widths, groups, places_s, clips, slot_of, band_of, mask_places, counts
    )
    load_split.wait()
    load_spec.wait()
    v_band[...] = jnp.zeros_like(v_band)
    columns = v_band.shape[1] // w_split.shape[0]
    for k in range(w_split.shape[0]):
        for h in range(0, columns, LANES):
            width = min(LANES, columns - h)
            at = slots * slot_rows + SLOT_PAD * (h // LANES)
            v_band[:, k * columns + h : k * columns + h + width] = w_split[k, at : at + SLOT_PAD, :width]
    x[...] = jnp.zeros_like(x)
    for a in (act0, act1):
        a[frames] = jnp.zeros_like(a[frames])

    for s in range(slots):
        unit, unused, valid, moving, entries = split_rows(spec, places_s[0, s], places_s[1, s], frames)
        row = v_band[s : s + 1, : 2 * wide + dmodel]
        z = (unit * (1.0 + row[:, :wide]) + row[:, wide : 2 * wide]) * valid
        y[s] = dot3(z, slot_weights(w_split, s, slot_rows), AB) + row[:, 2 * wide : 2 * wide + dmodel]
    for s in range(slots):
        x[:, s, :] = y[s]
    load_rnn.wait()
    load_vec(pack, vec)
    split_recurrence(pack, hi_ref, lo_ref)
    act = (act0, act1)

    def x_flat(start, size):
        return x[pl.ds(start // 16, size // 16)].reshape(size, dmodel)

    gates_forward(x_flat, act, pack, vec, frames * 16, 256)
    run_forward(
        CLIP_MOST, clip_places(clips, frames), act, (c0, c1), (h0, h1),
        pack, hi_ref, lo_ref, (s0, s1), (m0, m1),
    )
    leaving = [
        pltpu.make_async_copy(a, b, sems.at[1 + k])
        for k, (a, b) in enumerate(zip((act0, act1, c0, c1, h0, h1), saved))
    ]
    for copy in leaving:
        copy.start()
    total = output_forward(frames, (h0, h1), pack, vec)
    x_all = x[...].reshape(frames * 16, dmodel)
    mixed[...] = (x_all + total).reshape(frames, 16, dmodel)
    parts, unused_slots, quarter, unused = out.shape
    for s in range(slots):
        for q in range(parts):
            out[q, s] = mixed[q * quarter : (q + 1) * quarter, s, :]
    for copy in leaving:
        copy.wait()


def f32(shape):
    return jax.ShapeDtypeStruct(shape, jnp.float32)


def saved_shapes(count, hidden):
    return [f32((count, 16, 4 * hidden))] * 2 + [f32((count, 16, hidden))] * 4


def saved_scratch(count, hidden):
    return [pltpu.VMEM(x.shape, jnp.float32) for x in saved_shapes(count, hidden)]


def vec_scratch(dmodel, hidden):
    return pltpu.VMEM((1, 3 * dmodel + 8 * hidden), jnp.float32)


def rec_scratch(rows, hidden, turned=False):
    return [
        pltpu.VMEM((2, 4 * hidden, hidden) if turned else (2, hidden, 4 * hidden), jnp.bfloat16),
        pltpu.VMEM((2, 4 * hidden, hidden) if turned else (2, hidden, 4 * hidden), jnp.bfloat16),
    ] + [pltpu.VMEM((rows, hidden), jnp.float32)] * 4


SMEM = pl.BlockSpec(memory_space=pltpu.SMEM)
VMEM = pl.BlockSpec(memory_space=pltpu.VMEM)
ANY = pl.BlockSpec(memory_space=pl.ANY)
PARAMS = pltpu.CompilerParams(vmem_limit_bytes=VMEM_BYTES)


def cost(micros):
    return pl.CostEstimate(flops=int(micros * 1.1e9), bytes_accessed=int(micros * 3e6), transcendentals=0)


def time_forward(segments, widths, groups, spec, w_split, rnn, sizes):
    parts, slots, share, inner, direct, band_columns, slot_rows, hidden = sizes
    dmodel = w_split.shape[2]
    frames = spec.shape[0] // 2
    return pl.pallas_call(
        partial(time_forward_kernel, slot_rows, share, inner, direct),
        out_shape=table_shapes(slots, share, widths.shape[1], parts)
        + [
            f32((parts, slots, frames // parts, dmodel)), f32((SLOT_PAD, band_columns)), f32((frames, 16, dmodel)),
        ]
        + saved_shapes(frames + 1, hidden),
        in_specs=[SMEM] * 3 + [ANY] * 3,
        out_specs=[SMEM] * 5 + [VMEM] * 3 + [ANY] * 6,
        scratch_shapes=saved_scratch(frames + 1, hidden)
        + rec_scratch(16 * CLIPS, hidden)
        + [pltpu.VMEM((slots, frames, dmodel), jnp.float32)]
        + [pltpu.VMEM((frames, 16, dmodel), jnp.float32), vec_scratch(dmodel, hidden)]
        + [pltpu.VMEM(a.shape, jnp.float32) for a in (rnn, w_split, spec)]
        + [pltpu.SMEM((parts,), jnp.int32), pltpu.SemaphoreType.DMA((9,))],
        compiler_params=PARAMS,
        cost_estimate=cost(35),
        name="time_forward",
    )(segments, widths, groups, spec, w_split, rnn)


def time_backward_kernel(
    slot_rows, places_s, clips, my_outer, dy_in, spec_in, x_in, *refs,
):
    saved, refs = refs[:6], refs[6:]
    w_split_in, v_band, rnn_in, g_mask_vec, d_spec, g_split, g_rnn, *refs = refs
    act0, act1, c0, c1, h0, h1, *refs = refs
    hi_ref, lo_ref, s0, s1, m0, m1, dy, vec, g_vec, g_band, dh0, dh1, dz0, dz1, *refs = refs
    rnn, w_split, spec, x, sems = refs
    slots = dy_in.shape[1]
    frames, unused, dmodel = x.shape
    hidden = h0.shape[2]
    wide = w_split.shape[0] * slot_rows
    parts, unused_slots, quarter, unused = dy_in.shape
    pack, g_pack = Pack(rnn, dmodel, hidden), Pack(g_rnn, dmodel, hidden)
    pairs = [(rnn_in, rnn), (saved[4], h0), (saved[5], h1)]
    pairs += list(zip(saved[:4], (act0, act1, c0, c1)))
    pairs += [(w_split_in, w_split), (spec_in, spec), (x_in, x)]
    loads = [pltpu.make_async_copy(a, b, sems.at[k]) for k, (a, b) in enumerate(pairs)]
    for copy in loads:
        copy.start()
    dy[...] = jnp.zeros_like(dy)
    for s in range(slots):
        for q in range(parts):
            dy[q * quarter : (q + 1) * quarter, s, :] = dy_in[q, s]
    for copy in loads[:3]:
        copy.wait()
    load_vec(pack, vec)
    dy_flat = dy[...].reshape(frames * 16, dmodel)
    states_backward(frames, dy_flat, (dh0, dh1), (h0, h1), pack, g_pack)
    for d in (dh0, dh1):
        d[frames] = jnp.zeros_like(d[frames])
    for copy in loads[3:7]:
        copy.wait()
    run_backward(
        CLIP_MOST, clip_places(clips, frames), (act0, act1), (dz0, dz1), (c0, c1),
        (dh0, dh1), pack, hi_ref, lo_ref, (s0, s1), (m0, m1),
    )
    for copy in loads[7:]:
        copy.wait()
    frame = lax.broadcasted_iota(jnp.int32, ((frames - 1) * 16, 1), 0) // 16 + 1
    inside = jnp.ones(frame.shape, jnp.float32)
    for k in range(1, CLIPS):
        inside = jnp.where(frame == clips[0, k], 0.0, inside)
    x_flat = x[...].reshape(frames * 16, dmodel)
    dx = gates_backward(
        frames, x_flat, dy[...].reshape(frames * 16, dmodel), (dz0, dz1),
        lambda e: shifted((h0, h1)[e], e, frames, hidden, inside), pack, vec, g_pack, g_vec,
    )
    dy[...] = dx.reshape(frames, 16, dmodel)
    d_spec[...] = jnp.zeros_like(d_spec)
    g_split[:, slots * slot_rows :] = jnp.zeros_like(g_split[:, slots * slot_rows :])
    g_band[...] = jnp.zeros_like(g_band)

    for s in range(slots):
        edge, width = places_s[0, s], places_s[1, s]
        unit, scale, valid, moving, entries = split_rows(spec, edge, width, frames)
        row = v_band[s : s + 1, : 2 * wide + dmodel]
        gain = 1.0 + row[:, :wide]
        z = (unit * gain + row[:, wide : 2 * wide]) * valid
        demb = dy[:, s, :]
        demb_parts = split(demb)
        g_slot = dot_parts(split(z), demb_parts, ATB)
        for k in range(w_split.shape[0]):
            g_split[k, s * slot_rows : (s + 1) * slot_rows] = g_slot[k * slot_rows : (k + 1) * slot_rows]
        dz = dot_parts(demb_parts, split(slot_weights(w_split, s, slot_rows)), ABT) * valid
        g_band[s : s + 1, :wide] = column_sum(dz * unit)
        g_band[s : s + 1, wide : 2 * wide] = column_sum(dz)
        g_band[s : s + 1, 2 * wide : 2 * wide + dmodel] = column_sum(demb)
        du = dz * gain
        first = jnp.sum(du, axis=-1, keepdims=True) / entries
        second = jnp.sum(du * unit, axis=-1, keepdims=True) / entries
        dt = scale * (du - first - moving * unit * second) * valid
        base, shift = window_of(edge)
        stacked = jnp.concatenate([dt[:, :LANES], dt[:, LANES:]], axis=0)
        padded = jnp.concatenate([stacked, jnp.zeros_like(stacked)], axis=1)
        d_spec[:, pl.ds(base, 2 * LANES)] += pltpu.roll(padded, shift, 1)

    share = g_mask_vec.shape[0]
    for j in range(share):
        g_band[pl.ds(my_outer[0] * share + j, 1), 2 * wide + dmodel :] = g_mask_vec[j]
    gathered = g_band[...]
    blocks = w_split.shape[0]
    columns = gathered.shape[1] // blocks
    for k in range(blocks):
        for h in range(0, columns, LANES):
            width = min(LANES, columns - h)
            at = slots * slot_rows + SLOT_PAD * (h // LANES)
            g_split[k, at : at + SLOT_PAD, :width] = gathered[:, k * columns + h : k * columns + h + width]


def time_backward(
    slot_places, clips, my_outer, dy, spec, saved, w_split, v_band, rnn, g_mask_vec, slot_rows, hidden
):
    band_columns = v_band.shape[1]
    dmodel = w_split.shape[2]
    frames = spec.shape[0] // 2
    return pl.pallas_call(
        partial(time_backward_kernel, slot_rows),
        out_shape=[f32(spec.shape), f32(w_split.shape), f32(rnn.shape)],
        in_specs=[SMEM] * 3 + [VMEM] + [ANY] * (2 + 6 + 1) + [VMEM, ANY, VMEM],
        out_specs=[VMEM] * 3,
        scratch_shapes=saved_scratch(frames + 1, hidden)
        + rec_scratch(16 * CLIPS, hidden, True)
        + [pltpu.VMEM((frames, 16, dmodel), jnp.float32)] + [vec_scratch(dmodel, hidden)] * 2
        + [pltpu.VMEM((SLOT_PAD, band_columns), jnp.float32)]
        + [pltpu.VMEM((frames + 1, 16, hidden), jnp.float32)] * 2
        + [pltpu.VMEM((frames + 1, 16, 4 * hidden), jnp.float32)] * 2
        + [pltpu.VMEM(a.shape, jnp.float32) for a in (rnn, w_split, spec, saved[0])]
        + [pltpu.SemaphoreType.DMA((10,))],
        compiler_params=PARAMS,
        cost_estimate=cost(2),
        name="time_backward",
    )(slot_places, clips, my_outer, dy, spec, *saved, w_split, v_band, rnn, g_mask_vec)


def in_turn(core, mine, other):
    return [jnp.where(core == 0, mine, other), jnp.where(core == 0, other, mine)]


def pack_pieces(mask, wide):
    lead, r, w = mask.shape[:2], mask.shape[2], mask.shape[3] // 2
    mask = mask.reshape(lead + (r, 2, w)).transpose(0, 1, 3, 2, 4).reshape(lead + (2 * r, w))
    wide = wide.reshape(lead + (2, r // 2, w // 2)).transpose(0, 1, 3, 2, 4)
    return jnp.concatenate([mask, wide.reshape(lead + (r // 2, w))], axis=2)


def unpack_pieces(pack, r):
    lead, w = pack.shape[:2], pack.shape[3]
    mask = pack[:, :, : 2 * r].reshape(lead + (2, r, w)).transpose(0, 1, 3, 2, 4).reshape(lead + (r, 2 * w))
    wide = pack[:, :, 2 * r :].reshape(lead + (r // 2, 2, w // 2)).transpose(0, 1, 3, 2, 4)
    return mask, wide.reshape(lead + (r, w // 2))


def load_mask_piece(value, r):
    return jnp.concatenate([value[:r], value[r : 2 * r]], axis=1)


def load_wide_piece(value):
    half = value.shape[1] // 2
    return jnp.concatenate([value[:, :half], value[:, half:]], axis=0)


def mask_slot(core, width, v, x, mine, other, keep, send, g_vec):
    outer, total_rows, wide = mine.shape
    piece_rows = send.shape[1]
    frames = total_rows - piece_rows
    dmodel = x.shape[1]
    half = wide // 2
    mlp = (v.shape[1] - 2 * dmodel) - 2 * wide
    r = mlp // (2 * outer)
    w_wide, w_mask = [], []
    for g in range(outer):
        w_mask += in_turn(core, load_mask_piece(mine[g, : 2 * r], r), load_mask_piece(other[g, : 2 * r], r))
        w_wide += in_turn(
            core, load_wide_piece(mine[g, 2 * r : piece_rows]), load_wide_piece(other[g, 2 * r : piece_rows])
        )
    w_wide, w_mask = jnp.concatenate(w_wide, axis=0), jnp.concatenate(w_mask, axis=0)
    cot = jnp.concatenate([mine[g, piece_rows:] for g in range(outer)], axis=0)
    gain = 1.0 + v[:, :dmodel]
    unit, scale = norm_stats(x)
    p = split(unit * gain + v[:, dmodel : 2 * dmodel])
    wide_parts = split(w_wide)
    mask_parts = split(w_mask)
    q = jnp.tanh(dot_parts(p, wide_parts, ABT) + v[:, 2 * dmodel : 2 * dmodel + mlp])
    q_parts = split(q)
    raw = dot_parts(q_parts, mask_parts, AB) + v[:, 2 * dmodel + mlp :]
    lane = lax.broadcasted_iota(jnp.int32, (1, half), 1)
    inside = (lane < width).astype(jnp.float32)
    valid = jnp.concatenate([inside, inside], axis=1)
    value = raw[:, :wide]
    gate = sigmoid(raw[:, wide:])
    masks = value * gate * valid
    dm = cot * valid
    dr = jnp.concatenate([dm * gate, dm * value * gate * (1.0 - gate)], axis=1)
    dr_parts = split(dr)
    g_mask = dot_parts(q_parts, dr_parts, ATB)
    dq = dot_parts(dr_parts, mask_parts, ABT)
    da = dq * (1.0 - q * q)
    da_parts = split(da)
    g_wide = dot_parts(da_parts, p, ATB)
    for g in range(outer):
        first, second = slice(2 * g * r, (2 * g + 1) * r), slice((2 * g + 1) * r, (2 * g + 2) * r)
        for ref, got in zip((keep, send), in_turn(core, g_mask[first], g_mask[second])):
            ref[g, :r] = got[:, :wide]
            ref[g, r : 2 * r] = got[:, wide:]
        for ref, got in zip((keep, send), in_turn(core, g_wide[first], g_wide[second])):
            ref[g, 2 * r : piece_rows, :half] = got[: r // 2]
            ref[g, 2 * r : piece_rows, half:] = got[r // 2 :]
        keep[g, piece_rows:] = masks[g * frames : (g + 1) * frames]
    dp = dot_parts(da_parts, wide_parts, AB)
    g_vec[:, :dmodel] = column_sum(dp * unit)
    g_vec[:, dmodel : 2 * dmodel] = column_sum(dp)
    g_vec[:, 2 * dmodel : 2 * dmodel + mlp] = column_sum(da)
    g_vec[:, 2 * dmodel + mlp :] = column_sum(dr)
    return norm_back(dp * gain, unit, scale)


def mask_kernel(base, places, arrived, mine, other, v_band, keep, send, grad, g_vec):
    s = pl.program_id(0)
    parts, streams, unused, quarter, dmodel = arrived.shape
    order = [(q, g) for g in range(streams) for q in range(parts)]
    x = jnp.concatenate([arrived[q, g, 0] for q, g in order], axis=0)
    dx = mask_slot(
        places[1, 0], places[0, s], v_band[pl.ds(places[2, s], 1), base:], x,
        mine.at[:, 0], other.at[:, 0], keep.at[:, 0], send.at[:, 0], g_vec.at[0],
    )
    for k, (q, g) in enumerate(order):
        grad[q, g, 0] = dx[k * quarter : (k + 1) * quarter]


def mask_network(places, arrived, mine, other, v_band, base, piece_rows):
    parts, streams, slots, quarter, dmodel = arrived.shape
    outer, unused, rows, wide = mine.shape

    def second(count):
        return pl.BlockSpec((outer, 1, count, wide), lambda s: (0, s, 0, 0))

    moving = pl.BlockSpec((parts, streams, 1, quarter, dmodel), lambda s: (0, 0, s, 0, 0))
    columns = v_band.shape[1] - base
    vector = pl.BlockSpec((1, 1, columns), lambda s: (s, 0, 0))
    return pl.pallas_call(
        partial(mask_kernel, base),
        grid=(slots,),
        out_shape=[
            f32(mine.shape), f32((outer, slots, piece_rows, wide)), f32(arrived.shape), f32((slots, 1, columns)),
        ],
        in_specs=[SMEM, moving, second(rows), second(rows), VMEM],
        out_specs=[second(rows), second(piece_rows), moving, vector],
        compiler_params=PARAMS,
        cost_estimate=cost(12),
        name="mask_network",
    )(places, arrived, mine, other, v_band)


class Links:
    def __init__(self, bands, layers, send_sems, recv_sems):
        self.bands, self.layers = bands, layers
        self.band, self.stream = lax.axis_index("band"), lax.axis_index("stream")
        self.layer, self.core = lax.div(self.stream, CORES), lax.rem(self.stream, CORES)
        self.other = self.stream + 1 - 2 * self.core
        self.send_sems, self.recv_sems = send_sems, recv_sems
        self.started = []

    def band_to(self, m):
        return lax.rem(self.band + m, self.bands)

    def band_from(self, m):
        return lax.rem(self.band + self.bands - m, self.bands)

    def layer_to(self, k):
        return lax.rem(self.layer + k, self.layers)

    def layer_from(self, k):
        return lax.rem(self.layer + self.layers - k, self.layers)

    def band_beside(self, k):
        return lax.rem(self.band + 2, 4) if k % 4 >= 2 else self.band + 1 - 2 * lax.rem(self.band, 2)

    def band_across(self):
        return 3 - self.band

    def goal(self, k):
        beside = self.layer + 1 - 2 * lax.rem(self.layer, 2)
        return (beside, 3 - self.layer, lax.rem(self.layer + 2, 4), self.layer)[k]

    def own(self, layer):
        return layer * CORES + self.core

    def across(self, layer):
        return layer * CORES + 1 - self.core

    def greet(self, partners):
        barrier = pltpu.get_barrier_semaphore()
        for partner in partners:
            pl.semaphore_signal(barrier, inc=1, device_id=partner, device_id_type=MESH)
        pl.semaphore_wait(barrier, len(partners))

    def copy(self, source, target, index, partner):
        return pltpu.make_async_remote_copy(
            src_ref=source, dst_ref=target, send_sem=self.send_sems.at[index],
            recv_sem=self.recv_sems.at[index], device_id=partner, device_id_type=MESH,
        )

    def send(self, source, target, index, partner):
        copy = self.copy(source, target, index, partner)
        copy.start()
        self.started.append(copy)

    def arrive(self, target, index):
        self.copy(target, target, index, (self.band, self.other)).wait_recv()

    def finish(self):
        for copy in self.started:
            copy.wait_send()


def gather_kernel(
    bands, layers, intake, recurrence, outtake, scalers, splitter, banding, masker, widener, cot,
    rnn_all, split_all, later, pieces,
    vec_rows, own_later, band_rows, cot_here, staged, send_sems, recv_sems, local_sems,
):
    at = Links(bands, layers, send_sems, recv_sems)
    band, stream, other = at.band, at.stream, at.other
    rows_all = rnn_all.shape[1]
    quarter = rows_all // bands
    used = []

    def local(source, target):
        copy = pltpu.make_async_copy(source, target, local_sems.at[len(used)])
        copy.start()
        used.append(copy)
        return copy

    vec_rows[...] = jnp.zeros_like(vec_rows)
    for k in range(2):
        for h in range(0, scalers.shape[1], LANES):
            width = min(LANES, scalers.shape[1] - h)
            vec_rows[k, h // LANES : h // LANES + 1, :width] = scalers[k : k + 1, h : h + width]
    band_rows[...] = jnp.zeros_like(band_rows)
    slots = banding.shape[0]
    for h in range(0, banding.shape[1], LANES):
        width = min(LANES, banding.shape[1] - h)
        base = SLOT_PAD * (h // LANES)
        band_rows[base : base + slots, :width] = banding[:, h : h + width]

    def own_pack(k, target):
        a = intake.shape[1]
        b = a + recurrence.shape[1]
        c = b + outtake.shape[1]
        return [
            local(intake.at[k], target.at[pl.ds(0, a)]),
            local(recurrence.at[k], target.at[pl.ds(a, b - a)]),
            local(outtake.at[k], target.at[pl.ds(b, c - b)]),
            local(vec_rows.at[k], target.at[pl.ds(c, rows_all - c)]),
        ]

    mine, mine_split = rnn_all.at[stream], split_all.at[stream]
    first = own_pack(0, mine)
    split_rows_count = splitter.shape[0]
    second = [
        local(splitter, mine_split.at[pl.ds(0, split_rows_count)]),
        local(band_rows, mine_split.at[pl.ds(split_rows_count, band_rows.shape[0])]),
    ]
    at.greet(
        [(at.band_to(m), stream) for m in range(1, bands)]
        + [(band, at.own(at.layer_to(k))) for k in range(1, layers)]
        + [(band, other)]
    )
    steps = (2, 0, 1)
    turns = range(1, bands)

    def rows(b):
        return pl.ds(b * quarter, quarter)

    to_layer, to_layer_split, to_band = 0, layers, 2 * layers
    to_core = to_band + layers * bands
    to_core_split = to_core + layers * bands
    to_layer_later = to_core_split + layers

    def spread(piece, index):
        for k in (2, 0):
            at.send(piece, piece, index + k, (band, at.own(at.goal(k))))

    def relay(piece, index):
        at.send(piece, piece, index + 1, (band, at.own(at.goal(0))))

    def rnn_piece(k):
        return rnn_all.at[at.own(at.goal(k)), rows(band)]

    def split_piece(k):
        return split_all.at[at.own(at.goal(k))]

    def later_piece(k):
        return later.at[at.goal(k)]

    def hand_on(k):
        piece = rnn_piece(k)
        for m in turns:
            at.send(piece, piece, to_band + k * bands + m, (at.band_to(m), stream))
        at.send(piece, piece, to_core + k * bands, (band, other))

    for copy in first:
        copy.wait()
    spread(rnn_piece(3), to_layer)
    for copy in second:
        copy.wait()
    spread(mine_split, to_layer_split)
    at.send(mine, mine, to_core + 3 * bands, (band, other))
    at.send(mine_split, mine_split, to_core_split + 3, (band, other))
    third = own_pack(1, own_later)
    load_cot = local(cot, cot_here)
    r, wide = masker.shape[1], masker.shape[2] // 2
    half = wide // 2
    base = 2 * r + r // 2
    fill = [
        local(masker.at[:, :, pl.ds(0, wide)], staged.at[:, pl.ds(0, r), :]),
        local(masker.at[:, :, pl.ds(wide, wide)], staged.at[:, pl.ds(r, r), :]),
        local(widener.at[:, pl.ds(0, r // 2), :], staged.at[:, pl.ds(2 * r, r // 2), pl.ds(0, half)]),
        local(widener.at[:, pl.ds(r // 2, r // 2), :], staged.at[:, pl.ds(2 * r, r // 2), pl.ds(half, half)]),
    ]
    at.arrive(rnn_piece(2), to_layer + 2)
    relay(rnn_piece(2), to_layer)
    hand_on(2)
    for copy in third:
        copy.wait()
    later[at.layer] = own_later[rows(band), :]
    spread(later_piece(3), to_layer_later)
    at.arrive(rnn_piece(0), to_layer)
    hand_on(0)
    at.arrive(split_piece(2), to_layer_split + 2)
    relay(split_piece(2), to_layer_split)
    at.send(split_piece(2), split_piece(2), to_core_split + 2, (band, other))
    at.arrive(rnn_piece(1), to_layer + 1)
    hand_on(1)
    at.arrive(later_piece(2), to_layer_later + 2)
    relay(later_piece(2), to_layer_later)
    load_cot.wait()
    for s in range(slots):
        for part in range(2):
            staged[s, base:, part * half : (part + 1) * half] = cot_here[:, s, part, :]
    for copy in fill:
        copy.wait()
    rest = [local(staged, pieces)]
    for k in (0, 1):
        at.arrive(split_piece(k), to_layer_split + k)
        at.send(split_piece(k), split_piece(k), to_core_split + k, (band, other))
    for k in steps:
        for m in turns:
            piece = rnn_all.at[at.own(at.goal(k)), rows(at.band_from(m))]
            at.arrive(piece, to_band + k * bands + m)
            at.send(piece, piece, to_core + k * bands + m, (band, other))
    at.arrive(rnn_all.at[other], to_core + 3 * bands)
    at.arrive(split_all.at[other], to_core_split + 3)
    for k in steps:
        source = at.across(at.goal(k))
        for m in range(bands):
            at.arrive(rnn_all.at[source, rows(at.band_from(m))], to_core + k * bands + m)
        at.arrive(split_all.at[source], to_core_split + k)
    for k in (0, 1):
        at.arrive(later_piece(k), to_layer_later + k)
    at.finish()
    for copy in rest:
        copy.wait()


def gather_front(intake, recurrence, outtake, scalers, splitter, banding, masker, widener, cot, rows, bands, layers):
    count = 4 * layers + 2 * layers * bands
    streams = layers * CORES
    slots = banding.shape[0]
    strips = -(-banding.shape[1] // LANES)
    r, wide = masker.shape[1], masker.shape[2] // 2
    frames = cot.shape[0]
    weight_rows = intake.shape[1] + recurrence.shape[1] + outtake.shape[1]
    split_rows_count = splitter.shape[0] + SLOT_PAD * strips
    return pl.pallas_call(
        partial(gather_kernel, bands, layers),
        out_shape=[
            f32((streams, rows, LANES)), f32((streams, split_rows_count, LANES)), f32((layers, rows // bands, LANES)),
            f32((slots, 2 * r + r // 2 + frames, wide)),
        ],
        in_specs=[ANY, ANY, ANY, VMEM, ANY, VMEM, ANY, ANY, ANY],
        out_specs=[VMEM] * 3 + [ANY],
        scratch_shapes=[
            pltpu.VMEM((2, rows - weight_rows, LANES), jnp.float32),
            pltpu.VMEM((rows, LANES), jnp.float32),
            pltpu.VMEM((SLOT_PAD * strips, LANES), jnp.float32),
            pltpu.VMEM(cot.shape, jnp.float32),
            pltpu.VMEM((slots, 2 * r + r // 2 + frames, wide), jnp.float32),
            pltpu.SemaphoreType.DMA((count,)), pltpu.SemaphoreType.DMA((count,)), pltpu.SemaphoreType.DMA((20,)),
        ],
        compiler_params=pltpu.CompilerParams(
            collective_id=0, has_side_effects=True, vmem_limit_bytes=VMEM_BYTES
        ),
        cost_estimate=cost(30),
        name="gather_front",
    )(intake, recurrence, outtake, scalers, splitter, banding, masker, widener, cot)


def mask_exchange_kernel(
    base, bands, layers, places, source, mine_in, v_band,
    back, grad_back, g_vec,
    arrived, grad, mine, other, send, received, send_sems, recv_sems, local_sems,
):
    at = Links(bands, layers, send_sems, recv_sems)
    share, outer, piece_rows, wide = other.shape
    quarter = arrived.shape[3]
    partner = (at.band, at.other)
    turns = [(m, k) for k in range(layers) for m in range(bands) if m + k]
    stride = bands * layers
    to_back, to_core, to_core_back = share * stride, 2 * share * stride, 2 * share * stride + share
    at.greet([(at.band_to(m), at.own(at.layer_to(k))) for m, k in turns] + [partner])
    loads = []
    for j in range(share):
        loads.append(
            [
                pltpu.make_async_copy(mine_in.at[:, j], mine.at[j], local_sems.at[2 * j]),
                pltpu.make_async_copy(
                    source.at[at.band, at.layer, j], arrived.at[j, at.band, at.layer], local_sems.at[2 * j + 1]
                ),
            ]
        )
        for copy in loads[-1]:
            copy.start()
    for j in range(share):
        at.send(mine_in.at[:, j, pl.ds(0, piece_rows)], other.at[j], to_core + j, partner)
        for m, k in turns:
            band, layer = at.band_to(m), at.layer_to(k)
            at.send(
                source.at[band, layer, j], arrived.at[j, at.band, at.layer], j * stride + k * bands + m,
                (band, at.own(layer)),
            )
    order = [(q, g) for g in range(layers) for q in range(bands)]
    for j in range(share):
        for copy in loads[j]:
            copy.wait()
        at.arrive(other.at[j], to_core + j)
        for m, k in turns:
            at.arrive(arrived.at[j, at.band_from(m), at.layer_from(k)], j * stride + k * bands + m)
        x = jnp.concatenate([arrived[j, q, g] for q, g in order], axis=0)
        dx = mask_slot(
            at.core, places[0, j], v_band[pl.ds(at.layer * share + j, 1), base:], x,
            mine.at[j], other.at[j], back.at[:, j], send.at[j], g_vec.at[j],
        )
        for i, (q, g) in enumerate(order):
            grad[j, q, g] = dx[i * quarter : (i + 1) * quarter]
        for m, k in turns:
            band, layer = at.band_to(m), at.layer_to(k)
            at.send(
                grad.at[j, band, layer], grad_back.at[at.band, at.layer, j], to_back + j * stride + k * bands + m,
                (band, at.own(layer)),
            )
        at.send(send.at[j], received.at[j], to_core_back + j, partner)
        grad_back[at.band, at.layer, j] = grad[j, at.band, at.layer]
    for j in range(share):
        at.arrive(received.at[j], to_core_back + j)
        for g in range(outer):
            back[g, j, :piece_rows] += received[j, g]
    for j in range(share):
        for m, k in turns:
            at.arrive(grad_back.at[at.band_from(m), at.layer_from(k), j], to_back + j * stride + k * bands + m)
    at.finish()


def mask_exchange(places, source, mine, v_band, base, piece_rows):
    bands, layers, share, quarter, dmodel = source.shape
    outer, unused, rows, wide = mine.shape
    columns = v_band.shape[1] - base
    count = 2 * share * bands * layers + 2 * share

    def vmem(*shape):
        return pltpu.VMEM(shape, jnp.float32)

    return pl.pallas_call(
        partial(mask_exchange_kernel, base, bands, layers),
        out_shape=[f32(mine.shape), f32(source.shape), f32((share, 1, columns))],
        in_specs=[SMEM, ANY, ANY, VMEM],
        out_specs=[VMEM] * 3,
        scratch_shapes=[
            vmem(share, bands, layers, quarter, dmodel),
            vmem(share, bands, layers, quarter, dmodel),
            vmem(share, outer, rows, wide),
            vmem(share, outer, piece_rows, wide),
            vmem(share, outer, piece_rows, wide),
            vmem(share, outer, piece_rows, wide),
            pltpu.SemaphoreType.DMA((count,)),
            pltpu.SemaphoreType.DMA((count,)),
            pltpu.SemaphoreType.DMA((2 * share,)),
        ],
        compiler_params=pltpu.CompilerParams(
            collective_id=2, has_side_effects=True, vmem_limit_bytes=VMEM_BYTES
        ),
        cost_estimate=cost(28),
        name="mask_exchange",
    )(places, source, mine, v_band)


def band_places(bands):
    return lambda e, j: [j if e == 0 else bands - 1 - j]


def pack_quarter(at, rnn, layer, core, m):
    quarter = rnn.shape[1] // at.bands
    rows = pl.ds(pl.multiple_of(at.band_from(m) * quarter, 8), quarter)
    return rnn.at[layer * CORES + core, rows]


def start_pack(at, rnn, pieces, sems):
    if len(pieces) == 1:
        copies = [pltpu.make_async_copy(pieces[0], rnn, sems.at[0])]
    else:
        copies = []
        for m, ref in enumerate(pieces):
            for layer in range(ref.shape[0]):
                target = pack_quarter(at, rnn, layer, at.core, m)
                at.send(ref.at[layer], target, at.bands + len(copies), (at.band, at.other))
                copies.append(pltpu.make_async_copy(ref.at[layer], target, sems.at[len(copies)]))
    for copy in copies:
        copy.start()
    return copies


def await_pack(at, rnn, pieces, copies):
    for copy in copies:
        copy.wait()
    if len(pieces) > 1:
        layers = pieces[0].shape[0]
        for k in range(len(pieces) * layers):
            at.arrive(pack_quarter(at, rnn, k % layers, 1 - at.core, k // layers), at.bands + k)


def pack_loads(pieces):
    return 1 if len(pieces) == 1 else sum(x.shape[0] for x in pieces)


def to_slots(target, source, band_of):
    for s in range(target.shape[0]):
        target[s] = source[band_of[0, s]] * band_of[1, s].astype(jnp.float32)


def band_forward_kernel(count, parts, slot_of, band_of, arrived_in, *refs):
    pieces, refs = refs[:count], refs[count:]
    out, x, *refs = refs
    saved, rnn_out, refs = refs[:6], refs[6], refs[7:]
    act0, act1, c0, c1, h0, h1, hi_ref, lo_ref, s0, s1, m0, m1, vec, rnn, arrived, mixed, *refs = refs
    send_sems, recv_sems, pack_sems, sems = refs
    bands, unused, dmodel = x.shape
    pack = Pack(rnn, dmodel, h0.shape[2])
    at, come = swap_bands(parts, arrived_in, arrived, send_sems, recv_sems, sems.at[6], True)
    await_pack(at, rnn, pieces, start_pack(at, rnn, pieces, pack_sems))
    pack_leaves = pltpu.make_async_copy(rnn, rnn_out, sems.at[7])
    pack_leaves.start()
    load_vec(pack, vec)
    split_recurrence(pack, hi_ref, lo_ref)
    come()

    def fetch(b, carry):
        x[b] = arrived[slot_of[0, b]]
        return carry

    lax.fori_loop(0, bands, fetch, 0)
    act = (act0, act1)

    def x_flat(start, size):
        return x[...].reshape(bands * 16, dmodel)

    gates_forward(x_flat, act, pack, vec, bands * 16, bands * 16)
    run_forward(
        bands, band_places(bands), act, (c0, c1), (h0, h1), pack, hi_ref, lo_ref, (s0, s1), (m0, m1)
    )
    leaving = [
        pltpu.make_async_copy(a, b, sems.at[k])
        for k, (a, b) in enumerate(zip((act0, act1, c0, c1, h0, h1), saved))
    ]
    for copy in leaving:
        copy.start()
    total = output_forward(bands, (h0, h1), pack, vec)
    mixed[...] = (x[...].reshape(bands * 16, dmodel) + total).reshape(bands, 16, dmodel)
    to_slots(out, mixed, band_of)
    at.finish()
    pack_leaves.wait()
    for copy in leaving:
        copy.wait()


def swap_bands(parts, source, target, send_sems, recv_sems, local_sem, pair=False):
    at = Links(parts, 1, send_sems, recv_sems)
    slots = target.shape[0] // parts
    if parts == 1:
        local = pltpu.make_async_copy(source, target, local_sem)
        local.start()
        return at, local.wait
    partners = [(at.band_to(m), at.stream) for m in range(1, parts)]
    at.greet(partners + [(at.band, at.other)] if pair else partners)

    def part(ref, b):
        return ref.at[pl.ds(b * slots, slots)]

    for m in range(1, parts):
        at.send(part(source, at.band_to(m)), part(target, at.band), m, (at.band_to(m), at.stream))
    local = pltpu.make_async_copy(part(source, at.band), part(target, at.band), local_sem)
    local.start()

    def come():
        for m in range(1, parts):
            at.arrive(part(target, at.band_from(m)), m)
        local.wait()

    return at, come


def swap_scratch(count):
    return [pltpu.SemaphoreType.DMA((count,)), pltpu.SemaphoreType.DMA((count,))]


def remote(parts, number):
    if parts == 1:
        return PARAMS
    return pltpu.CompilerParams(collective_id=number, has_side_effects=True, vmem_limit_bytes=VMEM_BYTES)


def band_forward(slot_of, band_of, arrived, pieces, rnn_shape, parts, hidden):
    bands = slot_of.shape[1]
    dmodel = arrived.shape[2]
    return pl.pallas_call(
        partial(band_forward_kernel, len(pieces), parts),
        out_shape=[f32(arrived.shape), f32((bands, 16, dmodel))] + saved_shapes(bands, hidden) + [f32(rnn_shape)],
        in_specs=[SMEM] * 2 + [ANY] * (1 + len(pieces)),
        out_specs=[VMEM] * 2 + [ANY] * 7,
        scratch_shapes=saved_scratch(bands, hidden)
        + rec_scratch(16, hidden)
        + [vec_scratch(dmodel, hidden), pltpu.VMEM(rnn_shape, jnp.float32)]
        + [pltpu.VMEM(arrived.shape, jnp.float32), pltpu.VMEM((bands, 16, dmodel), jnp.float32)]
        + swap_scratch(parts + pack_loads(pieces))
        + [pltpu.SemaphoreType.DMA((pack_loads(pieces),)), pltpu.SemaphoreType.DMA((8,))],
        compiler_params=remote(parts, 1),
        cost_estimate=cost(35),
        name="band_forward",
    )(slot_of, band_of, arrived, *pieces)


def band_backward_kernel(parts, slot_of, band_of, arrived, rnn_in, x, *refs):
    saved, refs = refs[:6], refs[6:]
    out, outs, refs = refs[0], refs[1 : 1 + parts], refs[1 + parts :]
    act0, act1, c0, c1, h0, h1, *refs = refs
    hi_ref, lo_ref, s0, s1, m0, m1, dy, vec, g_vec, dh0, dh1, dz0, dz1, rnn, g_rnn, *refs = refs
    leaving, send_sems, recv_sems, sems = refs
    bands, unused, dmodel = x.shape
    hidden = h0.shape[2]
    pack, g_pack = Pack(rnn, dmodel, hidden), Pack(g_rnn, dmodel, hidden)
    pairs = [(rnn_in, rnn), (saved[4], h0), (saved[5], h1)] + list(zip(saved[:4], (act0, act1, c0, c1)))
    loads = [pltpu.make_async_copy(a, b, sems.at[k]) for k, (a, b) in enumerate(pairs)]
    for copy in loads:
        copy.start()

    def fetch(b, carry):
        dy[b] = arrived[slot_of[0, b]]
        return carry

    lax.fori_loop(0, bands, fetch, 0)
    for copy in loads[:3]:
        copy.wait()
    load_vec(pack, vec)
    states_backward(bands, dy[...].reshape(bands * 16, dmodel), (dh0, dh1), (h0, h1), pack, g_pack)
    for copy in loads[3:]:
        copy.wait()
    run_backward(
        bands, band_places(bands), (act0, act1), (dz0, dz1), (c0, c1), (dh0, dh1),
        pack, hi_ref, lo_ref, (s0, s1), (m0, m1),
    )
    x_all, dy_all = x[...].reshape(bands * 16, dmodel), dy[...].reshape(bands * 16, dmodel)
    dx = input_backward(bands, x_all, dy_all, (dz0, dz1), pack, vec, g_vec)
    dy[...] = dx.reshape(bands, 16, dmodel)
    to_slots(leaving, dy, band_of)
    at, come = swap_bands(parts, leaving, out, send_sems, recv_sems, sems.at[7])
    weights_backward(
        bands, x_all, (dz0, dz1), lambda e: shifted((h0, h1)[e], e, bands, hidden, 1.0), pack, vec, g_pack, g_vec
    )
    if parts == 1:
        outs[0][...] = g_rnn[...]
    else:
        for m in range(parts):
            outs[m][...] = g_rnn[at.band_to(m)]
    come()
    at.finish()


def band_backward(slot_of, band_of, arrived, rnn, saved, parts, hidden):
    bands = slot_of.shape[1]
    dmodel = arrived.shape[2]
    blocks, rows, unused = rnn.shape
    grad_shape = rnn.shape if parts == 1 else (parts, blocks, rows // parts, LANES)
    return pl.pallas_call(
        partial(band_backward_kernel, parts),
        out_shape=[f32(arrived.shape)] + [f32(grad_shape[-3:])] * parts,
        in_specs=[SMEM] * 2 + [VMEM, ANY, VMEM] + [ANY] * 6,
        out_specs=[VMEM] * (1 + parts),
        scratch_shapes=saved_scratch(bands, hidden)
        + rec_scratch(16, hidden, True)
        + [pltpu.VMEM((bands, 16, dmodel), jnp.float32)]
        + [vec_scratch(dmodel, hidden)] * 2
        + [pltpu.VMEM((bands, 16, hidden), jnp.float32)] * 2
        + [pltpu.VMEM((bands, 16, 4 * hidden), jnp.float32)] * 2
        + [pltpu.VMEM(rnn.shape, jnp.float32), pltpu.VMEM(grad_shape, jnp.float32)]
        + [pltpu.VMEM(arrived.shape, jnp.float32)]
        + swap_scratch(parts)
        + [pltpu.SemaphoreType.DMA((8,))],
        compiler_params=remote(parts, 3),
        cost_estimate=cost(38),
        name="band_backward",
    )(slot_of, band_of, arrived, rnn, *saved)


class Grads:
    def __init__(self, pieces, rnn0, rnn1, banded, dims):
        self.pieces, self.rnn, self.banded = pieces, (rnn0, rnn1), banded
        self.slots, self.slot_rows, self.r, self.piece_rows, self.dmodel, self.hidden = dims

    def piece(self, k, s):
        if k == 0:
            at = pl.ds(pl.multiple_of(s * self.slot_rows, self.slot_rows), self.slot_rows)
            return self.banded[at, :]
        if k == 1:
            return load_wide_piece(self.pieces[s, 2 * self.r : self.piece_rows])
        return load_mask_piece(self.pieces[s, : 2 * self.r], self.r)

    def of_slot(self, s):
        return [(k, (s,), self.piece(k, s)) for k in range(3)]

    def banding(self, columns):
        base = self.slots * self.slot_rows
        strips = []
        for h in range(0, columns, LANES):
            at = base + SLOT_PAD * (h // LANES)
            strips.append(self.banded[at : at + self.slots, : min(LANES, columns - h)])
        return jnp.concatenate(strips, axis=1)

    def rest(self, columns, share):
        found = [(3, (...,), self.banding(columns))]
        unused, out_rows, weight_rows, unused, vec_rows, unused = pack_rows(self.dmodel, self.hidden)
        for k in range(2):
            pack = self.rnn[k]
            at = 0
            for e in range(2):
                found.append((4, (k, e), pack[at : at + self.dmodel]))
                at += self.dmodel
            for e in range(2):
                found.append((5, (k, e), pack[at : at + self.hidden]))
                at += self.hidden
            found.append((6, (k,), pack[at : at + out_rows]))
            at += out_rows
            strips = [
                pack[at + r : at + r + 1, : min(LANES, share - r * LANES)] for r in range(vec_rows)
            ]
            found.append((7, (slice(k, k + 1),), jnp.concatenate(strips, axis=1)))
        return found


DECAYS = (DECAY_RATE,) * 3 + (0.0,) + (DECAY_RATE,) * 3 + (0.0,)


def lamb_moments(gradient, mean_old, power_old, factor):
    clipped = gradient * factor
    mean_new = BETA_ONE * mean_old + (1.0 - BETA_ONE) * clipped
    power_new = BETA_TWO * power_old + (1.0 - BETA_TWO) * clipped * clipped
    return (mean_new, power_new)


def lamb_direction(weight_matrix, mean_new, power_new, decay):
    corrected = mean_new / (1.0 - BETA_ONE**STEP)
    scale_root = jnp.sqrt(power_new / (1.0 - BETA_TWO**STEP)) + ADAM_EPS
    return corrected / scale_root + decay * weight_matrix


def add_up(rows, first):
    line = jnp.zeros((1, LANES), jnp.float32)
    lane = lax.broadcasted_iota(jnp.int32, (1, LANES), 1)
    for i, row in enumerate(rows):
        line = jnp.where(lane == first + i, jnp.sum(row, axis=1, keepdims=True), line)
    return line


def lane_of(line, i):
    lane = lax.broadcasted_iota(jnp.int32, (1, LANES), 1)
    return jnp.sum(jnp.where(lane == i, line, 0.0), axis=1, keepdims=True)


def finish_kernel(bands, layers, dims, g_rnn0, g_split, d_spec, back, *refs):
    g_rnn1, refs = refs[:bands], refs[bands:]
    state, refs = refs[:24], refs[24:]
    out, rnn0, rnn1, banded, spec_out = refs[:5]
    pieces, refs = refs[5], refs[6:]
    held_state, packs, refs = refs[:12], refs[12], refs[13:]
    (
        own0, own_split, parts1, sum1, from_core, from_core_split, from_core1, from_band, held,
        from_layer, from_layer_split, from_layer1, spec_in, spec_own, came, lines,
        local_sems, send_sems, recv_sems,
    ) = refs
    at = Links(bands, layers, send_sems, recv_sems)
    band, stream, other = at.band, at.stream, at.other
    streams = layers * CORES
    quarter = g_rnn0.shape[1] // bands
    spec_rows = d_spec.shape[0] // bands
    order = range(layers)
    turns = range(1, bands)
    taken = [0]

    def take(count):
        taken[0] += count
        return taken[0] - count

    locals_used = []

    def local(source, target):
        copy = pltpu.make_async_copy(source, target, local_sems.at[len(locals_used)])
        copy.start()
        locals_used.append(copy)
        return copy

    def rows(b):
        return pl.ds(pl.multiple_of(b * quarter, 8), quarter)

    def spec_part(b):
        return pl.ds(pl.multiple_of(b * spec_rows, 8), spec_rows)

    def stream_to(k):
        return lax.rem(stream + k, streams)

    at.greet(
        [(at.band_to(m), stream_to(k)) for k in range(streams) for m in range(bands) if m + k]
    )
    to_core, to_core_split, to_core1 = take(layers), take(layers), take(layers)
    to_layer, to_layer_split, to_layer1 = take(layers), take(layers), take(layers)
    to_band, to_all0, to_all1 = take(bands * layers), take(bands), take(bands)
    to_spec, to_spec_all = take(bands), take(bands)
    def pair_rnn(k):
        at.send(g_rnn0.at[at.across(at.goal(k))], from_core.at[k], to_core + k, (band, other))

    def pair_split(k):
        at.send(g_split.at[at.across(at.goal(k))], from_core_split.at[k], to_core_split + k, (band, other))

    pair_rnn(0)
    pair_rnn(1)
    for m in turns:
        to = at.band_to(m)
        at.send(d_spec.at[spec_part(to)], spec_in.at[m - 1], to_spec + m, (to, stream))
    load0 = [local(g_rnn0.at[at.own(at.goal(k))], own0.at[k]) for k in range(layers)]
    load_split = [local(g_split.at[at.own(at.goal(k))], own_split.at[k]) for k in range(layers)]
    load1 = [local(g, parts1.at[k]) for k, g in enumerate(g_rnn1)]
    load_spec = local(d_spec.at[spec_part(band)], spec_own)
    load_state = [local(back, pieces)]
    pack_base = sum(state[k].shape[1] for k in range(4, 7))
    for t in range(3):
        kind = state[8 * t : 8 * t + 8]
        load_state += [local(a, b) for a, b in zip(kind[:4], held_state[4 * t : 4 * t + 4])]
        for k in range(2):
            base = 0
            for a in kind[4:7]:
                load_state.append(local(a.at[k], packs.at[t, k, pl.ds(base, a.shape[1])]))
                base += a.shape[1]
            packs[t, k, base:] = jnp.zeros_like(packs[t, k, base:])
            length = kind[7].shape[1]
            for h in range(0, length, LANES):
                width = min(LANES, length - h)
                row = base + h // LANES
                packs[t, k, row : row + 1, :width] = kind[7][k : k + 1, h : h + width]
    def first_turn(acc, far, index, k):
        if k < 2:
            at.send(acc.at[k], far.at[k], index + k, (band, at.own(at.goal(0))))

    def second_turn(acc, far, index):
        at.arrive(far.at[1], index + 1)
        acc[2] += far[1]
        at.send(acc.at[2], far.at[2], index + 2, (band, at.own(at.goal(2))))

    def own_total(acc, far, index):
        at.arrive(far.at[0], index)
        at.arrive(far.at[2], index + 2)
        return acc[3] + far[0] + far[2]

    for k in order:
        at.arrive(from_core.at[k], to_core + k)
        if k < 2:
            pair_rnn(k + 2)
        else:
            pair_split(2 * k - 4)
            pair_split(2 * k - 3)
        load0[k].wait()
        from_core[k] += own0[k]
        for m, to in ((1, at.band_across()), (0, at.band_beside(k))):
            at.send(
                from_core.at[k, rows(to)], from_band.at[m, k], to_band + m * layers + k, (at.band_beside(k), stream)
            )
    for k in order:
        at.arrive(from_core_split.at[k], to_core_split + k)
        load_split[k].wait()
        from_core_split[k] += own_split[k]
        first_turn(from_core_split, from_layer_split, to_layer_split, k)
    for copy in load1:
        copy.wait()

    def block(k, carry):
        total = parts1[0, k]
        for b in range(1, bands):
            total = total + parts1[b, k]
        sum1[k] = total
        return carry

    lax.fori_loop(0, streams, block, 0)
    for k in order:
        at.send(sum1.at[at.across(at.goal(k))], from_core1.at[k], to_core1 + k, (band, other))
    for k in order:
        at.arrive(from_core1.at[k], to_core1 + k)
        from_core1[k] += sum1[at.own(at.goal(k))]
        first_turn(from_core1, from_layer1, to_layer1, k)
    for k in order:
        at.arrive(from_band.at[1, k], to_band + layers + k)
        to = at.band_beside(k + 2)
        from_core[k, rows(to)] += from_band[1, k]
        at.send(from_core.at[k, rows(to)], from_band.at[2, k], to_band + 2 * layers + k, (to, stream))
    weights, means, powers = held_state[:4], held_state[4:8], held_state[8:]
    grads = Grads(pieces, rnn0, rnn1, banded, dims)
    slots = dims[0]
    for copy in load_state:
        copy.wait()

    def add_squares(pairs, had):
        return tuple(a + column_sum(b * b) for a, b in zip(had, pairs))

    def early_slot(s, had):
        return add_squares(
            [weights[0][s], weights[1][s], weights[2][s], grads.piece(1, s), grads.piece(2, s)], had
        )

    early = lax.fori_loop(
        0, slots, early_slot, tuple(jnp.zeros((1, weights[k].shape[2]), jnp.float32) for k in (0, 1, 2, 1, 2))
    )
    row = lax.broadcasted_iota(jnp.int32, (quarter, LANES), 0) + band * quarter
    edges = [0]
    for a in state[4:7]:
        edges.append(edges[-1] + a.shape[1])

    def by_array(values):
        edge = edges + [bands * quarter]
        return [
            column_sum(jnp.where((row >= edge[i]) & (row < edge[i + 1]), values, 0.0)) for i in range(4)
        ]

    def both_modules(one):
        found = [by_array(one(k, rows(band))) for k in range(2)]
        return [a + b for a, b in zip(*found)]

    weight_rows = list(early[:3]) + [column_sum(weights[3][...] * weights[3][...])]
    weight_rows += both_modules(lambda k, q: packs[0, k, q] * packs[0, k, q])
    second_turn(from_core_split, from_layer_split, to_layer_split)
    second_turn(from_core1, from_layer1, to_layer1)
    for k in order:
        total = from_core[k, rows(band)]
        for m in (0, 2):
            at.arrive(from_band.at[m, k], to_band + m * layers + k)
            total = total + from_band[m, k]
        held[k] = total
        first_turn(held, from_layer, to_layer, k)
    second_turn(held, from_layer, to_layer)

    def gather_quarters(target, index):
        for m in turns:
            at.send(target.at[rows(band)], target.at[rows(band)], index + m, (at.band_to(m), stream))

    rnn1[rows(band)] = own_total(from_core1, from_layer1, to_layer1)
    banded[...] = own_total(from_core_split, from_layer_split, to_layer_split)
    rnn0[rows(band)] = own_total(held, from_layer, to_layer)

    def send_modules():
        gather_quarters(rnn1, to_all1)
        gather_quarters(rnn0, to_all0)

    def send_spectrum():
        load_spec.wait()
        total = spec_own[...]
        for m in turns:
            at.arrive(spec_in.at[m - 1], to_spec + m)
            total = total + spec_in[m - 1]
        spec_out[spec_part(band)] = total
        for m in turns:
            piece = spec_out.at[spec_part(band)]
            at.send(piece, piece, to_spec_all + m, (at.band_to(m), stream))

    everyone = [(m, k) for k in range(streams) for m in range(bands) if m + k]

    def everywhere(line, turn, meanwhile):
        index = take(streams * bands)
        own = lines.at[turn]
        own[...] = line
        for m, k in everyone:
            i = k * bands + m
            at.send(own, came.at[turn, i], index + i, (at.band_to(m), stream_to(k)))
        meanwhile()
        total = line
        for m, k in everyone:
            i = k * bands + m
            at.arrive(came.at[turn, i], index + i)
            total = total + came[turn, i]
        return total

    main = banded[: slots * dims[1]]
    band_grad = grads.banding(weights[3].shape[1])
    module_rows = both_modules(lambda k, q: (rnn0, rnn1)[k][q] * (rnn0, rnn1)[k][q])
    found = [column_sum(main * main), early[3], early[4], column_sum(band_grad * band_grad)] + module_rows
    grad_total = sum(jnp.sum(x, axis=1, keepdims=True) for x in found)
    totals = everywhere(add_up([grad_total] + weight_rows, 0), 0, send_modules)
    grad_norm = jnp.sqrt(lane_of(totals, 0))
    factor = jnp.minimum(1.0, CLIP_NORM / grad_norm)

    def direction(w, mean_old, power_old, g, decay):
        mean, power = lamb_moments(g, mean_old, power_old, factor)
        return lamb_direction(w, mean, power, decay)

    def slot(s, had):
        return add_squares(
            [
                direction(weights[k][s], means[k][s], powers[k][s], grads.piece(k, s), DECAYS[k])
                for k in range(3)
            ],
            had,
        )

    moved_rows = list(
        lax.fori_loop(0, slots, slot, tuple(jnp.zeros((1, weights[k].shape[2]), jnp.float32) for k in range(3)))
    )
    moved = direction(weights[3][...], means[3][...], powers[3][...], band_grad, DECAYS[3])
    moved_rows.append(column_sum(moved * moved))
    decay = jnp.where(row < edges[3], DECAYS[4], DECAYS[7])

    def module(k, q):
        got = direction(packs[0, k, q], packs[1, k, q], packs[2, k, q], (rnn0, rnn1)[k][q], decay)
        return got * got

    moved_rows += both_modules(module)
    moved = everywhere(add_up(moved_rows, 1), 1, send_spectrum)
    out[0:1] = jnp.sqrt(totals) / jnp.sqrt(moved + 1e-12)
    out[1:2] = jnp.broadcast_to(factor, (1, LANES))
    out[2:3] = jnp.broadcast_to(grad_norm, (1, LANES))
    out[3:8] = jnp.zeros((5, LANES), jnp.float32)
    for m in turns:
        at.arrive(rnn1.at[rows(at.band_from(m))], to_all1 + m)
        at.arrive(rnn0.at[rows(at.band_from(m))], to_all0 + m)
        at.arrive(spec_out.at[spec_part(at.band_from(m))], to_spec_all + m)
    at.finish()


def finish(g_rnn0, g_split, g_rnn1, d_spec, back, state, bands, layers, dims):
    streams = layers * CORES
    rows, split_count = g_rnn0.shape[1], g_split.shape[1]
    quarter = rows // bands
    spec_shape = (d_spec.shape[0] // bands, d_spec.shape[1])
    count = 6 * layers + bands * layers + 4 * bands + 2 * streams * bands
    tile = (8, LANES)

    def vmem(*shape):
        return pltpu.VMEM(shape, jnp.float32)

    return pl.pallas_call(
        partial(finish_kernel, bands, layers, dims),
        out_shape=[
            f32(tile), f32((rows, LANES)), f32((rows, LANES)), f32((split_count, LANES)), f32(d_spec.shape),
        ],
        in_specs=[ANY] * (4 + bands) + ([ANY] * 7 + [VMEM]) * 3,
        out_specs=[VMEM] * 5,
        scratch_shapes=[vmem(*back.shape)]
        + [vmem(*x.shape) for k, x in enumerate(state) if k % 8 < 4]
        + [vmem(3, 2, rows, LANES)]
        + [
            vmem(layers, rows, LANES),
            vmem(layers, split_count, LANES),
            vmem(bands, *g_rnn1[0].shape),
            vmem(streams, quarter, LANES),
            vmem(layers, rows, LANES),
            vmem(layers, split_count, LANES),
            vmem(layers, quarter, LANES),
            vmem(bands - 1, layers, quarter, LANES),
            vmem(layers, quarter, LANES),
            vmem(layers - 1, quarter, LANES),
            vmem(layers - 1, split_count, LANES),
            vmem(layers - 1, quarter, LANES),
            vmem(bands - 1, *spec_shape),
            vmem(*spec_shape),
            vmem(2, streams * bands, 1, LANES),
            vmem(2, 1, LANES),
            pltpu.SemaphoreType.DMA((2 * layers + bands + 2 + 12 + 18,)),
            pltpu.SemaphoreType.DMA((count,)),
            pltpu.SemaphoreType.DMA((count,)),
        ],
        compiler_params=pltpu.CompilerParams(
            collective_id=5, has_side_effects=True, vmem_limit_bytes=VMEM_BYTES
        ),
        cost_estimate=cost(60),
        name="finish",
    )(g_rnn0, g_split, d_spec, back, *g_rnn1, *state)


CHUNK = 4


def update_kernel(dims, scales, d_spec, pieces_in, rnn0_in, rnn1_in, banded_in, *refs):
    state, refs = refs[:24], refs[24:]
    results, masks_out, spec_out, norm_out, refs = refs[:24], refs[24], refs[25], refs[26], refs[27:]
    norm_out[...] = scales[2:3, 0:1]
    pieces, rnn0, rnn1, banded, refs = *refs[:4], refs[4:]
    here, refs = refs[:24], refs[24:]
    made, refs = refs[:24], refs[24:]
    masks, load_sems, store_sems = refs
    weights, means, powers = here[:8], here[8:16], here[16:]
    fresh, new_means, new_powers = made[:8], made[8:16], made[16:]
    slots, piece_rows = dims[0], dims[3]
    grads = Grads(pieces, rnn0, rnn1, banded, dims)
    factor = scales[1:2, 0:1]
    ratios = [lane_of(scales[0:1], 1 + k) for k in range(8)]
    used = [0, 0]

    def copy(pair, which):
        sems = (load_sems, store_sems)[which]
        made_copy = pltpu.make_async_copy(*pair, sems.at[used[which]])
        used[which] += 1
        made_copy.start()
        return made_copy

    def arrays(numbers, sources, targets):
        return [(sources[8 * t + k], targets[8 * t + k]) for k in numbers for t in range(3)]

    def cut(pair, c):
        part = pl.ds(c * CHUNK, CHUNK)
        return pair[0].at[part], pair[1].at[part]

    small = [copy(p, 0) for p in [(rnn0_in, rnn0), (rnn1_in, rnn1), (banded_in, banded)] + arrays(range(3, 8), state, here)]
    chunks = [
        [copy(cut(p, c), 0) for p in [(pieces_in, pieces)] + arrays(range(3), state, here)]
        for c in range(slots // CHUNK)
    ]
    half_rows = d_spec.shape[0] // 2
    for part in range(2):
        spec_out[:, part, :] = d_spec[part * half_rows : (part + 1) * half_rows, : spec_out.shape[2]]

    def one(k, where, g):
        w = weights[k][where]
        mean, power = lamb_moments(g, means[k][where], powers[k][where], factor)
        direction = lamb_direction(w, mean, power, DECAYS[k])
        fresh[k][where] = w - LEARN_RATE * ratios[k] * direction
        new_means[k][where] = mean
        new_powers[k][where] = power

    for got in small:
        got.wait()
    for part in grads.rest(weights[3].shape[1], weights[7].shape[1]):
        one(*part)
    stores = [copy(p, 1) for p in arrays(range(3, 8), made, results)]
    half = pieces.shape[2] // 2
    for c in range(slots // CHUNK):
        for got in chunks[c]:
            got.wait()

        def slot(s, carry):
            for part in grads.of_slot(s):
                one(*part)
            return carry

        lax.fori_loop(c * CHUNK, (c + 1) * CHUNK, slot, 0)
        stores += [copy(cut(p, c), 1) for p in arrays(range(3), made, results)]
    for s in range(slots):
        for part in range(2):
            masks[:, s, part, :] = pieces[s, piece_rows:, part * half : (part + 1) * half]
    stores.append(copy((masks, masks_out), 1))
    for sent in stores:
        sent.wait()


def update(scales, d_spec, grads, state, dims, bins):
    slots, rows, wide = grads[0].shape
    frames = rows - dims[3]
    masks_shape = (frames, slots, 2, wide // 2)
    loads = 18 + 10 * (slots // CHUNK)
    stores = 16 + 9 * (slots // CHUNK)
    return pl.pallas_call(
        partial(update_kernel, dims),
        out_shape=[f32(x.shape) for x in state] + [f32(masks_shape), f32((frames, 2, bins)), f32((1, 1))],
        in_specs=[VMEM] * 2 + [ANY] * 28,
        out_specs=[ANY] * 25 + [VMEM] * 2,
        scratch_shapes=[pltpu.VMEM(x.shape, jnp.float32) for x in tuple(grads) + tuple(state) * 2]
        + [pltpu.VMEM(masks_shape, jnp.float32)]
        + [pltpu.SemaphoreType.DMA((loads,)), pltpu.SemaphoreType.DMA((stores,))],
        compiler_params=PARAMS,
        cost_estimate=cost(10),
        name="update",
    )(scales, d_spec, *grads, *state)


def groups_of(size, slots):
    outer = math.gcd(size, slots)
    inner = size // outer
    across = [[g * inner + i for g in range(outer)] for i in range(inner)]
    within = [[g * inner + i for i in range(inner)] for g in range(outer)]
    return outer, inner, across, within


def sum_everywhere(values, sizes):
    n = sizes[0] * sizes[1]
    row = jnp.zeros((8, LANES), jnp.float32).at[0, : values.shape[0]].set(values)
    spread = jnp.broadcast_to(row[None], (n, 8, LANES))
    got = lax.all_to_all(spread, ("band", "stream"), 0, 0, tiled=True)
    return jnp.sum(got, axis=0)[0, : values.shape[0]]


def pass_along(x, axis, by):
    size = lax.axis_size(axis)
    return lax.ppermute(x, axis, [(k, (k + by) % size) for k in range(size)])


def swap_cores(x):
    return lax.ppermute(x, "stream", [(s, s ^ 1) for s in range(lax.axis_size("stream"))])


def share_slots(shard, outer, across, within, axis):
    slots = shard.shape[0]
    mine = lax.all_to_all(
        shard.reshape((outer, slots // outer) + shard.shape[1:]), "stream", 0, 0,
        axis_index_groups=across, tiled=True,
    )
    inner = len(within[0])
    if inner == CORES:
        return mine, swap_cores(mine)
    both = lax.all_gather(mine, "stream", axis_index_groups=within)
    both = both.reshape((CORES, inner // CORES) + mine.shape)
    if axis == 1:
        both = both.transpose(0, 2, 3, 1, 4, 5)
        both = both.reshape(both.shape[:3] + (-1, both.shape[5]))
    else:
        both = both.transpose(0, 2, 3, 4, 1, 5)
        both = both.reshape(both.shape[:4] + (-1,))
    return both[0], both[1]


def return_slots(keep, send, outer, inner, across, within, axis):
    if inner == CORES:
        mine = keep + swap_cores(send)
    else:
        both = jnp.stack([keep, send])
        half = inner // CORES
        if axis == 1:
            both = both.reshape(both.shape[:3] + (half, -1, both.shape[4])).transpose(0, 3, 1, 2, 4, 5)
        else:
            both = both.reshape(both.shape[:4] + (half, -1)).transpose(0, 4, 1, 2, 3, 5)
        both = both.reshape((inner,) + both.shape[2:])
        mine = lax.psum_scatter(both, "stream", axis_index_groups=within, tiled=False)
    back = lax.all_to_all(mine, "stream", 0, 0, axis_index_groups=across, tiled=True)
    return back.reshape((-1,) + back.shape[2:])


def pack_split(splitter, banding, blocks):
    slots, wide, dmodel = splitter.shape
    columns = banding.shape[1] // blocks
    strips = -(-columns // LANES)
    main = splitter.reshape(slots, blocks, wide // blocks, dmodel).transpose(1, 0, 2, 3)
    flat = banding.reshape(slots, blocks, columns).transpose(1, 0, 2)
    flat = jnp.pad(flat, ((0, 0), (0, SLOT_PAD - slots), (0, strips * LANES - columns)))
    flat = flat.reshape(blocks, SLOT_PAD, strips, LANES).transpose(0, 2, 1, 3)
    return jnp.concatenate(
        [main.reshape(blocks, slots * wide // blocks, dmodel), flat.reshape(blocks, -1, LANES)], axis=1
    )


def unpack_banding(pack, start, slots, columns):
    blocks = pack.shape[0]
    flat = pack[:, start:].reshape(blocks, -1, SLOT_PAD, LANES)[:, :, :slots].transpose(2, 0, 1, 3)
    return flat.reshape(slots, blocks, -1)[:, :, :columns].reshape(slots, blocks * columns)


def body(spectrum, segments, widths, groups, cotangent, *state):
    weights, means_old, powers_old = state[:8], state[8:16], state[16:]
    splitter, widener, masker, banding, intake, recurrence, outtake, scalers = weights
    group_count = lax.axis_size("band")
    stream_count = lax.axis_size("stream")
    my_stream = lax.axis_index("stream")
    slots = splitter.shape[0]
    frames = spectrum.shape[0]
    quarter = frames // group_count
    outer, inner, across, within = groups_of(stream_count, slots)
    share = slots // outer
    r = masker.shape[1] * stream_count // (2 * outer)
    dmodel = splitter.shape[2]
    hidden = recurrence.shape[2]
    wide = splitter.shape[1] * stream_count
    bins = spectrum.shape[2]
    blocks, out_rows, weight_rows, vec_share, vec_rows, rows = pack_rows(dmodel, hidden)
    slot_rows = wide // blocks
    columns = banding.shape[1] * stream_count // blocks
    direct = stream_count == blocks and inner == CORES and outer == 4 and group_count == 4

    padded = ((bins - 1) // LANES + 2) * LANES
    spec = jnp.pad(
        spectrum.transpose(1, 0, 2).reshape(2 * frames, bins), ((0, 0), (0, padded - bins))
    )

    if direct:
        rnn0, w_split, later, pieces = gather_front(
            intake.reshape(2, 2 * dmodel, LANES), recurrence.reshape(2, 2 * hidden, LANES), outtake, scalers,
            splitter.reshape(slots * slot_rows, dmodel), banding, masker, widener.transpose(0, 2, 1), cotangent,
            rows, group_count, outer,
        )
        near = [later] + [pass_along(later, "band", m) for m in range(1, group_count)]
        pieces = pieces.reshape((outer, share) + pieces.shape[1:])
        mine = lax.all_to_all(pieces, "stream", 0, 0, axis_index_groups=across, tiled=True)
    else:
        whole = (
            lax.all_gather(intake, "stream", axis=3, tiled=True),
            lax.all_gather(recurrence, "stream", axis=3, tiled=True),
            lax.all_gather(outtake, "stream", axis=1, tiled=True),
            lax.all_gather(scalers, "stream", axis=1, tiled=True),
        )
        rnn0, rnn1 = (
            pack_rnn(whole[0][k], whole[1][k], whole[2][k], whole[3][k : k + 1], rows, vec_share)
            for k in range(2)
        )
        w_split = pack_split(
            lax.all_gather(splitter, "stream", axis=1, tiled=True),
            lax.all_gather(banding, "stream", axis=1, tiled=True),
            blocks,
        )
        w_mask = share_slots(masker, outer, across, within, 1)
        w_wide = share_slots(widener.transpose(0, 2, 1), outer, across, within, 1)
        cot_parts = cotangent.reshape(frames, outer, share, wide).transpose(1, 2, 0, 3)
        cot = lax.all_to_all(cot_parts, "stream", 0, 0, axis_index_groups=across, tiled=True)
        mine, other = (
            jnp.concatenate([pack_pieces(w_mask[k], w_wide[k]), cot], axis=2) for k in range(CORES)
        )
    piece_rows = mine.shape[2] - frames
    base = 2 * wide + dmodel
    sizes = (group_count, slots, share, inner, direct, blocks * columns, slot_rows, hidden)
    got = time_forward(segments, widths[None], groups[None], spec, w_split, rnn0, sizes)
    slot_places, clips, slot_of, band_of, mask_places = got[:5]
    time_out, v_band, time_saved = got[5], got[6], got[7:]
    parts = group_count if direct else 1
    if direct:
        time_out, near = lax.optimization_barrier((time_out, near))
        rnn1 = near
    else:
        rnn1 = [rnn1]
        time_out = lax.all_to_all(time_out, "band", 0, 0, tiled=True)
    pack_shape = (blocks, rows, LANES)
    got = band_forward(
        slot_of, band_of, time_out.reshape(group_count * slots, quarter, dmodel), rnn1, pack_shape, parts, hidden
    )
    band_out, band_saved, rnn1 = got[0], got[1:8], got[8]
    band_out = band_out.reshape(group_count, outer, share, quarter, dmodel)
    if direct:
        back, grad_back, g_mask_vec = mask_exchange(mask_places, band_out, mine, v_band, base, piece_rows)
        back = lax.all_to_all(back, "stream", 0, 0, axis_index_groups=across, tiled=True)
        back = back.reshape((slots,) + back.shape[2:])
    else:
        band_out = lax.all_to_all(band_out, "stream", 1, 1, axis_index_groups=across, tiled=True)
        band_out = lax.all_to_all(band_out, "band", 0, 0, tiled=True)
        keep, send, grad_back, g_mask_vec = mask_network(
            mask_places, band_out, mine, other, v_band, base, piece_rows
        )
        grad_back = lax.all_to_all(grad_back, "band", 0, 0, tiled=True)
        grad_back = lax.all_to_all(grad_back, "stream", 1, 1, axis_index_groups=across, tiled=True)
        kept, sent = unpack_pieces(keep[:, :, :piece_rows], r), unpack_pieces(send, r)
        mask_reduced = return_slots(kept[0], sent[0], outer, inner, across, within, 1)
        widened_reduced = return_slots(kept[1], sent[1], outer, inner, across, within, 1).transpose(0, 2, 1)
        mask_parts = keep[:, :, piece_rows:]
        mask_parts = lax.all_to_all(mask_parts, "stream", 0, 0, axis_index_groups=across, tiled=True)
    grad_back = grad_back.reshape(group_count * slots, quarter, dmodel)
    band_grad, *g_rnn1 = band_backward(
        slot_of, band_of, grad_back, rnn1, band_saved, parts, hidden
    )
    grad_time = band_grad.reshape(group_count, slots, quarter, dmodel)
    if not direct:
        grad_time = lax.all_to_all(grad_time, "band", 0, 0, tiled=True)
    if direct:
        g_rnn1 = g_rnn1[:1] + [pass_along(g, "band", m) for m, g in enumerate(g_rnn1) if m]
    d_spec, g_split, g_rnn0 = time_backward(
        slot_places, clips, (my_stream // inner).astype(jnp.int32)[None], grad_time, spec, time_saved, w_split,
        v_band, rnn0, g_mask_vec, slot_rows, hidden,
    )
    if direct:
        dims = (slots, slot_rows, r, piece_rows, dmodel, hidden)
        state = tuple(x.transpose(0, 2, 1) if k % 8 == 1 else x for k, x in enumerate(state))
        scales, g_rnn0, g_rnn1, g_split, d_spec = finish(
            g_rnn0, g_split, g_rnn1, d_spec, back,
            tuple(x.reshape(2, -1, LANES) if k % 8 in (4, 5) else x for k, x in enumerate(state)),
            group_count, outer, dims,
        )
    else:
        d_spec = lax.psum(d_spec, "band")

    if not direct:
        masks = mask_parts.reshape(slots, frames, wide).transpose(1, 0, 2).reshape(cotangent.shape)
        spectrum_grad = d_spec.reshape(2, frames, padded)[:, :, :bins].transpose(1, 0, 2)

    if direct:
        *stepped, masks, spectrum_grad, grad_norm = update(scales, d_spec, (back, g_rnn0, g_rnn1, g_split), state, dims, bins)
        stepped = [x.transpose(0, 2, 1) if k % 8 == 1 else x for k, x in enumerate(stepped)]
        return (masks, spectrum_grad, grad_norm.reshape(())) + tuple(stepped)
    first, second = unpack_rnn(g_rnn0, dmodel, hidden), unpack_rnn(g_rnn1[0], dmodel, hidden)
    rnn_grads = [jnp.stack([a, b]) for a, b in zip(first[:3], second[:3])]
    rnn_grads.append(jnp.concatenate([first[3], second[3]], axis=0))
    rnn_grads = [
        lax.psum(lax.psum_scatter(g, "stream", scatter_dimension=d, tiled=True), "band")
        for g, d in zip(rnn_grads, (3, 3, 1, 1))
    ]
    g_band = unpack_banding(g_split, slots * slot_rows, slots, columns)
    g_split = g_split[:, : slots * slot_rows].reshape(blocks, slots, slot_rows, dmodel)
    g_split = g_split.transpose(1, 0, 2, 3).reshape(slots, wide, dmodel)
    split_reduced = lax.psum_scatter(g_split, "stream", scatter_dimension=1, tiled=True)
    band_reduced = lax.psum_scatter(g_band, "stream", scatter_dimension=1, tiled=True)
    reduced = (split_reduced, widened_reduced, mask_reduced, band_reduced) + tuple(rnn_grads)

    shares = (1.0,) * 4 + (1.0 / group_count,) * 4
    sizes = (group_count, stream_count)
    sums = [sum(jnp.sum(g * g) * part for g, part in zip(reduced, shares))]
    sums += [jnp.sum(w * w) * part for w, part in zip(weights, shares)]
    totals = sum_everywhere(jnp.stack(sums), sizes)
    grad_norm = jnp.sqrt(totals[0])
    factor = jnp.minimum(1.0, CLIP_NORM / grad_norm)
    moments = [lamb_moments(g, m, p, factor) for g, m, p in zip(reduced, means_old, powers_old)]
    directions = [lamb_direction(w, m, p, d) for w, (m, p), d in zip(weights, moments, DECAYS)]
    update_totals = sum_everywhere(
        jnp.stack([jnp.sum(d * d) * part for d, part in zip(directions, shares)]), sizes
    )
    ratios = jnp.sqrt(totals[1:]) / jnp.sqrt(update_totals + 1e-12)
    fresh = [w - LEARN_RATE * ratios[k] * d for k, (w, d) in enumerate(zip(weights, directions))]
    return (
        (masks, spectrum_grad, grad_norm)
        + tuple(fresh)
        + tuple(m for m, unused in moments)
        + tuple(p for unused, p in moments)
    )


def solution(mesh):
    stored = (
        P("band", "stream", None),
        P("band", None, "stream"),
        P("band", "stream", None),
        P("band", "stream"),
        P(None, None, None, "stream"),
        P(None, None, None, "stream"),
        P(None, "stream", None),
        P(None, "stream"),
    )
    frames_over = P("stream", None, None)
    mask_over = P("stream", "band", None, None)
    return jax.shard_map(
        body,
        mesh=mesh,
        in_specs=(frames_over, P("stream", None), P(), P(), mask_over) + stored * 3,
        out_specs=(mask_over, frames_over, P()) + stored * 3,
        check_vma=False,
    )
```

```python
from functools import partial
import math

import jax
import jax.numpy as jnp
from jax import lax
from jax.experimental import pallas as pl
from jax.experimental.pallas import tpu as pltpu
from jax.sharding import PartitionSpec as P

STEP = 10
CLIP_NORM = 5.0
LEARN_RATE = 0.5
BETA_ONE = 0.9
BETA_TWO = 0.999
ADAM_EPS = 1e-06
DECAY_RATE = 0.01
NORM_EPS = 1e-05
VAR_FLOOR = 0.25
CLIPS = 3
CLIP_MOST = 32
LANES = 128
VMEM_BYTES = 60 * 1024 * 1024
CORES = 2
SLOT_PAD = 16
MESH = pl.DeviceIdType.MESH

AB = (((1,), (0,)), ((), ()))
ABT = (((1,), (1,)), ((), ()))
ATB = (((0,), (0,)), ((), ()))


def split(x):
    hi = x.astype(jnp.bfloat16)
    lo = (x - hi.astype(jnp.float32)).astype(jnp.bfloat16)
    return hi, lo


def dot1(a, b, dims):
    return lax.dot_general(a, b, dims, preferred_element_type=jnp.float32)


def dot_parts(a, b, dims):
    return dot1(a[0], b[0], dims) + (dot1(a[1], b[0], dims) + dot1(a[0], b[1], dims))


def dot3(a, b, dims):
    return dot_parts(split(a), split(b), dims)


def sigmoid(x):
    return 0.5 * jnp.tanh(0.5 * x) + 0.5


def norm_stats(x):
    center = x - jnp.mean(x, axis=-1, keepdims=True)
    spread = jnp.mean(center * center, axis=-1, keepdims=True)
    scale = lax.rsqrt(spread + NORM_EPS)
    return center * scale, scale


def norm_back(grad_unit, unit, scale):
    first = jnp.mean(grad_unit, axis=-1, keepdims=True)
    second = jnp.mean(grad_unit * unit, axis=-1, keepdims=True)
    return scale * (grad_unit - first - unit * second)


def column_sum(x):
    return jnp.sum(x, axis=0, keepdims=True)


def pack_rows(dmodel, hidden):
    blocks = 4 * hidden // LANES
    out_rows = 2 * hidden // blocks
    weight_rows = 2 * dmodel + 2 * hidden + out_rows
    share = (2 * dmodel + 8 * hidden + dmodel) // blocks
    vec_rows = -(-share // LANES)
    return blocks, out_rows, weight_rows, share, vec_rows, -(-(weight_rows + vec_rows) // 32) * 32


def pack_rnn(w_in, w_rec, w_out, vec, rows, share):
    count = w_in.shape[2] // LANES
    parts = [
        w.reshape(2 * w.shape[1], count, LANES).transpose(1, 0, 2) for w in (w_in, w_rec)
    ] + [w_out.reshape(count, -1, LANES)]
    used = sum(p.shape[1] for p in parts)
    flat = jnp.pad(vec.reshape(count, share), ((0, 0), (0, (rows - used) * LANES - share)))
    return jnp.concatenate(parts + [flat.reshape(count, rows - used, LANES)], axis=1)


def unpack_rnn(pack, dmodel, hidden):
    blocks, out_rows, weight_rows, share, vec_rows, rows = pack_rows(dmodel, hidden)
    count = pack.shape[0]
    cuts = (0, 2 * dmodel, 2 * dmodel + 2 * hidden)
    w_in = pack[:, : cuts[1]].reshape(count, 2, dmodel, LANES).transpose(1, 2, 0, 3)
    w_rec = pack[:, cuts[1] : cuts[2]].reshape(count, 2, hidden, LANES).transpose(1, 2, 0, 3)
    return (
        w_in.reshape(2, dmodel, count * LANES),
        w_rec.reshape(2, hidden, count * LANES),
        pack[:, cuts[2] : weight_rows].reshape(count * out_rows, LANES),
        unpack_vec(pack, weight_rows, vec_rows, share),
    )


def unpack_vec(pack, weight_rows, vec_rows, share):
    count = pack.shape[0]
    flat = pack[:, weight_rows : weight_rows + vec_rows].reshape(count, vec_rows * LANES)
    return flat[:, :share].reshape(1, count * share)


class Pack:
    def __init__(self, ref, dmodel, hidden):
        self.ref, self.dmodel, self.hidden = ref, dmodel, hidden
        self.blocks, self.out_rows = pack_rows(dmodel, hidden)[:2]

    def intake(self, e, first, last):
        rows = slice(e * self.dmodel, (e + 1) * self.dmodel)
        return jnp.concatenate([self.ref[k, rows] for k in range(first, last)], axis=1)

    def recurrence(self, e, k):
        base = 2 * self.dmodel + e * self.hidden
        return self.ref[k, base : base + self.hidden]

    def outtake(self, e):
        base = 2 * self.dmodel + 2 * self.hidden
        half = self.blocks // 2
        return jnp.concatenate(
            [self.ref[k, base : base + self.out_rows] for k in range(half * e, half * (e + 1))], axis=0
        )

    def put(self, k, base, value):
        if len(self.ref.shape) == 3:
            self.ref[k, base : base + value.shape[0]] = value
            return
        quarter = self.ref.shape[2]
        done = 0
        while done < value.shape[0]:
            part, at = divmod(base + done, quarter)
            count = min(value.shape[0] - done, quarter - at)
            self.ref[part, k, at : at + count] = value[done : done + count]
            done += count

    def put_intake(self, e, q, value):
        for h in range(value.shape[1] // LANES):
            self.put(q * value.shape[1] // LANES + h, e * self.dmodel, value[:, h * LANES : (h + 1) * LANES])

    def put_recurrence(self, e, q, value):
        base = 2 * self.dmodel + e * self.hidden
        for h in range(value.shape[1] // LANES):
            self.put(q * value.shape[1] // LANES + h, base, value[:, h * LANES : (h + 1) * LANES])

    def put_outtake(self, e, value):
        base = 2 * self.dmodel + 2 * self.hidden
        for k in range(self.blocks // 2):
            self.put(self.blocks // 2 * e + k, base, value[k * self.out_rows : (k + 1) * self.out_rows])

    def put_vec(self, value):
        unused, unused, base, share, vec_rows, rows = pack_rows(self.dmodel, self.hidden)
        for k in range(self.blocks):
            block = [
                value[:, k * share + r * LANES : k * share + min(share, (r + 1) * LANES)] for r in range(vec_rows)
            ]
            block[-1] = jnp.concatenate(
                [block[-1], jnp.zeros((1, vec_rows * LANES - share), jnp.float32)], axis=1
            )
            block.append(jnp.zeros((rows - base - vec_rows, LANES), jnp.float32))
            self.put(k, base, jnp.concatenate(block, axis=0))


def load_vec(pack, vec):
    unused, unused, base, share, vec_rows, unused = pack_rows(pack.dmodel, pack.hidden)
    for k in range(pack.blocks):
        for r in range(vec_rows):
            width = min(LANES, share - r * LANES)
            at = k * share + r * LANES
            vec[0:1, at : at + width] = pack.ref[k, base + r : base + r + 1, :width]


def split_recurrence(pack, hi_ref, lo_ref):
    for e in range(2):
        for k in range(pack.blocks):
            part = slice(k * LANES, (k + 1) * LANES)
            hi_ref[e, :, part], lo_ref[e, :, part] = split(pack.recurrence(e, k))


def split_recurrence_turned(pack, hi_ref, lo_ref):
    for e in range(2):
        for k in range(pack.blocks):
            part = slice(k * LANES, (k + 1) * LANES)
            hi_ref[e, part], lo_ref[e, part] = split(pack.recurrence(e, k).T)


def gates_forward(x_flat, act, pack, vec, rows, block):
    hidden4 = 4 * pack.hidden
    dmodel = pack.dmodel
    parts = [split(pack.intake(e, 0, pack.blocks)) for e in range(2)]

    def one(r, carry):
        start = pl.multiple_of(r * block, block)
        unit, unused = norm_stats(x_flat(start, block))
        n = split(unit * (1.0 + vec[0:1, :dmodel]) + vec[0:1, dmodel : 2 * dmodel])
        for e in range(2):
            bias = vec[0:1, 2 * dmodel + hidden4 * e : 2 * dmodel + hidden4 * (e + 1)]
            z = dot_parts(n, parts[e], AB) + bias
            act[e][pl.ds(r * (block // 16), block // 16)] = z.reshape(block // 16, 16, hidden4)
        return carry

    lax.fori_loop(0, rows // block, one, 0)


def run_forward(steps, places, act, c, h, pack, hi_ref, lo_ref, state, memory):
    hidden = pack.hidden
    for e in range(2):
        state[e][...] = jnp.zeros_like(state[e])
        memory[e][...] = jnp.zeros_like(memory[e])

    def step(j, carry):
        work = []
        for e in range(2):
            at = places(e, j)
            prior = state[e][...]
            hi, lo = split(prior)
            rows = prior.shape[0]
            first = dot1(jnp.concatenate([hi, lo], axis=0), hi_ref[e], AB)
            drive = [act[e][p] for p in at]
            drive = drive[0] if len(drive) == 1 else jnp.concatenate(drive, axis=0)
            z = first[:rows] + first[rows:] + dot1(hi, lo_ref[e], AB) + drive
            work.append((at, z))
        for e in range(2):
            at, z = work[e]
            ingate = sigmoid(z[:, :hidden])
            forget = sigmoid(z[:, hidden : 2 * hidden])
            candidate = jnp.tanh(z[:, 2 * hidden : 3 * hidden])
            outgate = sigmoid(z[:, 3 * hidden :])
            before = memory[e][...]
            now = forget * before + ingate * candidate
            squashed = jnp.tanh(now)
            out = outgate * squashed
            memory[e][...] = now
            state[e][...] = out
            for k, p in enumerate(at):
                part = slice(16 * k, 16 * (k + 1))
                act[e][p, :, :hidden] = ingate[part]
                act[e][p, :, hidden : 2 * hidden] = forget[part]
                act[e][p, :, 2 * hidden : 3 * hidden] = candidate[part]
                act[e][p, :, 3 * hidden :] = outgate[part]
                c[e][p] = now[part]
                h[e][p] = out[part]
        return carry

    lax.fori_loop(0, steps, step, 0, unroll=4)


def output_forward(count, h, pack, vec):
    hidden = h[0].shape[2]
    dmodel = pack.dmodel
    total = vec[0:1, vec.shape[1] - dmodel :]
    for e in range(2):
        states = h[e][:count].reshape(count * 16, hidden)
        total = total + dot3(states, pack.outtake(e), AB)
    return total


def run_backward(steps, places, act, dz_ref, c, dh, pack, hi_ref, lo_ref, grad_h, grad_c):
    hidden = pack.hidden
    for e in range(2):
        grad_h[e][...] = jnp.zeros_like(grad_h[e])
        grad_c[e][...] = jnp.zeros_like(grad_c[e])

    def load(ref, at):
        got = [ref[p] for p in at]
        return got[0] if len(got) == 1 else jnp.concatenate(got, axis=0)

    def step(back, carry):
        j = steps - 1 - back
        later = jnp.minimum(j, 1).astype(jnp.float32)
        work = []
        for e in range(2):
            at = places(e, j)
            gates = load(act[e], at)
            ingate = gates[:, :hidden]
            forget = gates[:, hidden : 2 * hidden]
            candidate = gates[:, 2 * hidden : 3 * hidden]
            outgate = gates[:, 3 * hidden :]
            squashed = jnp.tanh(load(c[e], at))
            before = load(c[e], places(e, jnp.maximum(j - 1, 0))) * later
            total_h = load(dh[e], at) + grad_h[e][...]
            total_c = grad_c[e][...] + total_h * outgate * (1.0 - squashed * squashed)
            dz = jnp.concatenate(
                [
                    total_c * candidate * ingate * (1.0 - ingate),
                    total_c * before * forget * (1.0 - forget),
                    total_c * ingate * (1.0 - candidate * candidate),
                    total_h * squashed * outgate * (1.0 - outgate),
                ],
                axis=1,
            )
            grad_c[e][...] = total_c * forget
            for k, p in enumerate(at):
                dz_ref[e][p] = dz[16 * k : 16 * (k + 1)]
            work.append(dz)
        for e in range(2):
            hi, lo = split(work[e])
            rows = hi.shape[0]
            first = dot1(jnp.concatenate([hi, lo], axis=0), hi_ref[e], AB)
            grad_h[e][...] = first[:rows] + first[rows:] + dot1(hi, lo_ref[e], AB)
        return carry

    lax.fori_loop(0, steps, step, 0, unroll=4)


def states_backward(count, dy_flat, dh, h, pack, g_pack):
    hidden = h[0].shape[2]
    dy = split(dy_flat)
    for e in range(2):
        dh[e][:count] = dot_parts(dy, split(pack.outtake(e)), ABT).reshape(count, 16, hidden)
        g_pack.put_outtake(e, dot3_parts_first(h[e][:count].reshape(count * 16, hidden), dy))


def dot3_parts_first(a, b_parts):
    return dot_parts(split(a), b_parts, ATB)


def gates_backward(count, x_flat, dy_flat, dz_ref, before, pack, vec, g_pack, g_vec):
    dmodel, hidden = pack.dmodel, pack.hidden
    hidden4 = 4 * hidden
    rows = count * 16
    unit, scale = norm_stats(x_flat)
    gain = 1.0 + vec[0:1, :dmodel]
    n = unit * gain + vec[0:1, dmodel : 2 * dmodel]
    dn = jnp.zeros((rows, dmodel), jnp.float32)
    for e in range(2):
        left_hi, left_lo = split(jnp.concatenate([n, before(e)], axis=1).T)
        left = jnp.concatenate([left_hi, left_lo], axis=0)
        height = left_hi.shape[0]
        for q in range(4):
            part = slice(hidden * q, hidden * (q + 1))
            dz_q = dz_ref[e][:count, :, part].reshape(rows, hidden)
            dz = split(dz_q)
            first = dot1(left, dz[0], AB)
            got = first[:height] + first[height:] + dot1(left_hi, dz[1], AB)
            g_pack.put_intake(e, q, got[:dmodel])
            g_pack.put_recurrence(e, q, got[dmodel:])
            dn = dn + dot_parts(dz, split(pack.intake(e, q * pack.blocks // 4, (q + 1) * pack.blocks // 4)), ABT)
            base = 2 * dmodel + hidden4 * e + hidden * q
            g_vec[0:1, base : base + hidden] = column_sum(dz_q)
    g_vec[0:1, :dmodel] = column_sum(dn * unit)
    g_vec[0:1, dmodel : 2 * dmodel] = column_sum(dn)
    g_vec[0:1, vec.shape[1] - dmodel :] = column_sum(dy_flat)
    g_pack.put_vec(g_vec[...])
    return dy_flat + norm_back(dn * gain, unit, scale)


def input_backward(count, x_flat, dy_flat, dz_ref, pack, vec, g_vec):
    dmodel, hidden = pack.dmodel, pack.hidden
    rows = count * 16
    unit, scale = norm_stats(x_flat)
    gain = 1.0 + vec[0:1, :dmodel]
    dn = jnp.zeros((rows, dmodel), jnp.float32)
    for e in range(2):
        for q in range(4):
            part = slice(hidden * q, hidden * (q + 1))
            dz = split(dz_ref[e][:count, :, part].reshape(rows, hidden))
            dn = dn + dot_parts(dz, split(pack.intake(e, q * pack.blocks // 4, (q + 1) * pack.blocks // 4)), ABT)
    g_vec[0:1, :dmodel] = column_sum(dn * unit)
    g_vec[0:1, dmodel : 2 * dmodel] = column_sum(dn)
    g_vec[0:1, vec.shape[1] - dmodel :] = column_sum(dy_flat)
    return dy_flat + norm_back(dn * gain, unit, scale)


def weights_backward(count, x_flat, dz_ref, before, pack, vec, g_pack, g_vec):
    dmodel, hidden = pack.dmodel, pack.hidden
    rows = count * 16
    unit, unused = norm_stats(x_flat)
    n = unit * (1.0 + vec[0:1, :dmodel]) + vec[0:1, dmodel : 2 * dmodel]
    for e in range(2):
        left_hi, left_lo = split(jnp.concatenate([n, before(e)], axis=1).T)
        left = jnp.concatenate([left_hi, left_lo], axis=0)
        height = left_hi.shape[0]
        for q in range(4):
            part = slice(hidden * q, hidden * (q + 1))
            dz_q = dz_ref[e][:count, :, part].reshape(rows, hidden)
            dz = split(dz_q)
            first = dot1(left, dz[0], AB)
            got = first[:height] + first[height:] + dot1(left_hi, dz[1], AB)
            g_pack.put_intake(e, q, got[:dmodel])
            g_pack.put_recurrence(e, q, got[dmodel:])
            base = 2 * dmodel + 4 * hidden * e + hidden * q
            g_vec[0:1, base : base + hidden] = column_sum(dz_q)
    g_pack.put_vec(g_vec[...])


def shifted(ref, e, count, hidden, mask):
    rows = (count - 1) * 16
    zero = jnp.zeros((16, hidden), jnp.float32)
    if e == 0:
        kept = ref[: count - 1].reshape(rows, hidden) * mask
        return jnp.concatenate([zero, kept], axis=0)
    kept = ref[1:count].reshape(rows, hidden) * mask
    return jnp.concatenate([kept, zero], axis=0)


def tables_kernel(
    slots, share, inner, direct, segments, widths, groups, places, clips, slot_of, band_of, mask_places, counts
):
    band, stream = lax.axis_index("band"), lax.axis_index("stream")
    for s in range(slots):
        places[0, s] = 0
        places[1, s] = 0
    for s in range(band_of.shape[1]):
        band_of[0, s] = 0
        band_of[1, s] = 0
    for c in range(CLIPS):
        clips[1, c] = 0
    for g in range(counts.shape[0]):
        counts[g] = 0

    def one_band(b, edge):
        g = groups[0, b]
        rank = counts[g]
        counts[g] = rank + 1
        slot_of[0, b] = g * slots + rank
        band_of[0, g * slots + rank] = b
        band_of[1, g * slots + rank] = 1
        width = widths[0, b]

        @pl.when(g == band)
        def mine():
            places[0, rank] = edge
            places[1, rank] = width

        return edge + width

    lax.fori_loop(0, groups.shape[1], one_band, jnp.int32(0))

    def one_frame(t, carry):
        c = segments[0, t]
        clips[1, c] = clips[1, c] + 1
        return carry

    lax.fori_loop(0, segments.shape[1], one_frame, 0)
    start = jnp.int32(0)
    for c in range(CLIPS):
        clips[0, c] = start
        start = start + clips[1, c]
    for j in range(share):
        row = lax.div(stream, inner) * share + j
        mask_places[0, j] = places[1, row]
        mask_places[1, j] = lax.rem(stream, CORES) if direct else jnp.int32(0)
        mask_places[2, j] = row


def table_shapes(slots, share, bands, parts):
    shapes = ((2, slots), (2, CLIPS), (1, bands), (2, parts * slots), (3, share))
    return [jax.ShapeDtypeStruct(x, jnp.int32) for x in shapes]


def clip_places(clips, spare):
    def places(e, j):
        found = []
        for c in range(CLIPS):
            start, length = clips[0, c], clips[1, c]
            frame = start + j if e == 0 else start + length - 1 - j
            found.append(jnp.where(j < length, frame, spare))
        return found

    return places


def window_of(edge):
    base = pl.multiple_of((edge // LANES) * LANES, LANES)
    return base, lax.rem(edge, LANES)


def where_valid(width, frames):
    lane = lax.broadcasted_iota(jnp.int32, (frames, LANES), 1)
    inside = (lane < width).astype(jnp.float32)
    return jnp.concatenate([inside, inside], axis=1), jnp.maximum(2 * width, 1).astype(jnp.float32)


def split_rows(spec, edge, width, frames):
    wmax = LANES
    base, shift = window_of(edge)
    window = spec[:, pl.ds(base, 2 * LANES)]
    taken = pltpu.roll(window, lax.rem(2 * LANES - shift, 2 * LANES), 1)[:, :wmax]
    taken = jnp.concatenate([taken[:frames], taken[frames:]], axis=1)
    valid, entries = where_valid(width, frames)
    mean = jnp.sum(taken * valid, axis=-1, keepdims=True) / entries
    center = (taken - mean) * valid
    spread = jnp.sum(center * center, axis=-1, keepdims=True) / entries
    scale = lax.rsqrt(jnp.maximum(spread, VAR_FLOOR))
    moving = jnp.where(spread > VAR_FLOOR, 1.0, jnp.where(spread == VAR_FLOOR, 0.5, 0.0))
    return center * scale, scale, valid, moving, entries


def slot_weights(w_split, s, slot_rows):
    count = w_split.shape[0]
    at = pl.ds(pl.multiple_of(s * slot_rows, slot_rows), slot_rows)
    return jnp.concatenate([w_split[k, at, :] for k in range(count)], axis=0)


def time_forward_kernel(
    slot_rows, share, inner, direct, segments, widths, groups, spec_in, w_split_in, rnn_in,
    places_s, clips, slot_of, band_of, mask_places, out, v_band, x, *refs,
):
    saved, refs = refs[:6], refs[6:]
    act0, act1, c0, c1, h0, h1, hi_ref, lo_ref, s0, s1, m0, m1, y, mixed, vec, rnn, w_split, spec, *refs = refs
    counts, sems = refs
    slots = out.shape[1]
    frames, unused, dmodel = x.shape
    wide = w_split.shape[0] * slot_rows
    pack = Pack(rnn, dmodel, h0.shape[2])
    load_split = pltpu.make_async_copy(w_split_in, w_split, sems.at[7])
    load_spec = pltpu.make_async_copy(spec_in, spec, sems.at[8])
    load_rnn = pltpu.make_async_copy(rnn_in, rnn, sems.at[0])
    for copy in (load_split, load_spec, load_rnn):
        copy.start()
    tables_kernel(
        slots, share, inner, direct, segments, widths, groups, places_s, clips, slot_of, band_of, mask_places, counts
    )
    load_split.wait()
    load_spec.wait()
    v_band[...] = jnp.zeros_like(v_band)
    columns = v_band.shape[1] // w_split.shape[0]
    for k in range(w_split.shape[0]):
        for h in range(0, columns, LANES):
            width = min(LANES, columns - h)
            at = slots * slot_rows + SLOT_PAD * (h // LANES)
            v_band[:, k * columns + h : k * columns + h + width] = w_split[k, at : at + SLOT_PAD, :width]
    x[...] = jnp.zeros_like(x)
    for a in (act0, act1):
        a[frames] = jnp.zeros_like(a[frames])

    for s in range(slots):
        unit, unused, valid, moving, entries = split_rows(spec, places_s[0, s], places_s[1, s], frames)
        row = v_band[s : s + 1, : 2 * wide + dmodel]
        z = (unit * (1.0 + row[:, :wide]) + row[:, wide : 2 * wide]) * valid
        y[s] = dot3(z, slot_weights(w_split, s, slot_rows), AB) + row[:, 2 * wide : 2 * wide + dmodel]
    for s in range(slots):
        x[:, s, :] = y[s]
    load_rnn.wait()
    load_vec(pack, vec)
    split_recurrence(pack, hi_ref, lo_ref)
    act = (act0, act1)

    def x_flat(start, size):
        return x[pl.ds(start // 16, size // 16)].reshape(size, dmodel)

    gates_forward(x_flat, act, pack, vec, frames * 16, 256)
    run_forward(
        CLIP_MOST, clip_places(clips, frames), act, (c0, c1), (h0, h1),
        pack, hi_ref, lo_ref, (s0, s1), (m0, m1),
    )
    leaving = [
        pltpu.make_async_copy(a, b, sems.at[1 + k])
        for k, (a, b) in enumerate(zip((act0, act1, c0, c1, h0, h1), saved))
    ]
    for copy in leaving:
        copy.start()
    total = output_forward(frames, (h0, h1), pack, vec)
    x_all = x[...].reshape(frames * 16, dmodel)
    mixed[...] = (x_all + total).reshape(frames, 16, dmodel)
    parts, unused_slots, quarter, unused = out.shape
    for s in range(slots):
        for q in range(parts):
            out[q, s] = mixed[q * quarter : (q + 1) * quarter, s, :]
    for copy in leaving:
        copy.wait()


def f32(shape):
    return jax.ShapeDtypeStruct(shape, jnp.float32)


def saved_shapes(count, hidden):
    return [f32((count, 16, 4 * hidden))] * 2 + [f32((count, 16, hidden))] * 4


def saved_scratch(count, hidden):
    return [pltpu.VMEM(x.shape, jnp.float32) for x in saved_shapes(count, hidden)]


def vec_scratch(dmodel, hidden):
    return pltpu.VMEM((1, 3 * dmodel + 8 * hidden), jnp.float32)


def rec_scratch(rows, hidden, turned=False):
    return [
        pltpu.VMEM((2, 4 * hidden, hidden) if turned else (2, hidden, 4 * hidden), jnp.bfloat16),
        pltpu.VMEM((2, 4 * hidden, hidden) if turned else (2, hidden, 4 * hidden), jnp.bfloat16),
    ] + [pltpu.VMEM((rows, hidden), jnp.float32)] * 4


SMEM = pl.BlockSpec(memory_space=pltpu.SMEM)
VMEM = pl.BlockSpec(memory_space=pltpu.VMEM)
ANY = pl.BlockSpec(memory_space=pl.ANY)
PARAMS = pltpu.CompilerParams(vmem_limit_bytes=VMEM_BYTES)


def cost(micros):
    return pl.CostEstimate(flops=int(micros * 1.1e9), bytes_accessed=int(micros * 3e6), transcendentals=0)


def time_forward(segments, widths, groups, spec, w_split, rnn, sizes):
    parts, slots, share, inner, direct, band_columns, slot_rows, hidden = sizes
    dmodel = w_split.shape[2]
    frames = spec.shape[0] // 2
    return pl.pallas_call(
        partial(time_forward_kernel, slot_rows, share, inner, direct),
        out_shape=table_shapes(slots, share, widths.shape[1], parts)
        + [
            f32((parts, slots, frames // parts, dmodel)), f32((SLOT_PAD, band_columns)), f32((frames, 16, dmodel)),
        ]
        + saved_shapes(frames + 1, hidden),
        in_specs=[SMEM] * 3 + [ANY] * 3,
        out_specs=[SMEM] * 5 + [VMEM] * 3 + [ANY] * 6,
        scratch_shapes=saved_scratch(frames + 1, hidden)
        + rec_scratch(16 * CLIPS, hidden)
        + [pltpu.VMEM((slots, frames, dmodel), jnp.float32)]
        + [pltpu.VMEM((frames, 16, dmodel), jnp.float32), vec_scratch(dmodel, hidden)]
        + [pltpu.VMEM(a.shape, jnp.float32) for a in (rnn, w_split, spec)]
        + [pltpu.SMEM((parts,), jnp.int32), pltpu.SemaphoreType.DMA((9,))],
        compiler_params=PARAMS,
        cost_estimate=cost(35),
        name="time_forward",
    )(segments, widths, groups, spec, w_split, rnn)


def time_backward_kernel(
    slot_rows, places_s, clips, my_outer, dy_in, spec_in, x_in, *refs,
):
    saved, refs = refs[:6], refs[6:]
    w_split_in, v_band, rnn_in, g_mask_vec, d_spec, g_split, g_rnn_out, *refs = refs
    act0, act1, c0, c1, h0, h1, *refs = refs
    hi_ref, lo_ref, s0, s1, m0, m1, dy, vec, g_vec, g_band, dh0, dh1, dz0, dz1, *refs = refs
    rnn, w_split, spec, x, g_rnn, units, stats, sems = refs
    slots = dy_in.shape[1]
    frames, unused, dmodel = x.shape
    hidden = h0.shape[2]
    wide = w_split.shape[0] * slot_rows
    parts, unused_slots, quarter, unused = dy_in.shape
    pack, g_pack = Pack(rnn, dmodel, hidden), Pack(g_rnn, dmodel, hidden)
    pairs = [(rnn_in, rnn), (saved[4], h0), (saved[5], h1)]
    pairs += [(spec_in, spec)] + list(zip(saved[:4], (act0, act1, c0, c1)))
    pairs += [(w_split_in, w_split), (x_in, x)]
    loads = [pltpu.make_async_copy(a, b, sems.at[k]) for k, (a, b) in enumerate(pairs)]
    for copy in loads:
        copy.start()
    dy[...] = jnp.zeros_like(dy)
    for s in range(slots):
        for q in range(parts):
            dy[q * quarter : (q + 1) * quarter, s, :] = dy_in[q, s]
    for copy in loads[:3]:
        copy.wait()
    load_vec(pack, vec)
    dy_flat = dy[...].reshape(frames * 16, dmodel)
    split_recurrence_turned(pack, hi_ref, lo_ref)
    states_backward(frames, dy_flat, (dh0, dh1), (h0, h1), pack, g_pack)
    loads[3].wait()
    lane = lax.broadcasted_iota(jnp.int32, (frames, LANES), 1)
    for s in range(slots):
        unit, scale, valid, moving, entries = split_rows(spec, places_s[0, s], places_s[1, s], frames)
        units[s] = unit
        stats[s] = jnp.where(lane == 0, scale, moving)
    for d in (dh0, dh1):
        d[frames] = jnp.zeros_like(d[frames])
    for copy in loads[4:8]:
        copy.wait()
    run_backward(
        CLIP_MOST, clip_places(clips, frames), (act0, act1), (dz0, dz1), (c0, c1),
        (dh0, dh1), pack, hi_ref, lo_ref, (s0, s1), (m0, m1),
    )
    for copy in loads[8:]:
        copy.wait()
    frame = lax.broadcasted_iota(jnp.int32, ((frames - 1) * 16, 1), 0) // 16 + 1
    inside = jnp.ones(frame.shape, jnp.float32)
    for k in range(1, CLIPS):
        inside = jnp.where(frame == clips[0, k], 0.0, inside)
    x_flat = x[...].reshape(frames * 16, dmodel)
    dx = gates_backward(
        frames, x_flat, dy[...].reshape(frames * 16, dmodel), (dz0, dz1),
        lambda e: shifted((h0, h1)[e], e, frames, hidden, inside), pack, vec, g_pack, g_vec,
    )
    g_rnn_leaves = pltpu.make_async_copy(g_rnn, g_rnn_out, sems.at[10])
    g_rnn_leaves.start()
    dy[...] = dx.reshape(frames, 16, dmodel)
    d_spec[...] = jnp.zeros_like(d_spec)
    g_split[:, slots * slot_rows :] = jnp.zeros_like(g_split[:, slots * slot_rows :])
    g_band[...] = jnp.zeros_like(g_band)

    for s in range(slots):
        edge, width = places_s[0, s], places_s[1, s]
        unit, scale, moving = units[s], stats[s][:, 0:1], stats[s][:, 1:2]
        valid, entries = where_valid(width, frames)
        row = v_band[s : s + 1, : 2 * wide + dmodel]
        gain = 1.0 + row[:, :wide]
        z = (unit * gain + row[:, wide : 2 * wide]) * valid
        demb = dy[:, s, :]
        demb_parts = split(demb)
        g_slot = dot_parts(split(z), demb_parts, ATB)
        for k in range(w_split.shape[0]):
            g_split[k, s * slot_rows : (s + 1) * slot_rows] = g_slot[k * slot_rows : (k + 1) * slot_rows]
        dz = dot_parts(demb_parts, split(slot_weights(w_split, s, slot_rows)), ABT) * valid
        g_band[s : s + 1, :wide] = column_sum(dz * unit)
        g_band[s : s + 1, wide : 2 * wide] = column_sum(dz)
        g_band[s : s + 1, 2 * wide : 2 * wide + dmodel] = column_sum(demb)
        du = dz * gain
        first = jnp.sum(du, axis=-1, keepdims=True) / entries
        second = jnp.sum(du * unit, axis=-1, keepdims=True) / entries
        dt = scale * (du - first - moving * unit * second) * valid
        base, shift = window_of(edge)
        stacked = jnp.concatenate([dt[:, :LANES], dt[:, LANES:]], axis=0)
        padded = jnp.concatenate([stacked, jnp.zeros_like(stacked)], axis=1)
        d_spec[:, pl.ds(base, 2 * LANES)] += pltpu.roll(padded, shift, 1)

    share = g_mask_vec.shape[0]
    for j in range(share):
        g_band[pl.ds(my_outer[0] * share + j, 1), 2 * wide + dmodel :] = g_mask_vec[j]
    gathered = g_band[...]
    blocks = w_split.shape[0]
    columns = gathered.shape[1] // blocks
    for k in range(blocks):
        for h in range(0, columns, LANES):
            width = min(LANES, columns - h)
            at = slots * slot_rows + SLOT_PAD * (h // LANES)
            g_split[k, at : at + SLOT_PAD, :width] = gathered[:, k * columns + h : k * columns + h + width]
    g_rnn_leaves.wait()


def time_backward(
    slot_places, clips, my_outer, dy, spec, saved, w_split, v_band, rnn, g_mask_vec, slot_rows, hidden
):
    band_columns, slots = v_band.shape[1], dy.shape[1]
    dmodel = w_split.shape[2]
    frames = spec.shape[0] // 2
    return pl.pallas_call(
        partial(time_backward_kernel, slot_rows),
        out_shape=[f32(spec.shape), f32(w_split.shape), f32(rnn.shape)],
        in_specs=[SMEM] * 3 + [VMEM] + [ANY] * (2 + 6 + 1) + [VMEM, ANY, VMEM],
        out_specs=[VMEM, VMEM, ANY],
        scratch_shapes=saved_scratch(frames + 1, hidden)
        + rec_scratch(16 * CLIPS, hidden, True)
        + [pltpu.VMEM((frames, 16, dmodel), jnp.float32)] + [vec_scratch(dmodel, hidden)] * 2
        + [pltpu.VMEM((SLOT_PAD, band_columns), jnp.float32)]
        + [pltpu.VMEM((frames + 1, 16, hidden), jnp.float32)] * 2
        + [pltpu.VMEM((frames + 1, 16, 4 * hidden), jnp.float32)] * 2
        + [pltpu.VMEM(a.shape, jnp.float32) for a in (rnn, w_split, spec, saved[0], rnn)]
        + [pltpu.VMEM((slots, frames, w), jnp.float32) for w in (2 * LANES, LANES)]
        + [pltpu.SemaphoreType.DMA((11,))],
        compiler_params=PARAMS,
        cost_estimate=cost(2),
        name="time_backward",
    )(slot_places, clips, my_outer, dy, spec, *saved, w_split, v_band, rnn, g_mask_vec)


def in_turn(core, mine, other):
    return [jnp.where(core == 0, mine, other), jnp.where(core == 0, other, mine)]


def pack_pieces(mask, wide):
    lead, r, w = mask.shape[:2], mask.shape[2], mask.shape[3] // 2
    mask = mask.reshape(lead + (r, 2, w)).transpose(0, 1, 3, 2, 4).reshape(lead + (2 * r, w))
    wide = wide.reshape(lead + (2, r // 2, w // 2)).transpose(0, 1, 3, 2, 4)
    return jnp.concatenate([mask, wide.reshape(lead + (r // 2, w))], axis=2)


def unpack_pieces(pack, r):
    lead, w = pack.shape[:2], pack.shape[3]
    mask = pack[:, :, : 2 * r].reshape(lead + (2, r, w)).transpose(0, 1, 3, 2, 4).reshape(lead + (r, 2 * w))
    wide = pack[:, :, 2 * r :].reshape(lead + (r // 2, 2, w // 2)).transpose(0, 1, 3, 2, 4)
    return mask, wide.reshape(lead + (r, w // 2))


def load_mask_piece(value, r):
    return jnp.concatenate([value[:r], value[r : 2 * r]], axis=1)


def load_wide_piece(value):
    half = value.shape[1] // 2
    return jnp.concatenate([value[:, :half], value[:, half:]], axis=0)


def mask_slot(core, width, v, x, mine, other, keep, send, g_vec):
    outer, total_rows, wide = mine.shape
    piece_rows = send.shape[1]
    frames = total_rows - piece_rows
    dmodel = x.shape[1]
    half = wide // 2
    mlp = (v.shape[1] - 2 * dmodel) - 2 * wide
    r = mlp // (2 * outer)
    w_wide, w_mask = [], []
    for g in range(outer):
        w_mask += in_turn(core, load_mask_piece(mine[g, : 2 * r], r), load_mask_piece(other[g, : 2 * r], r))
        w_wide += in_turn(
            core, load_wide_piece(mine[g, 2 * r : piece_rows]), load_wide_piece(other[g, 2 * r : piece_rows])
        )
    w_wide, w_mask = jnp.concatenate(w_wide, axis=0), jnp.concatenate(w_mask, axis=0)
    cot = jnp.concatenate([mine[g, piece_rows:] for g in range(outer)], axis=0)
    gain = 1.0 + v[:, :dmodel]
    unit, scale = norm_stats(x)
    p = split(unit * gain + v[:, dmodel : 2 * dmodel])
    wide_parts = split(w_wide)
    mask_parts = split(w_mask)
    q = jnp.tanh(dot_parts(p, wide_parts, ABT) + v[:, 2 * dmodel : 2 * dmodel + mlp])
    q_parts = split(q)
    raw = dot_parts(q_parts, mask_parts, AB) + v[:, 2 * dmodel + mlp :]
    lane = lax.broadcasted_iota(jnp.int32, (1, half), 1)
    inside = (lane < width).astype(jnp.float32)
    valid = jnp.concatenate([inside, inside], axis=1)
    value = raw[:, :wide]
    gate = sigmoid(raw[:, wide:])
    masks = value * gate * valid
    dm = cot * valid
    dr = jnp.concatenate([dm * gate, dm * value * gate * (1.0 - gate)], axis=1)
    dr_parts = split(dr)
    g_mask = dot_parts(q_parts, dr_parts, ATB)
    dq = dot_parts(dr_parts, mask_parts, ABT)
    da = dq * (1.0 - q * q)
    da_parts = split(da)
    g_wide = dot_parts(da_parts, p, ATB)
    for g in range(outer):
        first, second = slice(2 * g * r, (2 * g + 1) * r), slice((2 * g + 1) * r, (2 * g + 2) * r)
        for ref, got in zip((keep, send), in_turn(core, g_mask[first], g_mask[second])):
            ref[g, :r] = got[:, :wide]
            ref[g, r : 2 * r] = got[:, wide:]
        for ref, got in zip((keep, send), in_turn(core, g_wide[first], g_wide[second])):
            ref[g, 2 * r : piece_rows, :half] = got[: r // 2]
            ref[g, 2 * r : piece_rows, half:] = got[r // 2 :]
        keep[g, piece_rows:] = masks[g * frames : (g + 1) * frames]
    dp = dot_parts(da_parts, wide_parts, AB)
    g_vec[:, :dmodel] = column_sum(dp * unit)
    g_vec[:, dmodel : 2 * dmodel] = column_sum(dp)
    g_vec[:, 2 * dmodel : 2 * dmodel + mlp] = column_sum(da)
    g_vec[:, 2 * dmodel + mlp :] = column_sum(dr)
    return norm_back(dp * gain, unit, scale)


def mask_kernel(base, places, arrived, mine, other, v_band, keep, send, grad, g_vec):
    s = pl.program_id(0)
    parts, streams, unused, quarter, dmodel = arrived.shape
    order = [(q, g) for g in range(streams) for q in range(parts)]
    x = jnp.concatenate([arrived[q, g, 0] for q, g in order], axis=0)
    dx = mask_slot(
        places[1, 0], places[0, s], v_band[pl.ds(places[2, s], 1), base:], x,
        mine.at[:, 0], other.at[:, 0], keep.at[:, 0], send.at[:, 0], g_vec.at[0],
    )
    for k, (q, g) in enumerate(order):
        grad[q, g, 0] = dx[k * quarter : (k + 1) * quarter]


def mask_network(places, arrived, mine, other, v_band, base, piece_rows):
    parts, streams, slots, quarter, dmodel = arrived.shape
    outer, unused, rows, wide = mine.shape

    def second(count):
        return pl.BlockSpec((outer, 1, count, wide), lambda s: (0, s, 0, 0))

    moving = pl.BlockSpec((parts, streams, 1, quarter, dmodel), lambda s: (0, 0, s, 0, 0))
    columns = v_band.shape[1] - base
    vector = pl.BlockSpec((1, 1, columns), lambda s: (s, 0, 0))
    return pl.pallas_call(
        partial(mask_kernel, base),
        grid=(slots,),
        out_shape=[
            f32(mine.shape), f32((outer, slots, piece_rows, wide)), f32(arrived.shape), f32((slots, 1, columns)),
        ],
        in_specs=[SMEM, moving, second(rows), second(rows), VMEM],
        out_specs=[second(rows), second(piece_rows), moving, vector],
        compiler_params=PARAMS,
        cost_estimate=cost(12),
        name="mask_network",
    )(places, arrived, mine, other, v_band)


class Links:
    def __init__(self, bands, layers, send_sems, recv_sems):
        self.bands, self.layers = bands, layers
        self.band, self.stream = lax.axis_index("band"), lax.axis_index("stream")
        self.layer, self.core = lax.div(self.stream, CORES), lax.rem(self.stream, CORES)
        self.other = self.stream + 1 - 2 * self.core
        self.send_sems, self.recv_sems = send_sems, recv_sems
        self.started = []

    def band_to(self, m):
        return lax.rem(self.band + m, self.bands)

    def band_from(self, m):
        return lax.rem(self.band + self.bands - m, self.bands)

    def layer_to(self, k):
        return lax.rem(self.layer + k, self.layers)

    def layer_from(self, k):
        return lax.rem(self.layer + self.layers - k, self.layers)

    def band_beside(self, k):
        return lax.rem(self.band + 2, 4) if k % 4 >= 2 else self.band + 1 - 2 * lax.rem(self.band, 2)

    def band_across(self):
        return 3 - self.band

    def goal(self, k):
        beside = self.layer + 1 - 2 * lax.rem(self.layer, 2)
        return (beside, 3 - self.layer, lax.rem(self.layer + 2, 4), self.layer)[k]

    def own(self, layer):
        return layer * CORES + self.core

    def across(self, layer):
        return layer * CORES + 1 - self.core

    def greet(self, partners):
        barrier = pltpu.get_barrier_semaphore()
        for partner in partners:
            pl.semaphore_signal(barrier, inc=1, device_id=partner, device_id_type=MESH)
        pl.semaphore_wait(barrier, len(partners))

    def copy(self, source, target, index, partner):
        return pltpu.make_async_remote_copy(
            src_ref=source, dst_ref=target, send_sem=self.send_sems.at[index],
            recv_sem=self.recv_sems.at[index], device_id=partner, device_id_type=MESH,
        )

    def send(self, source, target, index, partner):
        copy = self.copy(source, target, index, partner)
        copy.start()
        self.started.append(copy)

    def arrive(self, target, index):
        self.copy(target, target, index, (self.band, self.other)).wait_recv()

    def finish(self):
        for copy in self.started:
            copy.wait_send()


def gather_kernel(
    bands, layers, intake, recurrence, outtake, scalers, splitter, banding, masker, widener, cot,
    rnn_out, split_out, later, pieces,
    rnn_all, split_all, vec_rows, own_later, band_rows, cot_here, staged, send_sems, recv_sems, local_sems,
):
    at = Links(bands, layers, send_sems, recv_sems)
    band, stream, other = at.band, at.stream, at.other
    rows_all = rnn_all.shape[1]
    quarter = rows_all // bands
    used = []

    def local(source, target):
        copy = pltpu.make_async_copy(source, target, local_sems.at[len(used)])
        copy.start()
        used.append(copy)
        return copy

    vec_rows[...] = jnp.zeros_like(vec_rows)
    for k in range(2):
        for h in range(0, scalers.shape[1], LANES):
            width = min(LANES, scalers.shape[1] - h)
            vec_rows[k, h // LANES : h // LANES + 1, :width] = scalers[k : k + 1, h : h + width]
    band_rows[...] = jnp.zeros_like(band_rows)
    slots = banding.shape[0]
    for h in range(0, banding.shape[1], LANES):
        width = min(LANES, banding.shape[1] - h)
        base = SLOT_PAD * (h // LANES)
        band_rows[base : base + slots, :width] = banding[:, h : h + width]

    def own_pack(k, target):
        a = intake.shape[1]
        b = a + recurrence.shape[1]
        c = b + outtake.shape[1]
        return [
            local(intake.at[k], target.at[pl.ds(0, a)]),
            local(recurrence.at[k], target.at[pl.ds(a, b - a)]),
            local(outtake.at[k], target.at[pl.ds(b, c - b)]),
            local(vec_rows.at[k], target.at[pl.ds(c, rows_all - c)]),
        ]

    mine, mine_split = rnn_all.at[stream], split_all.at[stream]
    first = own_pack(0, mine)
    split_rows_count = splitter.shape[0]
    second = [
        local(splitter, mine_split.at[pl.ds(0, split_rows_count)]),
        local(band_rows, mine_split.at[pl.ds(split_rows_count, band_rows.shape[0])]),
    ]
    at.greet(
        [(at.band_to(m), stream) for m in range(1, bands)]
        + [(band, at.own(at.layer_to(k))) for k in range(1, layers)]
        + [(band, other)]
    )
    steps = (2, 0, 1)
    turns = range(1, bands)

    def rows(b):
        return pl.ds(b * quarter, quarter)

    to_layer, to_layer_split, to_band = 0, layers, 2 * layers
    to_core = to_band + layers * bands
    to_core_split = to_core + layers * bands
    to_layer_later = to_core_split + layers

    def spread(piece, index):
        for k in (2, 0):
            at.send(piece, piece, index + k, (band, at.own(at.goal(k))))

    def relay(piece, index):
        at.send(piece, piece, index + 1, (band, at.own(at.goal(0))))

    def rnn_piece(k):
        return rnn_all.at[at.own(at.goal(k)), rows(band)]

    def split_piece(k):
        return split_all.at[at.own(at.goal(k))]

    def later_piece(k):
        return later.at[at.goal(k)]

    def hand_on(k):
        piece = rnn_piece(k)
        for m in turns:
            at.send(piece, piece, to_band + k * bands + m, (at.band_to(m), stream))
        at.send(piece, piece, to_core + k * bands, (band, other))

    for copy in first:
        copy.wait()
    spread(rnn_piece(3), to_layer)
    for copy in second:
        copy.wait()
    spread(mine_split, to_layer_split)
    at.send(mine, mine, to_core + 3 * bands, (band, other))
    at.send(mine_split, mine_split, to_core_split + 3, (band, other))
    third = own_pack(1, own_later)
    load_cot = local(cot, cot_here)
    r, wide = masker.shape[1], masker.shape[2] // 2
    half = wide // 2
    base = 2 * r + r // 2
    fill = [
        local(masker.at[:, :, pl.ds(0, wide)], staged.at[:, pl.ds(0, r), :]),
        local(masker.at[:, :, pl.ds(wide, wide)], staged.at[:, pl.ds(r, r), :]),
        local(widener.at[:, pl.ds(0, r // 2), :], staged.at[:, pl.ds(2 * r, r // 2), pl.ds(0, half)]),
        local(widener.at[:, pl.ds(r // 2, r // 2), :], staged.at[:, pl.ds(2 * r, r // 2), pl.ds(half, half)]),
    ]
    at.arrive(rnn_piece(2), to_layer + 2)
    relay(rnn_piece(2), to_layer)
    hand_on(2)
    for copy in third:
        copy.wait()
    later[at.layer] = own_later[rows(band), :]
    spread(later_piece(3), to_layer_later)
    at.arrive(rnn_piece(0), to_layer)
    hand_on(0)
    at.arrive(split_piece(2), to_layer_split + 2)
    relay(split_piece(2), to_layer_split)
    at.send(split_piece(2), split_piece(2), to_core_split + 2, (band, other))
    at.arrive(rnn_piece(1), to_layer + 1)
    hand_on(1)
    at.arrive(later_piece(2), to_layer_later + 2)
    relay(later_piece(2), to_layer_later)
    load_cot.wait()
    for s in range(slots):
        for part in range(2):
            staged[s, base:, part * half : (part + 1) * half] = cot_here[:, s, part, :]
    for copy in fill:
        copy.wait()
    rest = [local(staged, pieces)]
    for k in (0, 1):
        at.arrive(split_piece(k), to_layer_split + k)
        at.send(split_piece(k), split_piece(k), to_core_split + k, (band, other))
    for k in steps:
        for m in turns:
            piece = rnn_all.at[at.own(at.goal(k)), rows(at.band_from(m))]
            at.arrive(piece, to_band + k * bands + m)
            at.send(piece, piece, to_core + k * bands + m, (band, other))

    def leave(source, target, block):
        rest.append(local(source.at[block], target.at[block]))

    leave(rnn_all, rnn_out, stream)
    leave(split_all, split_out, stream)
    at.arrive(rnn_all.at[other], to_core + 3 * bands)
    leave(rnn_all, rnn_out, other)
    at.arrive(split_all.at[other], to_core_split + 3)
    leave(split_all, split_out, other)
    for k in steps:
        leave(rnn_all, rnn_out, at.own(at.goal(k)))
        leave(split_all, split_out, at.own(at.goal(k)))
    for k in steps:
        source = at.across(at.goal(k))
        for m in range(bands):
            at.arrive(rnn_all.at[source, rows(at.band_from(m))], to_core + k * bands + m)
        leave(rnn_all, rnn_out, source)
        at.arrive(split_all.at[source], to_core_split + k)
        leave(split_all, split_out, source)
    for k in (0, 1):
        at.arrive(later_piece(k), to_layer_later + k)
    at.finish()
    for copy in rest:
        copy.wait()


def gather_front(intake, recurrence, outtake, scalers, splitter, banding, masker, widener, cot, rows, bands, layers):
    count = 4 * layers + 2 * layers * bands
    streams = layers * CORES
    slots = banding.shape[0]
    strips = -(-banding.shape[1] // LANES)
    r, wide = masker.shape[1], masker.shape[2] // 2
    frames = cot.shape[0]
    weight_rows = intake.shape[1] + recurrence.shape[1] + outtake.shape[1]
    split_rows_count = splitter.shape[0] + SLOT_PAD * strips
    return pl.pallas_call(
        partial(gather_kernel, bands, layers),
        out_shape=[
            f32((streams, rows, LANES)), f32((streams, split_rows_count, LANES)), f32((layers, rows // bands, LANES)),
            f32((slots, 2 * r + r // 2 + frames, wide)),
        ],
        in_specs=[ANY, ANY, ANY, VMEM, ANY, VMEM, ANY, ANY, ANY],
        out_specs=[ANY, ANY, VMEM, ANY],
        scratch_shapes=[
            pltpu.VMEM((streams, rows, LANES), jnp.float32),
            pltpu.VMEM((streams, split_rows_count, LANES), jnp.float32),
            pltpu.VMEM((2, rows - weight_rows, LANES), jnp.float32),
            pltpu.VMEM((rows, LANES), jnp.float32),
            pltpu.VMEM((SLOT_PAD * strips, LANES), jnp.float32),
            pltpu.VMEM(cot.shape, jnp.float32),
            pltpu.VMEM((slots, 2 * r + r // 2 + frames, wide), jnp.float32),
            pltpu.SemaphoreType.DMA((count,)), pltpu.SemaphoreType.DMA((count,)), pltpu.SemaphoreType.DMA((20 + 2 * streams,)),
        ],
        compiler_params=pltpu.CompilerParams(
            collective_id=0, has_side_effects=True, vmem_limit_bytes=VMEM_BYTES
        ),
        cost_estimate=cost(30),
        name="gather_front",
    )(intake, recurrence, outtake, scalers, splitter, banding, masker, widener, cot)


def mask_exchange_kernel(
    base, bands, layers, places, source, mine_in, v_band,
    back, grad_back, g_vec,
    arrived, grad, mine, other, send, received, send_sems, recv_sems, local_sems,
):
    at = Links(bands, layers, send_sems, recv_sems)
    share, outer, piece_rows, wide = other.shape
    quarter = arrived.shape[3]
    partner = (at.band, at.other)
    turns = [(m, k) for k in range(layers) for m in range(bands) if m + k]
    stride = bands * layers
    to_back, to_core, to_core_back = share * stride, 2 * share * stride, 2 * share * stride + share
    at.greet([(at.band_to(m), at.own(at.layer_to(k))) for m, k in turns] + [partner])
    loads = []
    for j in range(share):
        loads.append(
            [
                pltpu.make_async_copy(mine_in.at[:, j], mine.at[j], local_sems.at[2 * j]),
                pltpu.make_async_copy(
                    source.at[at.band, at.layer, j], arrived.at[j, at.band, at.layer], local_sems.at[2 * j + 1]
                ),
            ]
        )
        for copy in loads[-1]:
            copy.start()
    for j in range(share):
        at.send(mine_in.at[:, j, pl.ds(0, piece_rows)], other.at[j], to_core + j, partner)
        for m, k in turns:
            band, layer = at.band_to(m), at.layer_to(k)
            at.send(
                source.at[band, layer, j], arrived.at[j, at.band, at.layer], j * stride + k * bands + m,
                (band, at.own(layer)),
            )
    order = [(q, g) for g in range(layers) for q in range(bands)]
    for j in range(share):
        for copy in loads[j]:
            copy.wait()
        at.arrive(other.at[j], to_core + j)
        for m, k in turns:
            at.arrive(arrived.at[j, at.band_from(m), at.layer_from(k)], j * stride + k * bands + m)
        x = jnp.concatenate([arrived[j, q, g] for q, g in order], axis=0)
        dx = mask_slot(
            at.core, places[0, j], v_band[pl.ds(at.layer * share + j, 1), base:], x,
            mine.at[j], other.at[j], back.at[:, j], send.at[j], g_vec.at[j],
        )
        for i, (q, g) in enumerate(order):
            grad[j, q, g] = dx[i * quarter : (i + 1) * quarter]
        for m, k in turns:
            band, layer = at.band_to(m), at.layer_to(k)
            at.send(
                grad.at[j, band, layer], grad_back.at[at.band, at.layer, j], to_back + j * stride + k * bands + m,
                (band, at.own(layer)),
            )
        at.send(send.at[j], received.at[j], to_core_back + j, partner)
        grad_back[at.band, at.layer, j] = grad[j, at.band, at.layer]
    for j in range(share):
        at.arrive(received.at[j], to_core_back + j)
        for g in range(outer):
            back[g, j, :piece_rows] += received[j, g]
    for j in range(share):
        for m, k in turns:
            at.arrive(grad_back.at[at.band_from(m), at.layer_from(k), j], to_back + j * stride + k * bands + m)
    at.finish()


def mask_exchange(places, source, mine, v_band, base, piece_rows):
    bands, layers, share, quarter, dmodel = source.shape
    outer, unused, rows, wide = mine.shape
    columns = v_band.shape[1] - base
    count = 2 * share * bands * layers + 2 * share

    def vmem(*shape):
        return pltpu.VMEM(shape, jnp.float32)

    return pl.pallas_call(
        partial(mask_exchange_kernel, base, bands, layers),
        out_shape=[f32(mine.shape), f32(source.shape), f32((share, 1, columns))],
        in_specs=[SMEM, ANY, ANY, VMEM],
        out_specs=[VMEM] * 3,
        scratch_shapes=[
            vmem(share, bands, layers, quarter, dmodel),
            vmem(share, bands, layers, quarter, dmodel),
            vmem(share, outer, rows, wide),
            vmem(share, outer, piece_rows, wide),
            vmem(share, outer, piece_rows, wide),
            vmem(share, outer, piece_rows, wide),
            pltpu.SemaphoreType.DMA((count,)),
            pltpu.SemaphoreType.DMA((count,)),
            pltpu.SemaphoreType.DMA((2 * share,)),
        ],
        compiler_params=pltpu.CompilerParams(
            collective_id=2, has_side_effects=True, vmem_limit_bytes=VMEM_BYTES
        ),
        cost_estimate=cost(28),
        name="mask_exchange",
    )(places, source, mine, v_band)


def band_places(bands):
    return lambda e, j: [j if e == 0 else bands - 1 - j]


def pack_quarter(at, rnn, layer, core, m):
    quarter = rnn.shape[1] // at.bands
    rows = pl.ds(pl.multiple_of(at.band_from(m) * quarter, 8), quarter)
    return rnn.at[layer * CORES + core, rows]


def start_pack(at, rnn, pieces, sems):
    if len(pieces) == 1:
        copies = [pltpu.make_async_copy(pieces[0], rnn, sems.at[0])]
    else:
        copies = []
        for m, ref in enumerate(pieces):
            for layer in range(ref.shape[0]):
                target = pack_quarter(at, rnn, layer, at.core, m)
                at.send(ref.at[layer], target, at.bands + len(copies), (at.band, at.other))
                copies.append(pltpu.make_async_copy(ref.at[layer], target, sems.at[len(copies)]))
    for copy in copies:
        copy.start()
    return copies


def await_pack(at, rnn, pieces, copies):
    for copy in copies:
        copy.wait()
    if len(pieces) > 1:
        layers = pieces[0].shape[0]
        for k in range(len(pieces) * layers):
            at.arrive(pack_quarter(at, rnn, k % layers, 1 - at.core, k // layers), at.bands + k)


def pack_loads(pieces):
    return 1 if len(pieces) == 1 else sum(x.shape[0] for x in pieces)


def to_slots(target, source, band_of):
    for s in range(target.shape[0]):
        target[s] = source[band_of[0, s]] * band_of[1, s].astype(jnp.float32)


def band_forward_kernel(count, parts, slot_of, band_of, arrived_in, *refs):
    pieces, refs = refs[:count], refs[count:]
    out, x, *refs = refs
    saved, rnn_out, refs = refs[:6], refs[6], refs[7:]
    act0, act1, c0, c1, h0, h1, hi_ref, lo_ref, s0, s1, m0, m1, vec, rnn, arrived, mixed, *refs = refs
    send_sems, recv_sems, pack_sems, sems = refs
    bands, unused, dmodel = x.shape
    pack = Pack(rnn, dmodel, h0.shape[2])
    at, come = swap_bands(parts, arrived_in, arrived, send_sems, recv_sems, sems.at[6], True)
    await_pack(at, rnn, pieces, start_pack(at, rnn, pieces, pack_sems))
    pack_leaves = pltpu.make_async_copy(rnn, rnn_out, sems.at[7])
    pack_leaves.start()
    load_vec(pack, vec)
    split_recurrence(pack, hi_ref, lo_ref)
    come()

    def fetch(b, carry):
        x[b] = arrived[slot_of[0, b]]
        return carry

    lax.fori_loop(0, bands, fetch, 0)
    act = (act0, act1)

    def x_flat(start, size):
        return x[...].reshape(bands * 16, dmodel)

    gates_forward(x_flat, act, pack, vec, bands * 16, bands * 16)
    run_forward(
        bands, band_places(bands), act, (c0, c1), (h0, h1), pack, hi_ref, lo_ref, (s0, s1), (m0, m1)
    )
    leaving = [
        pltpu.make_async_copy(a, b, sems.at[k])
        for k, (a, b) in enumerate(zip((act0, act1, c0, c1, h0, h1), saved))
    ]
    for copy in leaving:
        copy.start()
    total = output_forward(bands, (h0, h1), pack, vec)
    mixed[...] = (x[...].reshape(bands * 16, dmodel) + total).reshape(bands, 16, dmodel)
    to_slots(out, mixed, band_of)
    at.finish()
    pack_leaves.wait()
    for copy in leaving:
        copy.wait()


def swap_bands(parts, source, target, send_sems, recv_sems, local_sem, pair=False):
    at = Links(parts, 1, send_sems, recv_sems)
    slots = target.shape[0] // parts
    if parts == 1:
        local = pltpu.make_async_copy(source, target, local_sem)
        local.start()
        return at, local.wait
    partners = [(at.band_to(m), at.stream) for m in range(1, parts)]
    at.greet(partners + [(at.band, at.other)] if pair else partners)

    def part(ref, b):
        return ref.at[pl.ds(b * slots, slots)]

    for m in range(1, parts):
        at.send(part(source, at.band_to(m)), part(target, at.band), m, (at.band_to(m), at.stream))
    local = pltpu.make_async_copy(part(source, at.band), part(target, at.band), local_sem)
    local.start()

    def come():
        for m in range(1, parts):
            at.arrive(part(target, at.band_from(m)), m)
        local.wait()

    return at, come


def swap_scratch(count):
    return [pltpu.SemaphoreType.DMA((count,)), pltpu.SemaphoreType.DMA((count,))]


def remote(parts, number):
    if parts == 1:
        return PARAMS
    return pltpu.CompilerParams(collective_id=number, has_side_effects=True, vmem_limit_bytes=VMEM_BYTES)


def band_forward(slot_of, band_of, arrived, pieces, rnn_shape, parts, hidden):
    bands = slot_of.shape[1]
    dmodel = arrived.shape[2]
    return pl.pallas_call(
        partial(band_forward_kernel, len(pieces), parts),
        out_shape=[f32(arrived.shape), f32((bands, 16, dmodel))] + saved_shapes(bands, hidden) + [f32(rnn_shape)],
        in_specs=[SMEM] * 2 + [ANY] * (1 + len(pieces)),
        out_specs=[VMEM] * 2 + [ANY] * 7,
        scratch_shapes=saved_scratch(bands, hidden)
        + rec_scratch(16, hidden)
        + [vec_scratch(dmodel, hidden), pltpu.VMEM(rnn_shape, jnp.float32)]
        + [pltpu.VMEM(arrived.shape, jnp.float32), pltpu.VMEM((bands, 16, dmodel), jnp.float32)]
        + swap_scratch(parts + pack_loads(pieces))
        + [pltpu.SemaphoreType.DMA((pack_loads(pieces),)), pltpu.SemaphoreType.DMA((8,))],
        compiler_params=remote(parts, 1),
        cost_estimate=cost(35),
        name="band_forward",
    )(slot_of, band_of, arrived, *pieces)


def band_backward_kernel(parts, slot_of, band_of, arrived, rnn_in, x, *refs):
    saved, refs = refs[:6], refs[6:]
    out, outs, refs = refs[0], refs[1 : 1 + parts], refs[1 + parts :]
    act0, act1, c0, c1, h0, h1, *refs = refs
    hi_ref, lo_ref, s0, s1, m0, m1, dy, vec, g_vec, dh0, dh1, dz0, dz1, rnn, g_rnn, *refs = refs
    leaving, send_sems, recv_sems, sems = refs
    bands, unused, dmodel = x.shape
    hidden = h0.shape[2]
    pack, g_pack = Pack(rnn, dmodel, hidden), Pack(g_rnn, dmodel, hidden)
    pairs = [(rnn_in, rnn), (saved[4], h0), (saved[5], h1)] + list(zip(saved[:4], (act0, act1, c0, c1)))
    loads = [pltpu.make_async_copy(a, b, sems.at[k]) for k, (a, b) in enumerate(pairs)]
    for copy in loads:
        copy.start()

    def fetch(b, carry):
        dy[b] = arrived[slot_of[0, b]]
        return carry

    lax.fori_loop(0, bands, fetch, 0)
    for copy in loads[:3]:
        copy.wait()
    load_vec(pack, vec)
    split_recurrence_turned(pack, hi_ref, lo_ref)
    states_backward(bands, dy[...].reshape(bands * 16, dmodel), (dh0, dh1), (h0, h1), pack, g_pack)
    for copy in loads[3:]:
        copy.wait()
    run_backward(
        bands, band_places(bands), (act0, act1), (dz0, dz1), (c0, c1), (dh0, dh1),
        pack, hi_ref, lo_ref, (s0, s1), (m0, m1),
    )
    x_all, dy_all = x[...].reshape(bands * 16, dmodel), dy[...].reshape(bands * 16, dmodel)
    dx = input_backward(bands, x_all, dy_all, (dz0, dz1), pack, vec, g_vec)
    dy[...] = dx.reshape(bands, 16, dmodel)
    to_slots(leaving, dy, band_of)
    at, come = swap_bands(parts, leaving, out, send_sems, recv_sems, sems.at[7])
    weights_backward(
        bands, x_all, (dz0, dz1), lambda e: shifted((h0, h1)[e], e, bands, hidden, 1.0), pack, vec, g_pack, g_vec
    )
    leave = [
        pltpu.make_async_copy(g_rnn if parts == 1 else g_rnn.at[at.band_to(m)], outs[m], sems.at[8 + m])
        for m in range(parts)
    ]
    for copy in leave:
        copy.start()
    come()
    at.finish()
    for copy in leave:
        copy.wait()


def band_backward(slot_of, band_of, arrived, rnn, saved, parts, hidden):
    bands = slot_of.shape[1]
    dmodel = arrived.shape[2]
    blocks, rows, unused = rnn.shape
    grad_shape = rnn.shape if parts == 1 else (parts, blocks, rows // parts, LANES)
    return pl.pallas_call(
        partial(band_backward_kernel, parts),
        out_shape=[f32(arrived.shape)] + [f32(grad_shape[-3:])] * parts,
        in_specs=[SMEM] * 2 + [VMEM, ANY, VMEM] + [ANY] * 6,
        out_specs=[VMEM] + [ANY] * parts,
        scratch_shapes=saved_scratch(bands, hidden)
        + rec_scratch(16, hidden, True)
        + [pltpu.VMEM((bands, 16, dmodel), jnp.float32)]
        + [vec_scratch(dmodel, hidden)] * 2
        + [pltpu.VMEM((bands, 16, hidden), jnp.float32)] * 2
        + [pltpu.VMEM((bands, 16, 4 * hidden), jnp.float32)] * 2
        + [pltpu.VMEM(rnn.shape, jnp.float32), pltpu.VMEM(grad_shape, jnp.float32)]
        + [pltpu.VMEM(arrived.shape, jnp.float32)]
        + swap_scratch(parts)
        + [pltpu.SemaphoreType.DMA((8 + parts,))],
        compiler_params=remote(parts, 3),
        cost_estimate=cost(38),
        name="band_backward",
    )(slot_of, band_of, arrived, rnn, *saved)


class Grads:
    def __init__(self, pieces, rnn0, rnn1, banded, dims):
        self.pieces, self.rnn, self.banded = pieces, (rnn0, rnn1), banded
        self.slots, self.slot_rows, self.r, self.piece_rows, self.dmodel, self.hidden = dims

    def piece(self, k, s):
        if k == 0:
            at = pl.ds(pl.multiple_of(s * self.slot_rows, self.slot_rows), self.slot_rows)
            return self.banded[at, :]
        if k == 1:
            return load_wide_piece(self.pieces[s, 2 * self.r : self.piece_rows])
        return load_mask_piece(self.pieces[s, : 2 * self.r], self.r)

    def of_slot(self, s):
        return [(k, (s,), self.piece(k, s)) for k in range(3)]

    def banding(self, columns):
        base = self.slots * self.slot_rows
        strips = []
        for h in range(0, columns, LANES):
            at = base + SLOT_PAD * (h // LANES)
            strips.append(self.banded[at : at + self.slots, : min(LANES, columns - h)])
        return jnp.concatenate(strips, axis=1)

    def rest(self, columns, share):
        found = [(3, (...,), self.banding(columns))]
        unused, out_rows, weight_rows, unused, vec_rows, unused = pack_rows(self.dmodel, self.hidden)
        for k in range(2):
            pack = self.rnn[k]
            at = 0
            for e in range(2):
                found.append((4, (k, e), pack[at : at + self.dmodel]))
                at += self.dmodel
            for e in range(2):
                found.append((5, (k, e), pack[at : at + self.hidden]))
                at += self.hidden
            found.append((6, (k,), pack[at : at + out_rows]))
            at += out_rows
            strips = [
                pack[at + r : at + r + 1, : min(LANES, share - r * LANES)] for r in range(vec_rows)
            ]
            found.append((7, (slice(k, k + 1),), jnp.concatenate(strips, axis=1)))
        return found


DECAYS = (DECAY_RATE,) * 3 + (0.0,) + (DECAY_RATE,) * 3 + (0.0,)


def lamb_moments(gradient, mean_old, power_old, factor):
    clipped = gradient * factor
    mean_new = BETA_ONE * mean_old + (1.0 - BETA_ONE) * clipped
    power_new = BETA_TWO * power_old + (1.0 - BETA_TWO) * clipped * clipped
    return (mean_new, power_new)


def lamb_direction(weight_matrix, mean_new, power_new, decay):
    corrected = mean_new / (1.0 - BETA_ONE**STEP)
    scale_root = jnp.sqrt(power_new / (1.0 - BETA_TWO**STEP)) + ADAM_EPS
    return corrected / scale_root + decay * weight_matrix


def add_up(rows, first):
    line = jnp.zeros((1, LANES), jnp.float32)
    lane = lax.broadcasted_iota(jnp.int32, (1, LANES), 1)
    for i, row in enumerate(rows):
        line = jnp.where(lane == first + i, jnp.sum(row, axis=1, keepdims=True), line)
    return line


def lane_of(line, i):
    lane = lax.broadcasted_iota(jnp.int32, (1, LANES), 1)
    return jnp.sum(jnp.where(lane == i, line, 0.0), axis=1, keepdims=True)


def finish_kernel(bands, layers, dims, g_rnn0, g_split, d_spec, back, *refs):
    g_rnn1, refs = refs[:bands], refs[bands:]
    state, refs = refs[:24], refs[24:]
    out, rnn0, rnn1, banded, spec_out = refs[:5]
    pieces, refs = refs[5], refs[6:]
    held_state, packs, refs = refs[:12], refs[12], refs[13:]
    (
        own0, own_split, parts1, sum1, from_core, from_core_split, from_core1, from_band, held,
        from_layer, from_layer_split, from_layer1, spec_in, spec_own, came, lines,
        local_sems, send_sems, recv_sems,
    ) = refs
    at = Links(bands, layers, send_sems, recv_sems)
    band, stream, other = at.band, at.stream, at.other
    streams = layers * CORES
    quarter = g_rnn0.shape[1] // bands
    spec_rows = d_spec.shape[0] // bands
    order = range(layers)
    turns = range(1, bands)
    taken = [0]

    def take(count):
        taken[0] += count
        return taken[0] - count

    locals_used = []

    def local(source, target):
        copy = pltpu.make_async_copy(source, target, local_sems.at[len(locals_used)])
        copy.start()
        locals_used.append(copy)
        return copy

    def rows(b):
        return pl.ds(pl.multiple_of(b * quarter, 8), quarter)

    def spec_part(b):
        return pl.ds(pl.multiple_of(b * spec_rows, 8), spec_rows)

    def stream_to(k):
        return lax.rem(stream + k, streams)

    at.greet(
        [(at.band_to(m), stream_to(k)) for k in range(streams) for m in range(bands) if m + k]
    )
    to_core, to_core_split, to_core1 = take(layers), take(layers), take(layers)
    to_layer, to_layer_split, to_layer1 = take(layers), take(layers), take(layers)
    to_band, to_all0, to_all1 = take(bands * layers), take(bands), take(bands)
    to_spec, to_spec_all = take(bands), take(bands)
    def pair_rnn(k):
        at.send(g_rnn0.at[at.across(at.goal(k))], from_core.at[k], to_core + k, (band, other))

    def pair_split(k):
        at.send(g_split.at[at.across(at.goal(k))], from_core_split.at[k], to_core_split + k, (band, other))

    pair_rnn(0)
    pair_rnn(1)
    for m in turns:
        to = at.band_to(m)
        at.send(d_spec.at[spec_part(to)], spec_in.at[m - 1], to_spec + m, (to, stream))
    load0 = [local(g_rnn0.at[at.own(at.goal(k))], own0.at[k]) for k in range(layers)]
    load_split = [local(g_split.at[at.own(at.goal(k))], own_split.at[k]) for k in range(layers)]
    load1 = [local(g, parts1.at[k]) for k, g in enumerate(g_rnn1)]
    load_spec = local(d_spec.at[spec_part(band)], spec_own)
    load_state = [local(back, pieces)]
    pack_base = sum(state[k].shape[1] for k in range(4, 7))
    for t in range(3):
        kind = state[8 * t : 8 * t + 8]
        load_state += [local(a, b) for a, b in zip(kind[:4], held_state[4 * t : 4 * t + 4])]
        for k in range(2):
            base = 0
            for a in kind[4:7]:
                load_state.append(local(a.at[k], packs.at[t, k, pl.ds(base, a.shape[1])]))
                base += a.shape[1]
            packs[t, k, base:] = jnp.zeros_like(packs[t, k, base:])
            length = kind[7].shape[1]
            for h in range(0, length, LANES):
                width = min(LANES, length - h)
                row = base + h // LANES
                packs[t, k, row : row + 1, :width] = kind[7][k : k + 1, h : h + width]
    def first_turn(acc, far, index, k):
        if k < 2:
            at.send(acc.at[k], far.at[k], index + k, (band, at.own(at.goal(0))))

    def second_turn(acc, far, index):
        at.arrive(far.at[1], index + 1)
        acc[2] += far[1]
        at.send(acc.at[2], far.at[2], index + 2, (band, at.own(at.goal(2))))

    def own_total(acc, far, index):
        at.arrive(far.at[0], index)
        at.arrive(far.at[2], index + 2)
        return acc[3] + far[0] + far[2]

    for k in order:
        at.arrive(from_core.at[k], to_core + k)
        if k < 2:
            pair_rnn(k + 2)
        else:
            pair_split(2 * k - 4)
            pair_split(2 * k - 3)
        load0[k].wait()
        from_core[k] += own0[k]
        for m, to in ((1, at.band_across()), (0, at.band_beside(k))):
            at.send(
                from_core.at[k, rows(to)], from_band.at[m, k], to_band + m * layers + k, (at.band_beside(k), stream)
            )
    for k in order:
        at.arrive(from_core_split.at[k], to_core_split + k)
        load_split[k].wait()
        from_core_split[k] += own_split[k]
        first_turn(from_core_split, from_layer_split, to_layer_split, k)
    for copy in load1:
        copy.wait()

    def block(k, carry):
        total = parts1[0, k]
        for b in range(1, bands):
            total = total + parts1[b, k]
        sum1[k] = total
        return carry

    lax.fori_loop(0, streams, block, 0)
    for k in order:
        at.send(sum1.at[at.across(at.goal(k))], from_core1.at[k], to_core1 + k, (band, other))
    for k in order:
        at.arrive(from_core1.at[k], to_core1 + k)
        from_core1[k] += sum1[at.own(at.goal(k))]
        first_turn(from_core1, from_layer1, to_layer1, k)
    for k in order:
        at.arrive(from_band.at[1, k], to_band + layers + k)
        to = at.band_beside(k + 2)
        from_core[k, rows(to)] += from_band[1, k]
        at.send(from_core.at[k, rows(to)], from_band.at[2, k], to_band + 2 * layers + k, (to, stream))
    weights, means, powers = held_state[:4], held_state[4:8], held_state[8:]
    grads = Grads(pieces, rnn0, rnn1, banded, dims)
    slots = dims[0]
    for copy in load_state:
        copy.wait()

    def add_squares(pairs, had):
        return tuple(a + column_sum(b * b) for a, b in zip(had, pairs))

    def early_slot(s, had):
        return add_squares(
            [weights[0][s], weights[1][s], weights[2][s], grads.piece(1, s), grads.piece(2, s)], had
        )

    early = lax.fori_loop(
        0, slots, early_slot, tuple(jnp.zeros((1, weights[k].shape[2]), jnp.float32) for k in (0, 1, 2, 1, 2))
    )
    row = lax.broadcasted_iota(jnp.int32, (quarter, LANES), 0) + band * quarter
    edges = [0]
    for a in state[4:7]:
        edges.append(edges[-1] + a.shape[1])

    def by_array(values):
        edge = edges + [bands * quarter]
        return [
            column_sum(jnp.where((row >= edge[i]) & (row < edge[i + 1]), values, 0.0)) for i in range(4)
        ]

    def both_modules(one):
        found = [by_array(one(k, rows(band))) for k in range(2)]
        return [a + b for a, b in zip(*found)]

    weight_rows = list(early[:3]) + [column_sum(weights[3][...] * weights[3][...])]
    weight_rows += both_modules(lambda k, q: packs[0, k, q] * packs[0, k, q])
    second_turn(from_core_split, from_layer_split, to_layer_split)
    second_turn(from_core1, from_layer1, to_layer1)
    for k in order:
        total = from_core[k, rows(band)]
        for m in (0, 2):
            at.arrive(from_band.at[m, k], to_band + m * layers + k)
            total = total + from_band[m, k]
        held[k] = total
        first_turn(held, from_layer, to_layer, k)
    second_turn(held, from_layer, to_layer)

    def gather_quarters(target, index):
        for m in turns:
            at.send(target.at[rows(band)], target.at[rows(band)], index + m, (at.band_to(m), stream))

    rnn1[rows(band)] = own_total(from_core1, from_layer1, to_layer1)
    banded[...] = own_total(from_core_split, from_layer_split, to_layer_split)
    rnn0[rows(band)] = own_total(held, from_layer, to_layer)

    def send_modules():
        gather_quarters(rnn1, to_all1)
        gather_quarters(rnn0, to_all0)

    def send_spectrum():
        load_spec.wait()
        total = spec_own[...]
        for m in turns:
            at.arrive(spec_in.at[m - 1], to_spec + m)
            total = total + spec_in[m - 1]
        spec_out[spec_part(band)] = total
        for m in turns:
            piece = spec_out.at[spec_part(band)]
            at.send(piece, piece, to_spec_all + m, (at.band_to(m), stream))

    everyone = [(m, k) for k in range(streams) for m in range(bands) if m + k]

    def everywhere(line, turn, meanwhile):
        index = take(streams * bands)
        own = lines.at[turn]
        own[...] = line
        for m, k in everyone:
            i = k * bands + m
            at.send(own, came.at[turn, i], index + i, (at.band_to(m), stream_to(k)))
        meanwhile()
        total = line
        for m, k in everyone:
            i = k * bands + m
            at.arrive(came.at[turn, i], index + i)
            total = total + came[turn, i]
        return total

    main = banded[: slots * dims[1]]
    band_grad = grads.banding(weights[3].shape[1])
    module_rows = both_modules(lambda k, q: (rnn0, rnn1)[k][q] * (rnn0, rnn1)[k][q])
    found = [column_sum(main * main), early[3], early[4], column_sum(band_grad * band_grad)] + module_rows
    grad_total = sum(jnp.sum(x, axis=1, keepdims=True) for x in found)
    totals = everywhere(add_up([grad_total] + weight_rows, 0), 0, send_modules)
    grad_norm = jnp.sqrt(lane_of(totals, 0))
    factor = jnp.minimum(1.0, CLIP_NORM / grad_norm)

    def direction(w, mean_old, power_old, g, decay):
        mean, power = lamb_moments(g, mean_old, power_old, factor)
        return lamb_direction(w, mean, power, decay)

    def slot(s, had):
        return add_squares(
            [
                direction(weights[k][s], means[k][s], powers[k][s], grads.piece(k, s), DECAYS[k])
                for k in range(3)
            ],
            had,
        )

    moved_rows = list(
        lax.fori_loop(0, slots, slot, tuple(jnp.zeros((1, weights[k].shape[2]), jnp.float32) for k in range(3)))
    )
    moved = direction(weights[3][...], means[3][...], powers[3][...], band_grad, DECAYS[3])
    moved_rows.append(column_sum(moved * moved))
    decay = jnp.where(row < edges[3], DECAYS[4], DECAYS[7])

    def module(k, q):
        got = direction(packs[0, k, q], packs[1, k, q], packs[2, k, q], (rnn0, rnn1)[k][q], decay)
        return got * got

    moved_rows += both_modules(module)
    moved = everywhere(add_up(moved_rows, 1), 1, send_spectrum)
    out[0:1] = jnp.sqrt(totals) / jnp.sqrt(moved + 1e-12)
    out[1:2] = jnp.broadcast_to(factor, (1, LANES))
    out[2:3] = jnp.broadcast_to(grad_norm, (1, LANES))
    out[3:8] = jnp.zeros((5, LANES), jnp.float32)
    for m in turns:
        at.arrive(rnn1.at[rows(at.band_from(m))], to_all1 + m)
        at.arrive(rnn0.at[rows(at.band_from(m))], to_all0 + m)
        at.arrive(spec_out.at[spec_part(at.band_from(m))], to_spec_all + m)
    at.finish()


def finish(g_rnn0, g_split, g_rnn1, d_spec, back, state, bands, layers, dims):
    streams = layers * CORES
    rows, split_count = g_rnn0.shape[1], g_split.shape[1]
    quarter = rows // bands
    spec_shape = (d_spec.shape[0] // bands, d_spec.shape[1])
    count = 6 * layers + bands * layers + 4 * bands + 2 * streams * bands
    tile = (8, LANES)

    def vmem(*shape):
        return pltpu.VMEM(shape, jnp.float32)

    return pl.pallas_call(
        partial(finish_kernel, bands, layers, dims),
        out_shape=[
            f32(tile), f32((rows, LANES)), f32((rows, LANES)), f32((split_count, LANES)), f32(d_spec.shape),
        ],
        in_specs=[ANY] * (4 + bands) + ([ANY] * 7 + [VMEM]) * 3,
        out_specs=[VMEM] * 5,
        scratch_shapes=[vmem(*back.shape)]
        + [vmem(*x.shape) for k, x in enumerate(state) if k % 8 < 4]
        + [vmem(3, 2, rows, LANES)]
        + [
            vmem(layers, rows, LANES),
            vmem(layers, split_count, LANES),
            vmem(bands, *g_rnn1[0].shape),
            vmem(streams, quarter, LANES),
            vmem(layers, rows, LANES),
            vmem(layers, split_count, LANES),
            vmem(layers, quarter, LANES),
            vmem(bands - 1, layers, quarter, LANES),
            vmem(layers, quarter, LANES),
            vmem(layers - 1, quarter, LANES),
            vmem(layers - 1, split_count, LANES),
            vmem(layers - 1, quarter, LANES),
            vmem(bands - 1, *spec_shape),
            vmem(*spec_shape),
            vmem(2, streams * bands, 1, LANES),
            vmem(2, 1, LANES),
            pltpu.SemaphoreType.DMA((2 * layers + bands + 2 + 12 + 18,)),
            pltpu.SemaphoreType.DMA((count,)),
            pltpu.SemaphoreType.DMA((count,)),
        ],
        compiler_params=pltpu.CompilerParams(
            collective_id=5, has_side_effects=True, vmem_limit_bytes=VMEM_BYTES
        ),
        cost_estimate=cost(60),
        name="finish",
    )(g_rnn0, g_split, d_spec, back, *g_rnn1, *state)


CHUNK = 4


def update_kernel(dims, scales, d_spec, pieces_in, rnn0_in, rnn1_in, banded_in, *refs):
    state, refs = refs[:24], refs[24:]
    results, masks_out, spec_out, norm_out, refs = refs[:24], refs[24], refs[25], refs[26], refs[27:]
    norm_out[...] = scales[2:3, 0:1]
    pieces, rnn0, rnn1, banded, refs = *refs[:4], refs[4:]
    here, refs = refs[:24], refs[24:]
    made, refs = refs[:24], refs[24:]
    masks, load_sems, store_sems = refs
    weights, means, powers = here[:8], here[8:16], here[16:]
    fresh, new_means, new_powers = made[:8], made[8:16], made[16:]
    slots, piece_rows = dims[0], dims[3]
    grads = Grads(pieces, rnn0, rnn1, banded, dims)
    factor = scales[1:2, 0:1]
    ratios = [lane_of(scales[0:1], 1 + k) for k in range(8)]
    used = [0, 0]

    def copy(pair, which):
        sems = (load_sems, store_sems)[which]
        made_copy = pltpu.make_async_copy(*pair, sems.at[used[which]])
        used[which] += 1
        made_copy.start()
        return made_copy

    def arrays(numbers, sources, targets):
        return [(sources[8 * t + k], targets[8 * t + k]) for k in numbers for t in range(3)]

    def cut(pair, c):
        part = pl.ds(c * CHUNK, CHUNK)
        return pair[0].at[part], pair[1].at[part]

    small = [copy(p, 0) for p in [(rnn0_in, rnn0), (rnn1_in, rnn1), (banded_in, banded)] + arrays(range(3, 8), state, here)]
    chunks = [
        [copy(cut(p, c), 0) for p in [(pieces_in, pieces)] + arrays(range(3), state, here)]
        for c in range(slots // CHUNK)
    ]
    half_rows = d_spec.shape[0] // 2
    for part in range(2):
        spec_out[:, part, :] = d_spec[part * half_rows : (part + 1) * half_rows, : spec_out.shape[2]]

    def one(k, where, g):
        w = weights[k][where]
        mean, power = lamb_moments(g, means[k][where], powers[k][where], factor)
        direction = lamb_direction(w, mean, power, DECAYS[k])
        fresh[k][where] = w - LEARN_RATE * ratios[k] * direction
        new_means[k][where] = mean
        new_powers[k][where] = power

    for got in small:
        got.wait()
    for part in grads.rest(weights[3].shape[1], weights[7].shape[1]):
        one(*part)
    stores = [copy(p, 1) for p in arrays(range(3, 8), made, results)]
    half = pieces.shape[2] // 2
    for c in range(slots // CHUNK):
        for got in chunks[c]:
            got.wait()

        def slot(s, carry):
            for part in grads.of_slot(s):
                one(*part)
            return carry

        lax.fori_loop(c * CHUNK, (c + 1) * CHUNK, slot, 0)
        stores += [copy(cut(p, c), 1) for p in arrays(range(3), made, results)]
    for s in range(slots):
        for part in range(2):
            masks[:, s, part, :] = pieces[s, piece_rows:, part * half : (part + 1) * half]
    stores.append(copy((masks, masks_out), 1))
    for sent in stores:
        sent.wait()


def update(scales, d_spec, grads, state, dims, bins):
    slots, rows, wide = grads[0].shape
    frames = rows - dims[3]
    masks_shape = (frames, slots, 2, wide // 2)
    loads = 18 + 10 * (slots // CHUNK)
    stores = 16 + 9 * (slots // CHUNK)
    return pl.pallas_call(
        partial(update_kernel, dims),
        out_shape=[f32(x.shape) for x in state] + [f32(masks_shape), f32((frames, 2, bins)), f32((1, 1))],
        in_specs=[VMEM] * 2 + [ANY] * 28,
        out_specs=[ANY] * 25 + [VMEM] * 2,
        scratch_shapes=[pltpu.VMEM(x.shape, jnp.float32) for x in tuple(grads) + tuple(state) * 2]
        + [pltpu.VMEM(masks_shape, jnp.float32)]
        + [pltpu.SemaphoreType.DMA((loads,)), pltpu.SemaphoreType.DMA((stores,))],
        compiler_params=PARAMS,
        cost_estimate=cost(10),
        name="update",
    )(scales, d_spec, *grads, *state)


def groups_of(size, slots):
    outer = math.gcd(size, slots)
    inner = size // outer
    across = [[g * inner + i for g in range(outer)] for i in range(inner)]
    within = [[g * inner + i for i in range(inner)] for g in range(outer)]
    return outer, inner, across, within


def sum_everywhere(values, sizes):
    n = sizes[0] * sizes[1]
    row = jnp.zeros((8, LANES), jnp.float32).at[0, : values.shape[0]].set(values)
    spread = jnp.broadcast_to(row[None], (n, 8, LANES))
    got = lax.all_to_all(spread, ("band", "stream"), 0, 0, tiled=True)
    return jnp.sum(got, axis=0)[0, : values.shape[0]]


def pass_along(x, axis, by):
    size = lax.axis_size(axis)
    return lax.ppermute(x, axis, [(k, (k + by) % size) for k in range(size)])


def swap_cores(x):
    return lax.ppermute(x, "stream", [(s, s ^ 1) for s in range(lax.axis_size("stream"))])


def share_slots(shard, outer, across, within, axis):
    slots = shard.shape[0]
    mine = lax.all_to_all(
        shard.reshape((outer, slots // outer) + shard.shape[1:]), "stream", 0, 0,
        axis_index_groups=across, tiled=True,
    )
    inner = len(within[0])
    if inner == CORES:
        return mine, swap_cores(mine)
    both = lax.all_gather(mine, "stream", axis_index_groups=within)
    both = both.reshape((CORES, inner // CORES) + mine.shape)
    if axis == 1:
        both = both.transpose(0, 2, 3, 1, 4, 5)
        both = both.reshape(both.shape[:3] + (-1, both.shape[5]))
    else:
        both = both.transpose(0, 2, 3, 4, 1, 5)
        both = both.reshape(both.shape[:4] + (-1,))
    return both[0], both[1]


def return_slots(keep, send, outer, inner, across, within, axis):
    if inner == CORES:
        mine = keep + swap_cores(send)
    else:
        both = jnp.stack([keep, send])
        half = inner // CORES
        if axis == 1:
            both = both.reshape(both.shape[:3] + (half, -1, both.shape[4])).transpose(0, 3, 1, 2, 4, 5)
        else:
            both = both.reshape(both.shape[:4] + (half, -1)).transpose(0, 4, 1, 2, 3, 5)
        both = both.reshape((inner,) + both.shape[2:])
        mine = lax.psum_scatter(both, "stream", axis_index_groups=within, tiled=False)
    back = lax.all_to_all(mine, "stream", 0, 0, axis_index_groups=across, tiled=True)
    return back.reshape((-1,) + back.shape[2:])


def pack_split(splitter, banding, blocks):
    slots, wide, dmodel = splitter.shape
    columns = banding.shape[1] // blocks
    strips = -(-columns // LANES)
    main = splitter.reshape(slots, blocks, wide // blocks, dmodel).transpose(1, 0, 2, 3)
    flat = banding.reshape(slots, blocks, columns).transpose(1, 0, 2)
    flat = jnp.pad(flat, ((0, 0), (0, SLOT_PAD - slots), (0, strips * LANES - columns)))
    flat = flat.reshape(blocks, SLOT_PAD, strips, LANES).transpose(0, 2, 1, 3)
    return jnp.concatenate(
        [main.reshape(blocks, slots * wide // blocks, dmodel), flat.reshape(blocks, -1, LANES)], axis=1
    )


def unpack_banding(pack, start, slots, columns):
    blocks = pack.shape[0]
    flat = pack[:, start:].reshape(blocks, -1, SLOT_PAD, LANES)[:, :, :slots].transpose(2, 0, 1, 3)
    return flat.reshape(slots, blocks, -1)[:, :, :columns].reshape(slots, blocks * columns)


def body(spectrum, segments, widths, groups, cotangent, *state):
    weights, means_old, powers_old = state[:8], state[8:16], state[16:]
    splitter, widener, masker, banding, intake, recurrence, outtake, scalers = weights
    group_count = lax.axis_size("band")
    stream_count = lax.axis_size("stream")
    my_stream = lax.axis_index("stream")
    slots = splitter.shape[0]
    frames = spectrum.shape[0]
    quarter = frames // group_count
    outer, inner, across, within = groups_of(stream_count, slots)
    share = slots // outer
    r = masker.shape[1] * stream_count // (2 * outer)
    dmodel = splitter.shape[2]
    hidden = recurrence.shape[2]
    wide = splitter.shape[1] * stream_count
    bins = spectrum.shape[2]
    blocks, out_rows, weight_rows, vec_share, vec_rows, rows = pack_rows(dmodel, hidden)
    slot_rows = wide // blocks
    columns = banding.shape[1] * stream_count // blocks
    direct = stream_count == blocks and inner == CORES and outer == 4 and group_count == 4

    padded = ((bins - 1) // LANES + 2) * LANES
    spec = jnp.pad(
        spectrum.transpose(1, 0, 2).reshape(2 * frames, bins), ((0, 0), (0, padded - bins))
    )

    if direct:
        rnn0, w_split, later, pieces = gather_front(
            intake.reshape(2, 2 * dmodel, LANES), recurrence.reshape(2, 2 * hidden, LANES), outtake, scalers,
            splitter.reshape(slots * slot_rows, dmodel), banding, masker, widener.transpose(0, 2, 1), cotangent,
            rows, group_count, outer,
        )
        near = [later] + [pass_along(later, "band", m) for m in range(1, group_count)]
        pieces = pieces.reshape((outer, share) + pieces.shape[1:])
        mine = lax.all_to_all(pieces, "stream", 0, 0, axis_index_groups=across, tiled=True)
    else:
        whole = (
            lax.all_gather(intake, "stream", axis=3, tiled=True),
            lax.all_gather(recurrence, "stream", axis=3, tiled=True),
            lax.all_gather(outtake, "stream", axis=1, tiled=True),
            lax.all_gather(scalers, "stream", axis=1, tiled=True),
        )
        rnn0, rnn1 = (
            pack_rnn(whole[0][k], whole[1][k], whole[2][k], whole[3][k : k + 1], rows, vec_share)
            for k in range(2)
        )
        w_split = pack_split(
            lax.all_gather(splitter, "stream", axis=1, tiled=True),
            lax.all_gather(banding, "stream", axis=1, tiled=True),
            blocks,
        )
        w_mask = share_slots(masker, outer, across, within, 1)
        w_wide = share_slots(widener.transpose(0, 2, 1), outer, across, within, 1)
        cot_parts = cotangent.reshape(frames, outer, share, wide).transpose(1, 2, 0, 3)
        cot = lax.all_to_all(cot_parts, "stream", 0, 0, axis_index_groups=across, tiled=True)
        mine, other = (
            jnp.concatenate([pack_pieces(w_mask[k], w_wide[k]), cot], axis=2) for k in range(CORES)
        )
    piece_rows = mine.shape[2] - frames
    base = 2 * wide + dmodel
    sizes = (group_count, slots, share, inner, direct, blocks * columns, slot_rows, hidden)
    got = time_forward(segments, widths[None], groups[None], spec, w_split, rnn0, sizes)
    slot_places, clips, slot_of, band_of, mask_places = got[:5]
    time_out, v_band, time_saved = got[5], got[6], got[7:]
    parts = group_count if direct else 1
    if direct:
        time_out, near = lax.optimization_barrier((time_out, near))
        rnn1 = near
    else:
        rnn1 = [rnn1]
        time_out = lax.all_to_all(time_out, "band", 0, 0, tiled=True)
    pack_shape = (blocks, rows, LANES)
    got = band_forward(
        slot_of, band_of, time_out.reshape(group_count * slots, quarter, dmodel), rnn1, pack_shape, parts, hidden
    )
    band_out, band_saved, rnn1 = got[0], got[1:8], got[8]
    band_out = band_out.reshape(group_count, outer, share, quarter, dmodel)
    if direct:
        back, grad_back, g_mask_vec = mask_exchange(mask_places, band_out, mine, v_band, base, piece_rows)
        back = lax.all_to_all(back, "stream", 0, 0, axis_index_groups=across, tiled=True)
        back = back.reshape((slots,) + back.shape[2:])
    else:
        band_out = lax.all_to_all(band_out, "stream", 1, 1, axis_index_groups=across, tiled=True)
        band_out = lax.all_to_all(band_out, "band", 0, 0, tiled=True)
        keep, send, grad_back, g_mask_vec = mask_network(
            mask_places, band_out, mine, other, v_band, base, piece_rows
        )
        grad_back = lax.all_to_all(grad_back, "band", 0, 0, tiled=True)
        grad_back = lax.all_to_all(grad_back, "stream", 1, 1, axis_index_groups=across, tiled=True)
        kept, sent = unpack_pieces(keep[:, :, :piece_rows], r), unpack_pieces(send, r)
        mask_reduced = return_slots(kept[0], sent[0], outer, inner, across, within, 1)
        widened_reduced = return_slots(kept[1], sent[1], outer, inner, across, within, 1).transpose(0, 2, 1)
        mask_parts = keep[:, :, piece_rows:]
        mask_parts = lax.all_to_all(mask_parts, "stream", 0, 0, axis_index_groups=across, tiled=True)
    grad_back = grad_back.reshape(group_count * slots, quarter, dmodel)
    band_grad, *g_rnn1 = band_backward(
        slot_of, band_of, grad_back, rnn1, band_saved, parts, hidden
    )
    grad_time = band_grad.reshape(group_count, slots, quarter, dmodel)
    if not direct:
        grad_time = lax.all_to_all(grad_time, "band", 0, 0, tiled=True)
    if direct:
        g_rnn1 = g_rnn1[:1] + [pass_along(g, "band", m) for m, g in enumerate(g_rnn1) if m]
    d_spec, g_split, g_rnn0 = time_backward(
        slot_places, clips, (my_stream // inner).astype(jnp.int32)[None], grad_time, spec, time_saved, w_split,
        v_band, rnn0, g_mask_vec, slot_rows, hidden,
    )
    if direct:
        dims = (slots, slot_rows, r, piece_rows, dmodel, hidden)
        state = tuple(x.transpose(0, 2, 1) if k % 8 == 1 else x for k, x in enumerate(state))
        scales, g_rnn0, g_rnn1, g_split, d_spec = finish(
            g_rnn0, g_split, g_rnn1, d_spec, back,
            tuple(x.reshape(2, -1, LANES) if k % 8 in (4, 5) else x for k, x in enumerate(state)),
            group_count, outer, dims,
        )
    else:
        d_spec = lax.psum(d_spec, "band")

    if not direct:
        masks = mask_parts.reshape(slots, frames, wide).transpose(1, 0, 2).reshape(cotangent.shape)
        spectrum_grad = d_spec.reshape(2, frames, padded)[:, :, :bins].transpose(1, 0, 2)

    if direct:
        *stepped, masks, spectrum_grad, grad_norm = update(scales, d_spec, (back, g_rnn0, g_rnn1, g_split), state, dims, bins)
        stepped = [x.transpose(0, 2, 1) if k % 8 == 1 else x for k, x in enumerate(stepped)]
        return (masks, spectrum_grad, grad_norm.reshape(())) + tuple(stepped)
    first, second = unpack_rnn(g_rnn0, dmodel, hidden), unpack_rnn(g_rnn1[0], dmodel, hidden)
    rnn_grads = [jnp.stack([a, b]) for a, b in zip(first[:3], second[:3])]
    rnn_grads.append(jnp.concatenate([first[3], second[3]], axis=0))
    rnn_grads = [
        lax.psum(lax.psum_scatter(g, "stream", scatter_dimension=d, tiled=True), "band")
        for g, d in zip(rnn_grads, (3, 3, 1, 1))
    ]
    g_band = unpack_banding(g_split, slots * slot_rows, slots, columns)
    g_split = g_split[:, : slots * slot_rows].reshape(blocks, slots, slot_rows, dmodel)
    g_split = g_split.transpose(1, 0, 2, 3).reshape(slots, wide, dmodel)
    split_reduced = lax.psum_scatter(g_split, "stream", scatter_dimension=1, tiled=True)
    band_reduced = lax.psum_scatter(g_band, "stream", scatter_dimension=1, tiled=True)
    reduced = (split_reduced, widened_reduced, mask_reduced, band_reduced) + tuple(rnn_grads)

    shares = (1.0,) * 4 + (1.0 / group_count,) * 4
    sizes = (group_count, stream_count)
    sums = [sum(jnp.sum(g * g) * part for g, part in zip(reduced, shares))]
    sums += [jnp.sum(w * w) * part for w, part in zip(weights, shares)]
    totals = sum_everywhere(jnp.stack(sums), sizes)
    grad_norm = jnp.sqrt(totals[0])
    factor = jnp.minimum(1.0, CLIP_NORM / grad_norm)
    moments = [lamb_moments(g, m, p, factor) for g, m, p in zip(reduced, means_old, powers_old)]
    directions = [lamb_direction(w, m, p, d) for w, (m, p), d in zip(weights, moments, DECAYS)]
    update_totals = sum_everywhere(
        jnp.stack([jnp.sum(d * d) * part for d, part in zip(directions, shares)]), sizes
    )
    ratios = jnp.sqrt(totals[1:]) / jnp.sqrt(update_totals + 1e-12)
    fresh = [w - LEARN_RATE * ratios[k] * d for k, (w, d) in enumerate(zip(weights, directions))]
    return (
        (masks, spectrum_grad, grad_norm)
        + tuple(fresh)
        + tuple(m for m, unused in moments)
        + tuple(p for unused, p in moments)
    )


def solution(mesh):
    stored = (
        P("band", "stream", None),
        P("band", None, "stream"),
        P("band", "stream", None),
        P("band", "stream"),
        P(None, None, None, "stream"),
        P(None, None, None, "stream"),
        P(None, "stream", None),
        P(None, "stream"),
    )
    frames_over = P("stream", None, None)
    mask_over = P("stream", "band", None, None)
    return jax.shard_map(
        body,
        mesh=mesh,
        in_specs=(frames_over, P("stream", None), P(), P(), mask_over) + stored * 3,
        out_specs=(mask_over, frames_over, P()) + stored * 3,
        check_vma=False,
    )
```

```python
from functools import partial
import math

import jax
import jax.numpy as jnp
from jax import lax
from jax.experimental import pallas as pl
from jax.experimental.pallas import tpu as pltpu
from jax.sharding import PartitionSpec as P

STEP = 10
CLIP_NORM = 5.0
LEARN_RATE = 0.5
BETA_ONE = 0.9
BETA_TWO = 0.999
ADAM_EPS = 1e-06
DECAY_RATE = 0.01
NORM_EPS = 1e-05
VAR_FLOOR = 0.25
CLIPS = 3
CLIP_MOST = 32
LANES = 128
VMEM_BYTES = 60 * 1024 * 1024
CORES = 2
SLOT_PAD = 16
MESH = pl.DeviceIdType.MESH

AB = (((1,), (0,)), ((), ()))
ABT = (((1,), (1,)), ((), ()))
ATB = (((0,), (0,)), ((), ()))


def split(x):
    hi = x.astype(jnp.bfloat16)
    lo = (x - hi.astype(jnp.float32)).astype(jnp.bfloat16)
    return hi, lo


def dot1(a, b, dims):
    return lax.dot_general(a, b, dims, preferred_element_type=jnp.float32)


def dot_parts(a, b, dims):
    return dot1(a[0], b[0], dims) + (dot1(a[1], b[0], dims) + dot1(a[0], b[1], dims))


def dot3(a, b, dims):
    return dot_parts(split(a), split(b), dims)


def sigmoid(x):
    return 0.5 * jnp.tanh(0.5 * x) + 0.5


def norm_stats(x):
    center = x - jnp.mean(x, axis=-1, keepdims=True)
    spread = jnp.mean(center * center, axis=-1, keepdims=True)
    scale = lax.rsqrt(spread + NORM_EPS)
    return center * scale, scale


def norm_back(grad_unit, unit, scale):
    first = jnp.mean(grad_unit, axis=-1, keepdims=True)
    second = jnp.mean(grad_unit * unit, axis=-1, keepdims=True)
    return scale * (grad_unit - first - unit * second)


def column_sum(x):
    return jnp.sum(x, axis=0, keepdims=True)


def pack_rows(dmodel, hidden):
    blocks = 4 * hidden // LANES
    out_rows = 2 * hidden // blocks
    weight_rows = 2 * dmodel + 2 * hidden + out_rows
    share = (2 * dmodel + 8 * hidden + dmodel) // blocks
    vec_rows = -(-share // LANES)
    return blocks, out_rows, weight_rows, share, vec_rows, -(-(weight_rows + vec_rows) // 32) * 32


def pack_rnn(w_in, w_rec, w_out, vec, rows, share):
    count = w_in.shape[2] // LANES
    parts = [
        w.reshape(2 * w.shape[1], count, LANES).transpose(1, 0, 2) for w in (w_in, w_rec)
    ] + [w_out.reshape(count, -1, LANES)]
    used = sum(p.shape[1] for p in parts)
    flat = jnp.pad(vec.reshape(count, share), ((0, 0), (0, (rows - used) * LANES - share)))
    return jnp.concatenate(parts + [flat.reshape(count, rows - used, LANES)], axis=1)


def unpack_rnn(pack, dmodel, hidden):
    blocks, out_rows, weight_rows, share, vec_rows, rows = pack_rows(dmodel, hidden)
    count = pack.shape[0]
    cuts = (0, 2 * dmodel, 2 * dmodel + 2 * hidden)
    w_in = pack[:, : cuts[1]].reshape(count, 2, dmodel, LANES).transpose(1, 2, 0, 3)
    w_rec = pack[:, cuts[1] : cuts[2]].reshape(count, 2, hidden, LANES).transpose(1, 2, 0, 3)
    return (
        w_in.reshape(2, dmodel, count * LANES),
        w_rec.reshape(2, hidden, count * LANES),
        pack[:, cuts[2] : weight_rows].reshape(count * out_rows, LANES),
        unpack_vec(pack, weight_rows, vec_rows, share),
    )


def unpack_vec(pack, weight_rows, vec_rows, share):
    count = pack.shape[0]
    flat = pack[:, weight_rows : weight_rows + vec_rows].reshape(count, vec_rows * LANES)
    return flat[:, :share].reshape(1, count * share)


class Pack:
    def __init__(self, ref, dmodel, hidden):
        self.ref, self.dmodel, self.hidden = ref, dmodel, hidden
        self.blocks, self.out_rows = pack_rows(dmodel, hidden)[:2]

    def intake(self, e, first, last):
        rows = slice(e * self.dmodel, (e + 1) * self.dmodel)
        return jnp.concatenate([self.ref[k, rows] for k in range(first, last)], axis=1)

    def recurrence(self, e, k):
        base = 2 * self.dmodel + e * self.hidden
        return self.ref[k, base : base + self.hidden]

    def outtake(self, e):
        base = 2 * self.dmodel + 2 * self.hidden
        half = self.blocks // 2
        return jnp.concatenate(
            [self.ref[k, base : base + self.out_rows] for k in range(half * e, half * (e + 1))], axis=0
        )

    def put(self, k, base, value):
        if len(self.ref.shape) == 3:
            self.ref[k, base : base + value.shape[0]] = value
            return
        quarter = self.ref.shape[2]
        done = 0
        while done < value.shape[0]:
            part, at = divmod(base + done, quarter)
            count = min(value.shape[0] - done, quarter - at)
            self.ref[part, k, at : at + count] = value[done : done + count]
            done += count

    def put_intake(self, e, q, value):
        for h in range(value.shape[1] // LANES):
            self.put(q * value.shape[1] // LANES + h, e * self.dmodel, value[:, h * LANES : (h + 1) * LANES])

    def put_recurrence(self, e, q, value):
        base = 2 * self.dmodel + e * self.hidden
        for h in range(value.shape[1] // LANES):
            self.put(q * value.shape[1] // LANES + h, base, value[:, h * LANES : (h + 1) * LANES])

    def put_outtake(self, e, value):
        base = 2 * self.dmodel + 2 * self.hidden
        for k in range(self.blocks // 2):
            self.put(self.blocks // 2 * e + k, base, value[k * self.out_rows : (k + 1) * self.out_rows])

    def put_vec(self, value):
        unused, unused, base, share, vec_rows, rows = pack_rows(self.dmodel, self.hidden)
        for k in range(self.blocks):
            block = [
                value[:, k * share + r * LANES : k * share + min(share, (r + 1) * LANES)] for r in range(vec_rows)
            ]
            block[-1] = jnp.concatenate(
                [block[-1], jnp.zeros((1, vec_rows * LANES - share), jnp.float32)], axis=1
            )
            block.append(jnp.zeros((rows - base - vec_rows, LANES), jnp.float32))
            self.put(k, base, jnp.concatenate(block, axis=0))


def load_vec(pack, vec):
    unused, unused, base, share, vec_rows, unused = pack_rows(pack.dmodel, pack.hidden)
    for k in range(pack.blocks):
        for r in range(vec_rows):
            width = min(LANES, share - r * LANES)
            at = k * share + r * LANES
            vec[0:1, at : at + width] = pack.ref[k, base + r : base + r + 1, :width]


def split_recurrence(pack, hi_ref, lo_ref):
    for e in range(2):
        for k in range(pack.blocks):
            part = slice(k * LANES, (k + 1) * LANES)
            hi_ref[e, :, part], lo_ref[e, :, part] = split(pack.recurrence(e, k))


def split_recurrence_turned(pack, hi_ref, lo_ref):
    for e in range(2):
        for k in range(pack.blocks):
            part = slice(k * LANES, (k + 1) * LANES)
            hi_ref[e, part], lo_ref[e, part] = split(pack.recurrence(e, k).T)


def gates_forward(x_flat, act, pack, vec, rows, block):
    hidden4 = 4 * pack.hidden
    dmodel = pack.dmodel
    parts = [split(pack.intake(e, 0, pack.blocks)) for e in range(2)]

    def one(r, carry):
        start = pl.multiple_of(r * block, block)
        unit, unused = norm_stats(x_flat(start, block))
        n = split(unit * (1.0 + vec[0:1, :dmodel]) + vec[0:1, dmodel : 2 * dmodel])
        for e in range(2):
            bias = vec[0:1, 2 * dmodel + hidden4 * e : 2 * dmodel + hidden4 * (e + 1)]
            z = dot_parts(n, parts[e], AB) + bias
            act[e][pl.ds(r * (block // 16), block // 16)] = z.reshape(block // 16, 16, hidden4)
        return carry

    lax.fori_loop(0, rows // block, one, 0)


def run_forward(steps, places, act, c, h, pack, hi_ref, lo_ref, state, memory):
    hidden = pack.hidden
    for e in range(2):
        state[e][...] = jnp.zeros_like(state[e])
        memory[e][...] = jnp.zeros_like(memory[e])

    def step(j, carry):
        work = []
        for e in range(2):
            at = places(e, j)
            prior = state[e][...]
            hi, lo = split(prior)
            rows = prior.shape[0]
            first = dot1(jnp.concatenate([hi, lo], axis=0), hi_ref[e], AB)
            drive = [act[e][p] for p in at]
            drive = drive[0] if len(drive) == 1 else jnp.concatenate(drive, axis=0)
            z = first[:rows] + first[rows:] + dot1(hi, lo_ref[e], AB) + drive
            work.append((at, z))
        for e in range(2):
            at, z = work[e]
            ingate = sigmoid(z[:, :hidden])
            forget = sigmoid(z[:, hidden : 2 * hidden])
            candidate = jnp.tanh(z[:, 2 * hidden : 3 * hidden])
            outgate = sigmoid(z[:, 3 * hidden :])
            before = memory[e][...]
            now = forget * before + ingate * candidate
            squashed = jnp.tanh(now)
            out = outgate * squashed
            memory[e][...] = now
            state[e][...] = out
            for k, p in enumerate(at):
                part = slice(16 * k, 16 * (k + 1))
                act[e][p, :, :hidden] = ingate[part]
                act[e][p, :, hidden : 2 * hidden] = forget[part]
                act[e][p, :, 2 * hidden : 3 * hidden] = candidate[part]
                act[e][p, :, 3 * hidden :] = outgate[part]
                c[e][p] = now[part]
                h[e][p] = out[part]
        return carry

    lax.fori_loop(0, steps, step, 0, unroll=4)


def output_forward(count, h, pack, vec):
    hidden = h[0].shape[2]
    dmodel = pack.dmodel
    total = vec[0:1, vec.shape[1] - dmodel :]
    for e in range(2):
        states = h[e][:count].reshape(count * 16, hidden)
        total = total + dot3(states, pack.outtake(e), AB)
    return total


def run_backward(steps, places, act, dz_ref, c, dh, pack, hi_ref, lo_ref, grad_h, grad_c):
    hidden = pack.hidden
    for e in range(2):
        grad_h[e][...] = jnp.zeros_like(grad_h[e])
        grad_c[e][...] = jnp.zeros_like(grad_c[e])

    def load(ref, at):
        got = [ref[p] for p in at]
        return got[0] if len(got) == 1 else jnp.concatenate(got, axis=0)

    def step(back, carry):
        j = steps - 1 - back
        later = jnp.minimum(j, 1).astype(jnp.float32)
        work = []
        for e in range(2):
            at = places(e, j)
            gates = load(act[e], at)
            ingate = gates[:, :hidden]
            forget = gates[:, hidden : 2 * hidden]
            candidate = gates[:, 2 * hidden : 3 * hidden]
            outgate = gates[:, 3 * hidden :]
            squashed = jnp.tanh(load(c[e], at))
            before = load(c[e], places(e, jnp.maximum(j - 1, 0))) * later
            total_h = load(dh[e], at) + grad_h[e][...]
            total_c = grad_c[e][...] + total_h * outgate * (1.0 - squashed * squashed)
            dz = jnp.concatenate(
                [
                    total_c * candidate * ingate * (1.0 - ingate),
                    total_c * before * forget * (1.0 - forget),
                    total_c * ingate * (1.0 - candidate * candidate),
                    total_h * squashed * outgate * (1.0 - outgate),
                ],
                axis=1,
            )
            grad_c[e][...] = total_c * forget
            for k, p in enumerate(at):
                dz_ref[e][p] = dz[16 * k : 16 * (k + 1)]
            work.append(dz)
        for e in range(2):
            hi, lo = split(work[e])
            rows = hi.shape[0]
            first = dot1(jnp.concatenate([hi, lo], axis=0), hi_ref[e], AB)
            grad_h[e][...] = first[:rows] + first[rows:] + dot1(hi, lo_ref[e], AB)
        return carry

    lax.fori_loop(0, steps, step, 0, unroll=4)


def states_backward(count, dy_flat, dh, h, pack, g_pack):
    hidden = h[0].shape[2]
    dy = split(dy_flat)
    for e in range(2):
        dh[e][:count] = dot_parts(dy, split(pack.outtake(e)), ABT).reshape(count, 16, hidden)
        g_pack.put_outtake(e, dot3_parts_first(h[e][:count].reshape(count * 16, hidden), dy))


def dot3_parts_first(a, b_parts):
    return dot_parts(split(a), b_parts, ATB)


def gates_backward(count, x_flat, dy_flat, dz_ref, before, pack, vec, g_pack, g_vec):
    dmodel, hidden = pack.dmodel, pack.hidden
    hidden4 = 4 * hidden
    rows = count * 16
    unit, scale = norm_stats(x_flat)
    gain = 1.0 + vec[0:1, :dmodel]
    n = unit * gain + vec[0:1, dmodel : 2 * dmodel]
    dn = jnp.zeros((rows, dmodel), jnp.float32)
    for e in range(2):
        left_hi, left_lo = split(jnp.concatenate([n, before(e)], axis=1).T)
        left = jnp.concatenate([left_hi, left_lo], axis=0)
        height = left_hi.shape[0]
        for q in range(4):
            part = slice(hidden * q, hidden * (q + 1))
            dz_q = dz_ref[e][:count, :, part].reshape(rows, hidden)
            dz = split(dz_q)
            first = dot1(left, dz[0], AB)
            got = first[:height] + first[height:] + dot1(left_hi, dz[1], AB)
            g_pack.put_intake(e, q, got[:dmodel])
            g_pack.put_recurrence(e, q, got[dmodel:])
            dn = dn + dot_parts(dz, split(pack.intake(e, q * pack.blocks // 4, (q + 1) * pack.blocks // 4)), ABT)
            base = 2 * dmodel + hidden4 * e + hidden * q
            g_vec[0:1, base : base + hidden] = column_sum(dz_q)
    g_vec[0:1, :dmodel] = column_sum(dn * unit)
    g_vec[0:1, dmodel : 2 * dmodel] = column_sum(dn)
    g_vec[0:1, vec.shape[1] - dmodel :] = column_sum(dy_flat)
    g_pack.put_vec(g_vec[...])
    return dy_flat + norm_back(dn * gain, unit, scale)


def input_backward(count, x_flat, dy_flat, dz_ref, pack, vec, g_vec):
    dmodel, hidden = pack.dmodel, pack.hidden
    rows = count * 16
    unit, scale = norm_stats(x_flat)
    gain = 1.0 + vec[0:1, :dmodel]
    dn = jnp.zeros((rows, dmodel), jnp.float32)
    for e in range(2):
        for q in range(4):
            part = slice(hidden * q, hidden * (q + 1))
            dz = split(dz_ref[e][:count, :, part].reshape(rows, hidden))
            dn = dn + dot_parts(dz, split(pack.intake(e, q * pack.blocks // 4, (q + 1) * pack.blocks // 4)), ABT)
    g_vec[0:1, :dmodel] = column_sum(dn * unit)
    g_vec[0:1, dmodel : 2 * dmodel] = column_sum(dn)
    g_vec[0:1, vec.shape[1] - dmodel :] = column_sum(dy_flat)
    return dy_flat + norm_back(dn * gain, unit, scale)


def weights_backward(count, x_flat, dz_ref, before, pack, vec, g_pack, g_vec):
    dmodel, hidden = pack.dmodel, pack.hidden
    rows = count * 16
    unit, unused = norm_stats(x_flat)
    n = unit * (1.0 + vec[0:1, :dmodel]) + vec[0:1, dmodel : 2 * dmodel]
    for e in range(2):
        left_hi, left_lo = split(jnp.concatenate([n, before(e)], axis=1).T)
        left = jnp.concatenate([left_hi, left_lo], axis=0)
        height = left_hi.shape[0]
        for q in range(4):
            part = slice(hidden * q, hidden * (q + 1))
            dz_q = dz_ref[e][:count, :, part].reshape(rows, hidden)
            dz = split(dz_q)
            first = dot1(left, dz[0], AB)
            got = first[:height] + first[height:] + dot1(left_hi, dz[1], AB)
            g_pack.put_intake(e, q, got[:dmodel])
            g_pack.put_recurrence(e, q, got[dmodel:])
            base = 2 * dmodel + 4 * hidden * e + hidden * q
            g_vec[0:1, base : base + hidden] = column_sum(dz_q)
    g_pack.put_vec(g_vec[...])


def shifted(ref, e, count, hidden, mask):
    rows = (count - 1) * 16
    zero = jnp.zeros((16, hidden), jnp.float32)
    if e == 0:
        kept = ref[: count - 1].reshape(rows, hidden) * mask
        return jnp.concatenate([zero, kept], axis=0)
    kept = ref[1:count].reshape(rows, hidden) * mask
    return jnp.concatenate([kept, zero], axis=0)


def tables_kernel(
    slots, share, inner, direct, segments, widths, groups, places, clips, slot_of, band_of, mask_places, counts
):
    band, stream = lax.axis_index("band"), lax.axis_index("stream")
    for s in range(slots):
        places[0, s] = 0
        places[1, s] = 0
    for s in range(band_of.shape[1]):
        band_of[0, s] = 0
        band_of[1, s] = 0
    for c in range(CLIPS):
        clips[1, c] = 0
    for g in range(counts.shape[0]):
        counts[g] = 0

    def one_band(b, edge):
        g = groups[0, b]
        rank = counts[g]
        counts[g] = rank + 1
        slot_of[0, b] = g * slots + rank
        band_of[0, g * slots + rank] = b
        band_of[1, g * slots + rank] = 1
        width = widths[0, b]

        @pl.when(g == band)
        def mine():
            places[0, rank] = edge
            places[1, rank] = width

        return edge + width

    lax.fori_loop(0, groups.shape[1], one_band, jnp.int32(0))

    def one_frame(t, carry):
        c = segments[0, t]
        clips[1, c] = clips[1, c] + 1
        return carry

    lax.fori_loop(0, segments.shape[1], one_frame, 0)
    start = jnp.int32(0)
    for c in range(CLIPS):
        clips[0, c] = start
        start = start + clips[1, c]
    for j in range(share):
        row = lax.div(stream, inner) * share + j
        mask_places[0, j] = places[1, row]
        mask_places[1, j] = lax.rem(stream, CORES) if direct else jnp.int32(0)
        mask_places[2, j] = row


def table_shapes(slots, share, bands, parts):
    shapes = ((2, slots), (2, CLIPS), (1, bands), (2, parts * slots), (3, share))
    return [jax.ShapeDtypeStruct(x, jnp.int32) for x in shapes]


def clip_places(clips, spare):
    def places(e, j):
        found = []
        for c in range(CLIPS):
            start, length = clips[0, c], clips[1, c]
            frame = start + j if e == 0 else start + length - 1 - j
            found.append(jnp.where(j < length, frame, spare))
        return found

    return places


def window_of(edge):
    base = pl.multiple_of((edge // LANES) * LANES, LANES)
    return base, lax.rem(edge, LANES)


def where_valid(width, frames):
    lane = lax.broadcasted_iota(jnp.int32, (frames, LANES), 1)
    inside = (lane < width).astype(jnp.float32)
    return jnp.concatenate([inside, inside], axis=1), jnp.maximum(2 * width, 1).astype(jnp.float32)


def split_rows(spec, edge, width, frames):
    wmax = LANES
    base, shift = window_of(edge)
    window = spec[:, pl.ds(base, 2 * LANES)]
    taken = pltpu.roll(window, lax.rem(2 * LANES - shift, 2 * LANES), 1)[:, :wmax]
    taken = jnp.concatenate([taken[:frames], taken[frames:]], axis=1)
    valid, entries = where_valid(width, frames)
    mean = jnp.sum(taken * valid, axis=-1, keepdims=True) / entries
    center = (taken - mean) * valid
    spread = jnp.sum(center * center, axis=-1, keepdims=True) / entries
    scale = lax.rsqrt(jnp.maximum(spread, VAR_FLOOR))
    moving = jnp.where(spread > VAR_FLOOR, 1.0, jnp.where(spread == VAR_FLOOR, 0.5, 0.0))
    return center * scale, scale, valid, moving, entries


def slot_weights(w_split, s, slot_rows):
    count = w_split.shape[0]
    at = pl.ds(pl.multiple_of(s * slot_rows, slot_rows), slot_rows)
    return jnp.concatenate([w_split[k, at, :] for k in range(count)], axis=0)


def time_forward_kernel(
    slot_rows, share, inner, direct, segments, widths, groups, spec_in, w_split_in, rnn_in,
    places_s, clips, slot_of, band_of, mask_places, out, v_band, x, *refs,
):
    saved, refs = refs[:6], refs[6:]
    act0, act1, c0, c1, h0, h1, hi_ref, lo_ref, s0, s1, m0, m1, y, mixed, vec, rnn, w_split, spec, *refs = refs
    counts, sems = refs
    slots = out.shape[1]
    frames, unused, dmodel = x.shape
    wide = w_split.shape[0] * slot_rows
    pack = Pack(rnn, dmodel, h0.shape[2])
    load_split = pltpu.make_async_copy(w_split_in, w_split, sems.at[7])
    load_spec = pltpu.make_async_copy(spec_in, spec, sems.at[8])
    load_rnn = pltpu.make_async_copy(rnn_in, rnn, sems.at[0])
    for copy in (load_split, load_spec, load_rnn):
        copy.start()
    tables_kernel(
        slots, share, inner, direct, segments, widths, groups, places_s, clips, slot_of, band_of, mask_places, counts
    )
    load_split.wait()
    load_spec.wait()
    v_band[...] = jnp.zeros_like(v_band)
    columns = v_band.shape[1] // w_split.shape[0]
    for k in range(w_split.shape[0]):
        for h in range(0, columns, LANES):
            width = min(LANES, columns - h)
            at = slots * slot_rows + SLOT_PAD * (h // LANES)
            v_band[:, k * columns + h : k * columns + h + width] = w_split[k, at : at + SLOT_PAD, :width]
    x[...] = jnp.zeros_like(x)
    for a in (act0, act1):
        a[frames] = jnp.zeros_like(a[frames])

    for s in range(slots):
        unit, unused, valid, moving, entries = split_rows(spec, places_s[0, s], places_s[1, s], frames)
        row = v_band[s : s + 1, : 2 * wide + dmodel]
        z = (unit * (1.0 + row[:, :wide]) + row[:, wide : 2 * wide]) * valid
        y[s] = dot3(z, slot_weights(w_split, s, slot_rows), AB) + row[:, 2 * wide : 2 * wide + dmodel]
    for s in range(slots):
        x[:, s, :] = y[s]
    load_rnn.wait()
    load_vec(pack, vec)
    split_recurrence(pack, hi_ref, lo_ref)
    act = (act0, act1)

    def x_flat(start, size):
        return x[pl.ds(start // 16, size // 16)].reshape(size, dmodel)

    gates_forward(x_flat, act, pack, vec, frames * 16, 256)
    run_forward(
        CLIP_MOST, clip_places(clips, frames), act, (c0, c1), (h0, h1),
        pack, hi_ref, lo_ref, (s0, s1), (m0, m1),
    )
    leaving = [
        pltpu.make_async_copy(a, b, sems.at[1 + k])
        for k, (a, b) in enumerate(zip((act0, act1, c0, c1, h0, h1), saved))
    ]
    for copy in leaving:
        copy.start()
    total = output_forward(frames, (h0, h1), pack, vec)
    x_all = x[...].reshape(frames * 16, dmodel)
    mixed[...] = (x_all + total).reshape(frames, 16, dmodel)
    parts, unused_slots, quarter, unused = out.shape
    for s in range(slots):
        for q in range(parts):
            out[q, s] = mixed[q * quarter : (q + 1) * quarter, s, :]
    for copy in leaving:
        copy.wait()


def f32(shape):
    return jax.ShapeDtypeStruct(shape, jnp.float32)


def saved_shapes(count, hidden):
    return [f32((count, 16, 4 * hidden))] * 2 + [f32((count, 16, hidden))] * 4


def saved_scratch(count, hidden):
    return [pltpu.VMEM(x.shape, jnp.float32) for x in saved_shapes(count, hidden)]


def vec_scratch(dmodel, hidden):
    return pltpu.VMEM((1, 3 * dmodel + 8 * hidden), jnp.float32)


def rec_scratch(rows, hidden, turned=False):
    return [
        pltpu.VMEM((2, 4 * hidden, hidden) if turned else (2, hidden, 4 * hidden), jnp.bfloat16),
        pltpu.VMEM((2, 4 * hidden, hidden) if turned else (2, hidden, 4 * hidden), jnp.bfloat16),
    ] + [pltpu.VMEM((rows, hidden), jnp.float32)] * 4


SMEM = pl.BlockSpec(memory_space=pltpu.SMEM)
VMEM = pl.BlockSpec(memory_space=pltpu.VMEM)
ANY = pl.BlockSpec(memory_space=pl.ANY)
PARAMS = pltpu.CompilerParams(vmem_limit_bytes=VMEM_BYTES)


def cost(micros):
    return pl.CostEstimate(flops=int(micros * 1.1e9), bytes_accessed=int(micros * 3e6), transcendentals=0)


def time_forward(segments, widths, groups, spec, w_split, rnn, sizes):
    parts, slots, share, inner, direct, band_columns, slot_rows, hidden = sizes
    dmodel = w_split.shape[2]
    frames = spec.shape[0] // 2
    return pl.pallas_call(
        partial(time_forward_kernel, slot_rows, share, inner, direct),
        out_shape=table_shapes(slots, share, widths.shape[1], parts)
        + [
            f32((parts, slots, frames // parts, dmodel)), f32((SLOT_PAD, band_columns)), f32((frames, 16, dmodel)),
        ]
        + saved_shapes(frames + 1, hidden),
        in_specs=[SMEM] * 3 + [ANY] * 3,
        out_specs=[SMEM] * 5 + [VMEM] * 3 + [ANY] * 6,
        scratch_shapes=saved_scratch(frames + 1, hidden)
        + rec_scratch(16 * CLIPS, hidden)
        + [pltpu.VMEM((slots, frames, dmodel), jnp.float32)]
        + [pltpu.VMEM((frames, 16, dmodel), jnp.float32), vec_scratch(dmodel, hidden)]
        + [pltpu.VMEM(a.shape, jnp.float32) for a in (rnn, w_split, spec)]
        + [pltpu.SMEM((parts,), jnp.int32), pltpu.SemaphoreType.DMA((9,))],
        compiler_params=PARAMS,
        cost_estimate=cost(35),
        name="time_forward",
    )(segments, widths, groups, spec, w_split, rnn)


def time_backward_kernel(
    slot_rows, places_s, clips, my_outer, dy_in, spec_in, x_in, *refs,
):
    saved, refs = refs[:6], refs[6:]
    w_split_in, v_band, rnn_in, g_mask_vec, d_spec, g_split, g_rnn_out, *refs = refs
    act0, act1, c0, c1, h0, h1, *refs = refs
    hi_ref, lo_ref, s0, s1, m0, m1, dy, vec, g_vec, g_band, dh0, dh1, dz0, dz1, *refs = refs
    rnn, w_split, spec, x, g_rnn, units, stats, sems = refs
    slots = dy_in.shape[1]
    frames, unused, dmodel = x.shape
    hidden = h0.shape[2]
    wide = w_split.shape[0] * slot_rows
    parts, unused_slots, quarter, unused = dy_in.shape
    pack, g_pack = Pack(rnn, dmodel, hidden), Pack(g_rnn, dmodel, hidden)
    pairs = [(rnn_in, rnn), (saved[4], h0), (saved[5], h1)]
    pairs += [(spec_in, spec)] + list(zip(saved[:4], (act0, act1, c0, c1)))
    pairs += [(w_split_in, w_split), (x_in, x)]
    loads = [pltpu.make_async_copy(a, b, sems.at[k]) for k, (a, b) in enumerate(pairs)]
    for copy in loads:
        copy.start()
    dy[...] = jnp.zeros_like(dy)
    for s in range(slots):
        for q in range(parts):
            dy[q * quarter : (q + 1) * quarter, s, :] = dy_in[q, s]
    for copy in loads[:3]:
        copy.wait()
    load_vec(pack, vec)
    dy_flat = dy[...].reshape(frames * 16, dmodel)
    split_recurrence_turned(pack, hi_ref, lo_ref)
    states_backward(frames, dy_flat, (dh0, dh1), (h0, h1), pack, g_pack)
    loads[3].wait()
    lane = lax.broadcasted_iota(jnp.int32, (frames, LANES), 1)
    for s in range(slots):
        unit, scale, valid, moving, entries = split_rows(spec, places_s[0, s], places_s[1, s], frames)
        units[s] = unit
        stats[s] = jnp.where(lane == 0, scale, moving)
    for d in (dh0, dh1):
        d[frames] = jnp.zeros_like(d[frames])
    for copy in loads[4:8]:
        copy.wait()
    run_backward(
        CLIP_MOST, clip_places(clips, frames), (act0, act1), (dz0, dz1), (c0, c1),
        (dh0, dh1), pack, hi_ref, lo_ref, (s0, s1), (m0, m1),
    )
    for copy in loads[8:]:
        copy.wait()
    frame = lax.broadcasted_iota(jnp.int32, ((frames - 1) * 16, 1), 0) // 16 + 1
    inside = jnp.ones(frame.shape, jnp.float32)
    for k in range(1, CLIPS):
        inside = jnp.where(frame == clips[0, k], 0.0, inside)
    x_flat = x[...].reshape(frames * 16, dmodel)
    dx = gates_backward(
        frames, x_flat, dy[...].reshape(frames * 16, dmodel), (dz0, dz1),
        lambda e: shifted((h0, h1)[e], e, frames, hidden, inside), pack, vec, g_pack, g_vec,
    )
    g_rnn_leaves = pltpu.make_async_copy(g_rnn, g_rnn_out, sems.at[10])
    g_rnn_leaves.start()
    dy[...] = dx.reshape(frames, 16, dmodel)
    d_spec[...] = jnp.zeros_like(d_spec)
    g_split[:, slots * slot_rows :] = jnp.zeros_like(g_split[:, slots * slot_rows :])
    g_band[...] = jnp.zeros_like(g_band)

    for s in range(slots):
        edge, width = places_s[0, s], places_s[1, s]
        unit, scale, moving = units[s], stats[s][:, 0:1], stats[s][:, 1:2]
        valid, entries = where_valid(width, frames)
        row = v_band[s : s + 1, : 2 * wide + dmodel]
        gain = 1.0 + row[:, :wide]
        z = (unit * gain + row[:, wide : 2 * wide]) * valid
        demb = dy[:, s, :]
        demb_parts = split(demb)
        g_slot = dot_parts(split(z), demb_parts, ATB)
        for k in range(w_split.shape[0]):
            g_split[k, s * slot_rows : (s + 1) * slot_rows] = g_slot[k * slot_rows : (k + 1) * slot_rows]
        dz = dot_parts(demb_parts, split(slot_weights(w_split, s, slot_rows)), ABT) * valid
        g_band[s : s + 1, :wide] = column_sum(dz * unit)
        g_band[s : s + 1, wide : 2 * wide] = column_sum(dz)
        g_band[s : s + 1, 2 * wide : 2 * wide + dmodel] = column_sum(demb)
        du = dz * gain
        first = jnp.sum(du, axis=-1, keepdims=True) / entries
        second = jnp.sum(du * unit, axis=-1, keepdims=True) / entries
        dt = scale * (du - first - moving * unit * second) * valid
        base, shift = window_of(edge)
        stacked = jnp.concatenate([dt[:, :LANES], dt[:, LANES:]], axis=0)
        padded = jnp.concatenate([stacked, jnp.zeros_like(stacked)], axis=1)
        d_spec[:, pl.ds(base, 2 * LANES)] += pltpu.roll(padded, shift, 1)

    share = g_mask_vec.shape[0]
    for j in range(share):
        g_band[pl.ds(my_outer[0] * share + j, 1), 2 * wide + dmodel :] = g_mask_vec[j]
    gathered = g_band[...]
    blocks = w_split.shape[0]
    columns = gathered.shape[1] // blocks
    for k in range(blocks):
        for h in range(0, columns, LANES):
            width = min(LANES, columns - h)
            at = slots * slot_rows + SLOT_PAD * (h // LANES)
            g_split[k, at : at + SLOT_PAD, :width] = gathered[:, k * columns + h : k * columns + h + width]
    g_rnn_leaves.wait()


def time_backward(
    slot_places, clips, my_outer, dy, spec, saved, w_split, v_band, rnn, g_mask_vec, slot_rows, hidden
):
    band_columns, slots = v_band.shape[1], dy.shape[1]
    dmodel = w_split.shape[2]
    frames = spec.shape[0] // 2
    return pl.pallas_call(
        partial(time_backward_kernel, slot_rows),
        out_shape=[f32(spec.shape), f32(w_split.shape), f32(rnn.shape)],
        in_specs=[SMEM] * 3 + [VMEM] + [ANY] * (2 + 6 + 1) + [VMEM, ANY, VMEM],
        out_specs=[VMEM, VMEM, ANY],
        scratch_shapes=saved_scratch(frames + 1, hidden)
        + rec_scratch(16 * CLIPS, hidden, True)
        + [pltpu.VMEM((frames, 16, dmodel), jnp.float32)] + [vec_scratch(dmodel, hidden)] * 2
        + [pltpu.VMEM((SLOT_PAD, band_columns), jnp.float32)]
        + [pltpu.VMEM((frames + 1, 16, hidden), jnp.float32)] * 2
        + [pltpu.VMEM((frames + 1, 16, 4 * hidden), jnp.float32)] * 2
        + [pltpu.VMEM(a.shape, jnp.float32) for a in (rnn, w_split, spec, saved[0], rnn)]
        + [pltpu.VMEM((slots, frames, w), jnp.float32) for w in (2 * LANES, LANES)]
        + [pltpu.SemaphoreType.DMA((11,))],
        compiler_params=PARAMS,
        cost_estimate=cost(2),
        name="time_backward",
    )(slot_places, clips, my_outer, dy, spec, *saved, w_split, v_band, rnn, g_mask_vec)


def in_turn(core, mine, other):
    return [jnp.where(core == 0, mine, other), jnp.where(core == 0, other, mine)]


def pack_pieces(mask, wide):
    lead, r, w = mask.shape[:2], mask.shape[2], mask.shape[3] // 2
    mask = mask.reshape(lead + (r, 2, w)).transpose(0, 1, 3, 2, 4).reshape(lead + (2 * r, w))
    wide = wide.reshape(lead + (2, r // 2, w // 2)).transpose(0, 1, 3, 2, 4)
    return jnp.concatenate([mask, wide.reshape(lead + (r // 2, w))], axis=2)


def unpack_pieces(pack, r):
    lead, w = pack.shape[:2], pack.shape[3]
    mask = pack[:, :, : 2 * r].reshape(lead + (2, r, w)).transpose(0, 1, 3, 2, 4).reshape(lead + (r, 2 * w))
    wide = pack[:, :, 2 * r :].reshape(lead + (r // 2, 2, w // 2)).transpose(0, 1, 3, 2, 4)
    return mask, wide.reshape(lead + (r, w // 2))


def load_mask_piece(value, r):
    return jnp.concatenate([value[:r], value[r : 2 * r]], axis=1)


def load_wide_piece(value):
    half = value.shape[1] // 2
    return jnp.concatenate([value[:, :half], value[:, half:]], axis=0)


def mask_slot(core, width, v, x, mine, other, keep, send, g_vec):
    outer, total_rows, wide = mine.shape
    piece_rows = send.shape[1]
    frames = total_rows - piece_rows
    dmodel = x.shape[1]
    half = wide // 2
    mlp = (v.shape[1] - 2 * dmodel) - 2 * wide
    r = mlp // (2 * outer)
    w_wide, w_mask = [], []
    for g in range(outer):
        w_mask += in_turn(core, load_mask_piece(mine[g, : 2 * r], r), load_mask_piece(other[g, : 2 * r], r))
        w_wide += in_turn(
            core, load_wide_piece(mine[g, 2 * r : piece_rows]), load_wide_piece(other[g, 2 * r : piece_rows])
        )
    w_wide, w_mask = jnp.concatenate(w_wide, axis=0), jnp.concatenate(w_mask, axis=0)
    cot = jnp.concatenate([mine[g, piece_rows:] for g in range(outer)], axis=0)
    gain = 1.0 + v[:, :dmodel]
    unit, scale = norm_stats(x)
    p = split(unit * gain + v[:, dmodel : 2 * dmodel])
    wide_parts = split(w_wide)
    mask_parts = split(w_mask)
    q = jnp.tanh(dot_parts(p, wide_parts, ABT) + v[:, 2 * dmodel : 2 * dmodel + mlp])
    q_parts = split(q)
    raw = dot_parts(q_parts, mask_parts, AB) + v[:, 2 * dmodel + mlp :]
    lane = lax.broadcasted_iota(jnp.int32, (1, half), 1)
    inside = (lane < width).astype(jnp.float32)
    valid = jnp.concatenate([inside, inside], axis=1)
    value = raw[:, :wide]
    gate = sigmoid(raw[:, wide:])
    masks = value * gate * valid
    dm = cot * valid
    dr = jnp.concatenate([dm * gate, dm * value * gate * (1.0 - gate)], axis=1)
    dr_parts = split(dr)
    g_mask = dot_parts(q_parts, dr_parts, ATB)
    dq = dot_parts(dr_parts, mask_parts, ABT)
    da = dq * (1.0 - q * q)
    da_parts = split(da)
    g_wide = dot_parts(da_parts, p, ATB)
    for g in range(outer):
        first, second = slice(2 * g * r, (2 * g + 1) * r), slice((2 * g + 1) * r, (2 * g + 2) * r)
        for ref, got in zip((keep, send), in_turn(core, g_mask[first], g_mask[second])):
            ref[g, :r] = got[:, :wide]
            ref[g, r : 2 * r] = got[:, wide:]
        for ref, got in zip((keep, send), in_turn(core, g_wide[first], g_wide[second])):
            ref[g, 2 * r : piece_rows, :half] = got[: r // 2]
            ref[g, 2 * r : piece_rows, half:] = got[r // 2 :]
        keep[g, piece_rows:] = masks[g * frames : (g + 1) * frames]
    dp = dot_parts(da_parts, wide_parts, AB)
    g_vec[:, :dmodel] = column_sum(dp * unit)
    g_vec[:, dmodel : 2 * dmodel] = column_sum(dp)
    g_vec[:, 2 * dmodel : 2 * dmodel + mlp] = column_sum(da)
    g_vec[:, 2 * dmodel + mlp :] = column_sum(dr)
    return norm_back(dp * gain, unit, scale)


def mask_kernel(base, places, arrived, mine, other, v_band, keep, send, grad, g_vec):
    s = pl.program_id(0)
    parts, streams, unused, quarter, dmodel = arrived.shape
    order = [(q, g) for g in range(streams) for q in range(parts)]
    x = jnp.concatenate([arrived[q, g, 0] for q, g in order], axis=0)
    dx = mask_slot(
        places[1, 0], places[0, s], v_band[pl.ds(places[2, s], 1), base:], x,
        mine.at[:, 0], other.at[:, 0], keep.at[:, 0], send.at[:, 0], g_vec.at[0],
    )
    for k, (q, g) in enumerate(order):
        grad[q, g, 0] = dx[k * quarter : (k + 1) * quarter]


def mask_network(places, arrived, mine, other, v_band, base, piece_rows):
    parts, streams, slots, quarter, dmodel = arrived.shape
    outer, unused, rows, wide = mine.shape

    def second(count):
        return pl.BlockSpec((outer, 1, count, wide), lambda s: (0, s, 0, 0))

    moving = pl.BlockSpec((parts, streams, 1, quarter, dmodel), lambda s: (0, 0, s, 0, 0))
    columns = v_band.shape[1] - base
    vector = pl.BlockSpec((1, 1, columns), lambda s: (s, 0, 0))
    return pl.pallas_call(
        partial(mask_kernel, base),
        grid=(slots,),
        out_shape=[
            f32(mine.shape), f32((outer, slots, piece_rows, wide)), f32(arrived.shape), f32((slots, 1, columns)),
        ],
        in_specs=[SMEM, moving, second(rows), second(rows), VMEM],
        out_specs=[second(rows), second(piece_rows), moving, vector],
        compiler_params=PARAMS,
        cost_estimate=cost(12),
        name="mask_network",
    )(places, arrived, mine, other, v_band)


class Links:
    def __init__(self, bands, layers, send_sems, recv_sems):
        self.bands, self.layers = bands, layers
        self.band, self.stream = lax.axis_index("band"), lax.axis_index("stream")
        self.layer, self.core = lax.div(self.stream, CORES), lax.rem(self.stream, CORES)
        self.other = self.stream + 1 - 2 * self.core
        self.send_sems, self.recv_sems = send_sems, recv_sems
        self.started = []

    def band_to(self, m):
        return lax.rem(self.band + m, self.bands)

    def band_from(self, m):
        return lax.rem(self.band + self.bands - m, self.bands)

    def layer_to(self, k):
        return lax.rem(self.layer + k, self.layers)

    def layer_from(self, k):
        return lax.rem(self.layer + self.layers - k, self.layers)

    def band_beside(self, k):
        return lax.rem(self.band + 2, 4) if k % 4 >= 2 else self.band + 1 - 2 * lax.rem(self.band, 2)

    def band_across(self):
        return 3 - self.band

    def goal(self, k):
        beside = self.layer + 1 - 2 * lax.rem(self.layer, 2)
        return (beside, 3 - self.layer, lax.rem(self.layer + 2, 4), self.layer)[k]

    def own(self, layer):
        return layer * CORES + self.core

    def across(self, layer):
        return layer * CORES + 1 - self.core

    def greet(self, partners):
        barrier = pltpu.get_barrier_semaphore()
        for partner in partners:
            pl.semaphore_signal(barrier, inc=1, device_id=partner, device_id_type=MESH)
        pl.semaphore_wait(barrier, len(partners))

    def copy(self, source, target, index, partner):
        return pltpu.make_async_remote_copy(
            src_ref=source, dst_ref=target, send_sem=self.send_sems.at[index],
            recv_sem=self.recv_sems.at[index], device_id=partner, device_id_type=MESH,
        )

    def send(self, source, target, index, partner):
        copy = self.copy(source, target, index, partner)
        copy.start()
        self.started.append(copy)

    def arrive(self, target, index):
        self.copy(target, target, index, (self.band, self.other)).wait_recv()

    def finish(self):
        for copy in self.started:
            copy.wait_send()


def gather_kernel(
    bands, layers, intake, recurrence, outtake, scalers, splitter, banding, masker, widener, cot,
    rnn_out, split_out, later, pieces,
    rnn_all, split_all, vec_rows, own_later, band_rows, cot_here, staged, send_sems, recv_sems, local_sems,
):
    at = Links(bands, layers, send_sems, recv_sems)
    band, stream, other = at.band, at.stream, at.other
    rows_all = rnn_all.shape[1]
    quarter = rows_all // bands
    used = []

    def local(source, target):
        copy = pltpu.make_async_copy(source, target, local_sems.at[len(used)])
        copy.start()
        used.append(copy)
        return copy

    vec_rows[...] = jnp.zeros_like(vec_rows)
    for k in range(2):
        for h in range(0, scalers.shape[1], LANES):
            width = min(LANES, scalers.shape[1] - h)
            vec_rows[k, h // LANES : h // LANES + 1, :width] = scalers[k : k + 1, h : h + width]
    band_rows[...] = jnp.zeros_like(band_rows)
    slots = banding.shape[0]
    for h in range(0, banding.shape[1], LANES):
        width = min(LANES, banding.shape[1] - h)
        base = SLOT_PAD * (h // LANES)
        band_rows[base : base + slots, :width] = banding[:, h : h + width]

    def own_pack(k, target):
        a = intake.shape[1]
        b = a + recurrence.shape[1]
        c = b + outtake.shape[1]
        return [
            local(intake.at[k], target.at[pl.ds(0, a)]),
            local(recurrence.at[k], target.at[pl.ds(a, b - a)]),
            local(outtake.at[k], target.at[pl.ds(b, c - b)]),
            local(vec_rows.at[k], target.at[pl.ds(c, rows_all - c)]),
        ]

    mine, mine_split = rnn_all.at[stream], split_all.at[stream]
    first = own_pack(0, mine)
    split_rows_count = splitter.shape[0]
    second = [
        local(splitter, mine_split.at[pl.ds(0, split_rows_count)]),
        local(band_rows, mine_split.at[pl.ds(split_rows_count, band_rows.shape[0])]),
    ]
    at.greet(
        [(at.band_to(m), stream) for m in range(1, bands)]
        + [(band, at.own(at.layer_to(k))) for k in range(1, layers)]
        + [(band, other)]
    )
    steps = (2, 0, 1)
    turns = range(1, bands)

    def rows(b):
        return pl.ds(b * quarter, quarter)

    to_layer, to_layer_split, to_band = 0, layers, 2 * layers
    to_core = to_band + layers * bands
    to_core_split = to_core + layers * bands
    to_layer_later = to_core_split + layers

    def spread(piece, index):
        for k in (2, 0):
            at.send(piece, piece, index + k, (band, at.own(at.goal(k))))

    def relay(piece, index):
        at.send(piece, piece, index + 1, (band, at.own(at.goal(0))))

    def rnn_piece(k):
        return rnn_all.at[at.own(at.goal(k)), rows(band)]

    def split_piece(k):
        return split_all.at[at.own(at.goal(k))]

    def later_piece(k):
        return later.at[at.goal(k)]

    def hand_on(k):
        piece = rnn_piece(k)
        for m in turns:
            at.send(piece, piece, to_band + k * bands + m, (at.band_to(m), stream))
        at.send(piece, piece, to_core + k * bands, (band, other))

    for copy in first:
        copy.wait()
    spread(rnn_piece(3), to_layer)
    for copy in second:
        copy.wait()
    spread(mine_split, to_layer_split)
    at.send(mine, mine, to_core + 3 * bands, (band, other))
    at.send(mine_split, mine_split, to_core_split + 3, (band, other))
    third = own_pack(1, own_later)
    load_cot = local(cot, cot_here)
    r, wide = masker.shape[1], masker.shape[2] // 2
    half = wide // 2
    base = 2 * r + r // 2
    fill = [
        local(masker.at[:, :, pl.ds(0, wide)], staged.at[:, pl.ds(0, r), :]),
        local(masker.at[:, :, pl.ds(wide, wide)], staged.at[:, pl.ds(r, r), :]),
        local(widener.at[:, pl.ds(0, r // 2), :], staged.at[:, pl.ds(2 * r, r // 2), pl.ds(0, half)]),
        local(widener.at[:, pl.ds(r // 2, r // 2), :], staged.at[:, pl.ds(2 * r, r // 2), pl.ds(half, half)]),
    ]
    at.arrive(rnn_piece(2), to_layer + 2)
    relay(rnn_piece(2), to_layer)
    hand_on(2)
    for copy in third:
        copy.wait()
    later[at.layer] = own_later[rows(band), :]
    spread(later_piece(3), to_layer_later)
    at.arrive(rnn_piece(0), to_layer)
    hand_on(0)
    at.arrive(split_piece(2), to_layer_split + 2)
    relay(split_piece(2), to_layer_split)
    at.send(split_piece(2), split_piece(2), to_core_split + 2, (band, other))
    at.arrive(rnn_piece(1), to_layer + 1)
    hand_on(1)
    at.arrive(later_piece(2), to_layer_later + 2)
    relay(later_piece(2), to_layer_later)
    load_cot.wait()
    for s in range(slots):
        for part in range(2):
            staged[s, base:, part * half : (part + 1) * half] = cot_here[:, s, part, :]
    for copy in fill:
        copy.wait()
    rest = [local(staged, pieces)]
    for k in (0, 1):
        at.arrive(split_piece(k), to_layer_split + k)
        at.send(split_piece(k), split_piece(k), to_core_split + k, (band, other))
    for k in steps:
        for m in turns:
            piece = rnn_all.at[at.own(at.goal(k)), rows(at.band_from(m))]
            at.arrive(piece, to_band + k * bands + m)
            at.send(piece, piece, to_core + k * bands + m, (band, other))

    def leave(source, target, block):
        rest.append(local(source.at[block], target.at[block]))

    leave(rnn_all, rnn_out, stream)
    leave(split_all, split_out, stream)
    at.arrive(rnn_all.at[other], to_core + 3 * bands)
    leave(rnn_all, rnn_out, other)
    at.arrive(split_all.at[other], to_core_split + 3)
    leave(split_all, split_out, other)
    for k in steps:
        leave(rnn_all, rnn_out, at.own(at.goal(k)))
        leave(split_all, split_out, at.own(at.goal(k)))
    for k in steps:
        source = at.across(at.goal(k))
        for m in range(bands):
            at.arrive(rnn_all.at[source, rows(at.band_from(m))], to_core + k * bands + m)
        leave(rnn_all, rnn_out, source)
        at.arrive(split_all.at[source], to_core_split + k)
        leave(split_all, split_out, source)
    for k in (0, 1):
        at.arrive(later_piece(k), to_layer_later + k)
    at.finish()
    for copy in rest:
        copy.wait()


def gather_front(intake, recurrence, outtake, scalers, splitter, banding, masker, widener, cot, rows, bands, layers):
    count = 4 * layers + 2 * layers * bands
    streams = layers * CORES
    slots = banding.shape[0]
    strips = -(-banding.shape[1] // LANES)
    r, wide = masker.shape[1], masker.shape[2] // 2
    frames = cot.shape[0]
    weight_rows = intake.shape[1] + recurrence.shape[1] + outtake.shape[1]
    split_rows_count = splitter.shape[0] + SLOT_PAD * strips
    return pl.pallas_call(
        partial(gather_kernel, bands, layers),
        out_shape=[
            f32((streams, rows, LANES)), f32((streams, split_rows_count, LANES)), f32((layers, rows // bands, LANES)),
            f32((slots, 2 * r + r // 2 + frames, wide)),
        ],
        in_specs=[ANY, ANY, ANY, VMEM, ANY, VMEM, ANY, ANY, ANY],
        out_specs=[ANY, ANY, VMEM, ANY],
        scratch_shapes=[
            pltpu.VMEM((streams, rows, LANES), jnp.float32),
            pltpu.VMEM((streams, split_rows_count, LANES), jnp.float32),
            pltpu.VMEM((2, rows - weight_rows, LANES), jnp.float32),
            pltpu.VMEM((rows, LANES), jnp.float32),
            pltpu.VMEM((SLOT_PAD * strips, LANES), jnp.float32),
            pltpu.VMEM(cot.shape, jnp.float32),
            pltpu.VMEM((slots, 2 * r + r // 2 + frames, wide), jnp.float32),
            pltpu.SemaphoreType.DMA((count,)), pltpu.SemaphoreType.DMA((count,)), pltpu.SemaphoreType.DMA((20 + 2 * streams,)),
        ],
        compiler_params=pltpu.CompilerParams(
            collective_id=0, has_side_effects=True, vmem_limit_bytes=VMEM_BYTES
        ),
        cost_estimate=cost(30),
        name="gather_front",
    )(intake, recurrence, outtake, scalers, splitter, banding, masker, widener, cot)


def mask_exchange_kernel(
    base, bands, layers, places, source, mine_in, v_band,
    back, grad_back, g_vec,
    arrived, grad, mine, other, send, received, send_sems, recv_sems, local_sems,
):
    at = Links(bands, layers, send_sems, recv_sems)
    share, outer, piece_rows, wide = other.shape
    quarter = arrived.shape[3]
    partner = (at.band, at.other)
    turns = [(m, k) for k in range(layers) for m in range(bands) if m + k]
    stride = bands * layers
    to_back, to_core, to_core_back = share * stride, 2 * share * stride, 2 * share * stride + share
    at.greet([(at.band_to(m), at.own(at.layer_to(k))) for m, k in turns] + [partner])
    loads = []
    for j in range(share):
        loads.append(
            [
                pltpu.make_async_copy(mine_in.at[:, j], mine.at[j], local_sems.at[2 * j]),
                pltpu.make_async_copy(
                    source.at[at.band, at.layer, j], arrived.at[j, at.band, at.layer], local_sems.at[2 * j + 1]
                ),
            ]
        )
        for copy in loads[-1]:
            copy.start()
    for j in range(share):
        at.send(mine_in.at[:, j, pl.ds(0, piece_rows)], other.at[j], to_core + j, partner)
        for m, k in turns:
            band, layer = at.band_to(m), at.layer_to(k)
            at.send(
                source.at[band, layer, j], arrived.at[j, at.band, at.layer], j * stride + k * bands + m,
                (band, at.own(layer)),
            )
    order = [(q, g) for g in range(layers) for q in range(bands)]
    for j in range(share):
        for copy in loads[j]:
            copy.wait()
        at.arrive(other.at[j], to_core + j)
        for m, k in turns:
            at.arrive(arrived.at[j, at.band_from(m), at.layer_from(k)], j * stride + k * bands + m)
        x = jnp.concatenate([arrived[j, q, g] for q, g in order], axis=0)
        dx = mask_slot(
            at.core, places[0, j], v_band[pl.ds(at.layer * share + j, 1), base:], x,
            mine.at[j], other.at[j], back.at[:, j], send.at[j], g_vec.at[j],
        )
        for i, (q, g) in enumerate(order):
            grad[j, q, g] = dx[i * quarter : (i + 1) * quarter]
        for m, k in turns:
            band, layer = at.band_to(m), at.layer_to(k)
            at.send(
                grad.at[j, band, layer], grad_back.at[at.band, at.layer, j], to_back + j * stride + k * bands + m,
                (band, at.own(layer)),
            )
        at.send(send.at[j], received.at[j], to_core_back + j, partner)
        grad_back[at.band, at.layer, j] = grad[j, at.band, at.layer]
    for j in range(share):
        at.arrive(received.at[j], to_core_back + j)
        for g in range(outer):
            back[g, j, :piece_rows] += received[j, g]
    for j in range(share):
        for m, k in turns:
            at.arrive(grad_back.at[at.band_from(m), at.layer_from(k), j], to_back + j * stride + k * bands + m)
    at.finish()


def mask_exchange(places, source, mine, v_band, base, piece_rows):
    bands, layers, share, quarter, dmodel = source.shape
    outer, unused, rows, wide = mine.shape
    columns = v_band.shape[1] - base
    count = 2 * share * bands * layers + 2 * share

    def vmem(*shape):
        return pltpu.VMEM(shape, jnp.float32)

    return pl.pallas_call(
        partial(mask_exchange_kernel, base, bands, layers),
        out_shape=[f32(mine.shape), f32(source.shape), f32((share, 1, columns))],
        in_specs=[SMEM, ANY, ANY, VMEM],
        out_specs=[VMEM] * 3,
        scratch_shapes=[
            vmem(share, bands, layers, quarter, dmodel),
            vmem(share, bands, layers, quarter, dmodel),
            vmem(share, outer, rows, wide),
            vmem(share, outer, piece_rows, wide),
            vmem(share, outer, piece_rows, wide),
            vmem(share, outer, piece_rows, wide),
            pltpu.SemaphoreType.DMA((count,)),
            pltpu.SemaphoreType.DMA((count,)),
            pltpu.SemaphoreType.DMA((2 * share,)),
        ],
        compiler_params=pltpu.CompilerParams(
            collective_id=2, has_side_effects=True, vmem_limit_bytes=VMEM_BYTES
        ),
        cost_estimate=cost(28),
        name="mask_exchange",
    )(places, source, mine, v_band)


def band_places(bands):
    return lambda e, j: [j if e == 0 else bands - 1 - j]


def pack_quarter(at, rnn, layer, core, m):
    quarter = rnn.shape[1] // at.bands
    rows = pl.ds(pl.multiple_of(at.band_from(m) * quarter, 8), quarter)
    return rnn.at[layer * CORES + core, rows]


def start_pack(at, rnn, pieces, sems):
    if len(pieces) == 1:
        copies = [pltpu.make_async_copy(pieces[0], rnn, sems.at[0])]
    else:
        copies = []
        for m, ref in enumerate(pieces):
            for layer in range(ref.shape[0]):
                target = pack_quarter(at, rnn, layer, at.core, m)
                at.send(ref.at[layer], target, at.bands + len(copies), (at.band, at.other))
                copies.append(pltpu.make_async_copy(ref.at[layer], target, sems.at[len(copies)]))
    for copy in copies:
        copy.start()
    return copies


def await_pack(at, rnn, pieces, copies):
    for copy in copies:
        copy.wait()
    if len(pieces) > 1:
        layers = pieces[0].shape[0]
        for k in range(len(pieces) * layers):
            at.arrive(pack_quarter(at, rnn, k % layers, 1 - at.core, k // layers), at.bands + k)


def pack_loads(pieces):
    return 1 if len(pieces) == 1 else sum(x.shape[0] for x in pieces)


def to_slots(target, source, band_of):
    for s in range(target.shape[0]):
        target[s] = source[band_of[0, s]] * band_of[1, s].astype(jnp.float32)


def band_forward_kernel(count, parts, slot_of, band_of, arrived_in, *refs):
    pieces, refs = refs[:count], refs[count:]
    out, x, *refs = refs
    saved, rnn_out, refs = refs[:6], refs[6], refs[7:]
    act0, act1, c0, c1, h0, h1, hi_ref, lo_ref, s0, s1, m0, m1, vec, rnn, arrived, mixed, *refs = refs
    send_sems, recv_sems, pack_sems, sems = refs
    bands, unused, dmodel = x.shape
    pack = Pack(rnn, dmodel, h0.shape[2])
    at, come = swap_bands(parts, arrived_in, arrived, send_sems, recv_sems, sems.at[6], True)
    await_pack(at, rnn, pieces, start_pack(at, rnn, pieces, pack_sems))
    pack_leaves = pltpu.make_async_copy(rnn, rnn_out, sems.at[7])
    pack_leaves.start()
    load_vec(pack, vec)
    split_recurrence(pack, hi_ref, lo_ref)
    come()

    def fetch(b, carry):
        x[b] = arrived[slot_of[0, b]]
        return carry

    lax.fori_loop(0, bands, fetch, 0)
    act = (act0, act1)

    def x_flat(start, size):
        return x[...].reshape(bands * 16, dmodel)

    gates_forward(x_flat, act, pack, vec, bands * 16, bands * 16)
    run_forward(
        bands, band_places(bands), act, (c0, c1), (h0, h1), pack, hi_ref, lo_ref, (s0, s1), (m0, m1)
    )
    leaving = [
        pltpu.make_async_copy(a, b, sems.at[k])
        for k, (a, b) in enumerate(zip((act0, act1, c0, c1, h0, h1), saved))
    ]
    for copy in leaving:
        copy.start()
    total = output_forward(bands, (h0, h1), pack, vec)
    mixed[...] = (x[...].reshape(bands * 16, dmodel) + total).reshape(bands, 16, dmodel)
    to_slots(out, mixed, band_of)
    at.finish()
    pack_leaves.wait()
    for copy in leaving:
        copy.wait()


def swap_bands(parts, source, target, send_sems, recv_sems, local_sem, pair=False):
    at = Links(parts, 1, send_sems, recv_sems)
    slots = target.shape[0] // parts
    if parts == 1:
        local = pltpu.make_async_copy(source, target, local_sem)
        local.start()
        return at, local.wait
    partners = [(at.band_to(m), at.stream) for m in range(1, parts)]
    at.greet(partners + [(at.band, at.other)] if pair else partners)

    def part(ref, b):
        return ref.at[pl.ds(b * slots, slots)]

    for m in range(1, parts):
        at.send(part(source, at.band_to(m)), part(target, at.band), m, (at.band_to(m), at.stream))
    local = pltpu.make_async_copy(part(source, at.band), part(target, at.band), local_sem)
    local.start()

    def come():
        for m in range(1, parts):
            at.arrive(part(target, at.band_from(m)), m)
        local.wait()

    return at, come


def swap_scratch(count):
    return [pltpu.SemaphoreType.DMA((count,)), pltpu.SemaphoreType.DMA((count,))]


def remote(parts, number):
    if parts == 1:
        return PARAMS
    return pltpu.CompilerParams(collective_id=number, has_side_effects=True, vmem_limit_bytes=VMEM_BYTES)


def band_forward(slot_of, band_of, arrived, pieces, rnn_shape, parts, hidden):
    bands = slot_of.shape[1]
    dmodel = arrived.shape[2]
    return pl.pallas_call(
        partial(band_forward_kernel, len(pieces), parts),
        out_shape=[f32(arrived.shape), f32((bands, 16, dmodel))] + saved_shapes(bands, hidden) + [f32(rnn_shape)],
        in_specs=[SMEM] * 2 + [ANY] * (1 + len(pieces)),
        out_specs=[VMEM] * 2 + [ANY] * 7,
        scratch_shapes=saved_scratch(bands, hidden)
        + rec_scratch(16, hidden)
        + [vec_scratch(dmodel, hidden), pltpu.VMEM(rnn_shape, jnp.float32)]
        + [pltpu.VMEM(arrived.shape, jnp.float32), pltpu.VMEM((bands, 16, dmodel), jnp.float32)]
        + swap_scratch(parts + pack_loads(pieces))
        + [pltpu.SemaphoreType.DMA((pack_loads(pieces),)), pltpu.SemaphoreType.DMA((8,))],
        compiler_params=remote(parts, 1),
        cost_estimate=cost(35),
        name="band_forward",
    )(slot_of, band_of, arrived, *pieces)


def band_backward_kernel(parts, slot_of, band_of, arrived, rnn_in, x, *refs):
    saved, refs = refs[:6], refs[6:]
    out, outs, refs = refs[0], refs[1 : 1 + parts], refs[1 + parts :]
    act0, act1, c0, c1, h0, h1, *refs = refs
    hi_ref, lo_ref, s0, s1, m0, m1, dy, vec, g_vec, dh0, dh1, dz0, dz1, rnn, g_rnn, *refs = refs
    leaving, send_sems, recv_sems, sems = refs
    bands, unused, dmodel = x.shape
    hidden = h0.shape[2]
    pack, g_pack = Pack(rnn, dmodel, hidden), Pack(g_rnn, dmodel, hidden)
    pairs = [(rnn_in, rnn), (saved[4], h0), (saved[5], h1)] + list(zip(saved[:4], (act0, act1, c0, c1)))
    loads = [pltpu.make_async_copy(a, b, sems.at[k]) for k, (a, b) in enumerate(pairs)]
    for copy in loads:
        copy.start()

    def fetch(b, carry):
        dy[b] = arrived[slot_of[0, b]]
        return carry

    lax.fori_loop(0, bands, fetch, 0)
    for copy in loads[:3]:
        copy.wait()
    load_vec(pack, vec)
    split_recurrence_turned(pack, hi_ref, lo_ref)
    states_backward(bands, dy[...].reshape(bands * 16, dmodel), (dh0, dh1), (h0, h1), pack, g_pack)
    for copy in loads[3:]:
        copy.wait()
    run_backward(
        bands, band_places(bands), (act0, act1), (dz0, dz1), (c0, c1), (dh0, dh1),
        pack, hi_ref, lo_ref, (s0, s1), (m0, m1),
    )
    x_all, dy_all = x[...].reshape(bands * 16, dmodel), dy[...].reshape(bands * 16, dmodel)
    dx = input_backward(bands, x_all, dy_all, (dz0, dz1), pack, vec, g_vec)
    dy[...] = dx.reshape(bands, 16, dmodel)
    to_slots(leaving, dy, band_of)
    at, come = swap_bands(parts, leaving, out, send_sems, recv_sems, sems.at[7])
    weights_backward(
        bands, x_all, (dz0, dz1), lambda e: shifted((h0, h1)[e], e, bands, hidden, 1.0), pack, vec, g_pack, g_vec
    )
    leave = [
        pltpu.make_async_copy(g_rnn if parts == 1 else g_rnn.at[at.band_to(m)], outs[m], sems.at[8 + m])
        for m in range(parts)
    ]
    for copy in leave:
        copy.start()
    come()
    at.finish()
    for copy in leave:
        copy.wait()


def band_backward(slot_of, band_of, arrived, rnn, saved, parts, hidden):
    bands = slot_of.shape[1]
    dmodel = arrived.shape[2]
    blocks, rows, unused = rnn.shape
    grad_shape = rnn.shape if parts == 1 else (parts, blocks, rows // parts, LANES)
    return pl.pallas_call(
        partial(band_backward_kernel, parts),
        out_shape=[f32(arrived.shape)] + [f32(grad_shape[-3:])] * parts,
        in_specs=[SMEM] * 2 + [VMEM, ANY, VMEM] + [ANY] * 6,
        out_specs=[VMEM] + [ANY] * parts,
        scratch_shapes=saved_scratch(bands, hidden)
        + rec_scratch(16, hidden, True)
        + [pltpu.VMEM((bands, 16, dmodel), jnp.float32)]
        + [vec_scratch(dmodel, hidden)] * 2
        + [pltpu.VMEM((bands, 16, hidden), jnp.float32)] * 2
        + [pltpu.VMEM((bands, 16, 4 * hidden), jnp.float32)] * 2
        + [pltpu.VMEM(rnn.shape, jnp.float32), pltpu.VMEM(grad_shape, jnp.float32)]
        + [pltpu.VMEM(arrived.shape, jnp.float32)]
        + swap_scratch(parts)
        + [pltpu.SemaphoreType.DMA((8 + parts,))],
        compiler_params=remote(parts, 3),
        cost_estimate=cost(38),
        name="band_backward",
    )(slot_of, band_of, arrived, rnn, *saved)


class Grads:
    def __init__(self, pieces, rnn0, rnn1, banded, dims):
        self.pieces, self.rnn, self.banded = pieces, (rnn0, rnn1), banded
        self.slots, self.slot_rows, self.r, self.piece_rows, self.dmodel, self.hidden = dims

    def piece(self, k, s):
        if k == 0:
            at = pl.ds(pl.multiple_of(s * self.slot_rows, self.slot_rows), self.slot_rows)
            return self.banded[at, :]
        if k == 1:
            return load_wide_piece(self.pieces[s, 2 * self.r : self.piece_rows])
        return load_mask_piece(self.pieces[s, : 2 * self.r], self.r)

    def of_slot(self, s):
        return [(k, (s,), self.piece(k, s)) for k in range(3)]

    def banding(self, columns):
        base = self.slots * self.slot_rows
        strips = []
        for h in range(0, columns, LANES):
            at = base + SLOT_PAD * (h // LANES)
            strips.append(self.banded[at : at + self.slots, : min(LANES, columns - h)])
        return jnp.concatenate(strips, axis=1)

    def rest(self, columns, share):
        found = [(3, (...,), self.banding(columns))]
        unused, out_rows, weight_rows, unused, vec_rows, unused = pack_rows(self.dmodel, self.hidden)
        for k in range(2):
            pack = self.rnn[k]
            at = 0
            for e in range(2):
                found.append((4, (k, e), pack[at : at + self.dmodel]))
                at += self.dmodel
            for e in range(2):
                found.append((5, (k, e), pack[at : at + self.hidden]))
                at += self.hidden
            found.append((6, (k,), pack[at : at + out_rows]))
            at += out_rows
            strips = [
                pack[at + r : at + r + 1, : min(LANES, share - r * LANES)] for r in range(vec_rows)
            ]
            found.append((7, (slice(k, k + 1),), jnp.concatenate(strips, axis=1)))
        return found


DECAYS = (DECAY_RATE,) * 3 + (0.0,) + (DECAY_RATE,) * 3 + (0.0,)


def lamb_moments(gradient, mean_old, power_old, factor):
    clipped = gradient * factor
    mean_new = BETA_ONE * mean_old + (1.0 - BETA_ONE) * clipped
    power_new = BETA_TWO * power_old + (1.0 - BETA_TWO) * clipped * clipped
    return (mean_new, power_new)


def lamb_direction(weight_matrix, mean_new, power_new, decay):
    corrected = mean_new / (1.0 - BETA_ONE**STEP)
    scale_root = jnp.sqrt(power_new / (1.0 - BETA_TWO**STEP)) + ADAM_EPS
    return corrected / scale_root + decay * weight_matrix


def add_up(rows, first):
    line = jnp.zeros((1, LANES), jnp.float32)
    lane = lax.broadcasted_iota(jnp.int32, (1, LANES), 1)
    for i, row in enumerate(rows):
        line = jnp.where(lane == first + i, jnp.sum(row, axis=1, keepdims=True), line)
    return line


def lane_of(line, i):
    lane = lax.broadcasted_iota(jnp.int32, (1, LANES), 1)
    return jnp.sum(jnp.where(lane == i, line, 0.0), axis=1, keepdims=True)


def finish_kernel(bands, layers, dims, g_rnn0, g_split, d_spec, back, *refs):
    g_rnn1, refs = refs[:bands], refs[bands:]
    state, refs = refs[:24], refs[24:]
    out, rnn0, rnn1, banded, spec_out = refs[:5]
    pieces, refs = refs[5], refs[6:]
    held_state, packs, refs = refs[:12], refs[12], refs[13:]
    (
        own0, own_split, parts1, sum1, from_core, from_core_split, from_core1, from_band, held,
        from_layer, from_layer_split, from_layer1, spec_in, spec_own, came, lines,
        local_sems, send_sems, recv_sems,
    ) = refs
    at = Links(bands, layers, send_sems, recv_sems)
    band, stream, other = at.band, at.stream, at.other
    streams = layers * CORES
    quarter = g_rnn0.shape[1] // bands
    spec_rows = d_spec.shape[0] // bands
    order = range(layers)
    turns = range(1, bands)
    taken = [0]

    def take(count):
        taken[0] += count
        return taken[0] - count

    locals_used = []

    def local(source, target):
        copy = pltpu.make_async_copy(source, target, local_sems.at[len(locals_used)])
        copy.start()
        locals_used.append(copy)
        return copy

    def rows(b):
        return pl.ds(pl.multiple_of(b * quarter, 8), quarter)

    def spec_part(b):
        return pl.ds(pl.multiple_of(b * spec_rows, 8), spec_rows)

    def stream_to(k):
        return lax.rem(stream + k, streams)

    at.greet(
        [(at.band_to(m), stream_to(k)) for k in range(streams) for m in range(bands) if m + k]
    )
    to_core, to_core_split, to_core1 = take(layers), take(layers), take(layers)
    to_layer, to_layer_split, to_layer1 = take(layers), take(layers), take(layers)
    to_band, to_all0, to_all1 = take(bands * layers), take(bands), take(bands)
    to_spec, to_spec_all = take(bands), take(bands)
    def pair_rnn(k):
        at.send(g_rnn0.at[at.across(at.goal(k))], from_core.at[k], to_core + k, (band, other))

    def pair_split(k):
        at.send(g_split.at[at.across(at.goal(k))], from_core_split.at[k], to_core_split + k, (band, other))

    pair_rnn(0)
    pair_rnn(1)
    for m in turns:
        to = at.band_to(m)
        at.send(d_spec.at[spec_part(to)], spec_in.at[m - 1], to_spec + m, (to, stream))
    load0 = [local(g_rnn0.at[at.own(at.goal(k))], own0.at[k]) for k in range(layers)]
    load_split = [local(g_split.at[at.own(at.goal(k))], own_split.at[k]) for k in range(layers)]
    load1 = [local(g, parts1.at[k]) for k, g in enumerate(g_rnn1)]
    load_spec = local(d_spec.at[spec_part(band)], spec_own)
    load_state = [local(back, pieces)]
    pack_base = sum(state[k].shape[1] for k in range(4, 7))
    for t in range(3):
        kind = state[8 * t : 8 * t + 8]
        load_state += [local(a, b) for a, b in zip(kind[:4], held_state[4 * t : 4 * t + 4])]
        for k in range(2):
            base = 0
            for a in kind[4:7]:
                load_state.append(local(a.at[k], packs.at[t, k, pl.ds(base, a.shape[1])]))
                base += a.shape[1]
            packs[t, k, base:] = jnp.zeros_like(packs[t, k, base:])
            length = kind[7].shape[1]
            for h in range(0, length, LANES):
                width = min(LANES, length - h)
                row = base + h // LANES
                packs[t, k, row : row + 1, :width] = kind[7][k : k + 1, h : h + width]
    def first_turn(acc, far, index, k):
        if k < 2:
            at.send(acc.at[k], far.at[k], index + k, (band, at.own(at.goal(0))))

    def second_turn(acc, far, index):
        at.arrive(far.at[1], index + 1)
        acc[2] += far[1]
        at.send(acc.at[2], far.at[2], index + 2, (band, at.own(at.goal(2))))

    def own_total(acc, far, index):
        at.arrive(far.at[0], index)
        at.arrive(far.at[2], index + 2)
        return acc[3] + far[0] + far[2]

    for k in order:
        at.arrive(from_core.at[k], to_core + k)
        if k < 2:
            pair_rnn(k + 2)
        else:
            pair_split(2 * k - 4)
            pair_split(2 * k - 3)
        load0[k].wait()
        from_core[k] += own0[k]
        for m in turns:
            to = at.band_to(m)
            at.send(from_core.at[k, rows(to)], from_band.at[m - 1, k], to_band + (m - 1) * layers + k, (to, stream))
    for k in order:
        at.arrive(from_core_split.at[k], to_core_split + k)
        load_split[k].wait()
        from_core_split[k] += own_split[k]
        first_turn(from_core_split, from_layer_split, to_layer_split, k)
    for copy in load1:
        copy.wait()

    def block(k, carry):
        total = parts1[0, k]
        for b in range(1, bands):
            total = total + parts1[b, k]
        sum1[k] = total
        return carry

    lax.fori_loop(0, streams, block, 0)
    for k in order:
        at.send(sum1.at[at.across(at.goal(k))], from_core1.at[k], to_core1 + k, (band, other))
    for k in order:
        at.arrive(from_core1.at[k], to_core1 + k)
        from_core1[k] += sum1[at.own(at.goal(k))]
        first_turn(from_core1, from_layer1, to_layer1, k)
    weights, means, powers = held_state[:4], held_state[4:8], held_state[8:]
    grads = Grads(pieces, rnn0, rnn1, banded, dims)
    slots = dims[0]
    for copy in load_state:
        copy.wait()

    def add_squares(pairs, had):
        return tuple(a + column_sum(b * b) for a, b in zip(had, pairs))

    def early_slot(s, had):
        return add_squares(
            [weights[0][s], weights[1][s], weights[2][s], grads.piece(1, s), grads.piece(2, s)], had
        )

    early = lax.fori_loop(
        0, slots, early_slot, tuple(jnp.zeros((1, weights[k].shape[2]), jnp.float32) for k in (0, 1, 2, 1, 2))
    )
    row = lax.broadcasted_iota(jnp.int32, (quarter, LANES), 0) + band * quarter
    edges = [0]
    for a in state[4:7]:
        edges.append(edges[-1] + a.shape[1])

    def by_array(values):
        edge = edges + [bands * quarter]
        return [
            column_sum(jnp.where((row >= edge[i]) & (row < edge[i + 1]), values, 0.0)) for i in range(4)
        ]

    def both_modules(one):
        found = [by_array(one(k, rows(band))) for k in range(2)]
        return [a + b for a, b in zip(*found)]

    weight_rows = list(early[:3]) + [column_sum(weights[3][...] * weights[3][...])]
    weight_rows += both_modules(lambda k, q: packs[0, k, q] * packs[0, k, q])
    second_turn(from_core_split, from_layer_split, to_layer_split)
    second_turn(from_core1, from_layer1, to_layer1)
    for k in order:
        total = from_core[k, rows(band)]
        for m in range(bands - 1):
            at.arrive(from_band.at[m, k], to_band + m * layers + k)
            total = total + from_band[m, k]
        held[k] = total
        first_turn(held, from_layer, to_layer, k)
    second_turn(held, from_layer, to_layer)

    def gather_quarters(target, index):
        for m in turns:
            at.send(target.at[rows(band)], target.at[rows(band)], index + m, (at.band_to(m), stream))

    rnn1[rows(band)] = own_total(from_core1, from_layer1, to_layer1)
    banded[...] = own_total(from_core_split, from_layer_split, to_layer_split)
    rnn0[rows(band)] = own_total(held, from_layer, to_layer)

    def send_modules():
        gather_quarters(rnn1, to_all1)
        gather_quarters(rnn0, to_all0)

    def send_spectrum():
        load_spec.wait()
        total = spec_own[...]
        for m in turns:
            at.arrive(spec_in.at[m - 1], to_spec + m)
            total = total + spec_in[m - 1]
        spec_out[spec_part(band)] = total
        for m in turns:
            piece = spec_out.at[spec_part(band)]
            at.send(piece, piece, to_spec_all + m, (at.band_to(m), stream))

    everyone = [(m, k) for k in range(streams) for m in range(bands) if m + k]

    def everywhere(line, turn, meanwhile):
        index = take(streams * bands)
        own = lines.at[turn]
        own[...] = line
        for m, k in everyone:
            i = k * bands + m
            at.send(own, came.at[turn, i], index + i, (at.band_to(m), stream_to(k)))
        meanwhile()
        total = line
        for m, k in everyone:
            i = k * bands + m
            at.arrive(came.at[turn, i], index + i)
            total = total + came[turn, i]
        return total

    main = banded[: slots * dims[1]]
    band_grad = grads.banding(weights[3].shape[1])
    module_rows = both_modules(lambda k, q: (rnn0, rnn1)[k][q] * (rnn0, rnn1)[k][q])
    found = [column_sum(main * main), early[3], early[4], column_sum(band_grad * band_grad)] + module_rows
    grad_total = sum(jnp.sum(x, axis=1, keepdims=True) for x in found)
    totals = everywhere(add_up([grad_total] + weight_rows, 0), 0, send_modules)
    grad_norm = jnp.sqrt(lane_of(totals, 0))
    factor = jnp.minimum(1.0, CLIP_NORM / grad_norm)

    def direction(w, mean_old, power_old, g, decay):
        mean, power = lamb_moments(g, mean_old, power_old, factor)
        return lamb_direction(w, mean, power, decay)

    def slot(s, had):
        return add_squares(
            [
                direction(weights[k][s], means[k][s], powers[k][s], grads.piece(k, s), DECAYS[k])
                for k in range(3)
            ],
            had,
        )

    moved_rows = list(
        lax.fori_loop(0, slots, slot, tuple(jnp.zeros((1, weights[k].shape[2]), jnp.float32) for k in range(3)))
    )
    moved = direction(weights[3][...], means[3][...], powers[3][...], band_grad, DECAYS[3])
    moved_rows.append(column_sum(moved * moved))
    decay = jnp.where(row < edges[3], DECAYS[4], DECAYS[7])

    def module(k, q):
        got = direction(packs[0, k, q], packs[1, k, q], packs[2, k, q], (rnn0, rnn1)[k][q], decay)
        return got * got

    moved_rows += both_modules(module)
    moved = everywhere(add_up(moved_rows, 1), 1, send_spectrum)
    out[0:1] = jnp.sqrt(totals) / jnp.sqrt(moved + 1e-12)
    out[1:2] = jnp.broadcast_to(factor, (1, LANES))
    out[2:3] = jnp.broadcast_to(grad_norm, (1, LANES))
    out[3:8] = jnp.zeros((5, LANES), jnp.float32)
    for m in turns:
        at.arrive(rnn1.at[rows(at.band_from(m))], to_all1 + m)
        at.arrive(rnn0.at[rows(at.band_from(m))], to_all0 + m)
        at.arrive(spec_out.at[spec_part(at.band_from(m))], to_spec_all + m)
    at.finish()


def finish(g_rnn0, g_split, g_rnn1, d_spec, back, state, bands, layers, dims):
    streams = layers * CORES
    rows, split_count = g_rnn0.shape[1], g_split.shape[1]
    quarter = rows // bands
    spec_shape = (d_spec.shape[0] // bands, d_spec.shape[1])
    count = 6 * layers + bands * layers + 4 * bands + 2 * streams * bands
    tile = (8, LANES)

    def vmem(*shape):
        return pltpu.VMEM(shape, jnp.float32)

    return pl.pallas_call(
        partial(finish_kernel, bands, layers, dims),
        out_shape=[
            f32(tile), f32((rows, LANES)), f32((rows, LANES)), f32((split_count, LANES)), f32(d_spec.shape),
        ],
        in_specs=[ANY] * (4 + bands) + ([ANY] * 7 + [VMEM]) * 3,
        out_specs=[VMEM] * 5,
        scratch_shapes=[vmem(*back.shape)]
        + [vmem(*x.shape) for k, x in enumerate(state) if k % 8 < 4]
        + [vmem(3, 2, rows, LANES)]
        + [
            vmem(layers, rows, LANES),
            vmem(layers, split_count, LANES),
            vmem(bands, *g_rnn1[0].shape),
            vmem(streams, quarter, LANES),
            vmem(layers, rows, LANES),
            vmem(layers, split_count, LANES),
            vmem(layers, quarter, LANES),
            vmem(bands - 1, layers, quarter, LANES),
            vmem(layers, quarter, LANES),
            vmem(layers - 1, quarter, LANES),
            vmem(layers - 1, split_count, LANES),
            vmem(layers - 1, quarter, LANES),
            vmem(bands - 1, *spec_shape),
            vmem(*spec_shape),
            vmem(2, streams * bands, 1, LANES),
            vmem(2, 1, LANES),
            pltpu.SemaphoreType.DMA((2 * layers + bands + 2 + 12 + 18,)),
            pltpu.SemaphoreType.DMA((count,)),
            pltpu.SemaphoreType.DMA((count,)),
        ],
        compiler_params=pltpu.CompilerParams(
            collective_id=5, has_side_effects=True, vmem_limit_bytes=VMEM_BYTES
        ),
        cost_estimate=cost(60),
        name="finish",
    )(g_rnn0, g_split, d_spec, back, *g_rnn1, *state)


CHUNK = 4


def update_kernel(dims, scales, d_spec, pieces_in, rnn0_in, rnn1_in, banded_in, *refs):
    state, refs = refs[:24], refs[24:]
    results, masks_out, spec_out, norm_out, refs = refs[:24], refs[24], refs[25], refs[26], refs[27:]
    norm_out[...] = scales[2:3, 0:1]
    pieces, rnn0, rnn1, banded, refs = *refs[:4], refs[4:]
    here, refs = refs[:24], refs[24:]
    made, refs = refs[:24], refs[24:]
    masks, load_sems, store_sems = refs
    weights, means, powers = here[:8], here[8:16], here[16:]
    fresh, new_means, new_powers = made[:8], made[8:16], made[16:]
    slots, piece_rows = dims[0], dims[3]
    grads = Grads(pieces, rnn0, rnn1, banded, dims)
    factor = scales[1:2, 0:1]
    ratios = [lane_of(scales[0:1], 1 + k) for k in range(8)]
    used = [0, 0]

    def copy(pair, which):
        sems = (load_sems, store_sems)[which]
        made_copy = pltpu.make_async_copy(*pair, sems.at[used[which]])
        used[which] += 1
        made_copy.start()
        return made_copy

    def arrays(numbers, sources, targets):
        return [(sources[8 * t + k], targets[8 * t + k]) for k in numbers for t in range(3)]

    def cut(pair, c):
        part = pl.ds(c * CHUNK, CHUNK)
        return pair[0].at[part], pair[1].at[part]

    small = [copy(p, 0) for p in [(rnn0_in, rnn0), (rnn1_in, rnn1), (banded_in, banded)] + arrays(range(3, 8), state, here)]
    chunks = [
        [copy(cut(p, c), 0) for p in [(pieces_in, pieces)] + arrays(range(3), state, here)]
        for c in range(slots // CHUNK)
    ]
    half_rows = d_spec.shape[0] // 2
    for part in range(2):
        spec_out[:, part, :] = d_spec[part * half_rows : (part + 1) * half_rows, : spec_out.shape[2]]

    def one(k, where, g):
        w = weights[k][where]
        mean, power = lamb_moments(g, means[k][where], powers[k][where], factor)
        direction = lamb_direction(w, mean, power, DECAYS[k])
        fresh[k][where] = w - LEARN_RATE * ratios[k] * direction
        new_means[k][where] = mean
        new_powers[k][where] = power

    for got in small:
        got.wait()
    for part in grads.rest(weights[3].shape[1], weights[7].shape[1]):
        one(*part)
    stores = [copy(p, 1) for p in arrays(range(3, 8), made, results)]
    half = pieces.shape[2] // 2
    for c in range(slots // CHUNK):
        for got in chunks[c]:
            got.wait()

        def slot(s, carry):
            for part in grads.of_slot(s):
                one(*part)
            return carry

        lax.fori_loop(c * CHUNK, (c + 1) * CHUNK, slot, 0)
        stores += [copy(cut(p, c), 1) for p in arrays(range(3), made, results)]
    for s in range(slots):
        for part in range(2):
            masks[:, s, part, :] = pieces[s, piece_rows:, part * half : (part + 1) * half]
    stores.append(copy((masks, masks_out), 1))
    for sent in stores:
        sent.wait()


def update(scales, d_spec, grads, state, dims, bins):
    slots, rows, wide = grads[0].shape
    frames = rows - dims[3]
    masks_shape = (frames, slots, 2, wide // 2)
    loads = 18 + 10 * (slots // CHUNK)
    stores = 16 + 9 * (slots // CHUNK)
    return pl.pallas_call(
        partial(update_kernel, dims),
        out_shape=[f32(x.shape) for x in state] + [f32(masks_shape), f32((frames, 2, bins)), f32((1, 1))],
        in_specs=[VMEM] * 2 + [ANY] * 28,
        out_specs=[ANY] * 25 + [VMEM] * 2,
        scratch_shapes=[pltpu.VMEM(x.shape, jnp.float32) for x in tuple(grads) + tuple(state) * 2]
        + [pltpu.VMEM(masks_shape, jnp.float32)]
        + [pltpu.SemaphoreType.DMA((loads,)), pltpu.SemaphoreType.DMA((stores,))],
        compiler_params=PARAMS,
        cost_estimate=cost(10),
        name="update",
    )(scales, d_spec, *grads, *state)


def groups_of(size, slots):
    outer = math.gcd(size, slots)
    inner = size // outer
    across = [[g * inner + i for g in range(outer)] for i in range(inner)]
    within = [[g * inner + i for i in range(inner)] for g in range(outer)]
    return outer, inner, across, within


def sum_everywhere(values, sizes):
    n = sizes[0] * sizes[1]
    row = jnp.zeros((8, LANES), jnp.float32).at[0, : values.shape[0]].set(values)
    spread = jnp.broadcast_to(row[None], (n, 8, LANES))
    got = lax.all_to_all(spread, ("band", "stream"), 0, 0, tiled=True)
    return jnp.sum(got, axis=0)[0, : values.shape[0]]


def pass_along(x, axis, by):
    size = lax.axis_size(axis)
    return lax.ppermute(x, axis, [(k, (k + by) % size) for k in range(size)])


def swap_cores(x):
    return lax.ppermute(x, "stream", [(s, s ^ 1) for s in range(lax.axis_size("stream"))])


def share_slots(shard, outer, across, within, axis):
    slots = shard.shape[0]
    mine = lax.all_to_all(
        shard.reshape((outer, slots // outer) + shard.shape[1:]), "stream", 0, 0,
        axis_index_groups=across, tiled=True,
    )
    inner = len(within[0])
    if inner == CORES:
        return mine, swap_cores(mine)
    both = lax.all_gather(mine, "stream", axis_index_groups=within)
    both = both.reshape((CORES, inner // CORES) + mine.shape)
    if axis == 1:
        both = both.transpose(0, 2, 3, 1, 4, 5)
        both = both.reshape(both.shape[:3] + (-1, both.shape[5]))
    else:
        both = both.transpose(0, 2, 3, 4, 1, 5)
        both = both.reshape(both.shape[:4] + (-1,))
    return both[0], both[1]


def return_slots(keep, send, outer, inner, across, within, axis):
    if inner == CORES:
        mine = keep + swap_cores(send)
    else:
        both = jnp.stack([keep, send])
        half = inner // CORES
        if axis == 1:
            both = both.reshape(both.shape[:3] + (half, -1, both.shape[4])).transpose(0, 3, 1, 2, 4, 5)
        else:
            both = both.reshape(both.shape[:4] + (half, -1)).transpose(0, 4, 1, 2, 3, 5)
        both = both.reshape((inner,) + both.shape[2:])
        mine = lax.psum_scatter(both, "stream", axis_index_groups=within, tiled=False)
    back = lax.all_to_all(mine, "stream", 0, 0, axis_index_groups=across, tiled=True)
    return back.reshape((-1,) + back.shape[2:])


def pack_split(splitter, banding, blocks):
    slots, wide, dmodel = splitter.shape
    columns = banding.shape[1] // blocks
    strips = -(-columns // LANES)
    main = splitter.reshape(slots, blocks, wide // blocks, dmodel).transpose(1, 0, 2, 3)
    flat = banding.reshape(slots, blocks, columns).transpose(1, 0, 2)
    flat = jnp.pad(flat, ((0, 0), (0, SLOT_PAD - slots), (0, strips * LANES - columns)))
    flat = flat.reshape(blocks, SLOT_PAD, strips, LANES).transpose(0, 2, 1, 3)
    return jnp.concatenate(
        [main.reshape(blocks, slots * wide // blocks, dmodel), flat.reshape(blocks, -1, LANES)], axis=1
    )


def unpack_banding(pack, start, slots, columns):
    blocks = pack.shape[0]
    flat = pack[:, start:].reshape(blocks, -1, SLOT_PAD, LANES)[:, :, :slots].transpose(2, 0, 1, 3)
    return flat.reshape(slots, blocks, -1)[:, :, :columns].reshape(slots, blocks * columns)


def body(spectrum, segments, widths, groups, cotangent, *state):
    weights, means_old, powers_old = state[:8], state[8:16], state[16:]
    splitter, widener, masker, banding, intake, recurrence, outtake, scalers = weights
    group_count = lax.axis_size("band")
    stream_count = lax.axis_size("stream")
    my_stream = lax.axis_index("stream")
    slots = splitter.shape[0]
    frames = spectrum.shape[0]
    quarter = frames // group_count
    outer, inner, across, within = groups_of(stream_count, slots)
    share = slots // outer
    r = masker.shape[1] * stream_count // (2 * outer)
    dmodel = splitter.shape[2]
    hidden = recurrence.shape[2]
    wide = splitter.shape[1] * stream_count
    bins = spectrum.shape[2]
    blocks, out_rows, weight_rows, vec_share, vec_rows, rows = pack_rows(dmodel, hidden)
    slot_rows = wide // blocks
    columns = banding.shape[1] * stream_count // blocks
    direct = stream_count == blocks and inner == CORES and outer == 4 and group_count == 4

    padded = ((bins - 1) // LANES + 2) * LANES
    spec = jnp.pad(
        spectrum.transpose(1, 0, 2).reshape(2 * frames, bins), ((0, 0), (0, padded - bins))
    )

    if direct:
        rnn0, w_split, later, pieces = gather_front(
            intake.reshape(2, 2 * dmodel, LANES), recurrence.reshape(2, 2 * hidden, LANES), outtake, scalers,
            splitter.reshape(slots * slot_rows, dmodel), banding, masker, widener.transpose(0, 2, 1), cotangent,
            rows, group_count, outer,
        )
        near = [later] + [pass_along(later, "band", m) for m in range(1, group_count)]
        pieces = pieces.reshape((outer, share) + pieces.shape[1:])
        mine = lax.all_to_all(pieces, "stream", 0, 0, axis_index_groups=across, tiled=True)
    else:
        whole = (
            lax.all_gather(intake, "stream", axis=3, tiled=True),
            lax.all_gather(recurrence, "stream", axis=3, tiled=True),
            lax.all_gather(outtake, "stream", axis=1, tiled=True),
            lax.all_gather(scalers, "stream", axis=1, tiled=True),
        )
        rnn0, rnn1 = (
            pack_rnn(whole[0][k], whole[1][k], whole[2][k], whole[3][k : k + 1], rows, vec_share)
            for k in range(2)
        )
        w_split = pack_split(
            lax.all_gather(splitter, "stream", axis=1, tiled=True),
            lax.all_gather(banding, "stream", axis=1, tiled=True),
            blocks,
        )
        w_mask = share_slots(masker, outer, across, within, 1)
        w_wide = share_slots(widener.transpose(0, 2, 1), outer, across, within, 1)
        cot_parts = cotangent.reshape(frames, outer, share, wide).transpose(1, 2, 0, 3)
        cot = lax.all_to_all(cot_parts, "stream", 0, 0, axis_index_groups=across, tiled=True)
        mine, other = (
            jnp.concatenate([pack_pieces(w_mask[k], w_wide[k]), cot], axis=2) for k in range(CORES)
        )
    piece_rows = mine.shape[2] - frames
    base = 2 * wide + dmodel
    sizes = (group_count, slots, share, inner, direct, blocks * columns, slot_rows, hidden)
    got = time_forward(segments, widths[None], groups[None], spec, w_split, rnn0, sizes)
    slot_places, clips, slot_of, band_of, mask_places = got[:5]
    time_out, v_band, time_saved = got[5], got[6], got[7:]
    parts = group_count if direct else 1
    if direct:
        time_out, near = lax.optimization_barrier((time_out, near))
        rnn1 = near
    else:
        rnn1 = [rnn1]
        time_out = lax.all_to_all(time_out, "band", 0, 0, tiled=True)
    pack_shape = (blocks, rows, LANES)
    got = band_forward(
        slot_of, band_of, time_out.reshape(group_count * slots, quarter, dmodel), rnn1, pack_shape, parts, hidden
    )
    band_out, band_saved, rnn1 = got[0], got[1:8], got[8]
    band_out = band_out.reshape(group_count, outer, share, quarter, dmodel)
    if direct:
        back, grad_back, g_mask_vec = mask_exchange(mask_places, band_out, mine, v_band, base, piece_rows)
        back = lax.all_to_all(back, "stream", 0, 0, axis_index_groups=across, tiled=True)
        back = back.reshape((slots,) + back.shape[2:])
    else:
        band_out = lax.all_to_all(band_out, "stream", 1, 1, axis_index_groups=across, tiled=True)
        band_out = lax.all_to_all(band_out, "band", 0, 0, tiled=True)
        keep, send, grad_back, g_mask_vec = mask_network(
            mask_places, band_out, mine, other, v_band, base, piece_rows
        )
        grad_back = lax.all_to_all(grad_back, "band", 0, 0, tiled=True)
        grad_back = lax.all_to_all(grad_back, "stream", 1, 1, axis_index_groups=across, tiled=True)
        kept, sent = unpack_pieces(keep[:, :, :piece_rows], r), unpack_pieces(send, r)
        mask_reduced = return_slots(kept[0], sent[0], outer, inner, across, within, 1)
        widened_reduced = return_slots(kept[1], sent[1], outer, inner, across, within, 1).transpose(0, 2, 1)
        mask_parts = keep[:, :, piece_rows:]
        mask_parts = lax.all_to_all(mask_parts, "stream", 0, 0, axis_index_groups=across, tiled=True)
    grad_back = grad_back.reshape(group_count * slots, quarter, dmodel)
    band_grad, *g_rnn1 = band_backward(
        slot_of, band_of, grad_back, rnn1, band_saved, parts, hidden
    )
    grad_time = band_grad.reshape(group_count, slots, quarter, dmodel)
    if not direct:
        grad_time = lax.all_to_all(grad_time, "band", 0, 0, tiled=True)
    if direct:
        g_rnn1 = g_rnn1[:1] + [pass_along(g, "band", m) for m, g in enumerate(g_rnn1) if m]
    d_spec, g_split, g_rnn0 = time_backward(
        slot_places, clips, (my_stream // inner).astype(jnp.int32)[None], grad_time, spec, time_saved, w_split,
        v_band, rnn0, g_mask_vec, slot_rows, hidden,
    )
    if direct:
        dims = (slots, slot_rows, r, piece_rows, dmodel, hidden)
        state = tuple(x.transpose(0, 2, 1) if k % 8 == 1 else x for k, x in enumerate(state))
        scales, g_rnn0, g_rnn1, g_split, d_spec = finish(
            g_rnn0, g_split, g_rnn1, d_spec, back,
            tuple(x.reshape(2, -1, LANES) if k % 8 in (4, 5) else x for k, x in enumerate(state)),
            group_count, outer, dims,
        )
    else:
        d_spec = lax.psum(d_spec, "band")

    if not direct:
        masks = mask_parts.reshape(slots, frames, wide).transpose(1, 0, 2).reshape(cotangent.shape)
        spectrum_grad = d_spec.reshape(2, frames, padded)[:, :, :bins].transpose(1, 0, 2)

    if direct:
        *stepped, masks, spectrum_grad, grad_norm = update(scales, d_spec, (back, g_rnn0, g_rnn1, g_split), state, dims, bins)
        stepped = [x.transpose(0, 2, 1) if k % 8 == 1 else x for k, x in enumerate(stepped)]
        return (masks, spectrum_grad, grad_norm.reshape(())) + tuple(stepped)
    first, second = unpack_rnn(g_rnn0, dmodel, hidden), unpack_rnn(g_rnn1[0], dmodel, hidden)
    rnn_grads = [jnp.stack([a, b]) for a, b in zip(first[:3], second[:3])]
    rnn_grads.append(jnp.concatenate([first[3], second[3]], axis=0))
    rnn_grads = [
        lax.psum(lax.psum_scatter(g, "stream", scatter_dimension=d, tiled=True), "band")
        for g, d in zip(rnn_grads, (3, 3, 1, 1))
    ]
    g_band = unpack_banding(g_split, slots * slot_rows, slots, columns)
    g_split = g_split[:, : slots * slot_rows].reshape(blocks, slots, slot_rows, dmodel)
    g_split = g_split.transpose(1, 0, 2, 3).reshape(slots, wide, dmodel)
    split_reduced = lax.psum_scatter(g_split, "stream", scatter_dimension=1, tiled=True)
    band_reduced = lax.psum_scatter(g_band, "stream", scatter_dimension=1, tiled=True)
    reduced = (split_reduced, widened_reduced, mask_reduced, band_reduced) + tuple(rnn_grads)

    shares = (1.0,) * 4 + (1.0 / group_count,) * 4
    sizes = (group_count, stream_count)
    sums = [sum(jnp.sum(g * g) * part for g, part in zip(reduced, shares))]
    sums += [jnp.sum(w * w) * part for w, part in zip(weights, shares)]
    totals = sum_everywhere(jnp.stack(sums), sizes)
    grad_norm = jnp.sqrt(totals[0])
    factor = jnp.minimum(1.0, CLIP_NORM / grad_norm)
    moments = [lamb_moments(g, m, p, factor) for g, m, p in zip(reduced, means_old, powers_old)]
    directions = [lamb_direction(w, m, p, d) for w, (m, p), d in zip(weights, moments, DECAYS)]
    update_totals = sum_everywhere(
        jnp.stack([jnp.sum(d * d) * part for d, part in zip(directions, shares)]), sizes
    )
    ratios = jnp.sqrt(totals[1:]) / jnp.sqrt(update_totals + 1e-12)
    fresh = [w - LEARN_RATE * ratios[k] * d for k, (w, d) in enumerate(zip(weights, directions))]
    return (
        (masks, spectrum_grad, grad_norm)
        + tuple(fresh)
        + tuple(m for m, unused in moments)
        + tuple(p for unused, p in moments)
    )


def solution(mesh):
    stored = (
        P("band", "stream", None),
        P("band", None, "stream"),
        P("band", "stream", None),
        P("band", "stream"),
        P(None, None, None, "stream"),
        P(None, None, None, "stream"),
        P(None, "stream", None),
        P(None, "stream"),
    )
    frames_over = P("stream", None, None)
    mask_over = P("stream", "band", None, None)
    return jax.shard_map(
        body,
        mesh=mesh,
        in_specs=(frames_over, P("stream", None), P(), P(), mask_over) + stored * 3,
        out_specs=(mask_over, frames_over, P()) + stored * 3,
        check_vma=False,
    )
```
